32 devices in a mesh: dp: 16 (over z, y, x), mp: 2 (over core).
Axes of the slice: x: 2, y: 2, z: 4, core: 2. Of those that a mesh axis runs over, the one named last changes fastest.
Arguments:
- spectrogram: bfloat16 [64, 1024, 128], P(('dp', 'mp')), may hold values from -6 to 6
- keep: int32 [64, 154], P(('dp', 'mp')), may hold values from 0 to 511, as said below
- counts: int32 [64], P(('dp', 'mp')), may hold values from 51 to 154, as said below
- enc_qkv: float32 [768, 2304], P('dp'), may hold values from -0.21875 to 0.21875
- enc_out: float32 [768, 768], P('dp'), may hold values from -1.75 to 1.75
- enc_up: float32 [768, 3072], P('dp'), may hold values from -0.21875 to 0.21875
- enc_down: float32 [3072, 768], P('dp'), may hold values from -0.109375 to 0.109375
- dec_qkv: float32 [512, 1536], P('dp'), may hold values from -0.25 to 0.25
- dec_out: float32 [512, 512], P('dp'), may hold values from -1 to 1
- dec_up: float32 [512, 2048], P('dp'), may hold values from -0.25 to 0.25
- dec_down: float32 [2048, 512], P('dp'), may hold values from -0.125 to 0.125
- mom_enc_qkv: float32 [768, 2304], P('dp'), may hold values from -4.7683716e-06 to 4.7683716e-06
- mom_enc_out: float32 [768, 768], P('dp'), may hold values from -4.7683716e-06 to 4.7683716e-06
- mom_enc_up: float32 [768, 3072], P('dp'), may hold values from -4.7683716e-06 to 4.7683716e-06
- mom_enc_down: float32 [3072, 768], P('dp'), may hold values from -4.7683716e-06 to 4.7683716e-06
- mom_dec_qkv: float32 [512, 1536], P('dp'), may hold values from -4.7683716e-06 to 4.7683716e-06
- mom_dec_out: float32 [512, 512], P('dp'), may hold values from -4.7683716e-06 to 4.7683716e-06
- mom_dec_up: float32 [512, 2048], P('dp'), may hold values from -4.7683716e-06 to 4.7683716e-06
- mom_dec_down: float32 [2048, 512], P('dp'), may hold values from -4.7683716e-06 to 4.7683716e-06
- patch_maps: float32 [256, 1280], P('dp'), may hold values from -0.375 to 0.375
- patch_first: float32 [256, 1280], P('dp'), may hold values from -4.7683716e-06 to 4.7683716e-06
- patch_second: float32 [256, 1280], P('dp'), may hold values from 4.5601797e-15 to 1.8240719e-14
- embed_map: float32 [768, 512], P('dp'), may hold values from -0.21875 to 0.21875
- embed_first: float32 [768, 512], P('dp'), may hold values from -4.7683716e-06 to 4.7683716e-06
- embed_second: float32 [768, 512], P('dp'), may hold values from 4.5601797e-15 to 1.8240719e-14
- vectors: float32 [19968], P('dp'), may hold values from -4 to 4
- vector_first: float32 [19968], P('dp'), may hold values from -2.2888184e-05 to 2.2888184e-05
- vector_second: float32 [19968], P('dp'), may hold values from 1.1856468e-13 to 4.56018e-13
Outputs:
- loss_sum: float32 [], replicated
- mask_count: float32 [], replicated
- grad_norm: float32 [], replicated
- new_enc_qkv: float32 [768, 2304], P('dp')
- new_enc_out: float32 [768, 768], P('dp')
- new_enc_up: float32 [768, 3072], P('dp')
- new_enc_down: float32 [3072, 768], P('dp')
- new_dec_qkv: float32 [512, 1536], P('dp')
- new_dec_out: float32 [512, 512], P('dp')
- new_dec_up: float32 [512, 2048], P('dp')
- new_dec_down: float32 [2048, 512], P('dp')
- new_mom_enc_qkv: float32 [768, 2304], P('dp')
- new_mom_enc_out: float32 [768, 768], P('dp')
- new_mom_enc_up: float32 [768, 3072], P('dp')
- new_mom_enc_down: float32 [3072, 768], P('dp')
- new_mom_dec_qkv: float32 [512, 1536], P('dp')
- new_mom_dec_out: float32 [512, 512], P('dp')
- new_mom_dec_up: float32 [512, 2048], P('dp')
- new_mom_dec_down: float32 [2048, 512], P('dp')
- new_patch_maps: float32 [256, 1280], P('dp')
- new_patch_first: float32 [256, 1280], P('dp')
- new_patch_second: float32 [256, 1280], P('dp')
- new_embed_map: float32 [768, 512], P('dp')
- new_embed_first: float32 [768, 512], P('dp')
- new_embed_second: float32 [768, 512], P('dp')
- new_vectors: float32 [19968], P('dp')
- new_vector_first: float32 [19968], P('dp')
- new_vector_second: float32 [19968], P('dp')
The draws below stay inside these ranges and needn't reach their ends.
Inputs may be any that keep to these rules, and one draw needn't show every extreme that they name: `keep`: in each row the 154 entries are distinct patch numbers; only the first counts entries of a clip are visible. `counts`: some clip has exactly 154 visible patches in every draw.
All inputs are finite; a program needn't handle non-finite values.
Results may differ from the reference program's by a relative error of at most 0.011.
Values may be sent and summed in bfloat16 or wider, within the bound.
A program may use at most 256 MiB of HBM per device.

```python
import math
import jax
import jax.numpy as jnp
from jax import lax

D = 768
HEADS = 12
HEAD = 64
MLP = 3072
DD = 512
DHEADS = 16
DHEAD = 32
DMLP = 2048
PS = 16
GT = 64
GF = 8
WIN = 4
VIS = 154
NS_ITERS = 5
STEP = 10
PATCH = 256
SHIFT = 2
NPATCH = 512
FRAMES = 1024
MELS = 128
CLIPS = 64
NVEC = 19968
PARAMS = 10964480


def draw_keep(key, part):
    key = jax.random.fold_in(key, 11)
    clip_keys = jax.random.split(key, CLIPS)
    orders = jax.vmap(lambda clip_key: jax.random.permutation(clip_key, GT * GF))(clip_keys)
    return orders[:, :VIS].astype(jnp.int32)


def draw_counts(key, part):
    key = jax.random.fold_in(key, 12)
    first_key, second_key = jax.random.split(key)
    drawn = jax.random.randint(first_key, (CLIPS,), VIS // 3, VIS + 1)
    chosen = jax.random.randint(second_key, (), 0, CLIPS)
    return jnp.where(jnp.arange(CLIPS) == chosen, VIS, drawn).astype(jnp.int32)


def draw_vectors(key, part):
    key = jax.random.fold_in(key, 13)
    extents = [D] * 7 + [MLP] + [D] * 4 + [DD] * 9 + [DMLP] + [DD] * 3 + [PATCH]
    gain_slots = (0, 5, 9, 14, 19, 23)
    pieces = []
    for number, extent in enumerate(extents):
        piece_key = jax.random.fold_in(key, number)
        ramp = jnp.arange(extent, dtype=jnp.float32) / (extent - 1)
        if number in gain_slots:
            level = 0.6 * jnp.exp(ramp * jnp.log(3.0))
            pieces.append(level * jnp.exp(jax.random.uniform(piece_key, (extent,), jnp.float32, -0.2, 0.2)))
        elif number == 13:
            pieces.append(jnp.clip(jax.random.normal(piece_key, (extent,), jnp.float32), -4.0, 4.0))
        else:
            pieces.append(jnp.clip(0.2 * jax.random.normal(piece_key, (extent,), jnp.float32), -0.8, 0.8))
    return jnp.concatenate(pieces)


def block_levels(own_key, shape, cuts, least, largest):
    level, own = 1.0, jax.random.fold_in(own_key, 6)
    for dim, blocks in cuts:
        steps = jnp.exp(jax.random.uniform(jax.random.fold_in(own, dim), (blocks,), jnp.float32, least / len(cuts), largest / len(cuts)))
        level = level * jnp.repeat(steps, shape[dim] // blocks).reshape([-1 if axis == dim else 1 for axis in range(len(shape))])
    return level


def bell_draw(own_key, shape, scale, reach, shards=(), kind=jnp.bfloat16):
    gain = block_levels(own_key, shape, shards, -0.22, 0.18) if shards else 1.0
    result = jax.random.normal(own_key, shape, jnp.float32) * scale * gain
    return jnp.minimum(jnp.maximum(result, -reach), reach).astype(kind)


def setup_inputs(seed: int = 0) -> dict:
    seeds = jax.random.split(jax.random.key(seed), 29)
    return {
        "spectrogram": bell_draw(seeds[0], (CLIPS, FRAMES, MELS), 1.0, 6.0, ((0, 32),)),
        "keep": draw_keep(jax.random.fold_in(seeds[28], 71), 0),
        "counts": draw_counts(jax.random.fold_in(seeds[28], 71), 0),
        "enc_qkv": bell_draw(seeds[3], (D, 3 * D), D ** -0.5, 0.21875, ((0, 16),), jnp.float32),
        "enc_out": bell_draw(seeds[4], (D, D), (D // 64) ** -0.5, 1.75, ((0, 16),), jnp.float32),
        "enc_up": bell_draw(seeds[5], (D, MLP), D ** -0.5, 0.21875, ((0, 16),), jnp.float32),
        "enc_down": bell_draw(seeds[6], (MLP, D), MLP ** -0.5, 0.109375, ((0, 16),), jnp.float32),
        "dec_qkv": bell_draw(seeds[7], (DD, 3 * DD), DD ** -0.5, 0.25, ((0, 16),), jnp.float32),
        "dec_out": bell_draw(seeds[8], (DD, DD), (DD // 16) ** -0.5, 1.0, ((0, 16),), jnp.float32),
        "dec_up": bell_draw(seeds[9], (DD, DMLP), DD ** -0.5, 0.25, ((0, 16),), jnp.float32),
        "dec_down": bell_draw(seeds[10], (DMLP, DD), DMLP ** -0.5, 0.125, ((0, 16),), jnp.float32),
        "mom_enc_qkv": bell_draw(seeds[11], (D, 3 * D), (0.001 / PARAMS ** 0.5), 4.76837158203125e-06, ((0, 16),), jnp.float32),
        "mom_enc_out": bell_draw(seeds[12], (D, D), (0.001 / PARAMS ** 0.5), 4.76837158203125e-06, ((0, 16),), jnp.float32),
        "mom_enc_up": bell_draw(seeds[13], (D, MLP), (0.001 / PARAMS ** 0.5), 4.76837158203125e-06, ((0, 16),), jnp.float32),
        "mom_enc_down": bell_draw(seeds[14], (MLP, D), (0.001 / PARAMS ** 0.5), 4.76837158203125e-06, ((0, 16),), jnp.float32),
        "mom_dec_qkv": bell_draw(seeds[15], (DD, 3 * DD), (0.001 / PARAMS ** 0.5), 4.76837158203125e-06, ((0, 16),), jnp.float32),
        "mom_dec_out": bell_draw(seeds[16], (DD, DD), (0.001 / PARAMS ** 0.5), 4.76837158203125e-06, ((0, 16),), jnp.float32),
        "mom_dec_up": bell_draw(seeds[17], (DD, DMLP), (0.001 / PARAMS ** 0.5), 4.76837158203125e-06, ((0, 16),), jnp.float32),
        "mom_dec_down": bell_draw(seeds[18], (DMLP, DD), (0.001 / PARAMS ** 0.5), 4.76837158203125e-06, ((0, 16),), jnp.float32),
        "patch_maps": bell_draw(seeds[19], (PATCH, D + DD), PATCH ** -0.5, 0.375, ((0, 16),), jnp.float32),
        "patch_first": bell_draw(seeds[20], (PATCH, D + DD), (0.001 / PARAMS ** 0.5), 4.76837158203125e-06, ((0, 16),), jnp.float32),
        "patch_second": jnp.clip(jnp.exp(math.log(1.8240718993849797e-14) - 1.3862944 * jax.random.uniform(seeds[21], (PATCH, D + DD), jnp.float32) ** block_levels(seeds[21], (PATCH, D + DD), ((0, 16),), -0.2, 0.2)), 4.560179748462449e-15, 1.8240718993849797e-14),
        "embed_map": bell_draw(seeds[22], (D, DD), D ** -0.5, 0.21875, ((0, 16),), jnp.float32),
        "embed_first": bell_draw(seeds[23], (D, DD), (0.001 / PARAMS ** 0.5), 4.76837158203125e-06, ((0, 16),), jnp.float32),
        "embed_second": jnp.clip(jnp.exp(math.log(1.8240718993849797e-14) - 1.3862944 * jax.random.uniform(seeds[24], (D, DD), jnp.float32) ** block_levels(seeds[24], (D, DD), ((0, 16),), -0.2, 0.2)), 4.560179748462449e-15, 1.8240718993849797e-14),
        "vectors": draw_vectors(jax.random.fold_in(seeds[28], 71), 0),
        "vector_first": bell_draw(seeds[26], (NVEC,), (0.005 / PARAMS ** 0.5), 2.288818359375e-05, ((0, 16),), jnp.float32),
        "vector_second": jnp.clip(jnp.exp(math.log(4.560179816225085e-13) - 1.34707363 * jax.random.uniform(seeds[27], (NVEC,), jnp.float32) ** block_levels(seeds[27], (NVEC,), ((0, 16),), -0.2, 0.2)), 1.1856467684815547e-13, 4.560179816225085e-13),
    }


HIGH = lax.Precision.HIGHEST
CLIP_MAX = 0.001
LR_MUON = 0.1
LR_ADAM = 0.05
DECAY = 0.01
NS_A = 3.4445
NS_B = -4.775
NS_C = 2.0315

@jax.custom_vjp
def low(v):
    return lax.optimization_barrier(v.astype(jnp.bfloat16)).astype(jnp.float32)

@jax.custom_vjp
def low_back(v):
    return v

def low_keep(v):
    return (low(v), None)

def low_pass(kept, grad):
    return (grad,)

def back_keep(v):
    return (v, None)

def back_low(kept, grad):
    return (low(grad),)
low.defvjp(low_keep, low_pass)
low_back.defvjp(back_keep, back_low)

def product(inputs, matrix):
    return low_back(jnp.dot(low(inputs), matrix, precision=HIGH))

def score_product(queries, key_rows):
    return low_back(jnp.einsum('bqhd,bkhd->bhqk', low(queries), low(key_rows), precision=HIGH))

def value_product(softmax_rows, values):
    return low_back(jnp.einsum('bhqk,bkhd->bqhd', low(softmax_rows), low(values), precision=HIGH))

def unpack(vectors):
    extents = [D] * 7 + [MLP] + [D] * 4 + [DD] * 9 + [DMLP] + [DD] * 3 + [PATCH]
    pieces = []
    offset = 0
    for extent in extents:
        pieces.append(vectors[offset:offset + extent])
        offset += extent
    return pieces

def layer_norm(hidden, scaling, offset):
    centred = hidden - lax.optimization_barrier(jnp.mean(hidden, axis=-1, keepdims=True))
    variance = lax.optimization_barrier(jnp.mean(centred * centred, axis=-1, keepdims=True))
    return centred * lax.rsqrt(variance + 1e-06) * scaling + offset

def sinusoid(channels):
    quarter = channels // 4
    frequency = 1.0 / 10000.0 ** (jnp.arange(quarter, dtype=jnp.float32) / quarter)
    position = jnp.arange(GT * GF)
    time_rows = (position // GF).astype(jnp.float32)[:, None] * frequency
    freq_cols = (position % GF).astype(jnp.float32)[:, None] * frequency
    return jnp.concatenate([jnp.sin(time_rows), jnp.cos(time_rows), jnp.sin(freq_cols), jnp.cos(freq_cols)], axis=1)

def patchify(spec):
    clip_total = spec.shape[0]
    arranged = spec.reshape(clip_total, GT, PS, GF, PS).transpose(0, 1, 3, 2, 4)
    return arranged.reshape(clip_total, GT * GF, PS * PS)

def window_mask():
    time_rows = jnp.arange(GT)
    freq_cols = jnp.arange(GF)
    time_part = (time_rows >= GT - WIN).astype(jnp.int32) + (time_rows >= GT - SHIFT).astype(jnp.int32)
    freq_part = (freq_cols >= GF - WIN).astype(jnp.int32) + (freq_cols >= GF - SHIFT).astype(jnp.int32)
    region = time_part[:, None] * 3 + freq_part[None, :]
    region = region.reshape(GT // WIN, WIN, GF // WIN, WIN).transpose(0, 2, 1, 3).reshape(-1, WIN * WIN)
    return region[:, :, None] == region[:, None, :]

def to_windows(grid_rows):
    clip_total = grid_rows.shape[0]
    channels = grid_rows.shape[2]
    arranged = jnp.roll(grid_rows.reshape(clip_total, GT, GF, channels), (-SHIFT, -SHIFT), axis=(1, 2))
    arranged = arranged.reshape(clip_total, GT // WIN, WIN, GF // WIN, WIN, channels).transpose(0, 1, 3, 2, 4, 5)
    return arranged.reshape(-1, WIN * WIN, channels)

def from_windows(windows, clip_total):
    channels = windows.shape[-1]
    arranged = windows.reshape(clip_total, GT // WIN, GF // WIN, WIN, WIN, channels).transpose(0, 1, 3, 2, 4, 5)
    arranged = jnp.roll(arranged.reshape(clip_total, GT, GF, channels), (SHIFT, SHIFT), axis=(1, 2))
    return arranged.reshape(clip_total, GT * GF, channels)

def attend(queries, key_rows, values, allowed, scaling):
    scores = score_product(queries, key_rows) * scaling
    scores = jnp.where(allowed, scores, -1e+30)
    scores = scores - lax.optimization_barrier(jnp.max(scores, axis=-1, keepdims=True))
    exponent = jnp.exp(scores)
    softmax_rows = exponent / lax.optimization_barrier(jnp.sum(exponent, axis=-1, keepdims=True))
    return value_product(softmax_rows, values)

def encode(weights, patches, keep, counts):
    pieces = unpack(weights[10])
    clip_total = patches.shape[0]
    picked = jnp.take_along_axis(patches, keep[:, :, None], axis=1)
    hidden = product(picked, weights[8][:, :D]) + pieces[11] + sinusoid(D)[keep]
    normed = layer_norm(hidden, pieces[0], pieces[1])
    joined = product(normed, weights[0])
    queries = (joined[..., :D] + pieces[2]).reshape(clip_total, VIS, HEADS, HEAD)
    key_rows = joined[..., D:2 * D].reshape(clip_total, VIS, HEADS, HEAD)
    values = (joined[..., 2 * D:] + pieces[3]).reshape(clip_total, VIS, HEADS, HEAD)
    visible = (jnp.arange(VIS)[None, :] < counts[:, None])[:, None, None, :]
    attended = attend(queries, key_rows, values, visible, HEAD ** (-0.5)).reshape(clip_total, VIS, D)
    hidden = hidden + product(attended, weights[1]) + pieces[4]
    normed = layer_norm(hidden, pieces[5], pieces[6])
    inner = jax.nn.gelu(product(normed, weights[2]) + pieces[7], approximate=False)
    hidden = hidden + product(inner, weights[3]) + pieces[8]
    return layer_norm(hidden, pieces[9], pieces[10])

def decode(weights, latent, patches, keep, counts):
    pieces = unpack(weights[10])[12:]
    clip_total = latent.shape[0]
    placed = product(latent, weights[9]) + pieces[0]
    visible = jnp.arange(VIS)[None, :] < counts[:, None]
    target_rows = jnp.where(visible, keep, NPATCH)
    clip_rows = jnp.arange(clip_total)[:, None]
    filled = jnp.zeros((clip_total, NPATCH + 1, DD), jnp.float32).at[clip_rows, target_rows].add(placed)[:, :NPATCH]
    visible_cells = jnp.zeros((clip_total, NPATCH + 1), jnp.float32).at[clip_rows, target_rows].add(1.0)[:, :NPATCH]
    hidden = filled + (1.0 - visible_cells)[..., None] * pieces[1] + sinusoid(DD)
    normed = layer_norm(hidden, pieces[2], pieces[3])
    windows = to_windows(product(normed, weights[4]))
    queries = (windows[..., :DD] + pieces[4]).reshape(-1, WIN * WIN, DHEADS, DHEAD)
    key_rows = windows[..., DD:2 * DD].reshape(-1, WIN * WIN, DHEADS, DHEAD)
    values = (windows[..., 2 * DD:] + pieces[5]).reshape(-1, WIN * WIN, DHEADS, DHEAD)
    allowed = jnp.tile(window_mask(), (clip_total, 1, 1))[:, None, :, :]
    attended = attend(queries, key_rows, values, allowed, DHEAD ** (-0.5)).reshape(-1, WIN * WIN, DD)
    hidden = hidden + product(from_windows(attended, clip_total), weights[5]) + pieces[6]
    normed = layer_norm(hidden, pieces[7], pieces[8])
    inner = jax.nn.gelu(product(normed, weights[6]) + pieces[9], approximate=False)
    hidden = hidden + product(inner, weights[7]) + pieces[10]
    normed = layer_norm(hidden, pieces[11], pieces[12])
    predicted = product(normed, weights[8][:, D:].T) + pieces[13]
    centred = patches - lax.optimization_barrier(jnp.mean(patches, axis=-1, keepdims=True))
    target = centred * lax.rsqrt(lax.optimization_barrier(jnp.mean(centred * centred, axis=-1, keepdims=True)) + 1e-06)
    deviation = predicted - target
    patch_error = lax.optimization_barrier(jnp.mean(deviation * deviation, axis=-1))
    return jnp.sum((1.0 - visible_cells) * patch_error)

def group_loss(masters, spec_group, keep_group, count_group):
    patches = patchify(spec_group)
    rounded = tuple((low(weight) for weight in masters))
    latent = encode(rounded, patches, keep_group, count_group)
    return decode(rounded, latent, patches, keep_group, count_group)

def orthogonalize(matrix):
    upright = matrix.shape[0] > matrix.shape[1]
    iterate = matrix if upright else matrix.T
    iterate = iterate / (jnp.sqrt(jnp.sum(iterate * iterate)) + 1e-07)
    for iteration in range(NS_ITERS):
        gram_sum = jnp.dot(iterate.T, iterate, precision=HIGH)
        polynomial = NS_B * gram_sum + NS_C * jnp.dot(gram_sum, gram_sum, precision=HIGH)
        iterate = NS_A * iterate + jnp.dot(iterate, polynomial, precision=HIGH)
    return iterate if upright else iterate.T

def adam_update(weight, first_moment, second_moment, gradient, decay):
    first_moment = 0.5 * first_moment + 0.5 * gradient
    second_moment = 0.95 * second_moment + 0.05 * gradient * gradient
    direction = first_moment / (1.0 - 0.5 ** STEP) / (jnp.sqrt(second_moment / (1.0 - 0.95 ** STEP)) + 1e-08)
    return (weight - LR_ADAM * (direction + decay * weight), first_moment, second_moment)

def reference(spectrogram, keep, counts, enc_qkv, enc_out, enc_up, enc_down, dec_qkv, dec_out, dec_up, dec_down, mom_enc_qkv, mom_enc_out, mom_enc_up, mom_enc_down, mom_dec_qkv, mom_dec_out, mom_dec_up, mom_dec_down, patch_maps, patch_first, patch_second, embed_map, embed_first, embed_second, vectors, vector_first, vector_second):
    masters = (enc_qkv, enc_out, enc_up, enc_down, dec_qkv, dec_out, dec_up, dec_down, patch_maps, embed_map, vectors)
    moments = (mom_enc_qkv, mom_enc_out, mom_enc_up, mom_enc_down, mom_dec_qkv, mom_dec_out, mom_dec_up, mom_dec_down)
    mask_count = jnp.sum(NPATCH - counts).astype(jnp.float32)
    cotangent = 1.0 / mask_count
    groups = CLIPS // 8
    spec_groups = spectrogram.astype(jnp.float32).reshape(groups, 8, FRAMES, MELS)
    keep_groups = keep.reshape(groups, 8, VIS)
    count_groups = counts.reshape(groups, 8)

    def visit(carry, batch_part):
        running, gradients = carry
        group_value, pullback = jax.vjp(lambda params: group_loss(params, batch_part[0], batch_part[1], batch_part[2]), masters)
        group_grads, = pullback(cotangent)
        return ((running + group_value, jax.tree.map(jnp.add, gradients, group_grads)), None)
    initial = (jnp.zeros((), jnp.float32), tuple((jnp.zeros_like(weight) for weight in masters)))
    (loss_sum, gradients), unused = lax.scan(visit, initial, (spec_groups, keep_groups, count_groups))
    squares = jnp.zeros((), jnp.float32)
    for gradient in gradients:
        squares = squares + jnp.sum(gradient * gradient)
    grad_norm = jnp.sqrt(squares)
    factor = jnp.minimum(1.0, CLIP_MAX / (grad_norm + 1e-06))
    clipped = [gradient * factor for gradient in gradients]
    new_weights = []
    new_moments = []
    for number in range(8):
        renewed = 0.5 * moments[number] + clipped[number]
        height, breadth = masters[number].shape
        step_rate = LR_MUON * 0.2 * math.sqrt(max(height, breadth))
        new_weights.append(masters[number] * (1.0 - LR_MUON * DECAY) - step_rate * orthogonalize(renewed))
        new_moments.append(renewed)
    patch_new = adam_update(patch_maps, patch_first, patch_second, clipped[8], DECAY)
    embed_new = adam_update(embed_map, embed_first, embed_second, clipped[9], DECAY)
    vector_new = adam_update(vectors, vector_first, vector_second, clipped[10], 0.0)
    return (loss_sum, mask_count, grad_norm, new_weights[0], new_weights[1], new_weights[2], new_weights[3], new_weights[4], new_weights[5], new_weights[6], new_weights[7], new_moments[0], new_moments[1], new_moments[2], new_moments[3], new_moments[4], new_moments[5], new_moments[6], new_moments[7], patch_new[0], patch_new[1], patch_new[2], embed_new[0], embed_new[1], embed_new[2], vector_new[0], vector_new[1], vector_new[2])
```

```python
from functools import partial
import functools
import math

import jax
import jax.numpy as jnp
import numpy as np
from jax import lax
from jax.experimental import pallas as pl
from jax.experimental.pallas import tpu as pltpu
from jax.sharding import PartitionSpec as P

D = 768
HEADS = 12
HEAD = 64
MLP = 3072
DD = 512
DHEADS = 16
DHEAD = 32
DMLP = 2048
PS = 16
GT = 64
GF = 8
WIN = 4
VIS = 154
NS_ITERS = 5
STEP = 10
PATCH = 256
SHIFT = 2
NPATCH = 512


HIGH = lax.Precision.HIGHEST
CLIP_MAX = 0.001
LR_MUON = 0.1
LR_ADAM = 0.05
DECAY = 0.01
NS_A = 3.4445
NS_B = -4.775
NS_C = 2.0315
LONG_COLS = (True, True, True, False, True, True, True, False)


def shortened(x):
    return jax.tree.map(lambda a: a.astype(jnp.bfloat16) if a.dtype == jnp.float32 else a, x)


def narrow_core(value):
    return lax.optimization_barrier(value.astype(jnp.bfloat16)).astype(jnp.float32)


def narrow_keep(value):
    return (narrow_core(value), None)


def narrow_pass(kept, grad):
    return (grad,)


def same_core(value):
    return value


def same_keep(value):
    return (value, None)


def same_back(kept, grad):
    return (narrow_core(grad),)


def narrow(value):
    wrapped = jax.custom_vjp(narrow_core)
    wrapped.defvjp(narrow_keep, narrow_pass)
    return wrapped(value)


def narrow_grad(value):
    wrapped = jax.custom_vjp(same_core)
    wrapped.defvjp(same_keep, same_back)
    return wrapped(value)


def product(inputs, matrix):
    return narrow_grad(jnp.dot(narrow(inputs), narrow(matrix), preferred_element_type=jnp.float32))


def score_product(queries, key_rows):
    return narrow_grad(
        jnp.einsum(
            "bqhd,bkhd->bhqk", narrow(queries), narrow(key_rows), preferred_element_type=jnp.float32
        )
    )


def value_product(softmax_rows, values):
    return narrow_grad(
        jnp.einsum(
            "bhqk,bkhd->bqhd",
            narrow(softmax_rows),
            narrow(values),
            preferred_element_type=jnp.float32,
        )
    )


def unpack(vectors):
    extents = [D] * 7 + [MLP] + [D] * 4 + [DD] * 9 + [DMLP] + [DD] * 3 + [PATCH]
    pieces = []
    offset = 0
    for extent in extents:
        pieces.append(vectors[offset : offset + extent])
        offset += extent
    return pieces


def layer_norm(hidden, scaling, offset):
    centred = hidden - jnp.mean(hidden, axis=-1, keepdims=True)
    variance = jnp.mean(centred * centred, axis=-1, keepdims=True)
    return centred * lax.rsqrt(variance + 1e-06) * scaling + offset


def sinusoid(channels):
    quarter = channels // 4
    frequency = 1.0 / 10000.0 ** (jnp.arange(quarter, dtype=jnp.float32) / quarter)
    position = jnp.arange(GT * GF)
    time_rows = (position // GF).astype(jnp.float32)[:, None] * frequency
    freq_cols = (position % GF).astype(jnp.float32)[:, None] * frequency
    return jnp.concatenate(
        [jnp.sin(time_rows), jnp.cos(time_rows), jnp.sin(freq_cols), jnp.cos(freq_cols)], axis=1
    )


def patchify(spec):
    clip_total = spec.shape[0]
    arranged = spec.reshape(clip_total, GT, PS, GF, PS).transpose(0, 1, 3, 2, 4)
    return arranged.reshape(clip_total, GT * GF, PS * PS)


def window_mask():
    time_rows = jnp.arange(GT)
    freq_cols = jnp.arange(GF)
    time_part = (time_rows >= GT - WIN).astype(jnp.int32) + (time_rows >= GT - SHIFT).astype(
        jnp.int32
    )
    freq_part = (freq_cols >= GF - WIN).astype(jnp.int32) + (freq_cols >= GF - SHIFT).astype(
        jnp.int32
    )
    region = time_part[:, None] * 3 + freq_part[None, :]
    region = (
        region.reshape(GT // WIN, WIN, GF // WIN, WIN).transpose(0, 2, 1, 3).reshape(-1, WIN * WIN)
    )
    return region[:, :, None] == region[:, None, :]


def to_windows(grid_rows):
    clip_total = grid_rows.shape[0]
    channels = grid_rows.shape[2]
    arranged = jnp.roll(
        grid_rows.reshape(clip_total, GT, GF, channels), (-SHIFT, -SHIFT), axis=(1, 2)
    )
    arranged = arranged.reshape(clip_total, GT // WIN, WIN, GF // WIN, WIN, channels).transpose(
        0, 1, 3, 2, 4, 5
    )
    return arranged.reshape(-1, WIN * WIN, channels)


def from_windows(windows, clip_total):
    channels = windows.shape[-1]
    arranged = windows.reshape(clip_total, GT // WIN, GF // WIN, WIN, WIN, channels).transpose(
        0, 1, 3, 2, 4, 5
    )
    arranged = jnp.roll(arranged.reshape(clip_total, GT, GF, channels), (SHIFT, SHIFT), axis=(1, 2))
    return arranged.reshape(clip_total, GT * GF, channels)


def attend(queries, key_rows, values, allowed, scaling):
    scores = score_product(queries, key_rows) * scaling
    scores = jnp.where(allowed, scores, -1e30)
    scores = scores - jnp.max(scores, axis=-1, keepdims=True)
    exponent = jnp.exp(scores)
    softmax_rows = exponent / jnp.sum(exponent, axis=-1, keepdims=True)
    return value_product(softmax_rows, values)


def encode(weights, patches, keep, counts):
    pieces = unpack(weights[10])
    clip_total = patches.shape[0]
    picked = jnp.take_along_axis(patches, keep[:, :, None], axis=1)
    hidden = product(picked, weights[8][:, :D]) + pieces[11] + sinusoid(D)[keep]
    normed = layer_norm(hidden, pieces[0], pieces[1])
    joined = product(normed, weights[0])
    queries = (joined[..., :D] + pieces[2]).reshape(clip_total, VIS, HEADS, HEAD)
    key_rows = joined[..., D : 2 * D].reshape(clip_total, VIS, HEADS, HEAD)
    values = (joined[..., 2 * D :] + pieces[3]).reshape(clip_total, VIS, HEADS, HEAD)
    visible = (jnp.arange(VIS)[None, :] < counts[:, None])[:, None, None, :]
    attended = attend(queries, key_rows, values, visible, HEAD ** (-0.5)).reshape(
        clip_total, VIS, D
    )
    hidden = hidden + product(attended, weights[1]) + pieces[4]
    normed = layer_norm(hidden, pieces[5], pieces[6])
    inner = jax.nn.gelu(product(normed, weights[2]) + pieces[7], approximate=False)
    hidden = hidden + product(inner, weights[3]) + pieces[8]
    return layer_norm(hidden, pieces[9], pieces[10])


def decode(weights, latent, patches, keep, counts):
    pieces = unpack(weights[10])[12:]
    clip_total = latent.shape[0]
    placed = product(latent, weights[9]) + pieces[0]
    visible = jnp.arange(VIS)[None, :] < counts[:, None]
    target_rows = jnp.where(visible, keep, NPATCH)
    clip_rows = jnp.arange(clip_total)[:, None]
    filled = (
        jnp.zeros((clip_total, NPATCH + 1, DD), jnp.float32)
        .at[clip_rows, target_rows]
        .add(placed)[:, :NPATCH]
    )
    visible_cells = (
        jnp.zeros((clip_total, NPATCH + 1), jnp.float32)
        .at[clip_rows, target_rows]
        .add(1.0)[:, :NPATCH]
    )
    hidden = filled + (1.0 - visible_cells)[..., None] * pieces[1] + sinusoid(DD)
    normed = layer_norm(hidden, pieces[2], pieces[3])
    windows = to_windows(product(normed, weights[4]))
    queries = (windows[..., :DD] + pieces[4]).reshape(-1, WIN * WIN, DHEADS, DHEAD)
    key_rows = windows[..., DD : 2 * DD].reshape(-1, WIN * WIN, DHEADS, DHEAD)
    values = (windows[..., 2 * DD :] + pieces[5]).reshape(-1, WIN * WIN, DHEADS, DHEAD)
    allowed = jnp.tile(window_mask(), (clip_total, 1, 1))[:, None, :, :]
    attended = attend(queries, key_rows, values, allowed, DHEAD ** (-0.5)).reshape(
        -1, WIN * WIN, DD
    )
    hidden = hidden + product(from_windows(attended, clip_total), weights[5]) + pieces[6]
    normed = layer_norm(hidden, pieces[7], pieces[8])
    inner = jax.nn.gelu(product(normed, weights[6]) + pieces[9], approximate=False)
    hidden = hidden + product(inner, weights[7]) + pieces[10]
    normed = layer_norm(hidden, pieces[11], pieces[12])
    predicted = product(normed, weights[8][:, D:].T) + pieces[13]
    centred = patches - jnp.mean(patches, axis=-1, keepdims=True)
    target = centred * lax.rsqrt(jnp.mean(centred * centred, axis=-1, keepdims=True) + 1e-06)
    deviation = predicted - target
    patch_error = jnp.mean(deviation * deviation, axis=-1)
    return jnp.sum((1.0 - visible_cells) * patch_error)


def take_half(shard, number, core):
    if LONG_COLS[number]:
        extent = shard.shape[1] // 2
        return lax.dynamic_slice_in_dim(shard, core * extent, extent, 1)
    extent = shard.shape[0] // 2
    return lax.dynamic_slice_in_dim(shard, core * extent, extent, 0)


def arrange(gathered_half, number, long_max, short_max):
    upright = gathered_half.T if LONG_COLS[number] else gathered_half
    return jnp.pad(upright, ((0, long_max - upright.shape[0]), (0, short_max - upright.shape[1])))


def disperse(iterate, number, height, breadth, devices, flat_max):
    if LONG_COLS[number]:
        piece = iterate[: breadth // 2, :height].T.reshape(
            devices, height // devices * (breadth // 2)
        )
    else:
        piece = iterate[: height // 2, :breadth].reshape(devices, height // 2 // devices * breadth)
    return jnp.pad(piece, ((0, 0), (0, flat_max - piece.shape[1])))


def restore(row_piece, number, height, breadth, devices):
    if LONG_COLS[number]:
        return row_piece[: height // devices * (breadth // 2)].reshape(
            height // devices, breadth // 2
        )
    return row_piece[: height // 2 // devices * breadth].reshape(height // 2 // devices, breadth)


def adam_update(weight, first_moment, second_moment, gradient, decay):
    first_moment = 0.5 * first_moment + 0.5 * gradient
    second_moment = 0.95 * second_moment + 0.05 * gradient * gradient
    direction = (
        first_moment / (1.0 - 0.5**STEP) / (jnp.sqrt(second_moment / (1.0 - 0.95**STEP)) + 1e-08)
    )
    return (weight - LR_ADAM * (direction + decay * weight), first_moment, second_moment)


MESH_ID = pl.DeviceIdType.MESH
VEC_ROWS, VEC_COLS = 16, 256
GATHER_TURNS = (2, 2, 0, 1, 2, 0, 0, 1, 2, 1, 2)
REDUCE_TURNS = (2, 2, 0, 1, 2, 0, 0, 1, 0, 1, 2)
OWNERS = (0, 3, 5, 6, 8, 11, 13, 14)
SLOTS = 160


def bit_count(devices):
    return devices.bit_length() - 1


def bit_order(levels, turn):
    down = list(range(levels - 1, -1, -1))
    turn = turn % levels
    return down[levels - turn :] + down[: levels - turn]


def own_bits(levels):
    me = lax.axis_index("dp")
    return me, [lax.rem(lax.div(me, 2**bit), 2) for bit in range(levels)]


def place(levels, free, own, flip=None):
    spots = []
    for bit in range(levels - 1, -1, -1):
        if bit in free:
            spots.append(slice(None))
        elif bit == flip:
            spots.append(1 - own[bit])
        else:
            spots.append(own[bit])
    return tuple(spots)


def partner(me, own, bit):
    return me + (1 - 2 * own[bit]) * 2**bit


def greet(me, own, levels, core):
    barrier = pltpu.get_barrier_semaphore()
    for bit in range(levels):
        pl.semaphore_signal(
            barrier,
            inc=1,
            device_id={"dp": partner(me, own, bit), "mp": core},
            device_id_type=MESH_ID,
        )
    pl.semaphore_signal(barrier, inc=1, device_id={"dp": me, "mp": 1 - core}, device_id_type=MESH_ID)
    pl.semaphore_wait(barrier, levels + 1)


def add_up(me, own, core, levels, total, landing, send_sem, recv_sem):
    for stage in range(levels + 1):
        if stage < levels:
            to = {"dp": partner(me, own, stage), "mp": core}
        else:
            to = {"dp": me, "mp": 1 - core}
        swap = pltpu.make_async_remote_copy(
            src_ref=total,
            dst_ref=landing.at[stage],
            send_sem=send_sem.at[stage],
            recv_sem=recv_sem.at[stage],
            device_id=to,
            device_id_type=MESH_ID,
        )
        swap.start()
        swap.wait()
        total[...] = total[...] + landing[stage]


def gather_kernel(levels, turns, count, *refs):
    shards, tally = refs[:count], refs[count]
    wholes, tally_out = refs[count + 1 : 2 * count + 1], refs[2 * count + 1]
    here_sem, send_sem, recv_sem, cross_send, cross_recv = refs[2 * count + 2 : 2 * count + 7]
    tally_land, tally_send, tally_recv = refs[2 * count + 7 :]
    me, own = own_bits(levels)
    core = lax.axis_index("mp")
    greet(me, own, levels, core)
    orders = [bit_order(levels, turn) for turn in turns]

    def half(number, which):
        width = shards[number].shape[1] // 2
        return (slice(None), pl.ds(pl.multiple_of(which * width, 128), width))

    def hop(number, stage, flip):
        order = orders[number]
        spot = place(levels, order[:stage], own, order[stage] if flip else None)
        target = wholes[number].at[spot + half(number, core)]
        source = target if stage or flip else shards[number].at[half(number, core)]
        return pltpu.make_async_remote_copy(
            src_ref=source,
            dst_ref=target,
            send_sem=send_sem.at[number, stage],
            recv_sem=recv_sem.at[number, stage],
            device_id={"dp": partner(me, own, order[stage]), "mp": core},
            device_id_type=MESH_ID,
        )

    def cross(number, stage, which):
        order = orders[number]
        spot = place(levels, order[:stage], own, order[stage])
        target = wholes[number].at[spot + half(number, which)]
        return pltpu.make_async_remote_copy(
            src_ref=target,
            dst_ref=target,
            send_sem=cross_send.at[number, stage],
            recv_sem=cross_recv.at[number, stage],
            device_id={"dp": me, "mp": 1 - core},
            device_id_type=MESH_ID,
        )

    def keep(number):
        spot = place(levels, (), own)
        return pltpu.make_async_copy(shards[number], wholes[number].at[spot], here_sem.at[number])

    for number in range(count):
        hop(number, 0, False).start()
    for number in range(count):
        keep(number).start()
    tally_out[...] = tally[...]
    add_up(me, own, core, levels, tally_out, tally_land, tally_send, tally_recv)
    for number in range(count):
        keep(number).wait()
    for stage in range(levels):
        for number in range(count):
            hop(number, stage, True).wait_recv()
            if stage + 1 < levels:
                hop(number, stage + 1, False).start()
            cross(number, stage, core).start()
    for stage in range(levels):
        for number in range(count):
            hop(number, stage, False).wait_send()
            cross(number, stage, core).wait_send()
            cross(number, stage, 1 - core).wait_recv()


def gather_rows(shards, tally, devices, turns):
    levels, count = bit_count(devices), len(shards)
    lead = (2,) * levels
    dma = pltpu.SemaphoreType.DMA
    vmem = pl.BlockSpec(memory_space=pltpu.VMEM)
    found = pl.pallas_call(
        functools.partial(gather_kernel, levels, turns, count),
        out_shape=[jax.ShapeDtypeStruct(lead + shard.shape, shard.dtype) for shard in shards]
        + [jax.ShapeDtypeStruct((8, 128), jnp.float32)],
        in_specs=[pl.BlockSpec(memory_space=pl.ANY)] * count + [vmem],
        out_specs=[pl.BlockSpec(memory_space=pl.ANY)] * count + [vmem],
        scratch_shapes=[dma((count,))]
        + [dma((count, levels))] * 4
        + [pltpu.VMEM((levels + 1, 8, 128), jnp.float32)]
        + [dma((levels + 1,))] * 2,
        compiler_params=pltpu.CompilerParams(collective_id=1, has_side_effects=True),
        name="gather_rows",
    )(*shards, tally)
    return found[:count], found[count]


def reduce_kernel(levels, turns, count, *refs):
    grads, stats_in = refs[:count], refs[count]
    sums, stats_out = refs[count + 1 : 2 * count + 1], refs[2 * count + 1]
    rest = refs[2 * count + 2 :]
    mine, theirs, rest = rest[:count], rest[count : 2 * count], rest[2 * count :]
    kept, rest = rest[:count], rest[count:]
    landing, rest = rest[: count * levels], rest[count * levels :]
    stats_land, here_sem, pair_send, pair_recv, send_sem, recv_sem, last_send, last_recv, stats_send, stats_recv = rest
    me, own = own_bits(levels)
    core = lax.axis_index("mp")
    greet(me, own, levels, core)
    orders = [bit_order(levels, turn)[::-1] for turn in turns]

    def half(number, which):
        width = grads[number].shape[-1] // 2
        return (slice(None), pl.ds(pl.multiple_of(which * width, 128), width))

    every = (slice(None),) * levels

    def pair(number):
        return pltpu.make_async_remote_copy(
            src_ref=grads[number].at[every + half(number, 1 - core)],
            dst_ref=theirs[number],
            send_sem=pair_send.at[number],
            recv_sem=pair_recv.at[number],
            device_id={"dp": me, "mp": 1 - core},
            device_id_type=MESH_ID,
        )

    def load(number):
        return pltpu.make_async_copy(
            grads[number].at[every + half(number, core)], mine[number], here_sem.at[number]
        )

    def hop(number, stage):
        order = orders[number]
        spot = place(levels, order[stage + 1 :], own, order[stage])
        return pltpu.make_async_remote_copy(
            src_ref=theirs[number].at[spot],
            dst_ref=landing[number * levels + stage],
            send_sem=send_sem.at[number, stage],
            recv_sem=recv_sem.at[number, stage],
            device_id={"dp": partner(me, own, order[stage]), "mp": core},
            device_id_type=MESH_ID,
        )

    def share(number, which):
        region = sums[number].at[half(number, which)]
        return pltpu.make_async_remote_copy(
            src_ref=region,
            dst_ref=region,
            send_sem=last_send.at[number],
            recv_sem=last_recv.at[number],
            device_id={"dp": me, "mp": 1 - core},
            device_id_type=MESH_ID,
        )

    def fold(number, stage):
        order = orders[number]
        free = order[stage:]
        loose = [bit for bit in range(levels - 1, -1, -1) if bit in free and bit != order[stage]]

        @pl.loop(0, 2 ** len(loose))
        def add_block(block):
            found = {
                bit: lax.rem(lax.div(block, 2 ** (len(loose) - 1 - i)), 2) for i, bit in enumerate(loose)
            }

            def total(way):
                now = dict(found)
                now[order[stage]] = way
                full = tuple(now.get(bit, own[bit]) for bit in range(levels - 1, -1, -1))
                if stage == 0:
                    value = mine[number][full].astype(jnp.float32) + theirs[number][full].astype(jnp.float32)
                else:
                    spot = tuple(
                        now.get(bit, own[bit]) for bit in range(levels - 1, -1, -1) if bit != order[0]
                    )
                    land = tuple(now[bit] for bit in range(levels - 1, -1, -1) if bit in free)
                    value = kept[number][spot] + landing[number * levels + stage - 1][land].astype(jnp.float32)
                return full, value

            full, value = total(1 - own[order[stage]])
            theirs[number][full] = value.astype(theirs[number].dtype)
            full, value = total(own[order[stage]])
            spot = tuple(
                found.get(bit, own[bit]) for bit in range(levels - 1, -1, -1) if bit != order[0]
            )
            kept[number][spot] = value

    for number in range(count):
        pair(number).start()
        load(number).start()
    for number in range(count):
        load(number).wait()
        pair(number).wait_recv()
        fold(number, 0)
        hop(number, 0).start()
    for stage in range(levels - 1):
        for number in range(count):
            hop(number, stage).wait_recv()
            fold(number, stage + 1)
            hop(number, stage + 1).start()
    squares = jnp.zeros((8, 128), jnp.float32)
    for number in range(count):
        hop(number, levels - 1).wait_recv()
        spot = tuple(own[bit] for bit in range(levels - 1, -1, -1) if bit != orders[number][0])
        total = kept[number][spot] + landing[number * levels + levels - 1][...].astype(jnp.float32)
        sums[number][half(number, core)] = total
        share(number, core).start()
        rows, width = total.shape
        for row in range(0, rows, 8):
            for column in range(0, width, 128):
                part = total[row : row + 8, column : column + 128]
                squares = squares + part * part
    stats_out[0:8, :] = squares
    stats_out[8:16, :] = stats_in[...]
    add_up(me, own, core, levels, stats_out, stats_land, stats_send, stats_recv)
    for number in range(count):
        pair(number).wait_send()
        for stage in range(levels):
            hop(number, stage).wait_send()
        share(number, core).wait_send()
        share(number, 1 - core).wait_recv()


def reduce_rows(grads, stats, devices, turns):
    levels, count = bit_count(devices), len(grads)
    lead = (2,) * levels
    dma = pltpu.SemaphoreType.DMA
    shapes = [grad.shape[levels:] for grad in grads]
    halves = [(rows, columns // 2) for rows, columns in shapes]
    kinds = [grad.dtype for grad in grads]
    scratch = [pltpu.VMEM(lead + shape, kind) for shape, kind in zip(halves, kinds)] * 2
    scratch += [pltpu.VMEM(lead[1:] + shape, jnp.float32) for shape in halves]
    for shape, kind in zip(halves, kinds):
        for stage in range(levels):
            scratch.append(pltpu.VMEM((2,) * (levels - 1 - stage) + shape, kind))
    scratch.append(pltpu.VMEM((levels + 1, 16, 128), jnp.float32))
    scratch += [dma((count,))] * 3 + [dma((count, levels))] * 2 + [dma((count,))] * 2
    scratch += [dma((levels + 1,))] * 2
    vmem = pl.BlockSpec(memory_space=pltpu.VMEM)
    found = pl.pallas_call(
        functools.partial(reduce_kernel, levels, turns, count),
        out_shape=[jax.ShapeDtypeStruct(shape, jnp.float32) for shape in shapes]
        + [jax.ShapeDtypeStruct((16, 128), jnp.float32)],
        in_specs=[pl.BlockSpec(memory_space=pl.ANY)] * count + [vmem],
        out_specs=[vmem] * (count + 1),
        scratch_shapes=scratch,
        compiler_params=pltpu.CompilerParams(
            collective_id=2, has_side_effects=True, vmem_limit_bytes=56 * 2**20
        ),
        name="reduce_rows",
    )(*grads, stats)
    return found[:count], found[count]
def send_kernel(owners, count, devices, *refs):
    rows, wholes = refs[:count], refs[count : 2 * count]
    here_sem, send_sem, recv_sem, cross_send, cross_recv = refs[2 * count :]
    me, core = lax.axis_index("dp"), lax.axis_index("mp")
    barrier = pltpu.get_barrier_semaphore()
    owning = functools.reduce(jnp.logical_or, [me == owner for owner in owners])

    @pl.when(owning)
    def greet_all():
        @pl.loop(0, devices)
        def greet_one(other):
            @pl.when(other != me)
            def signal_one():
                pl.semaphore_signal(
                    barrier, inc=1, device_id={"dp": other, "mp": core}, device_id_type=MESH_ID
                )

        pl.semaphore_signal(
            barrier, inc=1, device_id={"dp": me, "mp": 1 - core}, device_id_type=MESH_ID
        )
        pl.semaphore_wait(barrier, count)

    @pl.when(jnp.logical_not(owning))
    def wait_owners():
        pl.semaphore_wait(barrier, count)

    def half(number, which):
        width = rows[number].shape[1] // 2
        return (slice(None), pl.ds(pl.multiple_of(which * width, 128), width))

    def hop(number, source):
        return pltpu.make_async_remote_copy(
            src_ref=rows[number].at[half(number, core)],
            dst_ref=wholes[number].at[(source,) + half(number, core)],
            send_sem=send_sem.at[number],
            recv_sem=recv_sem.at[number, source],
            device_id={"dp": owners[number], "mp": core},
            device_id_type=MESH_ID,
        )

    def cross(number, source, which):
        region = wholes[number].at[(source,) + half(number, which)]
        return pltpu.make_async_remote_copy(
            src_ref=region,
            dst_ref=region,
            send_sem=cross_send.at[number, source],
            recv_sem=cross_recv.at[number, source],
            device_id={"dp": me, "mp": 1 - core},
            device_id_type=MESH_ID,
        )

    for number in range(count):

        @pl.when(me != owners[number])
        def start_one(number=number):
            hop(number, me).start()

    for number in range(count):

        @pl.when(me == owners[number])
        def collect(number=number):
            own = pltpu.make_async_copy(rows[number], wholes[number].at[me], here_sem)
            own.start()

            @pl.loop(0, devices)
            def forward(source):
                @pl.when(source != me)
                def forward_one():
                    hop(number, source).wait_recv()
                    cross(number, source, core).start()

            own.wait()

            @pl.loop(0, devices)
            def finish(source):
                @pl.when(source != me)
                def finish_one():
                    cross(number, source, core).wait_send()
                    cross(number, source, 1 - core).wait_recv()

    for number in range(count):

        @pl.when(me != owners[number])
        def end_one(number=number):
            hop(number, me).wait_send()


def send_to_owners(rows, owners, devices):
    count = len(rows)
    dma = pltpu.SemaphoreType.DMA
    return pl.pallas_call(
        functools.partial(send_kernel, owners, count, devices),
        out_shape=[jax.ShapeDtypeStruct((devices,) + row.shape, row.dtype) for row in rows],
        in_specs=[pl.BlockSpec(memory_space=pl.ANY)] * count,
        out_specs=[pl.BlockSpec(memory_space=pl.ANY)] * count,
        scratch_shapes=[dma, dma((count,))] + [dma((count, devices))] * 3,
        compiler_params=pltpu.CompilerParams(collective_id=3, has_side_effects=True),
        name="send_to_owners",
    )(*rows)


def return_kernel(owners, count, devices, *refs):
    wholes, rows = refs[:count], refs[count : 2 * count]
    here_sem, send_sem, recv_sem, cross_send, cross_recv = refs[2 * count :]
    me, core = lax.axis_index("dp"), lax.axis_index("mp")
    barrier = pltpu.get_barrier_semaphore()
    owning = functools.reduce(jnp.logical_or, [me == owner for owner in owners])
    for owner in owners:

        @pl.when(me != owner)
        def greet_owner(owner=owner):
            pl.semaphore_signal(
                barrier, inc=1, device_id={"dp": owner, "mp": core}, device_id_type=MESH_ID
            )

    pl.semaphore_signal(barrier, inc=1, device_id={"dp": me, "mp": 1 - core}, device_id_type=MESH_ID)

    @pl.when(owning)
    def wait_all():
        pl.semaphore_wait(barrier, devices)

    @pl.when(jnp.logical_not(owning))
    def wait_pair():
        pl.semaphore_wait(barrier, 1)

    def half(number, which):
        width = rows[number].shape[1] // 2
        return (slice(None), pl.ds(pl.multiple_of(which * width, 128), width))

    def hop(number, target):
        return pltpu.make_async_remote_copy(
            src_ref=wholes[number].at[(target,) + half(number, core)],
            dst_ref=rows[number].at[half(number, core)],
            send_sem=send_sem.at[number, target],
            recv_sem=recv_sem.at[number],
            device_id={"dp": target, "mp": core},
            device_id_type=MESH_ID,
        )

    def cross(number, which):
        region = rows[number].at[half(number, which)]
        return pltpu.make_async_remote_copy(
            src_ref=region,
            dst_ref=region,
            send_sem=cross_send.at[number],
            recv_sem=cross_recv.at[number],
            device_id={"dp": me, "mp": 1 - core},
            device_id_type=MESH_ID,
        )

    for number in range(count):

        @pl.when(me == owners[number])
        def hand_out(number=number):
            own = pltpu.make_async_copy(
                wholes[number].at[(me,) + half(number, core)], rows[number].at[half(number, core)], here_sem
            )
            own.start()

            @pl.loop(0, devices)
            def start_one(target):
                @pl.when(target != me)
                def start_other():
                    hop(number, target).start()

            own.wait()

    for number in range(count):

        @pl.when(me != owners[number])
        def arrive(number=number):
            hop(number, me).wait_recv()

        cross(number, core).start()
    for number in range(count):
        cross(number, core).wait_send()
        cross(number, 1 - core).wait_recv()

        @pl.when(me == owners[number])
        def end_out(number=number):
            @pl.loop(0, devices)
            def end_one(target):
                @pl.when(target != me)
                def end_other():
                    hop(number, target).wait_send()


def return_rows(wholes, owners, devices):
    count = len(wholes)
    dma = pltpu.SemaphoreType.DMA
    return pl.pallas_call(
        functools.partial(return_kernel, owners, count, devices),
        out_shape=[jax.ShapeDtypeStruct(whole.shape[1:], whole.dtype) for whole in wholes],
        in_specs=[pl.BlockSpec(memory_space=pl.ANY)] * count,
        out_specs=[pl.BlockSpec(memory_space=pltpu.VMEM)] * count,
        scratch_shapes=[dma, dma((count, devices)), dma((count,)), dma((count,)), dma((count,))],
        compiler_params=pltpu.CompilerParams(collective_id=4, has_side_effects=True),
        name="return_rows",
    )(*wholes)


def muon_kernel(owners, shapes, *refs):
    count = len(owners)
    mats, outs = refs[:count], refs[count : 2 * count]
    exact, wide, wide_low, tall, wide_out, tall_out, gram, square, poly, chain, left, right, sem = refs[2 * count :]
    me, core = lax.axis_index("dp"), lax.axis_index("mp")
    side = gram.shape[0]
    step = 256
    bf = jnp.bfloat16

    def dims(number):
        height, breadth = shapes[number]
        return height, breadth, LONG_COLS[number]

    def span(index):
        return pl.ds(pl.multiple_of(index * step, step), step)

    def split(value):
        high = value.astype(bf)
        return high, (value - high.astype(jnp.float32)).astype(bf)

    gram[...] = jnp.zeros_like(gram)
    for number in range(count):

        @pl.when(me == owners[number])
        def start(number=number):
            height, breadth, long_cols = dims(number)
            short = min(height, breadth)
            held = (wide if long_cols else tall).at[:height, :breadth]
            fine = mats[number].dtype == jnp.float32
            load = pltpu.make_async_copy(mats[number], exact if fine else held, sem)
            load.start()
            load.wait()
            if fine:
                rest = wide_low

                @pl.loop(0, height // step)
                def part_rows(index):
                    high, low = split(exact[span(index), :])
                    held[span(index), :] = high
                    rest[span(index), :] = low

            @pl.loop(0, short // step)
            def gram_rows(index):
                if long_cols:
                    part = held[span(index), :]
                    dims_in = (((1,), (1,)), ((), ()))
                else:
                    part = held[:, span(index)]
                    dims_in = (((0,), (0,)), ((), ()))
                total = lax.dot_general(part, held[...], dims_in, preferred_element_type=jnp.float32)
                if fine:
                    total = total + lax.dot_general(
                        part, rest[...], dims_in, preferred_element_type=jnp.float32
                    )
                    total = total + lax.dot_general(
                        rest[span(index), :], held[...], dims_in, preferred_element_type=jnp.float32
                    )
                gram[span(index), :short] = total

    owning = functools.reduce(jnp.logical_or, [me == owner for owner in owners])

    @pl.when(owning)
    def iterate():
        def eye(index):
            row = lax.broadcasted_iota(jnp.int32, (step, side), 0) + index * step
            column = lax.broadcasted_iota(jnp.int32, (step, side), 1)
            return row == column

        trace = jnp.float32(0.0)
        for index in range(side // step):
            trace = trace + jnp.sum(jnp.where(eye(index), gram[index * step : (index + 1) * step, :], 0.0))
        scale = 1.0 / (jnp.sqrt(jnp.full((8, 128), trace, jnp.float32)) + 1e-07)
        scale = scale[0:1, 0:1]
        square_scale = scale * scale

        @pl.loop(0, side // step)
        def prepare(index):
            gram[span(index), :] = gram[span(index), :] * square_scale

        def set_left(source):
            @pl.loop(0, side // step)
            def set_rows(index):
                high, low = split(source[span(index), :])
                left[span(index), 0:side] = high
                left[span(index), side : 2 * side] = high
                left[span(index), 2 * side : 3 * side] = low

        def set_right(source):
            @pl.loop(0, side // step)
            def set_rows(index):
                high, low = split(source[span(index), :])
                right[pl.ds(pl.multiple_of(index * step, step), step), :] = high
                right[pl.ds(pl.multiple_of(side + index * step, step), step), :] = low
                right[pl.ds(pl.multiple_of(2 * side + index * step, step), step), :] = high

        def multiply(target):
            @pl.loop(0, side // step)
            def rows(index):
                target[span(index), :] = jnp.dot(
                    left[span(index), :], right[...], preferred_element_type=jnp.float32
                )

        @pl.loop(0, NS_ITERS)
        def newton(iteration):
            set_left(gram)
            set_right(gram)
            multiply(square)

            @pl.loop(0, side // step)
            def polynomial(index):
                ones = jnp.where(
                    lax.broadcasted_iota(jnp.int32, (step, side), 0) + index * step
                    == lax.broadcasted_iota(jnp.int32, (step, side), 1),
                    NS_A,
                    0.0,
                )
                poly[span(index), :] = ones + NS_B * gram[span(index), :] + NS_C * square[span(index), :]

            set_right(poly)

            @pl.when(iteration < NS_ITERS - 1)
            def advance():
                multiply(square)
                set_left(square)
                multiply(gram)

            @pl.when(iteration == 0)
            def first():
                chain[...] = poly[...]

            @pl.when(iteration > 0)
            def later():
                set_left(chain)
                multiply(chain)

        @pl.loop(0, side // step)
        def finish(index):
            high, low = split(chain[span(index), :] * scale)
            left[span(index), 0:side] = high
            left[span(index), side : 2 * side] = low

    for number in range(count):

        @pl.when(me == owners[number])
        def end(number=number):
            height, breadth, long_cols = dims(number)
            short = min(height, breadth)
            width = breadth // 2
            part = pl.ds(pl.multiple_of(core * width, 128), width)
            if long_cols:
                held, made = wide.at[:height, :breadth], wide_out.at[:height, :width]

                @pl.loop(0, height // step)
                def wide_rows(index):
                    total = jnp.dot(
                        left[span(index), :short], held[:, part], preferred_element_type=jnp.float32
                    ) + jnp.dot(
                        left[span(index), side : side + short],
                        held[:, part],
                        preferred_element_type=jnp.float32,
                    )
                    if mats[number].dtype == jnp.float32:
                        total = total + jnp.dot(
                            left[span(index), :short],
                            wide_low[:, part],
                            preferred_element_type=jnp.float32,
                        )
                    made[span(index), :] = total.astype(bf)
            else:
                held, made = tall.at[:height, :breadth], tall_out.at[:height, :width]

                @pl.loop(0, height // step)
                def tall_rows(index):
                    low = pl.ds(pl.multiple_of(side + core * width, 128), width)
                    total = jnp.dot(
                        held[span(index), :], left[:short, part], preferred_element_type=jnp.float32
                    ) + jnp.dot(
                        held[span(index), :], left[:short, low], preferred_element_type=jnp.float32
                    )
                    made[span(index), :] = total.astype(bf)

            save = pltpu.make_async_copy(made, outs[number].at[:, part], sem)
            save.start()
            save.wait()


def orthogonalize(mats, owners):
    count = len(mats)
    shapes = [mat.shape for mat in mats]
    side = max(min(shape) for shape in shapes)
    longest = max(max(shape) for shape in shapes)
    square = pltpu.VMEM((side, side), jnp.float32)
    (fine,) = [mat.shape for mat in mats if mat.dtype == jnp.float32]
    return pl.pallas_call(
        functools.partial(muon_kernel, owners, shapes),
        out_shape=[jax.ShapeDtypeStruct(shape, jnp.bfloat16) for shape in shapes],
        in_specs=[pl.BlockSpec(memory_space=pl.ANY)] * count,
        out_specs=[pl.BlockSpec(memory_space=pl.ANY)] * count,
        scratch_shapes=[
            pltpu.VMEM(fine, jnp.float32),
            pltpu.VMEM((side, longest), jnp.bfloat16),
            pltpu.VMEM(fine, jnp.bfloat16),
            pltpu.VMEM((longest, side), jnp.bfloat16),
            pltpu.VMEM((side, longest // 2), jnp.bfloat16),
            pltpu.VMEM((longest, side // 2), jnp.bfloat16),
            square,
            square,
            square,
            square,
            pltpu.VMEM((side, 3 * side), jnp.bfloat16),
            pltpu.VMEM((3 * side, side), jnp.bfloat16),
            pltpu.SemaphoreType.DMA,
        ],
        compiler_params=pltpu.CompilerParams(vmem_limit_bytes=56 * 2**20),
        name="orthogonalize",
    )(*mats)


def window_place(position):
    time_row = (position // GF + GT - SHIFT) % GT
    freq_col = (position % GF + GF - SHIFT) % GF
    window = (time_row // WIN) * (GF // WIN) + freq_col // WIN
    return window * (WIN * WIN) + (time_row % WIN) * WIN + freq_col % WIN


def window_sinusoid(channels):
    quarter = channels // 4
    frequency = 1.0 / 10000.0 ** (np.arange(quarter) / quarter)
    position = np.arange(NPATCH)
    time_rows = (position // GF)[:, None] * frequency
    freq_cols = (position % GF)[:, None] * frequency
    table = np.concatenate([np.sin(time_rows), np.cos(time_rows), np.sin(freq_cols), np.cos(freq_cols)], axis=1)
    moved = np.zeros_like(table)
    moved[window_place(position)] = table
    return moved.astype(np.float32)


def window_patches(spec):
    grid = spec.reshape(spec.shape[0], GT, PS, GF, PS)
    grid = jnp.roll(grid, (-SHIFT, -SHIFT), axis=(1, 3))
    grid = grid.reshape(spec.shape[0], GT // WIN, WIN, PS, GF // WIN, WIN, PS)
    return grid.transpose(0, 1, 4, 2, 5, 3, 6).reshape(spec.shape[0], NPATCH, PATCH)


@jax.custom_vjp
def times(inputs, matrix):
    return jnp.dot(inputs.astype(jnp.bfloat16), matrix.astype(jnp.bfloat16), preferred_element_type=jnp.float32)


def times_keep(inputs, matrix):
    short = inputs.astype(jnp.bfloat16)
    return jnp.dot(short, matrix.astype(jnp.bfloat16), preferred_element_type=jnp.float32), (short, matrix)


def times_back(kept, grad):
    short, matrix = kept
    grad = grad.astype(jnp.bfloat16)
    back = lax.dot_general(
        grad, matrix.astype(jnp.bfloat16), (((1,), (1,)), ((), ())), preferred_element_type=jnp.float32
    )
    gain = lax.dot_general(short, grad, (((0,), (0,)), ((), ())), preferred_element_type=jnp.float32)
    return back, gain.astype(matrix.dtype)


times.defvjp(times_keep, times_back)


def pair_product(spec, left_spec, right_spec):
    @jax.custom_vjp
    def apply(left, right):
        return jnp.einsum(
            spec, left.astype(jnp.bfloat16), right.astype(jnp.bfloat16), preferred_element_type=jnp.float32
        )

    def keep(left, right):
        left, right = left.astype(jnp.bfloat16), right.astype(jnp.bfloat16)
        return jnp.einsum(spec, left, right, preferred_element_type=jnp.float32), (left, right)

    def back(kept, grad):
        left, right = kept
        grad = grad.astype(jnp.bfloat16)
        return (
            jnp.einsum(left_spec, grad, right, preferred_element_type=jnp.float32),
            jnp.einsum(right_spec, grad, left, preferred_element_type=jnp.float32),
        )

    apply.defvjp(keep, back)
    return apply


scores_of = pair_product("bqhd,bkhd->bhqk", "bhqk,bkhd->bqhd", "bhqk,bqhd->bkhd")
mix_of = pair_product("bhqk,bkhd->bqhd", "bqhd,bkhd->bhqk", "bqhd,bhqk->bkhd")


def attend_short(queries, key_rows, values, allowed, scaling):
    scores = scores_of(queries, key_rows) * scaling
    scores = jnp.where(allowed, scores, -1e30)
    scores = scores - jnp.max(scores, axis=-1, keepdims=True)
    exponent = jnp.exp(scores)
    return mix_of(exponent / jnp.sum(exponent, axis=-1, keepdims=True), values)


def local_loss(weights, patches, keep, counts):
    clips = patches.shape[0]
    pieces = unpack(weights[10])
    keep = jnp.pad(keep, ((0, 0), (0, SLOTS - VIS)))
    spot = window_place(keep)
    chosen = (spot[:, :, None] == jnp.arange(NPATCH)[None, None, :]).astype(jnp.float32)
    shown = chosen * (jnp.arange(SLOTS)[None, :] < counts[:, None])[:, :, None]
    picked = jnp.einsum("cjp,cpv->cjv", chosen.astype(jnp.bfloat16), patches, preferred_element_type=jnp.float32)
    where = jnp.einsum("cjp,pd->cjd", chosen, window_sinusoid(D), precision=HIGH)
    hidden = times(picked.reshape(-1, PATCH), weights[8][:, :D]) + pieces[11] + where.reshape(-1, D)
    normed = layer_norm(hidden, pieces[0], pieces[1])
    joined = times(normed, weights[0])
    queries = (joined[:, :D] + pieces[2]).reshape(clips, SLOTS, HEADS, HEAD)
    key_rows = joined[:, D : 2 * D].reshape(clips, SLOTS, HEADS, HEAD)
    values = (joined[:, 2 * D :] + pieces[3]).reshape(clips, SLOTS, HEADS, HEAD)
    visible = (jnp.arange(SLOTS)[None, :] < counts[:, None])[:, None, None, :]
    attended = attend_short(queries, key_rows, values, visible, HEAD ** (-0.5)).reshape(-1, D)
    hidden = hidden + times(attended, weights[1]) + pieces[4]
    normed = layer_norm(hidden, pieces[5], pieces[6])
    inner = jax.nn.gelu(times(normed, weights[2]) + pieces[7], approximate=False)
    hidden = hidden + times(inner, weights[3]) + pieces[8]
    latent = layer_norm(hidden, pieces[9], pieces[10])

    pieces = pieces[12:]
    placed = times(latent, weights[9]) + pieces[0]
    filled = jnp.einsum("cjp,cjd->cpd", shown, placed.reshape(clips, SLOTS, DD), precision=HIGH)
    cells = jnp.sum(shown, axis=1)
    hidden = filled + (1.0 - cells)[..., None] * pieces[1] + window_sinusoid(DD)
    hidden = hidden.reshape(-1, DD)
    normed = layer_norm(hidden, pieces[2], pieces[3])
    windows = times(normed, weights[4])
    queries = (windows[:, :DD] + pieces[4]).reshape(-1, WIN * WIN, DHEADS, DHEAD)
    key_rows = windows[:, DD : 2 * DD].reshape(-1, WIN * WIN, DHEADS, DHEAD)
    values = (windows[:, 2 * DD :] + pieces[5]).reshape(-1, WIN * WIN, DHEADS, DHEAD)
    allowed = jnp.tile(window_mask(), (clips, 1, 1))[:, None, :, :]
    attended = attend_short(queries, key_rows, values, allowed, DHEAD ** (-0.5)).reshape(-1, DD)
    hidden = hidden + times(attended, weights[5]) + pieces[6]
    normed = layer_norm(hidden, pieces[7], pieces[8])
    inner = jax.nn.gelu(times(normed, weights[6]) + pieces[9], approximate=False)
    hidden = hidden + times(inner, weights[7]) + pieces[10]
    normed = layer_norm(hidden, pieces[11], pieces[12])
    predicted = times(normed, weights[8][:, D:].T) + pieces[13]
    patches = patches.astype(jnp.float32).reshape(-1, PATCH)
    centred = patches - jnp.mean(patches, axis=-1, keepdims=True)
    target = centred * lax.rsqrt(jnp.mean(centred * centred, axis=-1, keepdims=True) + 1e-06)
    deviation = predicted - target
    patch_error = jnp.mean(deviation * deviation, axis=-1)
    return jnp.sum((1.0 - cells.reshape(-1)) * patch_error)


def quick_body(
    spectrogram, keep, counts, *rest
):
    masters = rest[:8] + (rest[16], rest[19], rest[22])
    moments = rest[8:16]
    devices = lax.axis_size("dp")
    lead = (2,) * bit_count(devices)
    own = [weight.astype(jnp.bfloat16) for weight in masters]
    vector_rows = own[10].shape[0]
    spare = VEC_ROWS * VEC_COLS
    own[10] = jnp.pad(own[10], (0, spare - vector_rows)).reshape(VEC_ROWS, VEC_COLS)
    row = lax.broadcasted_iota(jnp.int32, (8, 128), 0)
    column = lax.broadcasted_iota(jnp.int32, (8, 128), 1)
    first = jnp.logical_and(row == 0, column == 0)
    count_part = jnp.sum(NPATCH - counts).astype(jnp.float32)
    gathered, tally = gather_rows(own, jnp.where(first, count_part, 0.0), devices, GATHER_TURNS)
    mask_count = tally[0, 0]
    weights = [piece.reshape(-1, piece.shape[-1]) for piece in gathered[:10]]
    weights[4] = weights[4].astype(jnp.float32)
    vectors = gathered[10].reshape(devices, spare)[:, :vector_rows].reshape(-1).astype(jnp.float32)
    patches = window_patches(spectrogram)
    loss_part, pull = jax.vjp(
        lambda *params: local_loss(params, patches, keep, counts), *weights, vectors
    )
    grads = list(pull(1.0 / mask_count))
    grads[10] = jnp.pad(grads[10].reshape(devices, vector_rows), ((0, 0), (0, spare - vector_rows)))
    grads[10] = grads[10].reshape(lead + (VEC_ROWS, VEC_COLS))
    for number in range(10):
        grad = grads[number]
        grads[number] = grad.reshape(lead + (grad.shape[0] // devices, grad.shape[1]))
    reduced, stats = reduce_rows(grads, jnp.where(first, loss_part, 0.0), devices, REDUCE_TURNS)
    reduced = list(reduced)
    reduced[10] = reduced[10].reshape(-1)[:vector_rows]
    loss_sum = stats[8, 0]
    grad_norm = jnp.sqrt(jnp.sum(stats[:8]))
    factor = jnp.minimum(1.0, CLIP_MAX / (grad_norm + 1e-06))
    clipped = [gradient * factor for gradient in reduced]
    renewed = [0.5 * moments[number] + clipped[number] for number in range(8)]
    sent = [piece if number == 4 else piece.astype(jnp.bfloat16) for number, piece in enumerate(renewed)]
    collected = send_to_owners(sent, OWNERS, devices)
    made = orthogonalize([piece.reshape(-1, piece.shape[2]) for piece in collected], OWNERS)
    made = [piece.reshape(devices, -1, piece.shape[1]) for piece in made]
    whole = return_rows(made, OWNERS, devices)
    new_weights = []
    for number in range(8):
        height, breadth = masters[number].shape
        step_rate = LR_MUON * 0.2 * math.sqrt(max(height * devices, breadth))
        new_weights.append(
            masters[number] * (1.0 - LR_MUON * DECAY) - step_rate * whole[number].astype(jnp.float32)
        )
    patch_new = adam_update(*rest[16:19], clipped[8], DECAY)
    embed_new = adam_update(*rest[19:22], clipped[9], DECAY)
    vector_new = adam_update(*rest[22:25], clipped[10], 0.0)
    return (loss_sum, mask_count, grad_norm, *new_weights, *renewed, *patch_new, *embed_new, *vector_new)


def body(
    spectrogram,
    keep,
    counts,
    enc_qkv,
    enc_out,
    enc_up,
    enc_down,
    dec_qkv,
    dec_out,
    dec_up,
    dec_down,
    mom_enc_qkv,
    mom_enc_out,
    mom_enc_up,
    mom_enc_down,
    mom_dec_qkv,
    mom_dec_out,
    mom_dec_up,
    mom_dec_down,
    patch_maps,
    patch_first,
    patch_second,
    embed_map,
    embed_first,
    embed_second,
    vectors,
    vector_first,
    vector_second,
):
    masters = (
        enc_qkv,
        enc_out,
        enc_up,
        enc_down,
        dec_qkv,
        dec_out,
        dec_up,
        dec_down,
        patch_maps,
        embed_map,
        vectors,
    )
    moments = (
        mom_enc_qkv,
        mom_enc_out,
        mom_enc_up,
        mom_enc_down,
        mom_dec_qkv,
        mom_dec_out,
        mom_dec_up,
        mom_dec_down,
    )
    sent = tuple((weight.astype(jnp.bfloat16) for weight in masters))
    gathered = (
        lax.all_gather(sent[0], "dp", axis=0, tiled=True),
        lax.all_gather(sent[1], "dp", axis=0, tiled=True),
        lax.all_gather(sent[2], "dp", axis=0, tiled=True),
        lax.all_gather(sent[3], "dp", axis=0, tiled=True),
        lax.all_gather(sent[4], "dp", axis=0, tiled=True),
        lax.all_gather(sent[5], "dp", axis=0, tiled=True),
        lax.all_gather(sent[6], "dp", axis=0, tiled=True),
        lax.all_gather(sent[7], "dp", axis=0, tiled=True),
        lax.all_gather(sent[8], "dp", axis=0, tiled=True),
        lax.all_gather(sent[9], "dp", axis=0, tiled=True),
        lax.all_gather(sent[10], "dp", axis=0, tiled=True),
    )
    widened = tuple((piece.astype(jnp.float32) for piece in gathered))
    patches = patchify(spectrogram.astype(jnp.float32))
    latent = encode(widened, patches, keep, counts)
    loss_part = decode(widened, latent, patches, keep, counts)
    count_part = jnp.sum(NPATCH - counts).astype(jnp.float32)
    loss_sum, mask_count = lax.psum((loss_part, count_part), ("dp", "mp"))
    regathered = (
        lax.all_gather(sent[0], "dp", axis=0, tiled=True),
        lax.all_gather(sent[1], "dp", axis=0, tiled=True),
        lax.all_gather(sent[2], "dp", axis=0, tiled=True),
        lax.all_gather(sent[3], "dp", axis=0, tiled=True),
        lax.all_gather(sent[4], "dp", axis=0, tiled=True),
        lax.all_gather(sent[5], "dp", axis=0, tiled=True),
        lax.all_gather(sent[6], "dp", axis=0, tiled=True),
        lax.all_gather(sent[7], "dp", axis=0, tiled=True),
        lax.all_gather(sent[8], "dp", axis=0, tiled=True),
        lax.all_gather(sent[9], "dp", axis=0, tiled=True),
        lax.all_gather(sent[10], "dp", axis=0, tiled=True),
    )
    widened = tuple((piece.astype(jnp.float32) for piece in regathered))
    cotangent = 1.0 / mask_count
    unused, pull_decode = jax.vjp(
        lambda params, hidden: decode(params, hidden, patches, keep, counts), widened, latent
    )
    decode_grads, latent_grad = pull_decode(cotangent)
    unused, pull_encode = jax.vjp(lambda params: encode(params, patches, keep, counts), widened)
    (encode_grads,) = pull_encode(latent_grad)
    grads = jax.tree.map(jnp.add, decode_grads, encode_grads)
    reduced = (
        lax.psum_scatter(grads[0], "dp", scatter_dimension=0, tiled=True),
        lax.psum_scatter(grads[1], "dp", scatter_dimension=0, tiled=True),
        lax.psum_scatter(grads[2], "dp", scatter_dimension=0, tiled=True),
        lax.psum_scatter(grads[3], "dp", scatter_dimension=0, tiled=True),
        lax.psum_scatter(grads[4], "dp", scatter_dimension=0, tiled=True),
        lax.psum_scatter(grads[5], "dp", scatter_dimension=0, tiled=True),
        lax.psum_scatter(grads[6], "dp", scatter_dimension=0, tiled=True),
        lax.psum_scatter(grads[7], "dp", scatter_dimension=0, tiled=True),
        lax.psum_scatter(grads[8], "dp", scatter_dimension=0, tiled=True),
        lax.psum_scatter(grads[9], "dp", scatter_dimension=0, tiled=True),
        lax.psum_scatter(grads[10], "dp", scatter_dimension=0, tiled=True),
    )
    reduced = lax.psum(
        (
            reduced[0],
            reduced[1],
            reduced[2],
            reduced[3],
            reduced[4],
            reduced[5],
            reduced[6],
            reduced[7],
            reduced[8],
            reduced[9],
            reduced[10],
        ),
        "mp",
    )
    local_squares = functools.reduce(
        jnp.add, [jnp.sum(gradient * gradient) for gradient in reduced]
    )
    grad_norm = jnp.sqrt(lax.psum(local_squares, "dp"))
    factor = jnp.minimum(1.0, CLIP_MAX / (grad_norm + 1e-06))
    clipped = [gradient * factor for gradient in reduced]
    devices = lax.axis_size("dp")
    renewed = [0.5 * moments[number] + clipped[number] for number in range(8)]
    core = lax.axis_index("mp")
    halves = [take_half(renewed[number], number, core) for number in range(8)]
    shapes = [(masters[number].shape[0] * devices, masters[number].shape[1]) for number in range(8)]
    long_max = max((max(shape_pair) // 2 for shape_pair in shapes))
    short_max = max((min(shape_pair) for shape_pair in shapes))
    flat_max = max((shape_pair[0] * shape_pair[1] // (2 * devices) for shape_pair in shapes))
    owner = lax.axis_index("dp") % 8
    collected = (
        lax.all_gather(halves[0], "dp", axis=0, tiled=True),
        lax.all_gather(halves[1], "dp", axis=0, tiled=True),
        lax.all_gather(halves[2], "dp", axis=0, tiled=True),
        lax.all_gather(halves[3], "dp", axis=0, tiled=True),
        lax.all_gather(halves[4], "dp", axis=0, tiled=True),
        lax.all_gather(halves[5], "dp", axis=0, tiled=True),
        lax.all_gather(halves[6], "dp", axis=0, tiled=True),
        lax.all_gather(halves[7], "dp", axis=0, tiled=True),
    )
    iterate = lax.switch(
        owner,
        [partial(arrange, collected[number], number, long_max, short_max) for number in range(8)],
    )
    for iteration in range(NS_ITERS):
        gram_sum = lax.psum(jnp.dot(iterate.T, iterate, precision=HIGH), "mp")
        if iteration == 0:
            norm_scale = 1.0 / (jnp.sqrt(jnp.trace(gram_sum)) + 1e-07)
            iterate = iterate * norm_scale
            gram_sum = gram_sum * (norm_scale * norm_scale)
        polynomial = NS_B * gram_sum + NS_C * jnp.dot(gram_sum, gram_sum, precision=HIGH)
        iterate = NS_A * iterate + jnp.dot(iterate, polynomial, precision=HIGH)
    outgoing = lax.switch(
        owner,
        [
            partial(
                disperse, iterate, number, shapes[number][0], shapes[number][1], devices, flat_max
            )
            for number in range(8)
        ],
    )
    arriving = jax.tree.map(
        lambda part, own: part.astype(own.dtype),
        lax.all_to_all(shortened(outgoing), "dp", split_axis=0, concat_axis=0, tiled=True),
        outgoing,
    )
    mine = [
        restore(arriving[number], number, shapes[number][0], shapes[number][1], devices)
        for number in range(8)
    ]
    whole = (
        lax.all_gather(shortened(mine[0]), "mp", axis=1, tiled=True),
        lax.all_gather(shortened(mine[1]), "mp", axis=1, tiled=True),
        lax.all_gather(shortened(mine[2]), "mp", axis=1, tiled=True),
        lax.all_gather(shortened(mine[3]), "mp", axis=0, tiled=True),
        lax.all_gather(shortened(mine[4]), "mp", axis=1, tiled=True),
        lax.all_gather(shortened(mine[5]), "mp", axis=1, tiled=True),
        lax.all_gather(shortened(mine[6]), "mp", axis=1, tiled=True),
        lax.all_gather(shortened(mine[7]), "mp", axis=0, tiled=True),
    )
    new_weights = []
    for number in range(8):
        step_rate = LR_MUON * 0.2 * math.sqrt(max(shapes[number]))
        new_weights.append(masters[number] * (1.0 - LR_MUON * DECAY) - step_rate * whole[number])
    patch_new = adam_update(patch_maps, patch_first, patch_second, clipped[8], DECAY)
    embed_new = adam_update(embed_map, embed_first, embed_second, clipped[9], DECAY)
    vector_new = adam_update(vectors, vector_first, vector_second, clipped[10], 0.0)
    return (
        loss_sum,
        mask_count,
        grad_norm,
        new_weights[0],
        new_weights[1],
        new_weights[2],
        new_weights[3],
        new_weights[4],
        new_weights[5],
        new_weights[6],
        new_weights[7],
        renewed[0],
        renewed[1],
        renewed[2],
        renewed[3],
        renewed[4],
        renewed[5],
        renewed[6],
        renewed[7],
        patch_new[0],
        patch_new[1],
        patch_new[2],
        embed_new[0],
        embed_new[1],
        embed_new[2],
        vector_new[0],
        vector_new[1],
        vector_new[2],
    )


def solution(mesh):
    placed = (
        P(("dp", "mp"), None, None),
        P(("dp", "mp"), None),
        P(("dp", "mp")),
        P("dp", None),
        P("dp", None),
        P("dp", None),
        P("dp", None),
        P("dp", None),
        P("dp", None),
        P("dp", None),
        P("dp", None),
        P("dp", None),
        P("dp", None),
        P("dp", None),
        P("dp", None),
        P("dp", None),
        P("dp", None),
        P("dp", None),
        P("dp", None),
        P("dp", None),
        P("dp", None),
        P("dp", None),
        P("dp", None),
        P("dp", None),
        P("dp", None),
        P("dp"),
        P("dp"),
        P("dp"),
    )
    return jax.shard_map(
        quick_body if mesh.shape["dp"] == 16 else body,
        mesh=mesh,
        in_specs=placed,
        out_specs=(
            P(),
            P(),
            P(),
            P("dp", None),
            P("dp", None),
            P("dp", None),
            P("dp", None),
            P("dp", None),
            P("dp", None),
            P("dp", None),
            P("dp", None),
            P("dp", None),
            P("dp", None),
            P("dp", None),
            P("dp", None),
            P("dp", None),
            P("dp", None),
            P("dp", None),
            P("dp", None),
            P("dp", None),
            P("dp", None),
            P("dp", None),
            P("dp", None),
            P("dp", None),
            P("dp", None),
            P("dp"),
            P("dp"),
            P("dp"),
        ),
        check_vma=False,
    )
```

```python
from functools import partial
import functools
import math

import jax
import jax.numpy as jnp
import numpy as np
from jax import lax
from jax.experimental import pallas as pl
from jax.experimental.pallas import tpu as pltpu
from jax.sharding import PartitionSpec as P

D = 768
HEADS = 12
HEAD = 64
MLP = 3072
DD = 512
DHEADS = 16
DHEAD = 32
DMLP = 2048
PS = 16
GT = 64
GF = 8
WIN = 4
VIS = 154
NS_ITERS = 5
STEP = 10
PATCH = 256
SHIFT = 2
NPATCH = 512


HIGH = lax.Precision.HIGHEST
CLIP_MAX = 0.001
LR_MUON = 0.1
LR_ADAM = 0.05
DECAY = 0.01
NS_A = 3.4445
NS_B = -4.775
NS_C = 2.0315
LONG_COLS = (True, True, True, False, True, True, True, False)


def shortened(x):
    return jax.tree.map(lambda a: a.astype(jnp.bfloat16) if a.dtype == jnp.float32 else a, x)


def narrow_core(value):
    return lax.optimization_barrier(value.astype(jnp.bfloat16)).astype(jnp.float32)


def narrow_keep(value):
    return (narrow_core(value), None)


def narrow_pass(kept, grad):
    return (grad,)


def same_core(value):
    return value


def same_keep(value):
    return (value, None)


def same_back(kept, grad):
    return (narrow_core(grad),)


def narrow(value):
    wrapped = jax.custom_vjp(narrow_core)
    wrapped.defvjp(narrow_keep, narrow_pass)
    return wrapped(value)


def narrow_grad(value):
    wrapped = jax.custom_vjp(same_core)
    wrapped.defvjp(same_keep, same_back)
    return wrapped(value)


def product(inputs, matrix):
    return narrow_grad(jnp.dot(narrow(inputs), narrow(matrix), preferred_element_type=jnp.float32))


def score_product(queries, key_rows):
    return narrow_grad(
        jnp.einsum(
            "bqhd,bkhd->bhqk", narrow(queries), narrow(key_rows), preferred_element_type=jnp.float32
        )
    )


def value_product(softmax_rows, values):
    return narrow_grad(
        jnp.einsum(
            "bhqk,bkhd->bqhd",
            narrow(softmax_rows),
            narrow(values),
            preferred_element_type=jnp.float32,
        )
    )


def unpack(vectors):
    extents = [D] * 7 + [MLP] + [D] * 4 + [DD] * 9 + [DMLP] + [DD] * 3 + [PATCH]
    pieces = []
    offset = 0
    for extent in extents:
        pieces.append(vectors[offset : offset + extent])
        offset += extent
    return pieces


def layer_norm(hidden, scaling, offset):
    centred = hidden - jnp.mean(hidden, axis=-1, keepdims=True)
    variance = jnp.mean(centred * centred, axis=-1, keepdims=True)
    return centred * lax.rsqrt(variance + 1e-06) * scaling + offset


def sinusoid(channels):
    quarter = channels // 4
    frequency = 1.0 / 10000.0 ** (jnp.arange(quarter, dtype=jnp.float32) / quarter)
    position = jnp.arange(GT * GF)
    time_rows = (position // GF).astype(jnp.float32)[:, None] * frequency
    freq_cols = (position % GF).astype(jnp.float32)[:, None] * frequency
    return jnp.concatenate(
        [jnp.sin(time_rows), jnp.cos(time_rows), jnp.sin(freq_cols), jnp.cos(freq_cols)], axis=1
    )


def patchify(spec):
    clip_total = spec.shape[0]
    arranged = spec.reshape(clip_total, GT, PS, GF, PS).transpose(0, 1, 3, 2, 4)
    return arranged.reshape(clip_total, GT * GF, PS * PS)


def window_mask():
    time_rows = jnp.arange(GT)
    freq_cols = jnp.arange(GF)
    time_part = (time_rows >= GT - WIN).astype(jnp.int32) + (time_rows >= GT - SHIFT).astype(
        jnp.int32
    )
    freq_part = (freq_cols >= GF - WIN).astype(jnp.int32) + (freq_cols >= GF - SHIFT).astype(
        jnp.int32
    )
    region = time_part[:, None] * 3 + freq_part[None, :]
    region = (
        region.reshape(GT // WIN, WIN, GF // WIN, WIN).transpose(0, 2, 1, 3).reshape(-1, WIN * WIN)
    )
    return region[:, :, None] == region[:, None, :]


def to_windows(grid_rows):
    clip_total = grid_rows.shape[0]
    channels = grid_rows.shape[2]
    arranged = jnp.roll(
        grid_rows.reshape(clip_total, GT, GF, channels), (-SHIFT, -SHIFT), axis=(1, 2)
    )
    arranged = arranged.reshape(clip_total, GT // WIN, WIN, GF // WIN, WIN, channels).transpose(
        0, 1, 3, 2, 4, 5
    )
    return arranged.reshape(-1, WIN * WIN, channels)


def from_windows(windows, clip_total):
    channels = windows.shape[-1]
    arranged = windows.reshape(clip_total, GT // WIN, GF // WIN, WIN, WIN, channels).transpose(
        0, 1, 3, 2, 4, 5
    )
    arranged = jnp.roll(arranged.reshape(clip_total, GT, GF, channels), (SHIFT, SHIFT), axis=(1, 2))
    return arranged.reshape(clip_total, GT * GF, channels)


def attend(queries, key_rows, values, allowed, scaling):
    scores = score_product(queries, key_rows) * scaling
    scores = jnp.where(allowed, scores, -1e30)
    scores = scores - jnp.max(scores, axis=-1, keepdims=True)
    exponent = jnp.exp(scores)
    softmax_rows = exponent / jnp.sum(exponent, axis=-1, keepdims=True)
    return value_product(softmax_rows, values)


def encode(weights, patches, keep, counts):
    pieces = unpack(weights[10])
    clip_total = patches.shape[0]
    picked = jnp.take_along_axis(patches, keep[:, :, None], axis=1)
    hidden = product(picked, weights[8][:, :D]) + pieces[11] + sinusoid(D)[keep]
    normed = layer_norm(hidden, pieces[0], pieces[1])
    joined = product(normed, weights[0])
    queries = (joined[..., :D] + pieces[2]).reshape(clip_total, VIS, HEADS, HEAD)
    key_rows = joined[..., D : 2 * D].reshape(clip_total, VIS, HEADS, HEAD)
    values = (joined[..., 2 * D :] + pieces[3]).reshape(clip_total, VIS, HEADS, HEAD)
    visible = (jnp.arange(VIS)[None, :] < counts[:, None])[:, None, None, :]
    attended = attend(queries, key_rows, values, visible, HEAD ** (-0.5)).reshape(
        clip_total, VIS, D
    )
    hidden = hidden + product(attended, weights[1]) + pieces[4]
    normed = layer_norm(hidden, pieces[5], pieces[6])
    inner = jax.nn.gelu(product(normed, weights[2]) + pieces[7], approximate=False)
    hidden = hidden + product(inner, weights[3]) + pieces[8]
    return layer_norm(hidden, pieces[9], pieces[10])


def decode(weights, latent, patches, keep, counts):
    pieces = unpack(weights[10])[12:]
    clip_total = latent.shape[0]
    placed = product(latent, weights[9]) + pieces[0]
    visible = jnp.arange(VIS)[None, :] < counts[:, None]
    target_rows = jnp.where(visible, keep, NPATCH)
    clip_rows = jnp.arange(clip_total)[:, None]
    filled = (
        jnp.zeros((clip_total, NPATCH + 1, DD), jnp.float32)
        .at[clip_rows, target_rows]
        .add(placed)[:, :NPATCH]
    )
    visible_cells = (
        jnp.zeros((clip_total, NPATCH + 1), jnp.float32)
        .at[clip_rows, target_rows]
        .add(1.0)[:, :NPATCH]
    )
    hidden = filled + (1.0 - visible_cells)[..., None] * pieces[1] + sinusoid(DD)
    normed = layer_norm(hidden, pieces[2], pieces[3])
    windows = to_windows(product(normed, weights[4]))
    queries = (windows[..., :DD] + pieces[4]).reshape(-1, WIN * WIN, DHEADS, DHEAD)
    key_rows = windows[..., DD : 2 * DD].reshape(-1, WIN * WIN, DHEADS, DHEAD)
    values = (windows[..., 2 * DD :] + pieces[5]).reshape(-1, WIN * WIN, DHEADS, DHEAD)
    allowed = jnp.tile(window_mask(), (clip_total, 1, 1))[:, None, :, :]
    attended = attend(queries, key_rows, values, allowed, DHEAD ** (-0.5)).reshape(
        -1, WIN * WIN, DD
    )
    hidden = hidden + product(from_windows(attended, clip_total), weights[5]) + pieces[6]
    normed = layer_norm(hidden, pieces[7], pieces[8])
    inner = jax.nn.gelu(product(normed, weights[6]) + pieces[9], approximate=False)
    hidden = hidden + product(inner, weights[7]) + pieces[10]
    normed = layer_norm(hidden, pieces[11], pieces[12])
    predicted = product(normed, weights[8][:, D:].T) + pieces[13]
    centred = patches - jnp.mean(patches, axis=-1, keepdims=True)
    target = centred * lax.rsqrt(jnp.mean(centred * centred, axis=-1, keepdims=True) + 1e-06)
    deviation = predicted - target
    patch_error = jnp.mean(deviation * deviation, axis=-1)
    return jnp.sum((1.0 - visible_cells) * patch_error)


def take_half(shard, number, core):
    if LONG_COLS[number]:
        extent = shard.shape[1] // 2
        return lax.dynamic_slice_in_dim(shard, core * extent, extent, 1)
    extent = shard.shape[0] // 2
    return lax.dynamic_slice_in_dim(shard, core * extent, extent, 0)


def arrange(gathered_half, number, long_max, short_max):
    upright = gathered_half.T if LONG_COLS[number] else gathered_half
    return jnp.pad(upright, ((0, long_max - upright.shape[0]), (0, short_max - upright.shape[1])))


def disperse(iterate, number, height, breadth, devices, flat_max):
    if LONG_COLS[number]:
        piece = iterate[: breadth // 2, :height].T.reshape(
            devices, height // devices * (breadth // 2)
        )
    else:
        piece = iterate[: height // 2, :breadth].reshape(devices, height // 2 // devices * breadth)
    return jnp.pad(piece, ((0, 0), (0, flat_max - piece.shape[1])))


def restore(row_piece, number, height, breadth, devices):
    if LONG_COLS[number]:
        return row_piece[: height // devices * (breadth // 2)].reshape(
            height // devices, breadth // 2
        )
    return row_piece[: height // 2 // devices * breadth].reshape(height // 2 // devices, breadth)


def adam_update(weight, first_moment, second_moment, gradient, decay):
    first_moment = 0.5 * first_moment + 0.5 * gradient
    second_moment = 0.95 * second_moment + 0.05 * gradient * gradient
    direction = (
        first_moment / (1.0 - 0.5**STEP) / (jnp.sqrt(second_moment / (1.0 - 0.95**STEP)) + 1e-08)
    )
    return (weight - LR_ADAM * (direction + decay * weight), first_moment, second_moment)


MESH_ID = pl.DeviceIdType.MESH
VEC_ROWS, VEC_COLS = 16, 256
AXIS_ORDERS = ((3, 2, 1, 0), (3, 2, 0, 1), (0, 3, 2, 1), (1, 3, 2, 0), (0, 1, 3, 2), (1, 0, 3, 2))
GATHER_PARTS = (3, 1, 4, 4, 1, 1, 2, 2, 1, 1, 1)
REDUCE_PARTS = (3, 1, 4, 4, 2, 1, 2, 2, 1, 1, 1)
TALL = (3, 7)
GATHER_TURNS = (5, 1, 3, 2, 1, 0, 3, 0, 1, 5, 1, 5, 1, 5, 1, 0, 0, 1, 0, 5, 3)
GATHER_FIRST = (3, 2, 17, 15, 4, 7, 10, 6, 19, 9, 16, 12, 8, 13, 20, 11, 0, 5, 14, 1, 18)
GATHER_STEPS = ((3, 0), (2, 0), (17, 0), (6, 0), (19, 0), (15, 0), (9, 0), (13, 0), (20, 0), (11, 0), (4, 0), (0, 0), (19, 1), (7, 0), (9, 1), (10, 0), (13, 1), (16, 0), (11, 1), (12, 0), (0, 1), (8, 0), (5, 0), (14, 0), (1, 0), (18, 0), (3, 1), (17, 1), (2, 1), (15, 1), (6, 1), (20, 1), (4, 1), (17, 2), (15, 2), (7, 1), (19, 2), (4, 2), (10, 1), (17, 3), (9, 2), (15, 3), (7, 2), (13, 2), (16, 1), (10, 2), (4, 3), (12, 1), (11, 2), (7, 3), (16, 2), (8, 1), (12, 2), (0, 2), (5, 1), (14, 1), (10, 3), (1, 1), (18, 1), (16, 3), (3, 2), (8, 2), (2, 2), (12, 3), (14, 2), (6, 2), (5, 2), (20, 2), (1, 2), (18, 2), (19, 3), (2, 3), (3, 3), (9, 3), (6, 3), (13, 3), (8, 3), (5, 3), (11, 3), (14, 3), (20, 3), (18, 3), (0, 3), (1, 3))
REDUCE_TURNS = (1, 0, 1, 1, 1, 1, 2, 1, 0, 1, 4, 0, 3, 2, 2, 3, 3, 3, 5, 4, 3, 0)
REDUCE_FIRST = (10, 1, 13, 9, 18, 6, 7, 5, 11, 21, 8, 12, 16, 0, 17, 3, 20, 19, 4, 14, 2, 15)
REDUCE_STEPS = ((10, 0), (1, 0), (13, 0), (18, 0), (11, 0), (21, 0), (9, 0), (10, 1), (13, 1), (8, 0), (6, 0), (18, 1), (19, 0), (12, 0), (7, 0), (13, 2), (6, 1), (19, 1), (16, 0), (5, 0), (12, 1), (1, 1), (6, 2), (17, 0), (16, 1), (20, 0), (1, 2), (0, 0), (12, 2), (17, 1), (15, 0), (16, 2), (20, 1), (3, 0), (1, 3), (9, 1), (18, 2), (17, 2), (15, 1), (4, 0), (7, 1), (13, 3), (20, 2), (9, 2), (11, 1), (5, 1), (6, 3), (15, 2), (7, 2), (14, 0), (21, 1), (9, 3), (11, 2), (0, 1), (5, 2), (7, 3), (3, 1), (14, 1), (21, 2), (2, 0), (11, 3), (0, 2), (10, 2), (4, 1), (5, 3), (3, 2), (8, 1), (14, 2), (21, 3), (19, 2), (2, 1), (12, 3), (10, 3), (0, 3), (16, 3), (4, 2), (18, 3), (14, 3), (17, 3), (19, 3), (20, 3), (3, 3), (15, 3), (8, 2), (2, 2), (4, 3), (8, 3), (2, 3))
OWNERS = (4, 11, 5, 10, 6, 9, 7, 8)
SLOTS = 160


def bit_count(devices):
    return devices.bit_length() - 1


def cut_pieces(parts, shapes):
    found = []
    for number, count in enumerate(parts):
        rows, width = shapes[number]
        for part in range(count):
            if number in TALL:
                found.append((number, part * (rows // count), rows // count, 0, width))
            else:
                found.append((number, 0, rows, part * (width // count), width // count))
    return found


def own_bits(levels):
    me = lax.axis_index("dp")
    return me, [lax.rem(lax.div(me, 2**bit), 2) for bit in range(levels)]


def place(levels, free, own, flip=None):
    spots = []
    for bit in range(levels - 1, -1, -1):
        if bit in free:
            spots.append(slice(None))
        elif bit == flip:
            spots.append(1 - own[bit])
        else:
            spots.append(own[bit])
    return tuple(spots)


def partner(me, own, bit):
    return me + (1 - 2 * own[bit]) * 2**bit


def greet(me, own, levels, core):
    barrier = pltpu.get_barrier_semaphore()
    for bit in range(levels):
        pl.semaphore_signal(
            barrier,
            inc=1,
            device_id={"dp": partner(me, own, bit), "mp": core},
            device_id_type=MESH_ID,
        )
    pl.semaphore_signal(barrier, inc=1, device_id={"dp": me, "mp": 1 - core}, device_id_type=MESH_ID)
    pl.semaphore_wait(barrier, levels + 1)


def add_up(me, own, core, levels, total, landing, send_sem, recv_sem):
    for stage in range(levels + 1):
        if stage < levels:
            to = {"dp": partner(me, own, stage), "mp": core}
        else:
            to = {"dp": me, "mp": 1 - core}
        swap = pltpu.make_async_remote_copy(
            src_ref=total,
            dst_ref=landing.at[stage],
            send_sem=send_sem.at[stage],
            recv_sem=recv_sem.at[stage],
            device_id=to,
            device_id_type=MESH_ID,
        )
        swap.start()
        swap.wait()
        total[...] = total[...] + landing[stage]


def gather_kernel(levels, pieces, count, *refs):
    shards, tally = refs[:count], refs[count]
    wholes, tally_out = refs[count + 1 : 2 * count + 1], refs[2 * count + 1]
    short, rest = refs[2 * count + 2 : 3 * count + 2], refs[3 * count + 2 :]
    here_sem, send_sem, recv_sem, cross_send, cross_recv, tally_land, tally_send, tally_recv = rest
    me, own = own_bits(levels)
    core = lax.axis_index("mp")
    greet(me, own, levels, core)
    orders = [AXIS_ORDERS[turn] for turn in GATHER_TURNS]

    def cut(piece, which):
        number, row, rows, column, columns = pieces[piece]
        width = shards[number].shape[1] // 2
        return (pl.ds(row, rows), pl.ds(pl.multiple_of(which * width + column, 128), columns))

    def hop(piece, stage, flip):
        order, number = orders[piece], pieces[piece][0]
        spot = place(levels, order[:stage], own, order[stage] if flip else None)
        target = wholes[number].at[spot + cut(piece, core)]
        source = target if stage or flip else short[number].at[cut(piece, core)]
        return pltpu.make_async_remote_copy(
            src_ref=source,
            dst_ref=target,
            send_sem=send_sem.at[piece, stage],
            recv_sem=recv_sem.at[piece, stage],
            device_id={"dp": partner(me, own, order[stage]), "mp": core},
            device_id_type=MESH_ID,
        )

    def cross(piece, stage, which):
        order, number = orders[piece], pieces[piece][0]
        spot = place(levels, order[:stage], own, order[stage])
        target = wholes[number].at[spot + cut(piece, which)]
        return pltpu.make_async_remote_copy(
            src_ref=target,
            dst_ref=target,
            send_sem=cross_send.at[piece, stage],
            recv_sem=cross_recv.at[piece, stage],
            device_id={"dp": me, "mp": 1 - core},
            device_id_type=MESH_ID,
        )

    def keep(number):
        spot = place(levels, (), own)
        return pltpu.make_async_copy(short[number], wholes[number].at[spot], here_sem.at[number])

    ready = set()
    for piece in GATHER_FIRST:
        number = pieces[piece][0]
        if number not in ready:
            ready.add(number)
            short[number][...] = shards[number][...].astype(jnp.bfloat16)
            keep(number).start()
        hop(piece, 0, False).start()
    tally_out[...] = tally[...]
    add_up(me, own, core, levels, tally_out, tally_land, tally_send, tally_recv)
    for number in range(count):
        keep(number).wait()
    for piece, stage in GATHER_STEPS:
        hop(piece, stage, True).wait_recv()
        if stage + 1 < levels:
            hop(piece, stage + 1, False).start()
        cross(piece, stage, core).start()
    for piece in range(len(pieces)):
        for stage in range(levels):
            hop(piece, stage, False).wait_send()
            cross(piece, stage, core).wait_send()
            cross(piece, stage, 1 - core).wait_recv()


def gather_rows(shards, tally, devices):
    levels, count = bit_count(devices), len(shards)
    lead = (2,) * levels
    pieces = cut_pieces(GATHER_PARTS, [(shard.shape[0], shard.shape[1] // 2) for shard in shards])
    dma = pltpu.SemaphoreType.DMA
    vmem = pl.BlockSpec(memory_space=pltpu.VMEM)
    found = pl.pallas_call(
        functools.partial(gather_kernel, levels, pieces, count),
        out_shape=[jax.ShapeDtypeStruct(lead + shard.shape, jnp.bfloat16) for shard in shards]
        + [jax.ShapeDtypeStruct((8, 128), jnp.float32)],
        in_specs=[vmem] * (count + 1),
        out_specs=[pl.BlockSpec(memory_space=pl.ANY)] * count + [vmem],
        scratch_shapes=[pltpu.VMEM(shard.shape, jnp.bfloat16) for shard in shards]
        + [dma((count,))]
        + [dma((len(pieces), levels))] * 4
        + [pltpu.VMEM((levels + 1, 8, 128), jnp.float32)]
        + [dma((levels + 1,))] * 2,
        compiler_params=pltpu.CompilerParams(
            collective_id=1, has_side_effects=True, vmem_limit_bytes=32 * 2**20
        ),
        name="gather_rows",
    )(*shards, tally)
    return found[:count], found[count]


def reduce_kernel(levels, pieces, count, owners, devices, *refs):
    blocks = len(owners)
    grads, stats_in, old = refs[:count], refs[count], refs[count + 1 : count + 1 + blocks]
    rest = refs[count + 1 + blocks :]
    sums, stats_out, wholes = rest[:count], rest[count], rest[count + 1 : count + 1 + blocks]
    rest = rest[count + 1 + blocks :]
    mine, theirs, rest = rest[:count], rest[count : 2 * count], rest[2 * count :]
    kept, rest = rest[:count], rest[count:]
    landing, rest = rest[: len(pieces) * levels], rest[len(pieces) * levels :]
    staged, rest = rest[:blocks], rest[blocks:]
    stats_land, here_sem, pair_send, pair_recv, send_sem, recv_sem, last_send, last_recv = rest[:8]
    stats_send, stats_recv, own_sem, out_send, out_recv, cross_send, cross_recv = rest[8:]
    me, own = own_bits(levels)
    core = lax.axis_index("mp")
    orders = [AXIS_ORDERS[turn][::-1] for turn in REDUCE_TURNS]
    owning = functools.reduce(jnp.logical_or, [me == owner for owner in owners])
    barrier = pltpu.get_barrier_semaphore()
    for bit in range(levels):
        pl.semaphore_signal(
            barrier,
            inc=1,
            device_id={"dp": partner(me, own, bit), "mp": core},
            device_id_type=MESH_ID,
        )
    pl.semaphore_signal(barrier, inc=1, device_id={"dp": me, "mp": 1 - core}, device_id_type=MESH_ID)

    @pl.when(owning)
    def greet_all():
        @pl.loop(0, devices)
        def greet_one(other):
            @pl.when(other != me)
            def signal_one():
                pl.semaphore_signal(
                    barrier, inc=1, device_id={"dp": other, "mp": core}, device_id_type=MESH_ID
                )

        pl.semaphore_wait(barrier, levels + blocks)

    @pl.when(jnp.logical_not(owning))
    def wait_owners():
        pl.semaphore_wait(barrier, levels + 1 + blocks)

    def half(number, which):
        width = sums[number].shape[1] // 2
        return (slice(None), pl.ds(pl.multiple_of(which * width, 128), width))

    def cut(piece):
        number, row, rows, column, columns = pieces[piece]
        return (pl.ds(row, rows), pl.ds(column, columns))

    def side(piece, which):
        number, row, rows, column, columns = pieces[piece]
        width = sums[number].shape[1] // 2
        return (pl.ds(row, rows), pl.ds(pl.multiple_of(which * width + column, 128), columns))

    every = (slice(None),) * levels

    def pair(piece):
        number = pieces[piece][0]
        return pltpu.make_async_remote_copy(
            src_ref=grads[number].at[every + side(piece, 1 - core)],
            dst_ref=theirs[number].at[every + cut(piece)],
            send_sem=pair_send.at[piece],
            recv_sem=pair_recv.at[piece],
            device_id={"dp": me, "mp": 1 - core},
            device_id_type=MESH_ID,
        )

    def load(piece):
        number = pieces[piece][0]
        return pltpu.make_async_copy(
            grads[number].at[every + side(piece, core)],
            mine[number].at[every + cut(piece)],
            here_sem.at[piece],
        )

    def hop(piece, stage):
        order = orders[piece]
        spot = place(levels, order[stage + 1 :], own, order[stage])
        return pltpu.make_async_remote_copy(
            src_ref=theirs[pieces[piece][0]].at[spot + cut(piece)],
            dst_ref=landing[piece * levels + stage],
            send_sem=send_sem.at[piece, stage],
            recv_sem=recv_sem.at[piece, stage],
            device_id={"dp": partner(me, own, order[stage]), "mp": core},
            device_id_type=MESH_ID,
        )

    def share(number, which):
        region = sums[number].at[half(number, which)]
        return pltpu.make_async_remote_copy(
            src_ref=region,
            dst_ref=region,
            send_sem=last_send.at[number],
            recv_sem=last_recv.at[number],
            device_id={"dp": me, "mp": 1 - core},
            device_id_type=MESH_ID,
        )

    def deliver(number, source):
        return pltpu.make_async_remote_copy(
            src_ref=staged[number],
            dst_ref=wholes[number].at[(source,) + half(number, core)],
            send_sem=out_send.at[number],
            recv_sem=out_recv.at[number, source],
            device_id={"dp": owners[number], "mp": core},
            device_id_type=MESH_ID,
        )

    def deliver_here(number):
        return pltpu.make_async_copy(
            staged[number], wholes[number].at[(me,) + half(number, core)], own_sem
        )

    def cross(number, source, which):
        region = wholes[number].at[(source,) + half(number, which)]
        return pltpu.make_async_remote_copy(
            src_ref=region,
            dst_ref=region,
            send_sem=cross_send.at[number, source],
            recv_sem=cross_recv.at[number, source],
            device_id={"dp": me, "mp": 1 - core},
            device_id_type=MESH_ID,
        )

    def kept_spot(order, found):
        return tuple(found.get(bit, own[bit]) for bit in range(levels - 1, -1, -1) if bit != order[0])

    def fold(piece, stage):
        order, number = orders[piece], pieces[piece][0]
        free = order[stage:]
        loose = [bit for bit in range(levels - 1, -1, -1) if bit in free and bit != order[stage]]
        region = cut(piece)

        @pl.loop(0, 2 ** len(loose))
        def add_block(block):
            found = {
                bit: lax.rem(lax.div(block, 2 ** (len(loose) - 1 - i)), 2) for i, bit in enumerate(loose)
            }

            def total(way):
                now = dict(found)
                now[order[stage]] = way
                full = tuple(now.get(bit, own[bit]) for bit in range(levels - 1, -1, -1)) + region
                if stage == 0:
                    value = mine[number][full].astype(jnp.float32) + theirs[number][full].astype(jnp.float32)
                else:
                    land = tuple(now[bit] for bit in range(levels - 1, -1, -1) if bit in free)
                    arrived = landing[piece * levels + stage - 1][land].astype(jnp.float32)
                    value = kept[number][kept_spot(order, now) + region] + arrived
                return full, value

            full, value = total(1 - own[order[stage]])
            theirs[number][full] = value.astype(theirs[number].dtype)
            full, value = total(own[order[stage]])
            kept[number][kept_spot(order, found) + region] = value

    for piece in REDUCE_FIRST:
        pair(piece).start()
        load(piece).start()
    for piece in REDUCE_FIRST:
        load(piece).wait()
        pair(piece).wait_recv()
        fold(piece, 0)
        hop(piece, 0).start()
    squares = jnp.zeros((8, 128), jnp.float32)
    for piece, stage in REDUCE_STEPS:
        hop(piece, stage).wait_recv()
        if stage + 1 < levels:
            fold(piece, stage + 1)
            hop(piece, stage + 1).start()
        else:
            number = pieces[piece][0]
            arrived = landing[piece * levels + stage][...].astype(jnp.float32)
            total = kept[number][kept_spot(orders[piece], {}) + cut(piece)] + arrived
            sums[number][side(piece, core)] = total
            rows, width = total.shape
            for row in range(0, rows, 8):
                for column in range(0, width, 128):
                    part = total[row : row + 8, column : column + 128]
                    squares = squares + part * part
    for number in range(blocks, count):
        share(number, core).start()
    stats_out[0:8, :] = squares
    stats_out[8:16, :] = stats_in[...]
    add_up(me, own, core, levels, stats_out, stats_land, stats_send, stats_recv)
    norm = jnp.sqrt(jnp.sum(jnp.sum(stats_out[0:8, :], axis=0, keepdims=True), axis=1, keepdims=True))
    factor = jnp.minimum(1.0, CLIP_MAX / (norm + 1e-06))
    for number in range(blocks):
        region = half(number, core)
        renewed = 0.5 * old[number][region] + factor * sums[number][region]
        sums[number][region] = renewed
        staged[number][...] = renewed.astype(staged[number].dtype)
        share(number, core).start()

        @pl.when(me != owners[number])
        def start_one(number=number):
            deliver(number, me).start()

        @pl.when(me == owners[number])
        def start_here(number=number):
            deliver_here(number).start()

    for piece in range(len(pieces)):
        pair(piece).wait_send()
        for stage in range(levels):
            hop(piece, stage).wait_send()
    for number in range(blocks):

        @pl.when(me == owners[number])
        def collect(number=number):
            deliver_here(number).wait()

            @pl.loop(0, devices)
            def forward(source):
                @pl.when(source != me)
                def arrived():
                    deliver(number, source).wait_recv()

                cross(number, source, core).start()

            @pl.loop(0, devices)
            def finish(source):
                cross(number, source, core).wait_send()
                cross(number, source, 1 - core).wait_recv()

        @pl.when(me != owners[number])
        def end_one(number=number):
            deliver(number, me).wait_send()

    for number in range(count):
        share(number, core).wait_send()
        share(number, 1 - core).wait_recv()


def reduce_rows(grads, stats, old, owners, devices):
    levels, count, blocks = bit_count(devices), len(grads), len(old)
    lead = (2,) * levels
    dma = pltpu.SemaphoreType.DMA
    shapes = [grad.shape[levels:] for grad in grads]
    halves = [(rows, columns // 2) for rows, columns in shapes]
    kinds = [grad.dtype for grad in grads]
    pieces = cut_pieces(REDUCE_PARTS, halves)
    scratch = [pltpu.VMEM(lead + shape, kind) for shape, kind in zip(halves, kinds)] * 2
    scratch += [pltpu.VMEM(lead[1:] + shape, jnp.float32) for shape in halves]
    for number, row, rows, column, columns in pieces:
        for stage in range(levels):
            scratch.append(pltpu.VMEM((2,) * (levels - 1 - stage) + (rows, columns), kinds[number]))
    scratch += [pltpu.VMEM(halves[number], kinds[number]) for number in range(blocks)]
    scratch.append(pltpu.VMEM((levels + 1, 16, 128), jnp.float32))
    scratch += [dma((len(pieces),))] * 3 + [dma((len(pieces), levels))] * 2 + [dma((count,))] * 2
    scratch += [dma((levels + 1,))] * 2 + [dma, dma((blocks,))] + [dma((blocks, devices))] * 3
    vmem, anywhere = pl.BlockSpec(memory_space=pltpu.VMEM), pl.BlockSpec(memory_space=pl.ANY)
    found = pl.pallas_call(
        functools.partial(reduce_kernel, levels, pieces, count, owners, devices),
        out_shape=[jax.ShapeDtypeStruct(shape, jnp.float32) for shape in shapes]
        + [jax.ShapeDtypeStruct((16, 128), jnp.float32)]
        + [jax.ShapeDtypeStruct((devices,) + shapes[number], kinds[number]) for number in range(blocks)],
        in_specs=[anywhere] * count + [vmem] * (1 + blocks),
        out_specs=[vmem] * (count + 1) + [anywhere] * blocks,
        scratch_shapes=scratch,
        compiler_params=pltpu.CompilerParams(
            collective_id=2, has_side_effects=True, vmem_limit_bytes=60 * 2**20
        ),
        name="reduce_rows",
    )(*grads, stats, *old)
    return found[:blocks], found[blocks:count], found[count], found[count + 1 :]


def return_kernel(owners, count, devices, rates, *refs):
    wholes, masters, rest = refs[:count], refs[count : 2 * count], refs[2 * count :]
    stats, adam_in, rest = rest[0], rest[1:9], rest[9:]
    updated, adam_out, rest = rest[:count], rest[count : count + 6], rest[count + 6 :]
    rows, rest = rest[:count], rest[count:]
    here_sem, send_sem, recv_sem, cross_send, cross_recv = rest
    me, core = lax.axis_index("dp"), lax.axis_index("mp")
    barrier = pltpu.get_barrier_semaphore()
    owning = functools.reduce(jnp.logical_or, [me == owner for owner in owners])
    for owner in owners:

        @pl.when(me != owner)
        def greet_owner(owner=owner):
            pl.semaphore_signal(
                barrier, inc=1, device_id={"dp": owner, "mp": core}, device_id_type=MESH_ID
            )

    pl.semaphore_signal(barrier, inc=1, device_id={"dp": me, "mp": 1 - core}, device_id_type=MESH_ID)

    @pl.when(owning)
    def wait_all():
        pl.semaphore_wait(barrier, devices)

    @pl.when(jnp.logical_not(owning))
    def wait_pair():
        pl.semaphore_wait(barrier, 1)

    def half(number, which):
        width = rows[number].shape[1] // 2
        return (slice(None), pl.ds(pl.multiple_of(which * width, 128), width))

    def hop(number, target):
        return pltpu.make_async_remote_copy(
            src_ref=wholes[number].at[(target,) + half(number, core)],
            dst_ref=rows[number].at[half(number, core)],
            send_sem=send_sem.at[number, target],
            recv_sem=recv_sem.at[number],
            device_id={"dp": target, "mp": core},
            device_id_type=MESH_ID,
        )

    def cross(number, which):
        region = rows[number].at[half(number, which)]
        return pltpu.make_async_remote_copy(
            src_ref=region,
            dst_ref=region,
            send_sem=cross_send.at[number],
            recv_sem=cross_recv.at[number],
            device_id={"dp": me, "mp": 1 - core},
            device_id_type=MESH_ID,
        )

    for number in range(count):

        @pl.when(me == owners[number])
        def hand_out(number=number):
            own = pltpu.make_async_copy(
                wholes[number].at[(me,) + half(number, core)], rows[number].at[half(number, core)], here_sem
            )
            own.start()

            @pl.loop(0, devices)
            def start_one(target):
                @pl.when(target != me)
                def start_other():
                    hop(number, target).start()

            own.wait()

    norm = jnp.sqrt(jnp.sum(jnp.sum(stats[0:8, :], axis=0, keepdims=True), axis=1, keepdims=True))
    factor = jnp.minimum(1.0, CLIP_MAX / (norm + 1e-06))
    for place_in in range(2):
        weight, first, second, grad = [ref[...] for ref in adam_in[4 * place_in : 4 * place_in + 4]]
        made = adam_update(weight, first, second, grad * factor, DECAY)
        for place_out in range(3):
            adam_out[3 * place_in + place_out][...] = made[place_out]
    for number in range(count):

        @pl.when(me != owners[number])
        def arrive(number=number):
            hop(number, me).wait_recv()

        cross(number, core).start()
    for number in range(count):
        cross(number, core).wait_send()
        cross(number, 1 - core).wait_recv()
        updated[number][...] = masters[number][...] * (1.0 - LR_MUON * DECAY) - rates[number] * rows[
            number
        ][...].astype(jnp.float32)

        @pl.when(me == owners[number])
        def end_out(number=number):
            @pl.loop(0, devices)
            def end_one(target):
                @pl.when(target != me)
                def end_other():
                    hop(number, target).wait_send()


def return_rows(wholes, masters, stats, adam, owners, devices):
    count = len(wholes)
    rates = []
    for whole in wholes:
        rates.append(LR_MUON * 0.2 * math.sqrt(max(whole.shape[0] * whole.shape[1], whole.shape[2])))
    dma = pltpu.SemaphoreType.DMA
    vmem = pl.BlockSpec(memory_space=pltpu.VMEM)
    moved = (adam[0], adam[1], adam[2], adam[4], adam[5], adam[6])
    found = pl.pallas_call(
        functools.partial(return_kernel, owners, count, devices, rates),
        out_shape=[jax.ShapeDtypeStruct(master.shape, jnp.float32) for master in masters]
        + [jax.ShapeDtypeStruct(piece.shape, jnp.float32) for piece in moved],
        in_specs=[pl.BlockSpec(memory_space=pl.ANY)] * count + [vmem] * (count + 9),
        out_specs=[vmem] * (count + 6),
        scratch_shapes=[pltpu.VMEM(whole.shape[1:], whole.dtype) for whole in wholes]
        + [dma, dma((count, devices)), dma((count,)), dma((count,)), dma((count,))],
        compiler_params=pltpu.CompilerParams(
            collective_id=4, has_side_effects=True, vmem_limit_bytes=40 * 2**20
        ),
        name="return_rows",
    )(*wholes, *masters, stats, *adam)
    return found[:count], found[count : count + 3], found[count + 3 :]


def muon_kernel(owners, shapes, *refs):
    count = len(owners)
    mats, outs = refs[:count], refs[count : 2 * count]
    exact, wide, wide_low, tall, wide_out, tall_out, gram, square, poly, chain, left, right, sem = refs[2 * count :]
    me, core = lax.axis_index("dp"), lax.axis_index("mp")
    side = gram.shape[0]
    step = 256
    bf = jnp.bfloat16

    def dims(number):
        height, breadth = shapes[number]
        return height, breadth, LONG_COLS[number]

    def span(index):
        return pl.ds(pl.multiple_of(index * step, step), step)

    def split(value):
        high = value.astype(bf)
        return high, (value - high.astype(jnp.float32)).astype(bf)

    gram[...] = jnp.zeros_like(gram)
    for number in range(count):

        @pl.when(me == owners[number])
        def start(number=number):
            height, breadth, long_cols = dims(number)
            short = min(height, breadth)
            held = (wide if long_cols else tall).at[:height, :breadth]
            fine = mats[number].dtype == jnp.float32
            load = pltpu.make_async_copy(mats[number], exact if fine else held, sem)
            load.start()
            load.wait()
            if fine:
                rest = wide_low

                @pl.loop(0, height // step)
                def part_rows(index):
                    high, low = split(exact[span(index), :])
                    held[span(index), :] = high
                    rest[span(index), :] = low

            @pl.loop(0, short // step)
            def gram_rows(index):
                if long_cols:
                    part = held[span(index), :]
                    dims_in = (((1,), (1,)), ((), ()))
                else:
                    part = held[:, span(index)]
                    dims_in = (((0,), (0,)), ((), ()))
                total = lax.dot_general(part, held[...], dims_in, preferred_element_type=jnp.float32)
                if fine:
                    total = total + lax.dot_general(
                        part, rest[...], dims_in, preferred_element_type=jnp.float32
                    )
                    total = total + lax.dot_general(
                        rest[span(index), :], held[...], dims_in, preferred_element_type=jnp.float32
                    )
                gram[span(index), :short] = total

    owning = functools.reduce(jnp.logical_or, [me == owner for owner in owners])

    @pl.when(owning)
    def iterate():
        def eye(index):
            row = lax.broadcasted_iota(jnp.int32, (step, side), 0) + index * step
            column = lax.broadcasted_iota(jnp.int32, (step, side), 1)
            return row == column

        trace = jnp.float32(0.0)
        for index in range(side // step):
            trace = trace + jnp.sum(jnp.where(eye(index), gram[index * step : (index + 1) * step, :], 0.0))
        scale = 1.0 / (jnp.sqrt(jnp.full((8, 128), trace, jnp.float32)) + 1e-07)
        scale = scale[0:1, 0:1]
        square_scale = scale * scale

        @pl.loop(0, side // step)
        def prepare(index):
            gram[span(index), :] = gram[span(index), :] * square_scale

        def set_left(source):
            @pl.loop(0, side // step)
            def set_rows(index):
                high, low = split(source[span(index), :])
                left[span(index), 0:side] = high
                left[span(index), side : 2 * side] = high
                left[span(index), 2 * side : 3 * side] = low

        def set_right(source):
            @pl.loop(0, side // step)
            def set_rows(index):
                high, low = split(source[span(index), :])
                right[pl.ds(pl.multiple_of(index * step, step), step), :] = high
                right[pl.ds(pl.multiple_of(side + index * step, step), step), :] = low
                right[pl.ds(pl.multiple_of(2 * side + index * step, step), step), :] = high

        def multiply(target):
            @pl.loop(0, side // step)
            def rows(index):
                target[span(index), :] = jnp.dot(
                    left[span(index), :], right[...], preferred_element_type=jnp.float32
                )

        @pl.loop(0, NS_ITERS)
        def newton(iteration):
            set_left(gram)
            set_right(gram)
            multiply(square)

            @pl.loop(0, side // step)
            def polynomial(index):
                ones = jnp.where(
                    lax.broadcasted_iota(jnp.int32, (step, side), 0) + index * step
                    == lax.broadcasted_iota(jnp.int32, (step, side), 1),
                    NS_A,
                    0.0,
                )
                poly[span(index), :] = ones + NS_B * gram[span(index), :] + NS_C * square[span(index), :]

            set_right(poly)

            @pl.when(iteration < NS_ITERS - 1)
            def advance():
                multiply(square)
                set_left(square)
                multiply(gram)

            @pl.when(iteration == 0)
            def first():
                chain[...] = poly[...]

            @pl.when(iteration > 0)
            def later():
                set_left(chain)
                multiply(chain)

        @pl.loop(0, side // step)
        def finish(index):
            high, low = split(chain[span(index), :] * scale)
            left[span(index), 0:side] = high
            left[span(index), side : 2 * side] = low

    for number in range(count):

        @pl.when(me == owners[number])
        def end(number=number):
            height, breadth, long_cols = dims(number)
            short = min(height, breadth)
            width = breadth // 2
            part = pl.ds(pl.multiple_of(core * width, 128), width)
            if long_cols:
                held, made = wide.at[:height, :breadth], wide_out.at[:height, :width]

                @pl.loop(0, height // step)
                def wide_rows(index):
                    total = jnp.dot(
                        left[span(index), :short], held[:, part], preferred_element_type=jnp.float32
                    ) + jnp.dot(
                        left[span(index), side : side + short],
                        held[:, part],
                        preferred_element_type=jnp.float32,
                    )
                    if mats[number].dtype == jnp.float32:
                        total = total + jnp.dot(
                            left[span(index), :short],
                            wide_low[:, part],
                            preferred_element_type=jnp.float32,
                        )
                    made[span(index), :] = total.astype(bf)
            else:
                held, made = tall.at[:height, :breadth], tall_out.at[:height, :width]

                @pl.loop(0, height // step)
                def tall_rows(index):
                    low = pl.ds(pl.multiple_of(side + core * width, 128), width)
                    total = jnp.dot(
                        held[span(index), :], left[:short, part], preferred_element_type=jnp.float32
                    ) + jnp.dot(
                        held[span(index), :], left[:short, low], preferred_element_type=jnp.float32
                    )
                    made[span(index), :] = total.astype(bf)

            save = pltpu.make_async_copy(made, outs[number].at[:, part], sem)
            save.start()
            save.wait()


def orthogonalize(mats, owners):
    count = len(mats)
    shapes = [mat.shape for mat in mats]
    side = max(min(shape) for shape in shapes)
    longest = max(max(shape) for shape in shapes)
    square = pltpu.VMEM((side, side), jnp.float32)
    (fine,) = [mat.shape for mat in mats if mat.dtype == jnp.float32]
    return pl.pallas_call(
        functools.partial(muon_kernel, owners, shapes),
        out_shape=[jax.ShapeDtypeStruct(shape, jnp.bfloat16) for shape in shapes],
        in_specs=[pl.BlockSpec(memory_space=pl.ANY)] * count,
        out_specs=[pl.BlockSpec(memory_space=pl.ANY)] * count,
        scratch_shapes=[
            pltpu.VMEM(fine, jnp.float32),
            pltpu.VMEM((side, longest), jnp.bfloat16),
            pltpu.VMEM(fine, jnp.bfloat16),
            pltpu.VMEM((longest, side), jnp.bfloat16),
            pltpu.VMEM((side, longest // 2), jnp.bfloat16),
            pltpu.VMEM((longest, side // 2), jnp.bfloat16),
            square,
            square,
            square,
            square,
            pltpu.VMEM((side, 3 * side), jnp.bfloat16),
            pltpu.VMEM((3 * side, side), jnp.bfloat16),
            pltpu.SemaphoreType.DMA,
        ],
        compiler_params=pltpu.CompilerParams(vmem_limit_bytes=56 * 2**20),
        name="orthogonalize",
    )(*mats)


def window_place(position):
    time_row = (position // GF + GT - SHIFT) % GT
    freq_col = (position % GF + GF - SHIFT) % GF
    window = (time_row // WIN) * (GF // WIN) + freq_col // WIN
    return window * (WIN * WIN) + (time_row % WIN) * WIN + freq_col % WIN


def window_sinusoid(channels):
    quarter = channels // 4
    frequency = 1.0 / 10000.0 ** (np.arange(quarter) / quarter)
    position = np.arange(NPATCH)
    time_rows = (position // GF)[:, None] * frequency
    freq_cols = (position % GF)[:, None] * frequency
    table = np.concatenate([np.sin(time_rows), np.cos(time_rows), np.sin(freq_cols), np.cos(freq_cols)], axis=1)
    moved = np.zeros_like(table)
    moved[window_place(position)] = table
    return moved.astype(np.float32)


def window_patches(spec):
    position = np.arange(NPATCH)
    row = np.empty(NPATCH, np.int32)
    row[window_place(position)] = position
    rows = row[:, None]
    take = (rows // GF == np.arange(GT)[None, :]).astype(np.float32)
    column = lax.broadcasted_iota(jnp.int32, (NPATCH, PS * GF * PS), 1)
    inside = (column // PS) % GF == jnp.asarray(rows % GF)
    source = np.arange(PS * GF * PS)[:, None]
    target = np.arange(PATCH)[None, :]
    fold = np.logical_and(source // (GF * PS) == target // PS, source % PS == target % PS)
    lines = spec.reshape(spec.shape[0], GT, PS * GF * PS)
    spread = jnp.einsum(
        "rt,ctl->crl", jnp.asarray(take, jnp.bfloat16), lines, preferred_element_type=jnp.float32
    )
    spread = jnp.where(inside, spread, 0.0).astype(jnp.bfloat16)
    found = jnp.einsum(
        "crl,lq->crq", spread, jnp.asarray(fold, jnp.bfloat16), preferred_element_type=jnp.float32
    )
    return found.astype(jnp.bfloat16)


@jax.custom_vjp
def times(inputs, matrix):
    return jnp.dot(inputs.astype(jnp.bfloat16), matrix.astype(jnp.bfloat16), preferred_element_type=jnp.float32)


def times_keep(inputs, matrix):
    short = inputs.astype(jnp.bfloat16)
    return jnp.dot(short, matrix.astype(jnp.bfloat16), preferred_element_type=jnp.float32), (short, matrix)


def times_back(kept, grad):
    short, matrix = kept
    grad = grad.astype(jnp.bfloat16)
    back = lax.dot_general(
        grad, matrix.astype(jnp.bfloat16), (((1,), (1,)), ((), ())), preferred_element_type=jnp.float32
    )
    gain = lax.dot_general(short, grad, (((0,), (0,)), ((), ())), preferred_element_type=jnp.float32)
    return back, gain.astype(matrix.dtype)


times.defvjp(times_keep, times_back)


def soft_rows(scores, allowed, scaling):
    scores = jnp.where(allowed, scores * scaling, -1e30)
    exponent = jnp.exp(scores - jnp.max(scores, axis=-1, keepdims=True))
    return exponent / jnp.sum(exponent, axis=-1, keepdims=True)


def dot_rows(left, right):
    return lax.dot_general(left, right, (((1,), (1,)), ((), ())), preferred_element_type=jnp.float32)


def dot_columns(left, right):
    return lax.dot_general(left, right, (((0,), (0,)), ((), ())), preferred_element_type=jnp.float32)


def head_lanes(value, head, size):
    lane = lax.broadcasted_iota(jnp.int32, value.shape, 1)
    return jnp.where(lane // size == head, value, jnp.zeros_like(value))


def attention_kernel(size, joined, allowed, out):
    width = out.shape[1]
    per = 128 // size
    allow = jnp.broadcast_to(allowed[...], (out.shape[0], allowed.shape[1])) > 0.0
    for lane in range(0, width, 128):
        queries = joined[:, lane : lane + 128]
        key_rows = joined[:, width + lane : width + lane + 128]
        values = joined[:, 2 * width + lane : 2 * width + lane + 128]
        total = jnp.zeros(queries.shape, jnp.float32)
        for head in range(per):
            scores = dot_rows(queries, head_lanes(key_rows, head, size))
            soft = soft_rows(scores, allow, size ** (-0.5)).astype(jnp.bfloat16)
            total = total + jnp.dot(
                soft, head_lanes(values, head, size), preferred_element_type=jnp.float32
            )
        out[:, lane : lane + 128] = total.astype(jnp.bfloat16)


def attention_back_kernel(size, joined, allowed, grad, out, query_sum, value_sum):
    width = grad.shape[1]
    per = 128 // size
    scaling = size ** (-0.5)
    allow = jnp.broadcast_to(allowed[...], (grad.shape[0], allowed.shape[1])) > 0.0

    @pl.when(pl.program_id(0) == 0)
    def clear():
        query_sum[...] = jnp.zeros_like(query_sum)
        value_sum[...] = jnp.zeros_like(value_sum)

    for lane in range(0, width, 128):
        queries = joined[:, lane : lane + 128]
        key_rows = joined[:, width + lane : width + lane + 128]
        values = joined[:, 2 * width + lane : 2 * width + lane + 128]
        pull = grad[:, lane : lane + 128]
        query_grad = jnp.zeros(queries.shape, jnp.float32)
        key_grad = jnp.zeros(queries.shape, jnp.float32)
        value_grad = jnp.zeros(queries.shape, jnp.float32)
        for head in range(per):
            keys_here = head_lanes(key_rows, head, size)
            soft = soft_rows(dot_rows(queries, keys_here), allow, scaling)
            soft_grad = dot_rows(pull, head_lanes(values, head, size))
            score_grad = soft * (soft_grad - jnp.sum(soft * soft_grad, axis=-1, keepdims=True))
            score_grad = (score_grad * scaling).astype(jnp.bfloat16)
            query_grad = query_grad + jnp.dot(score_grad, keys_here, preferred_element_type=jnp.float32)
            key_grad = key_grad + dot_columns(score_grad, head_lanes(queries, head, size))
            value_grad = value_grad + dot_columns(soft.astype(jnp.bfloat16), head_lanes(pull, head, size))
        out[:, lane : lane + 128] = query_grad.astype(jnp.bfloat16)
        out[:, width + lane : width + lane + 128] = key_grad.astype(jnp.bfloat16)
        out[:, 2 * width + lane : 2 * width + lane + 128] = value_grad.astype(jnp.bfloat16)
        query_sum[0:1, lane : lane + 128] += jnp.sum(query_grad, axis=0, keepdims=True)
        value_sum[0:1, lane : lane + 128] += jnp.sum(value_grad, axis=0, keepdims=True)


def window_fold(value, heads):
    lane = lax.broadcasted_iota(jnp.int32, (1, 1, value.shape[1]), 2) // (WIN * WIN)
    value = value.reshape(heads, 8, WIN * WIN, value.shape[1])
    found = value[:, 0]
    for window in range(1, 8):
        found = jnp.where(lane == window, value[:, window], found)
    return found


def window_spread(value):
    heads = value.shape[0]
    short = value.astype(jnp.bfloat16)
    lane = lax.broadcasted_iota(jnp.int32, short.shape, 2) // (WIN * WIN)
    parts = []
    for head in range(heads):
        for window in range(8):
            parts.append(
                jnp.where(lane[head] == window, short[head], jnp.zeros_like(short[head]))
            )
    return jnp.concatenate(parts, axis=0)


def stack_heads(value, size):
    per = value.shape[1] // size
    return jnp.concatenate([head_lanes(value, head, size) for head in range(per)], axis=0)


def unstack_heads(value, size):
    rows = value.shape[1]
    per = value.shape[0] // rows
    lane = lax.broadcasted_iota(jnp.int32, (rows, rows), 1) // size
    found = value[:rows]
    for head in range(1, per):
        found = jnp.where(lane == head, value[head * rows : (head + 1) * rows], found)
    return found


def soft_fold(queries, keys_here, allow, size):
    scores = window_fold(dot_rows(keys_here, queries), 128 // size)
    scores = jnp.where(allow, scores * size ** (-0.5), -1e30)
    exponent = jnp.exp(scores - jnp.max(scores, axis=1, keepdims=True))
    return exponent / jnp.sum(exponent, axis=1, keepdims=True)


def window_kernel(size, joined, allowed, out):
    width = out.shape[1]
    allow = allowed[...][None] > 0.0
    for lane in range(0, width, 128):
        queries = joined[:, lane : lane + 128]
        keys_here = stack_heads(joined[:, width + lane : width + lane + 128], size)
        values_here = stack_heads(joined[:, 2 * width + lane : 2 * width + lane + 128], size)
        soft = window_spread(soft_fold(queries, keys_here, allow, size))
        out[:, lane : lane + 128] = dot_columns(soft, values_here).astype(jnp.bfloat16)


def window_back_kernel(size, joined, allowed, grad, out, query_sum, value_sum):
    width = grad.shape[1]
    allow = allowed[...][None] > 0.0

    @pl.when(pl.program_id(0) == 0)
    def clear():
        query_sum[...] = jnp.zeros_like(query_sum)
        value_sum[...] = jnp.zeros_like(value_sum)

    for lane in range(0, width, 128):
        queries = joined[:, lane : lane + 128]
        keys_here = stack_heads(joined[:, width + lane : width + lane + 128], size)
        values_here = stack_heads(joined[:, 2 * width + lane : 2 * width + lane + 128], size)
        pull = grad[:, lane : lane + 128]
        soft = soft_fold(queries, keys_here, allow, size)
        soft_grad = window_fold(dot_rows(values_here, pull), 128 // size)
        score_grad = soft * (soft_grad - jnp.sum(soft * soft_grad, axis=1, keepdims=True))
        score_grad = window_spread(score_grad * size ** (-0.5))
        soft = window_spread(soft)
        query_grad = dot_columns(score_grad, keys_here)
        key_grad = unstack_heads(jnp.dot(score_grad, queries, preferred_element_type=jnp.float32), size)
        value_grad = unstack_heads(jnp.dot(soft, pull, preferred_element_type=jnp.float32), size)
        out[:, lane : lane + 128] = query_grad.astype(jnp.bfloat16)
        out[:, width + lane : width + lane + 128] = key_grad.astype(jnp.bfloat16)
        out[:, 2 * width + lane : 2 * width + lane + 128] = value_grad.astype(jnp.bfloat16)
        query_sum[0:1, lane : lane + 128] += jnp.sum(query_grad, axis=0, keepdims=True)
        value_sum[0:1, lane : lane + 128] += jnp.sum(value_grad, axis=0, keepdims=True)


def attention_parts(joined, allowed, rows):
    steps = joined.shape[0] // rows
    period = allowed.shape[0]
    wide = pl.BlockSpec((rows, joined.shape[1]), lambda step: (step, 0))
    mask = pl.BlockSpec((None,) + allowed.shape[1:], lambda step: (lax.rem(step, period), 0, 0))
    narrow_rows = pl.BlockSpec((rows, joined.shape[1] // 3), lambda step: (step, 0))
    return steps, wide, mask, narrow_rows


def attention_forward(kernel, joined, allowed, rows, size):
    steps, wide, mask, part = attention_parts(joined, allowed, rows)
    return pl.pallas_call(
        functools.partial(kernel, size),
        grid=(steps,),
        out_shape=jax.ShapeDtypeStruct((joined.shape[0], joined.shape[1] // 3), jnp.bfloat16),
        in_specs=[wide, mask],
        out_specs=part,
        compiler_params=pltpu.CompilerParams(vmem_limit_bytes=40 * 2**20),
        name="attention_forward",
    )(joined, allowed)


def attention_backward(kernel, joined, allowed, grad, rows, size):
    steps, wide, mask, part = attention_parts(joined, allowed, rows)
    width = joined.shape[1] // 3
    total = pl.BlockSpec((8, width), lambda step: (0, 0))
    return pl.pallas_call(
        functools.partial(kernel, size),
        grid=(steps,),
        out_shape=[
            jax.ShapeDtypeStruct(joined.shape, jnp.bfloat16),
            jax.ShapeDtypeStruct((8, width), jnp.float32),
            jax.ShapeDtypeStruct((8, width), jnp.float32),
        ],
        in_specs=[wide, mask, part],
        out_specs=[wide, total, total],
        compiler_params=pltpu.CompilerParams(vmem_limit_bytes=40 * 2**20),
        name="attention_backward",
    )(joined, allowed, grad)


def attention_block(forward, backward, rows, size):
    def join(normed, matrix, query_bias, value_bias):
        width = matrix.shape[1] // 3
        bias = jnp.concatenate([query_bias, jnp.zeros((width,), jnp.float32), value_bias])
        joined = jnp.dot(normed, matrix.astype(jnp.bfloat16), preferred_element_type=jnp.float32)
        return (joined + bias).astype(jnp.bfloat16)

    @jax.custom_vjp
    def apply(normed, matrix, query_bias, value_bias, allowed):
        joined = join(normed.astype(jnp.bfloat16), matrix, query_bias, value_bias)
        return attention_forward(forward, joined, allowed, rows, size).astype(jnp.float32)

    def keep(normed, matrix, query_bias, value_bias, allowed):
        short = normed.astype(jnp.bfloat16)
        joined = join(short, matrix, query_bias, value_bias)
        made = attention_forward(forward, joined, allowed, rows, size).astype(jnp.float32)
        return made, (short, matrix, joined, allowed)

    def back(kept, grad):
        short, matrix, joined, allowed = kept
        pulled, query_sum, value_sum = attention_backward(
            backward, joined, allowed, grad.astype(jnp.bfloat16), rows, size
        )
        normed_grad = dot_rows(pulled, matrix.astype(jnp.bfloat16))
        matrix_grad = dot_columns(short, pulled).astype(matrix.dtype)
        return normed_grad, matrix_grad, query_sum[0], value_sum[0], jnp.zeros_like(allowed)

    apply.defvjp(keep, back)
    return apply


encoder_attention = attention_block(attention_kernel, attention_back_kernel, SLOTS, HEAD)
decoder_attention = attention_block(window_kernel, window_back_kernel, 8 * WIN * WIN, DHEAD)


def window_allowed():
    position = np.arange(NPATCH)
    window, inner = position // (WIN * WIN), position % (WIN * WIN)
    time_row = window // (GF // WIN) * WIN + inner // WIN
    freq_col = window % (GF // WIN) * WIN + inner % WIN
    region = (time_row >= GT - WIN).astype(np.int32) + (time_row >= GT - SHIFT)
    region = region * 3 + (freq_col >= GF - WIN) + (freq_col >= GF - SHIFT)
    region = region.reshape(-1, 8, 1, WIN * WIN)
    same = region == region.transpose(0, 1, 3, 2)
    return same.transpose(0, 2, 1, 3).reshape(-1, WIN * WIN, 8 * WIN * WIN).astype(np.float32)


@jax.custom_vjp
def gelu(value):
    return value * (0.5 + 0.5 * lax.erf(value * math.sqrt(0.5)))


def gelu_keep(value):
    portion = 0.5 + 0.5 * lax.erf(value * math.sqrt(0.5))
    slope = portion + value * jnp.exp(-0.5 * value * value) * (1.0 / math.sqrt(2.0 * math.pi))
    return value * portion, slope


def gelu_back(slope, grad):
    return (grad * slope,)


gelu.defvjp(gelu_keep, gelu_back)


def local_loss(weights, patches, keep, counts):
    clips = patches.shape[0]
    pieces = unpack(weights[10])
    keep = jnp.pad(keep, ((0, 0), (0, SLOTS - VIS)))
    spot = window_place(keep)
    chosen = (spot[:, :, None] == jnp.arange(NPATCH)[None, None, :]).astype(jnp.float32)
    shown = chosen * (jnp.arange(SLOTS)[None, :] < counts[:, None])[:, :, None]
    picked = jnp.einsum("cjp,cpv->cjv", chosen.astype(jnp.bfloat16), patches, preferred_element_type=jnp.float32)
    where = jnp.einsum("cjp,pd->cjd", chosen, window_sinusoid(D), precision=HIGH)
    hidden = times(picked.reshape(-1, PATCH), weights[8][:, :D]) + pieces[11] + where.reshape(-1, D)
    normed = layer_norm(hidden, pieces[0], pieces[1])
    visible = (jnp.arange(SLOTS)[None, :] < counts[:, None]).astype(jnp.float32)[:, None, :]
    attended = encoder_attention(normed, weights[0], pieces[2], pieces[3], visible)
    hidden = hidden + times(attended, weights[1]) + pieces[4]
    normed = layer_norm(hidden, pieces[5], pieces[6])
    inner = gelu(times(normed, weights[2]) + pieces[7])
    hidden = hidden + times(inner, weights[3]) + pieces[8]
    latent = layer_norm(hidden, pieces[9], pieces[10])

    pieces = pieces[12:]
    placed = times(latent, weights[9]) + pieces[0]
    filled = jnp.einsum("cjp,cjd->cpd", shown, placed.reshape(clips, SLOTS, DD), precision=HIGH)
    cells = jnp.sum(shown, axis=1)
    hidden = filled + (1.0 - cells)[..., None] * pieces[1] + window_sinusoid(DD)
    hidden = hidden.reshape(-1, DD)
    normed = layer_norm(hidden, pieces[2], pieces[3])
    attended = decoder_attention(normed, weights[4], pieces[4], pieces[5], jnp.asarray(window_allowed()))
    hidden = hidden + times(attended, weights[5]) + pieces[6]
    normed = layer_norm(hidden, pieces[7], pieces[8])
    inner = gelu(times(normed, weights[6]) + pieces[9])
    hidden = hidden + times(inner, weights[7]) + pieces[10]
    normed = layer_norm(hidden, pieces[11], pieces[12])
    predicted = times(normed, weights[8][:, D:].T) + pieces[13]
    patches = patches.astype(jnp.float32).reshape(-1, PATCH)
    centred = patches - jnp.mean(patches, axis=-1, keepdims=True)
    target = centred * lax.rsqrt(jnp.mean(centred * centred, axis=-1, keepdims=True) + 1e-06)
    deviation = predicted - target
    patch_error = jnp.mean(deviation * deviation, axis=-1)
    return jnp.sum((1.0 - cells.reshape(-1)) * patch_error)


def quick_body(
    spectrogram, keep, counts, *rest
):
    masters = rest[:8] + (rest[16], rest[19], rest[22])
    moments = rest[8:16]
    devices = lax.axis_size("dp")
    lead = (2,) * bit_count(devices)
    own = list(masters)
    vector_rows = own[10].shape[0]
    spare = VEC_ROWS * VEC_COLS
    own[10] = jnp.pad(own[10], (0, spare - vector_rows)).reshape(VEC_ROWS, VEC_COLS)
    row = lax.broadcasted_iota(jnp.int32, (8, 128), 0)
    column = lax.broadcasted_iota(jnp.int32, (8, 128), 1)
    first = jnp.logical_and(row == 0, column == 0)
    count_part = jnp.sum(NPATCH - counts).astype(jnp.float32)
    gathered, tally = gather_rows(own, jnp.where(first, count_part, 0.0), devices)
    mask_count = tally[0, 0]
    weights = [piece.reshape(-1, piece.shape[-1]) for piece in gathered[:10]]
    weights[4] = weights[4].astype(jnp.float32)
    vectors = gathered[10].reshape(devices, spare)[:, :vector_rows].reshape(-1).astype(jnp.float32)
    patches = window_patches(spectrogram)
    loss_part, pull = jax.vjp(
        lambda *params: local_loss(params, patches, keep, counts), *weights, vectors
    )
    grads = list(pull(1.0 / mask_count))
    grads[10] = jnp.pad(grads[10].reshape(devices, vector_rows), ((0, 0), (0, spare - vector_rows)))
    grads[10] = grads[10].reshape(lead + (VEC_ROWS, VEC_COLS))
    for number in range(10):
        grad = grads[number]
        grads[number] = grad.reshape(lead + (grad.shape[0] // devices, grad.shape[1]))
    renewed, others, stats, collected = reduce_rows(
        grads, jnp.where(first, loss_part, 0.0), moments, OWNERS, devices
    )
    loss_sum = stats[8, 0]
    grad_norm = jnp.sqrt(jnp.sum(stats[:8]))
    factor = jnp.minimum(1.0, CLIP_MAX / (grad_norm + 1e-06))
    made = orthogonalize([piece.reshape(-1, piece.shape[2]) for piece in collected], OWNERS)
    made = [piece.reshape(devices, -1, piece.shape[1]) for piece in made]
    adam = (*rest[16:19], others[0], *rest[19:22], others[1])
    new_weights, patch_new, embed_new = return_rows(made, masters[:8], stats, adam, OWNERS, devices)
    vector_grad = others[2].reshape(-1)[:vector_rows] * factor
    vector_new = adam_update(*rest[22:25], vector_grad, 0.0)
    return (loss_sum, mask_count, grad_norm, *new_weights, *renewed, *patch_new, *embed_new, *vector_new)


def body(
    spectrogram,
    keep,
    counts,
    enc_qkv,
    enc_out,
    enc_up,
    enc_down,
    dec_qkv,
    dec_out,
    dec_up,
    dec_down,
    mom_enc_qkv,
    mom_enc_out,
    mom_enc_up,
    mom_enc_down,
    mom_dec_qkv,
    mom_dec_out,
    mom_dec_up,
    mom_dec_down,
    patch_maps,
    patch_first,
    patch_second,
    embed_map,
    embed_first,
    embed_second,
    vectors,
    vector_first,
    vector_second,
):
    masters = (
        enc_qkv,
        enc_out,
        enc_up,
        enc_down,
        dec_qkv,
        dec_out,
        dec_up,
        dec_down,
        patch_maps,
        embed_map,
        vectors,
    )
    moments = (
        mom_enc_qkv,
        mom_enc_out,
        mom_enc_up,
        mom_enc_down,
        mom_dec_qkv,
        mom_dec_out,
        mom_dec_up,
        mom_dec_down,
    )
    sent = tuple((weight.astype(jnp.bfloat16) for weight in masters))
    gathered = (
        lax.all_gather(sent[0], "dp", axis=0, tiled=True),
        lax.all_gather(sent[1], "dp", axis=0, tiled=True),
        lax.all_gather(sent[2], "dp", axis=0, tiled=True),
        lax.all_gather(sent[3], "dp", axis=0, tiled=True),
        lax.all_gather(sent[4], "dp", axis=0, tiled=True),
        lax.all_gather(sent[5], "dp", axis=0, tiled=True),
        lax.all_gather(sent[6], "dp", axis=0, tiled=True),
        lax.all_gather(sent[7], "dp", axis=0, tiled=True),
        lax.all_gather(sent[8], "dp", axis=0, tiled=True),
        lax.all_gather(sent[9], "dp", axis=0, tiled=True),
        lax.all_gather(sent[10], "dp", axis=0, tiled=True),
    )
    widened = tuple((piece.astype(jnp.float32) for piece in gathered))
    patches = patchify(spectrogram.astype(jnp.float32))
    latent = encode(widened, patches, keep, counts)
    loss_part = decode(widened, latent, patches, keep, counts)
    count_part = jnp.sum(NPATCH - counts).astype(jnp.float32)
    loss_sum, mask_count = lax.psum((loss_part, count_part), ("dp", "mp"))
    regathered = (
        lax.all_gather(sent[0], "dp", axis=0, tiled=True),
        lax.all_gather(sent[1], "dp", axis=0, tiled=True),
        lax.all_gather(sent[2], "dp", axis=0, tiled=True),
        lax.all_gather(sent[3], "dp", axis=0, tiled=True),
        lax.all_gather(sent[4], "dp", axis=0, tiled=True),
        lax.all_gather(sent[5], "dp", axis=0, tiled=True),
        lax.all_gather(sent[6], "dp", axis=0, tiled=True),
        lax.all_gather(sent[7], "dp", axis=0, tiled=True),
        lax.all_gather(sent[8], "dp", axis=0, tiled=True),
        lax.all_gather(sent[9], "dp", axis=0, tiled=True),
        lax.all_gather(sent[10], "dp", axis=0, tiled=True),
    )
    widened = tuple((piece.astype(jnp.float32) for piece in regathered))
    cotangent = 1.0 / mask_count
    unused, pull_decode = jax.vjp(
        lambda params, hidden: decode(params, hidden, patches, keep, counts), widened, latent
    )
    decode_grads, latent_grad = pull_decode(cotangent)
    unused, pull_encode = jax.vjp(lambda params: encode(params, patches, keep, counts), widened)
    (encode_grads,) = pull_encode(latent_grad)
    grads = jax.tree.map(jnp.add, decode_grads, encode_grads)
    reduced = (
        lax.psum_scatter(grads[0], "dp", scatter_dimension=0, tiled=True),
        lax.psum_scatter(grads[1], "dp", scatter_dimension=0, tiled=True),
        lax.psum_scatter(grads[2], "dp", scatter_dimension=0, tiled=True),
        lax.psum_scatter(grads[3], "dp", scatter_dimension=0, tiled=True),
        lax.psum_scatter(grads[4], "dp", scatter_dimension=0, tiled=True),
        lax.psum_scatter(grads[5], "dp", scatter_dimension=0, tiled=True),
        lax.psum_scatter(grads[6], "dp", scatter_dimension=0, tiled=True),
        lax.psum_scatter(grads[7], "dp", scatter_dimension=0, tiled=True),
        lax.psum_scatter(grads[8], "dp", scatter_dimension=0, tiled=True),
        lax.psum_scatter(grads[9], "dp", scatter_dimension=0, tiled=True),
        lax.psum_scatter(grads[10], "dp", scatter_dimension=0, tiled=True),
    )
    reduced = lax.psum(
        (
            reduced[0],
            reduced[1],
            reduced[2],
            reduced[3],
            reduced[4],
            reduced[5],
            reduced[6],
            reduced[7],
            reduced[8],
            reduced[9],
            reduced[10],
        ),
        "mp",
    )
    local_squares = functools.reduce(
        jnp.add, [jnp.sum(gradient * gradient) for gradient in reduced]
    )
    grad_norm = jnp.sqrt(lax.psum(local_squares, "dp"))
    factor = jnp.minimum(1.0, CLIP_MAX / (grad_norm + 1e-06))
    clipped = [gradient * factor for gradient in reduced]
    devices = lax.axis_size("dp")
    renewed = [0.5 * moments[number] + clipped[number] for number in range(8)]
    core = lax.axis_index("mp")
    halves = [take_half(renewed[number], number, core) for number in range(8)]
    shapes = [(masters[number].shape[0] * devices, masters[number].shape[1]) for number in range(8)]
    long_max = max((max(shape_pair) // 2 for shape_pair in shapes))
    short_max = max((min(shape_pair) for shape_pair in shapes))
    flat_max = max((shape_pair[0] * shape_pair[1] // (2 * devices) for shape_pair in shapes))
    owner = lax.axis_index("dp") % 8
    collected = (
        lax.all_gather(halves[0], "dp", axis=0, tiled=True),
        lax.all_gather(halves[1], "dp", axis=0, tiled=True),
        lax.all_gather(halves[2], "dp", axis=0, tiled=True),
        lax.all_gather(halves[3], "dp", axis=0, tiled=True),
        lax.all_gather(halves[4], "dp", axis=0, tiled=True),
        lax.all_gather(halves[5], "dp", axis=0, tiled=True),
        lax.all_gather(halves[6], "dp", axis=0, tiled=True),
        lax.all_gather(halves[7], "dp", axis=0, tiled=True),
    )
    iterate = lax.switch(
        owner,
        [partial(arrange, collected[number], number, long_max, short_max) for number in range(8)],
    )
    for iteration in range(NS_ITERS):
        gram_sum = lax.psum(jnp.dot(iterate.T, iterate, precision=HIGH), "mp")
        if iteration == 0:
            norm_scale = 1.0 / (jnp.sqrt(jnp.trace(gram_sum)) + 1e-07)
            iterate = iterate * norm_scale
            gram_sum = gram_sum * (norm_scale * norm_scale)
        polynomial = NS_B * gram_sum + NS_C * jnp.dot(gram_sum, gram_sum, precision=HIGH)
        iterate = NS_A * iterate + jnp.dot(iterate, polynomial, precision=HIGH)
    outgoing = lax.switch(
        owner,
        [
            partial(
                disperse, iterate, number, shapes[number][0], shapes[number][1], devices, flat_max
            )
            for number in range(8)
        ],
    )
    arriving = jax.tree.map(
        lambda part, own: part.astype(own.dtype),
        lax.all_to_all(shortened(outgoing), "dp", split_axis=0, concat_axis=0, tiled=True),
        outgoing,
    )
    mine = [
        restore(arriving[number], number, shapes[number][0], shapes[number][1], devices)
        for number in range(8)
    ]
    whole = (
        lax.all_gather(shortened(mine[0]), "mp", axis=1, tiled=True),
        lax.all_gather(shortened(mine[1]), "mp", axis=1, tiled=True),
        lax.all_gather(shortened(mine[2]), "mp", axis=1, tiled=True),
        lax.all_gather(shortened(mine[3]), "mp", axis=0, tiled=True),
        lax.all_gather(shortened(mine[4]), "mp", axis=1, tiled=True),
        lax.all_gather(shortened(mine[5]), "mp", axis=1, tiled=True),
        lax.all_gather(shortened(mine[6]), "mp", axis=1, tiled=True),
        lax.all_gather(shortened(mine[7]), "mp", axis=0, tiled=True),
    )
    new_weights = []
    for number in range(8):
        step_rate = LR_MUON * 0.2 * math.sqrt(max(shapes[number]))
        new_weights.append(masters[number] * (1.0 - LR_MUON * DECAY) - step_rate * whole[number])
    patch_new = adam_update(patch_maps, patch_first, patch_second, clipped[8], DECAY)
    embed_new = adam_update(embed_map, embed_first, embed_second, clipped[9], DECAY)
    vector_new = adam_update(vectors, vector_first, vector_second, clipped[10], 0.0)
    return (
        loss_sum,
        mask_count,
        grad_norm,
        new_weights[0],
        new_weights[1],
        new_weights[2],
        new_weights[3],
        new_weights[4],
        new_weights[5],
        new_weights[6],
        new_weights[7],
        renewed[0],
        renewed[1],
        renewed[2],
        renewed[3],
        renewed[4],
        renewed[5],
        renewed[6],
        renewed[7],
        patch_new[0],
        patch_new[1],
        patch_new[2],
        embed_new[0],
        embed_new[1],
        embed_new[2],
        vector_new[0],
        vector_new[1],
        vector_new[2],
    )


def solution(mesh):
    placed = (
        P(("dp", "mp"), None, None),
        P(("dp", "mp"), None),
        P(("dp", "mp")),
        P("dp", None),
        P("dp", None),
        P("dp", None),
        P("dp", None),
        P("dp", None),
        P("dp", None),
        P("dp", None),
        P("dp", None),
        P("dp", None),
        P("dp", None),
        P("dp", None),
        P("dp", None),
        P("dp", None),
        P("dp", None),
        P("dp", None),
        P("dp", None),
        P("dp", None),
        P("dp", None),
        P("dp", None),
        P("dp", None),
        P("dp", None),
        P("dp", None),
        P("dp"),
        P("dp"),
        P("dp"),
    )
    return jax.shard_map(
        quick_body if mesh.shape["dp"] == 16 else body,
        mesh=mesh,
        in_specs=placed,
        out_specs=(
            P(),
            P(),
            P(),
            P("dp", None),
            P("dp", None),
            P("dp", None),
            P("dp", None),
            P("dp", None),
            P("dp", None),
            P("dp", None),
            P("dp", None),
            P("dp", None),
            P("dp", None),
            P("dp", None),
            P("dp", None),
            P("dp", None),
            P("dp", None),
            P("dp", None),
            P("dp", None),
            P("dp", None),
            P("dp", None),
            P("dp", None),
            P("dp", None),
            P("dp", None),
            P("dp", None),
            P("dp"),
            P("dp"),
            P("dp"),
        ),
        check_vma=False,
    )
```

```python
from functools import partial
import functools
import math

import jax
import jax.numpy as jnp
import numpy as np
from jax import lax
from jax.experimental import pallas as pl
from jax.experimental.pallas import tpu as pltpu
from jax.sharding import PartitionSpec as P

D = 768
HEADS = 12
HEAD = 64
MLP = 3072
DD = 512
DHEADS = 16
DHEAD = 32
DMLP = 2048
PS = 16
GT = 64
GF = 8
WIN = 4
VIS = 154
NS_ITERS = 5
STEP = 10
PATCH = 256
SHIFT = 2
NPATCH = 512


HIGH = lax.Precision.HIGHEST
CLIP_MAX = 0.001
LR_MUON = 0.1
LR_ADAM = 0.05
DECAY = 0.01
NS_A = 3.4445
NS_B = -4.775
NS_C = 2.0315
LONG_COLS = (True, True, True, False, True, True, True, False)


def shortened(x):
    return jax.tree.map(lambda a: a.astype(jnp.bfloat16) if a.dtype == jnp.float32 else a, x)


def narrow_core(value):
    return lax.optimization_barrier(value.astype(jnp.bfloat16)).astype(jnp.float32)


def narrow_keep(value):
    return (narrow_core(value), None)


def narrow_pass(kept, grad):
    return (grad,)


def same_core(value):
    return value


def same_keep(value):
    return (value, None)


def same_back(kept, grad):
    return (narrow_core(grad),)


def narrow(value):
    wrapped = jax.custom_vjp(narrow_core)
    wrapped.defvjp(narrow_keep, narrow_pass)
    return wrapped(value)


def narrow_grad(value):
    wrapped = jax.custom_vjp(same_core)
    wrapped.defvjp(same_keep, same_back)
    return wrapped(value)


def product(inputs, matrix):
    return narrow_grad(jnp.dot(narrow(inputs), narrow(matrix), preferred_element_type=jnp.float32))


def score_product(queries, key_rows):
    return narrow_grad(
        jnp.einsum(
            "bqhd,bkhd->bhqk", narrow(queries), narrow(key_rows), preferred_element_type=jnp.float32
        )
    )


def value_product(softmax_rows, values):
    return narrow_grad(
        jnp.einsum(
            "bhqk,bkhd->bqhd",
            narrow(softmax_rows),
            narrow(values),
            preferred_element_type=jnp.float32,
        )
    )


def unpack(vectors):
    extents = [D] * 7 + [MLP] + [D] * 4 + [DD] * 9 + [DMLP] + [DD] * 3 + [PATCH]
    pieces = []
    offset = 0
    for extent in extents:
        pieces.append(vectors[offset : offset + extent])
        offset += extent
    return pieces


def layer_norm(hidden, scaling, offset):
    centred = hidden - jnp.mean(hidden, axis=-1, keepdims=True)
    variance = jnp.mean(centred * centred, axis=-1, keepdims=True)
    return centred * lax.rsqrt(variance + 1e-06) * scaling + offset


def sinusoid(channels):
    quarter = channels // 4
    frequency = 1.0 / 10000.0 ** (jnp.arange(quarter, dtype=jnp.float32) / quarter)
    position = jnp.arange(GT * GF)
    time_rows = (position // GF).astype(jnp.float32)[:, None] * frequency
    freq_cols = (position % GF).astype(jnp.float32)[:, None] * frequency
    return jnp.concatenate(
        [jnp.sin(time_rows), jnp.cos(time_rows), jnp.sin(freq_cols), jnp.cos(freq_cols)], axis=1
    )


def patchify(spec):
    clip_total = spec.shape[0]
    arranged = spec.reshape(clip_total, GT, PS, GF, PS).transpose(0, 1, 3, 2, 4)
    return arranged.reshape(clip_total, GT * GF, PS * PS)


def window_mask():
    time_rows = jnp.arange(GT)
    freq_cols = jnp.arange(GF)
    time_part = (time_rows >= GT - WIN).astype(jnp.int32) + (time_rows >= GT - SHIFT).astype(
        jnp.int32
    )
    freq_part = (freq_cols >= GF - WIN).astype(jnp.int32) + (freq_cols >= GF - SHIFT).astype(
        jnp.int32
    )
    region = time_part[:, None] * 3 + freq_part[None, :]
    region = (
        region.reshape(GT // WIN, WIN, GF // WIN, WIN).transpose(0, 2, 1, 3).reshape(-1, WIN * WIN)
    )
    return region[:, :, None] == region[:, None, :]


def to_windows(grid_rows):
    clip_total = grid_rows.shape[0]
    channels = grid_rows.shape[2]
    arranged = jnp.roll(
        grid_rows.reshape(clip_total, GT, GF, channels), (-SHIFT, -SHIFT), axis=(1, 2)
    )
    arranged = arranged.reshape(clip_total, GT // WIN, WIN, GF // WIN, WIN, channels).transpose(
        0, 1, 3, 2, 4, 5
    )
    return arranged.reshape(-1, WIN * WIN, channels)


def from_windows(windows, clip_total):
    channels = windows.shape[-1]
    arranged = windows.reshape(clip_total, GT // WIN, GF // WIN, WIN, WIN, channels).transpose(
        0, 1, 3, 2, 4, 5
    )
    arranged = jnp.roll(arranged.reshape(clip_total, GT, GF, channels), (SHIFT, SHIFT), axis=(1, 2))
    return arranged.reshape(clip_total, GT * GF, channels)


def attend(queries, key_rows, values, allowed, scaling):
    scores = score_product(queries, key_rows) * scaling
    scores = jnp.where(allowed, scores, -1e30)
    scores = scores - jnp.max(scores, axis=-1, keepdims=True)
    exponent = jnp.exp(scores)
    softmax_rows = exponent / jnp.sum(exponent, axis=-1, keepdims=True)
    return value_product(softmax_rows, values)


def encode(weights, patches, keep, counts):
    pieces = unpack(weights[10])
    clip_total = patches.shape[0]
    picked = jnp.take_along_axis(patches, keep[:, :, None], axis=1)
    hidden = product(picked, weights[8][:, :D]) + pieces[11] + sinusoid(D)[keep]
    normed = layer_norm(hidden, pieces[0], pieces[1])
    joined = product(normed, weights[0])
    queries = (joined[..., :D] + pieces[2]).reshape(clip_total, VIS, HEADS, HEAD)
    key_rows = joined[..., D : 2 * D].reshape(clip_total, VIS, HEADS, HEAD)
    values = (joined[..., 2 * D :] + pieces[3]).reshape(clip_total, VIS, HEADS, HEAD)
    visible = (jnp.arange(VIS)[None, :] < counts[:, None])[:, None, None, :]
    attended = attend(queries, key_rows, values, visible, HEAD ** (-0.5)).reshape(
        clip_total, VIS, D
    )
    hidden = hidden + product(attended, weights[1]) + pieces[4]
    normed = layer_norm(hidden, pieces[5], pieces[6])
    inner = jax.nn.gelu(product(normed, weights[2]) + pieces[7], approximate=False)
    hidden = hidden + product(inner, weights[3]) + pieces[8]
    return layer_norm(hidden, pieces[9], pieces[10])


def decode(weights, latent, patches, keep, counts):
    pieces = unpack(weights[10])[12:]
    clip_total = latent.shape[0]
    placed = product(latent, weights[9]) + pieces[0]
    visible = jnp.arange(VIS)[None, :] < counts[:, None]
    target_rows = jnp.where(visible, keep, NPATCH)
    clip_rows = jnp.arange(clip_total)[:, None]
    filled = (
        jnp.zeros((clip_total, NPATCH + 1, DD), jnp.float32)
        .at[clip_rows, target_rows]
        .add(placed)[:, :NPATCH]
    )
    visible_cells = (
        jnp.zeros((clip_total, NPATCH + 1), jnp.float32)
        .at[clip_rows, target_rows]
        .add(1.0)[:, :NPATCH]
    )
    hidden = filled + (1.0 - visible_cells)[..., None] * pieces[1] + sinusoid(DD)
    normed = layer_norm(hidden, pieces[2], pieces[3])
    windows = to_windows(product(normed, weights[4]))
    queries = (windows[..., :DD] + pieces[4]).reshape(-1, WIN * WIN, DHEADS, DHEAD)
    key_rows = windows[..., DD : 2 * DD].reshape(-1, WIN * WIN, DHEADS, DHEAD)
    values = (windows[..., 2 * DD :] + pieces[5]).reshape(-1, WIN * WIN, DHEADS, DHEAD)
    allowed = jnp.tile(window_mask(), (clip_total, 1, 1))[:, None, :, :]
    attended = attend(queries, key_rows, values, allowed, DHEAD ** (-0.5)).reshape(
        -1, WIN * WIN, DD
    )
    hidden = hidden + product(from_windows(attended, clip_total), weights[5]) + pieces[6]
    normed = layer_norm(hidden, pieces[7], pieces[8])
    inner = jax.nn.gelu(product(normed, weights[6]) + pieces[9], approximate=False)
    hidden = hidden + product(inner, weights[7]) + pieces[10]
    normed = layer_norm(hidden, pieces[11], pieces[12])
    predicted = product(normed, weights[8][:, D:].T) + pieces[13]
    centred = patches - jnp.mean(patches, axis=-1, keepdims=True)
    target = centred * lax.rsqrt(jnp.mean(centred * centred, axis=-1, keepdims=True) + 1e-06)
    deviation = predicted - target
    patch_error = jnp.mean(deviation * deviation, axis=-1)
    return jnp.sum((1.0 - visible_cells) * patch_error)


def take_half(shard, number, core):
    if LONG_COLS[number]:
        extent = shard.shape[1] // 2
        return lax.dynamic_slice_in_dim(shard, core * extent, extent, 1)
    extent = shard.shape[0] // 2
    return lax.dynamic_slice_in_dim(shard, core * extent, extent, 0)


def arrange(gathered_half, number, long_max, short_max):
    upright = gathered_half.T if LONG_COLS[number] else gathered_half
    return jnp.pad(upright, ((0, long_max - upright.shape[0]), (0, short_max - upright.shape[1])))


def disperse(iterate, number, height, breadth, devices, flat_max):
    if LONG_COLS[number]:
        piece = iterate[: breadth // 2, :height].T.reshape(
            devices, height // devices * (breadth // 2)
        )
    else:
        piece = iterate[: height // 2, :breadth].reshape(devices, height // 2 // devices * breadth)
    return jnp.pad(piece, ((0, 0), (0, flat_max - piece.shape[1])))


def restore(row_piece, number, height, breadth, devices):
    if LONG_COLS[number]:
        return row_piece[: height // devices * (breadth // 2)].reshape(
            height // devices, breadth // 2
        )
    return row_piece[: height // 2 // devices * breadth].reshape(height // 2 // devices, breadth)


def adam_update(weight, first_moment, second_moment, gradient, decay):
    first_moment = 0.5 * first_moment + 0.5 * gradient
    second_moment = 0.95 * second_moment + 0.05 * gradient * gradient
    direction = (
        first_moment / (1.0 - 0.5**STEP) / (jnp.sqrt(second_moment / (1.0 - 0.95**STEP)) + 1e-08)
    )
    return (weight - LR_ADAM * (direction + decay * weight), first_moment, second_moment)


MESH_ID = pl.DeviceIdType.MESH
VEC_ROWS, VEC_COLS = 16, 256
AXIS_ORDERS = ((0, 1, 2, 3), (0, 1, 3, 2), (0, 2, 1, 3), (0, 2, 3, 1), (0, 3, 1, 2), (0, 3, 2, 1), (1, 0, 2, 3), (1, 0, 3, 2), (1, 2, 0, 3), (1, 2, 3, 0), (1, 3, 0, 2), (1, 3, 2, 0), (2, 0, 1, 3), (2, 0, 3, 1), (2, 1, 0, 3), (2, 1, 3, 0), (2, 3, 0, 1), (2, 3, 1, 0), (3, 0, 1, 2), (3, 0, 2, 1), (3, 1, 0, 2), (3, 1, 2, 0), (3, 2, 0, 1), (3, 2, 1, 0))
GATHER_PARTS = (3, 1, 4, 4, 1, 1, 2, 2, 1, 1, 1)
REDUCE_PARTS = (3, 1, 4, 4, 2, 1, 2, 2, 1, 1, 1)
TALL = (3, 7)
GATHER_TURNS = (19, 18, 22, 17, 13, 21, 22, 20, 3, 12, 11, 0, 17, 23, 16, 10, 23, 16, 11, 21, 21)
GATHER_FIRST = (6, 17, 20, 11, 7, 16, 8, 13, 12, 1, 4, 9, 19, 10, 3, 2, 15, 5, 0, 14, 18)
GATHER_STEPS = ((20, 11, 17, 6, 8, 10, 13, 15, 7, 16, 18, 19, 4, 1, 12, 9, 3, 2, 5, 14, 0), (20, 11, 7, 19, 4, 1, 17, 9, 6, 13, 8, 5, 0, 10, 16, 18, 15, 12, 3, 2, 14), (20, 7, 1, 17, 9, 13, 6, 16, 15, 11, 19, 4, 3, 12, 2, 8, 14, 10, 18, 5, 0), (20, 17, 13, 16, 6, 19, 7, 3, 4, 2, 1, 14, 12, 8, 18, 9, 10, 5, 15, 0, 11))
REDUCE_TURNS = (14, 1, 1, 6, 7, 2, 12, 8, 20, 3, 21, 6, 6, 0, 0, 21, 10, 13, 2, 0, 17, 4)
REDUCE_FIRST = (17, 21, 12, 9, 15, 18, 19, 4, 3, 11, 1, 10, 13, 20, 0, 7, 5, 16, 8, 14, 6, 2)
REDUCE_STEPS = ((21, 17, 12, 9, 19, 15, 18, 4, 20, 3, 11, 10, 1, 0, 7, 14, 16, 5, 8, 13, 6, 2), (21, 17, 19, 15, 9, 12, 10, 14, 1, 20, 0, 18, 4, 8, 3, 7, 11, 13, 2, 16, 6, 5), (21, 17, 19, 20, 15, 18, 9, 14, 0, 10, 12, 8, 7, 16, 1, 6, 4, 5, 3, 11, 13, 2), (21, 17, 20, 15, 9, 19, 10, 18, 14, 0, 12, 8, 1, 16, 7, 6, 4, 5, 3, 2, 13, 11))
OWNERS = (4, 11, 5, 10, 6, 9, 7, 8)
SLOTS = 160


def bit_count(devices):
    return devices.bit_length() - 1


def cut_pieces(parts, shapes):
    found = []
    for number, count in enumerate(parts):
        rows, width = shapes[number]
        for part in range(count):
            if number in TALL:
                found.append((number, part * (rows // count), rows // count, 0, width))
            else:
                found.append((number, 0, rows, part * (width // count), width // count))
    return found


def own_bits(levels):
    me = lax.axis_index("dp")
    return me, [lax.rem(lax.div(me, 2**bit), 2) for bit in range(levels)]


def place(levels, free, own, flip=None):
    spots = []
    for bit in range(levels - 1, -1, -1):
        if bit in free:
            spots.append(slice(None))
        elif bit == flip:
            spots.append(1 - own[bit])
        else:
            spots.append(own[bit])
    return tuple(spots)


def partner(me, own, bit):
    return me + (1 - 2 * own[bit]) * 2**bit


def greet(me, own, levels, core):
    barrier = pltpu.get_barrier_semaphore()
    for bit in range(levels):
        pl.semaphore_signal(
            barrier,
            inc=1,
            device_id={"dp": partner(me, own, bit), "mp": core},
            device_id_type=MESH_ID,
        )
    pl.semaphore_signal(barrier, inc=1, device_id={"dp": me, "mp": 1 - core}, device_id_type=MESH_ID)
    pl.semaphore_wait(barrier, levels + 1)


def add_up(me, core, devices, total, landing, send_sem, recv_sem, own_sem):
    def send(source, target):
        return pltpu.make_async_remote_copy(
            src_ref=total,
            dst_ref=landing.at[source],
            send_sem=send_sem.at[target],
            recv_sem=recv_sem.at[source],
            device_id={"dp": target, "mp": core},
            device_id_type=MESH_ID,
        )

    @pl.loop(0, devices)
    def start_one(other):
        @pl.when(other != me)
        def start_other():
            send(me, other).start()

    own = pltpu.make_async_copy(total, landing.at[me], own_sem)
    own.start()
    own.wait()

    @pl.loop(0, devices)
    def wait_one(other):
        @pl.when(other != me)
        def wait_other():
            send(other, me).wait_recv()
            send(me, other).wait_send()

    found = landing[0]
    for device in range(1, devices):
        found = found + landing[device]
    total[...] = found
    swap = pltpu.make_async_remote_copy(
        src_ref=total,
        dst_ref=landing.at[devices],
        send_sem=send_sem.at[devices],
        recv_sem=recv_sem.at[devices],
        device_id={"dp": me, "mp": 1 - core},
        device_id_type=MESH_ID,
    )
    swap.start()
    swap.wait()
    total[...] = total[...] + landing[devices]


def gather_kernel(levels, pieces, count, *refs):
    shards, tally = refs[:count], refs[count]
    wholes, tally_out = refs[count + 1 : 2 * count + 1], refs[2 * count + 1]
    short, rest = refs[2 * count + 2 : 3 * count + 2], refs[3 * count + 2 :]
    here_sem, send_sem, recv_sem, cross_send, cross_recv, tally_land, tally_send, tally_recv = rest
    me, own = own_bits(levels)
    core = lax.axis_index("mp")
    greet(me, own, levels, core)
    orders = [AXIS_ORDERS[turn] for turn in GATHER_TURNS]

    def cut(piece, which):
        number, row, rows, column, columns = pieces[piece]
        width = shards[number].shape[1] // 2
        return (pl.ds(row, rows), pl.ds(pl.multiple_of(which * width + column, 128), columns))

    def hop(piece, stage, flip):
        order, number = orders[piece], pieces[piece][0]
        spot = place(levels, order[:stage], own, order[stage] if flip else None)
        target = wholes[number].at[spot + cut(piece, core)]
        source = target if stage or flip else short[number].at[cut(piece, core)]
        return pltpu.make_async_remote_copy(
            src_ref=source,
            dst_ref=target,
            send_sem=send_sem.at[piece, stage],
            recv_sem=recv_sem.at[piece, stage],
            device_id={"dp": partner(me, own, order[stage]), "mp": core},
            device_id_type=MESH_ID,
        )

    def cross(piece, stage, which):
        order, number = orders[piece], pieces[piece][0]
        spot = place(levels, order[:stage], own, order[stage])
        target = wholes[number].at[spot + cut(piece, which)]
        return pltpu.make_async_remote_copy(
            src_ref=target,
            dst_ref=target,
            send_sem=cross_send.at[piece, stage],
            recv_sem=cross_recv.at[piece, stage],
            device_id={"dp": me, "mp": 1 - core},
            device_id_type=MESH_ID,
        )

    def keep(number):
        spot = place(levels, (), own)
        return pltpu.make_async_copy(short[number], wholes[number].at[spot], here_sem.at[number])

    ready = set()
    for piece in GATHER_FIRST:
        number = pieces[piece][0]
        if number not in ready:
            ready.add(number)
            short[number][...] = shards[number][...].astype(jnp.bfloat16)
            keep(number).start()
        hop(piece, 0, False).start()
    tally_out[...] = tally[...]

    def swap(stage):
        if stage < levels:
            to = {"dp": partner(me, own, stage), "mp": core}
        else:
            to = {"dp": me, "mp": 1 - core}
        return pltpu.make_async_remote_copy(
            src_ref=tally_out,
            dst_ref=tally_land.at[stage],
            send_sem=tally_send.at[stage],
            recv_sem=tally_recv.at[stage],
            device_id=to,
            device_id_type=MESH_ID,
        )

    def swap_end(stage):
        swap(stage).wait()
        tally_out[...] = tally_out[...] + tally_land[stage]

    swap(levels).start()
    for number in range(count):
        keep(number).wait()
    swap_end(levels)
    for stage, order in enumerate(GATHER_STEPS):
        swap(stage).start()
        for piece in order:
            hop(piece, stage, True).wait_recv()
            if stage + 1 < levels:
                hop(piece, stage + 1, False).start()
            cross(piece, stage, core).start()
        swap_end(stage)
    for piece in range(len(pieces)):
        for stage in range(levels):
            hop(piece, stage, False).wait_send()
            cross(piece, stage, core).wait_send()
            cross(piece, stage, 1 - core).wait_recv()


def gather_rows(shards, tally, devices):
    levels, count = bit_count(devices), len(shards)
    lead = (2,) * levels
    pieces = cut_pieces(GATHER_PARTS, [(shard.shape[0], shard.shape[1] // 2) for shard in shards])
    dma = pltpu.SemaphoreType.DMA
    vmem = pl.BlockSpec(memory_space=pltpu.VMEM)
    found = pl.pallas_call(
        functools.partial(gather_kernel, levels, pieces, count),
        out_shape=[jax.ShapeDtypeStruct(lead + shard.shape, jnp.bfloat16) for shard in shards]
        + [jax.ShapeDtypeStruct((8, 128), jnp.float32)],
        in_specs=[vmem] * (count + 1),
        out_specs=[pl.BlockSpec(memory_space=pl.ANY)] * count + [vmem],
        scratch_shapes=[pltpu.VMEM(shard.shape, jnp.bfloat16) for shard in shards]
        + [dma((count,))]
        + [dma((len(pieces), levels))] * 4
        + [pltpu.VMEM((levels + 1, 8, 128), jnp.float32)]
        + [dma((levels + 1,))] * 2,
        compiler_params=pltpu.CompilerParams(
            collective_id=1, has_side_effects=True, vmem_limit_bytes=32 * 2**20
        ),
        name="gather_rows",
    )(*shards, tally)
    return found[:count], found[count]


def reduce_kernel(levels, pieces, count, owners, devices, *refs):
    blocks = len(owners)
    grads, stats_in, old = refs[:count], refs[count], refs[count + 1 : count + 1 + blocks]
    rest = refs[count + 1 + blocks :]
    sums, stats_out, wholes = rest[:count], rest[count], rest[count + 1 : count + 1 + blocks]
    rest = rest[count + 1 + blocks :]
    mine, theirs, rest = rest[:count], rest[count : 2 * count], rest[2 * count :]
    kept, rest = rest[:count], rest[count:]
    landing, rest = rest[: len(pieces) * levels], rest[len(pieces) * levels :]
    staged, rest = rest[:blocks], rest[blocks:]
    stats_land, here_sem, pair_send, pair_recv, send_sem, recv_sem, last_send, last_recv = rest[:8]
    stats_send, stats_recv, own_sem, out_send, out_recv, cross_send, cross_recv = rest[8:]
    me, own = own_bits(levels)
    core = lax.axis_index("mp")
    orders = [AXIS_ORDERS[turn] for turn in REDUCE_TURNS]
    barrier = pltpu.get_barrier_semaphore()

    @pl.loop(0, devices)
    def greet_one(other):
        @pl.when(other != me)
        def signal_one():
            pl.semaphore_signal(
                barrier, inc=1, device_id={"dp": other, "mp": core}, device_id_type=MESH_ID
            )

    pl.semaphore_signal(barrier, inc=1, device_id={"dp": me, "mp": 1 - core}, device_id_type=MESH_ID)
    pl.semaphore_wait(barrier, devices)

    def half(number, which):
        width = sums[number].shape[1] // 2
        return (slice(None), pl.ds(pl.multiple_of(which * width, 128), width))

    def cut(piece):
        number, row, rows, column, columns = pieces[piece]
        return (pl.ds(row, rows), pl.ds(column, columns))

    def side(piece, which):
        number, row, rows, column, columns = pieces[piece]
        width = sums[number].shape[1] // 2
        return (pl.ds(row, rows), pl.ds(pl.multiple_of(which * width + column, 128), columns))

    every = (slice(None),) * levels

    def pair(piece):
        number = pieces[piece][0]
        return pltpu.make_async_remote_copy(
            src_ref=grads[number].at[every + side(piece, 1 - core)],
            dst_ref=theirs[number].at[every + cut(piece)],
            send_sem=pair_send.at[piece],
            recv_sem=pair_recv.at[piece],
            device_id={"dp": me, "mp": 1 - core},
            device_id_type=MESH_ID,
        )

    def load(piece):
        number = pieces[piece][0]
        return pltpu.make_async_copy(
            grads[number].at[every + side(piece, core)],
            mine[number].at[every + cut(piece)],
            here_sem.at[piece],
        )

    def hop(piece, stage):
        order = orders[piece]
        spot = place(levels, order[stage + 1 :], own, order[stage])
        return pltpu.make_async_remote_copy(
            src_ref=theirs[pieces[piece][0]].at[spot + cut(piece)],
            dst_ref=landing[piece * levels + stage],
            send_sem=send_sem.at[piece, stage],
            recv_sem=recv_sem.at[piece, stage],
            device_id={"dp": partner(me, own, order[stage]), "mp": core},
            device_id_type=MESH_ID,
        )

    def share(number, which):
        region = sums[number].at[half(number, which)]
        return pltpu.make_async_remote_copy(
            src_ref=region,
            dst_ref=region,
            send_sem=last_send.at[number],
            recv_sem=last_recv.at[number],
            device_id={"dp": me, "mp": 1 - core},
            device_id_type=MESH_ID,
        )

    def deliver(number, source):
        return pltpu.make_async_remote_copy(
            src_ref=staged[number],
            dst_ref=wholes[number].at[(source,) + half(number, core)],
            send_sem=out_send.at[number],
            recv_sem=out_recv.at[number, source],
            device_id={"dp": owners[number], "mp": core},
            device_id_type=MESH_ID,
        )

    def deliver_here(number):
        return pltpu.make_async_copy(
            staged[number], wholes[number].at[(me,) + half(number, core)], own_sem
        )

    def cross(number, source, which):
        region = wholes[number].at[(source,) + half(number, which)]
        return pltpu.make_async_remote_copy(
            src_ref=region,
            dst_ref=region,
            send_sem=cross_send.at[number, source],
            recv_sem=cross_recv.at[number, source],
            device_id={"dp": me, "mp": 1 - core},
            device_id_type=MESH_ID,
        )

    def kept_spot(order, found):
        return tuple(found.get(bit, own[bit]) for bit in range(levels - 1, -1, -1) if bit != order[0])

    def fold(piece, stage):
        order, number = orders[piece], pieces[piece][0]
        free = order[stage:]
        loose = [bit for bit in range(levels - 1, -1, -1) if bit in free and bit != order[stage]]
        region = cut(piece)

        @pl.loop(0, 2 ** len(loose))
        def add_block(block):
            found = {
                bit: lax.rem(lax.div(block, 2 ** (len(loose) - 1 - i)), 2) for i, bit in enumerate(loose)
            }

            def total(way):
                now = dict(found)
                now[order[stage]] = way
                full = tuple(now.get(bit, own[bit]) for bit in range(levels - 1, -1, -1)) + region
                if stage == 0:
                    value = mine[number][full].astype(jnp.float32) + theirs[number][full].astype(jnp.float32)
                else:
                    land = tuple(now[bit] for bit in range(levels - 1, -1, -1) if bit in free)
                    arrived = landing[piece * levels + stage - 1][land].astype(jnp.float32)
                    value = kept[number][kept_spot(order, now) + region] + arrived
                return full, value

            full, value = total(1 - own[order[stage]])
            theirs[number][full] = value.astype(theirs[number].dtype)
            full, value = total(own[order[stage]])
            kept[number][kept_spot(order, found) + region] = value

    for piece in REDUCE_FIRST:
        pair(piece).start()
        load(piece).start()
    for piece in REDUCE_FIRST:
        load(piece).wait()
        pair(piece).wait_recv()
        fold(piece, 0)
        hop(piece, 0).start()
    squares = jnp.zeros((8, 128), jnp.float32)
    for piece, stage in [(piece, stage) for stage in range(levels) for piece in REDUCE_STEPS[stage]]:
        hop(piece, stage).wait_recv()
        if stage + 1 < levels:
            fold(piece, stage + 1)
            hop(piece, stage + 1).start()
        else:
            number = pieces[piece][0]
            arrived = landing[piece * levels + stage][...].astype(jnp.float32)
            total = kept[number][kept_spot(orders[piece], {}) + cut(piece)] + arrived
            sums[number][side(piece, core)] = total
            rows, width = total.shape
            for row in range(0, rows, 8):
                for column in range(0, width, 128):
                    part = total[row : row + 8, column : column + 128]
                    squares = squares + part * part
    for number in range(blocks, count):
        share(number, core).start()
    row = lax.broadcasted_iota(jnp.int32, (8, 128), 0)
    stats_out[...] = jnp.where(row == 0, jnp.sum(squares, axis=0, keepdims=True), stats_in[...])
    add_up(me, core, devices, stats_out, stats_land, stats_send, stats_recv, own_sem)
    norm = jnp.sqrt(jnp.sum(stats_out[0:1, :], axis=1, keepdims=True))
    factor = jnp.minimum(1.0, CLIP_MAX / (norm + 1e-06))
    for number in range(blocks):
        region = half(number, core)
        renewed = 0.5 * old[number][region] + factor * sums[number][region]
        sums[number][region] = renewed
        staged[number][...] = renewed.astype(staged[number].dtype)
        share(number, core).start()

        @pl.when(me != owners[number])
        def start_one(number=number):
            deliver(number, me).start()

        @pl.when(me == owners[number])
        def start_here(number=number):
            deliver_here(number).start()

    for piece in range(len(pieces)):
        pair(piece).wait_send()
        for stage in range(levels):
            hop(piece, stage).wait_send()
    for number in range(blocks):

        @pl.when(me == owners[number])
        def collect(number=number):
            deliver_here(number).wait()

            @pl.loop(0, devices)
            def forward(source):
                @pl.when(source != me)
                def arrived():
                    deliver(number, source).wait_recv()

                cross(number, source, core).start()

            @pl.loop(0, devices)
            def finish(source):
                cross(number, source, core).wait_send()
                cross(number, source, 1 - core).wait_recv()

        @pl.when(me != owners[number])
        def end_one(number=number):
            deliver(number, me).wait_send()

    for number in range(count):
        share(number, core).wait_send()
        share(number, 1 - core).wait_recv()


def reduce_rows(grads, stats, old, owners, devices):
    levels, count, blocks = bit_count(devices), len(grads), len(old)
    lead = (2,) * levels
    dma = pltpu.SemaphoreType.DMA
    shapes = [grad.shape[levels:] for grad in grads]
    halves = [(rows, columns // 2) for rows, columns in shapes]
    kinds = [grad.dtype for grad in grads]
    pieces = cut_pieces(REDUCE_PARTS, halves)
    scratch = [pltpu.VMEM(lead + shape, kind) for shape, kind in zip(halves, kinds)] * 2
    scratch += [pltpu.VMEM(lead[1:] + shape, jnp.float32) for shape in halves]
    for number, row, rows, column, columns in pieces:
        for stage in range(levels):
            scratch.append(pltpu.VMEM((2,) * (levels - 1 - stage) + (rows, columns), kinds[number]))
    scratch += [pltpu.VMEM(halves[number], kinds[number]) for number in range(blocks)]
    scratch.append(pltpu.VMEM((devices + 1, 8, 128), jnp.float32))
    scratch += [dma((len(pieces),))] * 3 + [dma((len(pieces), levels))] * 2 + [dma((count,))] * 2
    scratch += [dma((devices + 1,))] * 2 + [dma, dma((blocks,))] + [dma((blocks, devices))] * 3
    vmem, anywhere = pl.BlockSpec(memory_space=pltpu.VMEM), pl.BlockSpec(memory_space=pl.ANY)
    found = pl.pallas_call(
        functools.partial(reduce_kernel, levels, pieces, count, owners, devices),
        out_shape=[jax.ShapeDtypeStruct(shape, jnp.float32) for shape in shapes]
        + [jax.ShapeDtypeStruct((8, 128), jnp.float32)]
        + [jax.ShapeDtypeStruct((devices,) + shapes[number], kinds[number]) for number in range(blocks)],
        in_specs=[anywhere] * count + [vmem] * (1 + blocks),
        out_specs=[vmem] * (count + 1) + [anywhere] * blocks,
        scratch_shapes=scratch,
        compiler_params=pltpu.CompilerParams(
            collective_id=2, has_side_effects=True, vmem_limit_bytes=60 * 2**20
        ),
        name="reduce_rows",
    )(*grads, stats, *old)
    return found[:blocks], found[blocks:count], found[count], found[count + 1 :]


def return_kernel(owners, count, devices, *refs):
    wholes, rows = refs[:count], refs[count : 2 * count]
    here_sem, send_sem, recv_sem, cross_send, cross_recv = refs[2 * count :]
    me, core = lax.axis_index("dp"), lax.axis_index("mp")
    barrier = pltpu.get_barrier_semaphore()
    owning = functools.reduce(jnp.logical_or, [me == owner for owner in owners])
    for owner in owners:

        @pl.when(me != owner)
        def greet_owner(owner=owner):
            pl.semaphore_signal(
                barrier, inc=1, device_id={"dp": owner, "mp": core}, device_id_type=MESH_ID
            )

    pl.semaphore_signal(barrier, inc=1, device_id={"dp": me, "mp": 1 - core}, device_id_type=MESH_ID)

    @pl.when(owning)
    def wait_all():
        pl.semaphore_wait(barrier, devices)

    @pl.when(jnp.logical_not(owning))
    def wait_pair():
        pl.semaphore_wait(barrier, 1)

    def half(number, which):
        width = rows[number].shape[1] // 2
        return (slice(None), pl.ds(pl.multiple_of(which * width, 128), width))

    def hop(number, target):
        return pltpu.make_async_remote_copy(
            src_ref=wholes[number].at[(target,) + half(number, core)],
            dst_ref=rows[number].at[half(number, core)],
            send_sem=send_sem.at[number, target],
            recv_sem=recv_sem.at[number],
            device_id={"dp": target, "mp": core},
            device_id_type=MESH_ID,
        )

    def cross(number, which):
        region = rows[number].at[half(number, which)]
        return pltpu.make_async_remote_copy(
            src_ref=region,
            dst_ref=region,
            send_sem=cross_send.at[number],
            recv_sem=cross_recv.at[number],
            device_id={"dp": me, "mp": 1 - core},
            device_id_type=MESH_ID,
        )

    for number in range(count):

        @pl.when(me == owners[number])
        def hand_out(number=number):
            own = pltpu.make_async_copy(
                wholes[number].at[(me,) + half(number, core)], rows[number].at[half(number, core)], here_sem
            )
            own.start()

            @pl.loop(0, devices)
            def start_one(target):
                @pl.when(target != me)
                def start_other():
                    hop(number, target).start()

            own.wait()

    for number in range(count):

        @pl.when(me != owners[number])
        def arrive(number=number):
            hop(number, me).wait_recv()

        cross(number, core).start()
    for number in range(count):
        cross(number, core).wait_send()
        cross(number, 1 - core).wait_recv()

        @pl.when(me == owners[number])
        def end_out(number=number):
            @pl.loop(0, devices)
            def end_one(target):
                @pl.when(target != me)
                def end_other():
                    hop(number, target).wait_send()


def return_rows(wholes, owners, devices):
    count = len(wholes)
    dma = pltpu.SemaphoreType.DMA
    vmem = pl.BlockSpec(memory_space=pltpu.VMEM)
    return pl.pallas_call(
        functools.partial(return_kernel, owners, count, devices),
        out_shape=[jax.ShapeDtypeStruct(whole.shape[1:], whole.dtype) for whole in wholes],
        in_specs=[pl.BlockSpec(memory_space=pl.ANY)] * count,
        out_specs=[vmem] * count,
        scratch_shapes=[dma, dma((count, devices)), dma((count,)), dma((count,)), dma((count,))],
        compiler_params=pltpu.CompilerParams(
            collective_id=4, has_side_effects=True, vmem_limit_bytes=60 * 2**20
        ),
        name="return_rows",
    )(*wholes)


def finish_kernel(count, rates, *refs):
    rows, masters, updated = refs[:count], refs[count : 2 * count], refs[2 * count :]
    for number in range(count):
        change = rates[number] * rows[number][...].astype(jnp.float32)
        updated[number][...] = masters[number][...] * (1.0 - LR_MUON * DECAY) - change


def finish(rows, masters, devices):
    count = len(rows)
    rates = []
    for master in masters:
        rates.append(LR_MUON * 0.2 * math.sqrt(max(master.shape[0] * devices, master.shape[1])))
    vmem = pl.BlockSpec(memory_space=pltpu.VMEM)
    return pl.pallas_call(
        functools.partial(finish_kernel, count, rates),
        out_shape=[jax.ShapeDtypeStruct(master.shape, jnp.float32) for master in masters],
        in_specs=[vmem] * (2 * count),
        out_specs=[vmem] * count,
        compiler_params=pltpu.CompilerParams(vmem_limit_bytes=56 * 2**20),
        name="finish",
    )(*rows, *masters)


def muon_kernel(owners, shapes, *refs):
    count = len(owners)
    mats, moved, stats, adam_in = refs[:count], refs[count : 2 * count], refs[2 * count], refs[2 * count + 1 :][:8]
    rest = refs[2 * count + 9 :]
    outs, moved_out, adam_out, rest = rest[:count], rest[count : 2 * count], rest[2 * count :][:6], rest[2 * count + 6 :]
    exact, wide, wide_low, tall, wide_out, tall_out, gram = rest[:7]
    base, poly, other, chain, sem, in_sem, out_sem = rest[7:14]
    held_rows = rest[14:]

    def move_in(number):
        return pltpu.make_async_copy(moved[number], held_rows[number], in_sem.at[number])

    def move_out(number):
        return pltpu.make_async_copy(held_rows[number], moved_out[number], out_sem.at[number])

    for number in range(count):
        move_in(number).start()
    norm = jnp.sqrt(jnp.sum(stats[0:1, :], axis=1, keepdims=True))
    factor = jnp.minimum(1.0, CLIP_MAX / (norm + 1e-06))
    for group in range(2):
        weight, first, second, grad = [ref[...] for ref in adam_in[4 * group : 4 * group + 4]]
        made = adam_update(weight, first, second, grad * factor, DECAY)
        for place_out in range(3):
            adam_out[3 * group + place_out][...] = made[place_out]
    me, core = lax.axis_index("dp"), lax.axis_index("mp")
    side = gram.shape[0]
    step = 256
    bf = jnp.bfloat16

    def dims(number):
        height, breadth = shapes[number]
        return height, breadth, LONG_COLS[number]

    def span(index):
        return pl.ds(pl.multiple_of(index * step, step), step)

    def split(value):
        high = value.astype(bf)
        return high, (value - high.astype(jnp.float32)).astype(bf)

    gram[...] = jnp.zeros_like(gram)
    for number in range(count):

        @pl.when(me == owners[number])
        def start(number=number):
            height, breadth, long_cols = dims(number)
            short = min(height, breadth)
            held = (wide if long_cols else tall).at[:height, :breadth]
            fine = mats[number].dtype == jnp.float32
            load = pltpu.make_async_copy(mats[number], exact if fine else held, sem)
            load.start()
            load.wait()
            if fine:
                rest = wide_low

                @pl.loop(0, height // step)
                def part_rows(index):
                    high, low = split(exact[span(index), :])
                    held[span(index), :] = high
                    rest[span(index), :] = low

            for index in range(short // step):
                first, beyond = slice(index * step, (index + 1) * step), slice(index * step, short)
                if long_cols:
                    total = dot_rows(held[first, :], held[beyond, :])
                    if fine:
                        total = total + dot_rows(held[first, :], rest[beyond, :])
                        total = total + dot_rows(rest[first, :], held[beyond, :])
                else:
                    total = dot_columns(held[:, first], held[:, beyond])
                gram[first, beyond] = total

    for number in range(count):
        move_in(number).wait()
        move_out(number).start()
    owning = functools.reduce(jnp.logical_or, [me == owner for owner in owners])

    @pl.when(owning)
    def iterate():
        parts = [
            (slice(index * step, (index + 1) * step), slice(index * step, side))
            for index in range(side // step)
        ]
        ones = lax.broadcasted_iota(jnp.int32, (step, step), 0) == lax.broadcasted_iota(
            jnp.int32, (step, step), 1
        )
        trace = jnp.float32(0.0)
        for first, beyond in parts:
            trace = trace + jnp.sum(jnp.where(ones, gram[first, first], 0.0))
        scale = 1.0 / (jnp.sqrt(jnp.full((8, 128), trace, jnp.float32)) + 1e-07)
        scale = scale[0:1, 0:1]

        def store(target, index, value):
            high, low = split(value)
            target[0, parts[index][0], parts[index][1]] = high
            target[1, parts[index][0], parts[index][1]] = low
            for later in range(index + 1, side // step):
                shift = (later - index) * step
                high, low = split(value[:, shift : shift + step].T)
                target[0, parts[later][0], parts[index][0]] = high
                target[1, parts[later][0], parts[index][0]] = low

        def product(left, right, index):
            first, beyond = parts[index]
            high, low = left[0, first, :], left[1, first, :]
            total = jnp.dot(high, right[0, :, beyond], preferred_element_type=jnp.float32)
            total = total + jnp.dot(high, right[1, :, beyond], preferred_element_type=jnp.float32)
            return total + jnp.dot(low, right[0, :, beyond], preferred_element_type=jnp.float32)

        for index, (first, beyond) in enumerate(parts):
            store(base, index, gram[first, beyond] * (scale * scale))

        @pl.loop(0, NS_ITERS)
        def newton(iteration):
            for index, (first, beyond) in enumerate(parts):
                now = base[0, first, beyond].astype(jnp.float32) + base[1, first, beyond].astype(jnp.float32)
                row = lax.broadcasted_iota(jnp.int32, now.shape, 0)
                column = lax.broadcasted_iota(jnp.int32, now.shape, 1)
                value = jnp.where(row == column, NS_A, 0.0) + NS_B * now
                store(poly, index, value + NS_C * product(base, base, index))

            @pl.when(iteration < NS_ITERS - 1)
            def advance():
                for index in range(len(parts)):
                    store(other, index, product(base, poly, index))
                for index in range(len(parts)):
                    store(base, index, product(other, poly, index))

            @pl.when(iteration == 0)
            def begin():
                chain[...] = poly[...]

            @pl.when(iteration > 0)
            def follow():
                for index in range(len(parts)):
                    store(other, index, product(chain, poly, index))
                chain[...] = other[...]

        for first, beyond in parts:
            value = chain[0, first, :].astype(jnp.float32) + chain[1, first, :].astype(jnp.float32)
            high, low = split(value * scale)
            other[0, first, :] = high
            other[1, first, :] = low

    for number in range(count):

        @pl.when(me == owners[number])
        def end(number=number):
            height, breadth, long_cols = dims(number)
            short = min(height, breadth)
            width = breadth // 2
            part = pl.ds(pl.multiple_of(core * width, 128), width)
            if long_cols:
                held, made = wide.at[:height, :breadth], wide_out.at[:height, :width]

                @pl.loop(0, height // step)
                def wide_rows(index):
                    total = jnp.dot(
                        other[0, span(index), :short], held[:, part], preferred_element_type=jnp.float32
                    ) + jnp.dot(
                        other[1, span(index), :short], held[:, part], preferred_element_type=jnp.float32
                    )
                    if mats[number].dtype == jnp.float32:
                        total = total + jnp.dot(
                            other[0, span(index), :short],
                            wide_low[:, part],
                            preferred_element_type=jnp.float32,
                        )
                    made[span(index), :] = total.astype(bf)
            else:
                held, made = tall.at[:height, :breadth], tall_out.at[:height, :width]

                @pl.loop(0, height // step)
                def tall_rows(index):
                    total = jnp.dot(
                        held[span(index), :], other[0, :short, part], preferred_element_type=jnp.float32
                    ) + jnp.dot(
                        held[span(index), :], other[1, :short, part], preferred_element_type=jnp.float32
                    )
                    made[span(index), :] = total.astype(bf)

            save = pltpu.make_async_copy(made, outs[number].at[:, part], sem)
            save.start()
            save.wait()

    for number in range(count):
        move_out(number).wait()


def orthogonalize(mats, moved, stats, adam, owners):
    count = len(mats)
    shapes = [mat.shape for mat in mats]
    side = max(min(shape) for shape in shapes)
    longest = max(max(shape) for shape in shapes)
    double = pltpu.VMEM((2, side, side), jnp.bfloat16)
    (fine,) = [mat.shape for mat in mats if mat.dtype == jnp.float32]
    vmem, anywhere = pl.BlockSpec(memory_space=pltpu.VMEM), pl.BlockSpec(memory_space=pl.ANY)
    renewed = (adam[0], adam[1], adam[2], adam[4], adam[5], adam[6])
    found = pl.pallas_call(
        functools.partial(muon_kernel, owners, shapes),
        out_shape=[jax.ShapeDtypeStruct(shape, jnp.bfloat16) for shape in shapes]
        + [jax.ShapeDtypeStruct(piece.shape, piece.dtype) for piece in moved]
        + [jax.ShapeDtypeStruct(piece.shape, piece.dtype) for piece in renewed],
        in_specs=[anywhere] * (2 * count) + [vmem] * 9,
        out_specs=[anywhere] * (2 * count) + [vmem] * 6,
        scratch_shapes=[
            pltpu.VMEM(fine, jnp.float32),
            pltpu.VMEM((side, longest), jnp.bfloat16),
            pltpu.VMEM(fine, jnp.bfloat16),
            pltpu.VMEM((longest, side), jnp.bfloat16),
            pltpu.VMEM((side, longest // 2), jnp.bfloat16),
            pltpu.VMEM((longest, side // 2), jnp.bfloat16),
            pltpu.VMEM((side, side), jnp.float32),
            double,
            double,
            double,
            double,
            pltpu.SemaphoreType.DMA,
            pltpu.SemaphoreType.DMA((count,)),
            pltpu.SemaphoreType.DMA((count,)),
        ]
        + [pltpu.VMEM(piece.shape, piece.dtype) for piece in moved],
        compiler_params=pltpu.CompilerParams(vmem_limit_bytes=60 * 2**20),
        name="orthogonalize",
    )(*mats, *moved, stats, *adam)
    return found[:count], found[count : 2 * count], found[2 * count : 2 * count + 3], found[2 * count + 3 :]


def window_place(position):
    time_row = (position // GF + GT - SHIFT) % GT
    freq_col = (position % GF + GF - SHIFT) % GF
    window = (time_row // WIN) * (GF // WIN) + freq_col // WIN
    return window * (WIN * WIN) + (time_row % WIN) * WIN + freq_col % WIN


def window_sinusoid(channels):
    quarter = channels // 4
    frequency = 1.0 / 10000.0 ** (np.arange(quarter) / quarter)
    position = np.arange(NPATCH)
    time_rows = (position // GF)[:, None] * frequency
    freq_cols = (position % GF)[:, None] * frequency
    table = np.concatenate([np.sin(time_rows), np.cos(time_rows), np.sin(freq_cols), np.cos(freq_cols)], axis=1)
    moved = np.zeros_like(table)
    moved[window_place(position)] = table
    return moved.astype(np.float32)


def window_patches(spec):
    position = np.arange(NPATCH)
    row = np.empty(NPATCH, np.int32)
    row[window_place(position)] = position
    rows = row[:, None]
    take = (rows // GF == np.arange(GT)[None, :]).astype(np.float32)
    column = lax.broadcasted_iota(jnp.int32, (NPATCH, PS * GF * PS), 1)
    inside = (column // PS) % GF == jnp.asarray(rows % GF)
    source = np.arange(PS * GF * PS)[:, None]
    target = np.arange(PATCH)[None, :]
    fold = np.logical_and(source // (GF * PS) == target // PS, source % PS == target % PS)
    lines = spec.reshape(spec.shape[0], GT, PS * GF * PS)
    spread = jnp.einsum(
        "rt,ctl->crl", jnp.asarray(take, jnp.bfloat16), lines, preferred_element_type=jnp.float32
    )
    spread = jnp.where(inside, spread, 0.0).astype(jnp.bfloat16)
    found = jnp.einsum(
        "crl,lq->crq", spread, jnp.asarray(fold, jnp.bfloat16), preferred_element_type=jnp.float32
    )
    return found.astype(jnp.bfloat16)


@jax.custom_vjp
def times(inputs, matrix):
    return jnp.dot(inputs.astype(jnp.bfloat16), matrix.astype(jnp.bfloat16), preferred_element_type=jnp.float32)


def times_keep(inputs, matrix):
    short = inputs.astype(jnp.bfloat16)
    return jnp.dot(short, matrix.astype(jnp.bfloat16), preferred_element_type=jnp.float32), (short, matrix)


def times_back(kept, grad):
    short, matrix = kept
    grad = grad.astype(jnp.bfloat16)
    back = lax.dot_general(
        grad, matrix.astype(jnp.bfloat16), (((1,), (1,)), ((), ())), preferred_element_type=jnp.float32
    )
    gain = lax.dot_general(short, grad, (((0,), (0,)), ((), ())), preferred_element_type=jnp.float32)
    return back, gain.astype(matrix.dtype)


times.defvjp(times_keep, times_back)


def soft_rows(scores, allowed, scaling):
    scores = jnp.where(allowed, scores * scaling, -1e30)
    exponent = jnp.exp(scores - jnp.max(scores, axis=-1, keepdims=True))
    return exponent / jnp.sum(exponent, axis=-1, keepdims=True)


def dot_rows(left, right):
    return lax.dot_general(left, right, (((1,), (1,)), ((), ())), preferred_element_type=jnp.float32)


def dot_columns(left, right):
    return lax.dot_general(left, right, (((0,), (0,)), ((), ())), preferred_element_type=jnp.float32)


def head_lanes(value, head, size):
    lane = lax.broadcasted_iota(jnp.int32, value.shape, 1)
    return jnp.where(lane // size == head, value, jnp.zeros_like(value))


def attention_kernel(size, joined, allowed, out):
    width = out.shape[1]
    per = 128 // size
    allow = jnp.broadcast_to(allowed[...], (out.shape[0], allowed.shape[1])) > 0.0
    for lane in range(0, width, 128):
        queries = joined[:, lane : lane + 128]
        key_rows = joined[:, width + lane : width + lane + 128]
        values = joined[:, 2 * width + lane : 2 * width + lane + 128]
        total = jnp.zeros(queries.shape, jnp.float32)
        for head in range(per):
            scores = dot_rows(queries, head_lanes(key_rows, head, size))
            soft = soft_rows(scores, allow, size ** (-0.5)).astype(jnp.bfloat16)
            total = total + jnp.dot(
                soft, head_lanes(values, head, size), preferred_element_type=jnp.float32
            )
        out[:, lane : lane + 128] = total.astype(jnp.bfloat16)


def attention_back_kernel(size, joined, allowed, grad, out, query_sum, value_sum):
    width = grad.shape[1]
    per = 128 // size
    scaling = size ** (-0.5)
    allow = jnp.broadcast_to(allowed[...], (grad.shape[0], allowed.shape[1])) > 0.0

    @pl.when(pl.program_id(0) == 0)
    def clear():
        query_sum[...] = jnp.zeros_like(query_sum)
        value_sum[...] = jnp.zeros_like(value_sum)

    for lane in range(0, width, 128):
        queries = joined[:, lane : lane + 128]
        key_rows = joined[:, width + lane : width + lane + 128]
        values = joined[:, 2 * width + lane : 2 * width + lane + 128]
        pull = grad[:, lane : lane + 128]
        query_grad = jnp.zeros(queries.shape, jnp.float32)
        key_grad = jnp.zeros(queries.shape, jnp.float32)
        value_grad = jnp.zeros(queries.shape, jnp.float32)
        for head in range(per):
            keys_here = head_lanes(key_rows, head, size)
            soft = soft_rows(dot_rows(queries, keys_here), allow, scaling)
            soft_grad = dot_rows(pull, head_lanes(values, head, size))
            score_grad = soft * (soft_grad - jnp.sum(soft * soft_grad, axis=-1, keepdims=True))
            score_grad = (score_grad * scaling).astype(jnp.bfloat16)
            query_grad = query_grad + jnp.dot(score_grad, keys_here, preferred_element_type=jnp.float32)
            key_grad = key_grad + dot_columns(score_grad, head_lanes(queries, head, size))
            value_grad = value_grad + dot_columns(soft.astype(jnp.bfloat16), head_lanes(pull, head, size))
        out[:, lane : lane + 128] = query_grad.astype(jnp.bfloat16)
        out[:, width + lane : width + lane + 128] = key_grad.astype(jnp.bfloat16)
        out[:, 2 * width + lane : 2 * width + lane + 128] = value_grad.astype(jnp.bfloat16)
        query_sum[0:1, lane : lane + 128] += jnp.sum(query_grad, axis=0, keepdims=True)
        value_sum[0:1, lane : lane + 128] += jnp.sum(value_grad, axis=0, keepdims=True)


def window_fold(value, heads):
    lane = lax.broadcasted_iota(jnp.int32, (1, 1, value.shape[1]), 2) // (WIN * WIN)
    value = value.reshape(heads, 8, WIN * WIN, value.shape[1])
    found = value[:, 0]
    for window in range(1, 8):
        found = jnp.where(lane == window, value[:, window], found)
    return found


def window_spread(value):
    heads = value.shape[0]
    short = value.astype(jnp.bfloat16)
    lane = lax.broadcasted_iota(jnp.int32, short.shape, 2) // (WIN * WIN)
    parts = []
    for head in range(heads):
        for window in range(8):
            parts.append(
                jnp.where(lane[head] == window, short[head], jnp.zeros_like(short[head]))
            )
    return jnp.concatenate(parts, axis=0)


def stack_heads(value, size):
    per = value.shape[1] // size
    return jnp.concatenate([head_lanes(value, head, size) for head in range(per)], axis=0)


def unstack_heads(value, size):
    rows = value.shape[1]
    per = value.shape[0] // rows
    lane = lax.broadcasted_iota(jnp.int32, (rows, rows), 1) // size
    found = value[:rows]
    for head in range(1, per):
        found = jnp.where(lane == head, value[head * rows : (head + 1) * rows], found)
    return found


def soft_fold(queries, keys_here, allow, size):
    scores = window_fold(dot_rows(keys_here, queries), 128 // size)
    scores = jnp.where(allow, scores * size ** (-0.5), -1e30)
    exponent = jnp.exp(scores - jnp.max(scores, axis=1, keepdims=True))
    return exponent / jnp.sum(exponent, axis=1, keepdims=True)


def window_kernel(size, joined, allowed, out):
    width = out.shape[1]
    allow = allowed[...][None] > 0.0
    for lane in range(0, width, 128):
        queries = joined[:, lane : lane + 128]
        keys_here = stack_heads(joined[:, width + lane : width + lane + 128], size)
        values_here = stack_heads(joined[:, 2 * width + lane : 2 * width + lane + 128], size)
        soft = window_spread(soft_fold(queries, keys_here, allow, size))
        out[:, lane : lane + 128] = dot_columns(soft, values_here).astype(jnp.bfloat16)


def window_back_kernel(size, joined, allowed, grad, out, query_sum, value_sum):
    width = grad.shape[1]
    allow = allowed[...][None] > 0.0

    @pl.when(pl.program_id(0) == 0)
    def clear():
        query_sum[...] = jnp.zeros_like(query_sum)
        value_sum[...] = jnp.zeros_like(value_sum)

    for lane in range(0, width, 128):
        queries = joined[:, lane : lane + 128]
        keys_here = stack_heads(joined[:, width + lane : width + lane + 128], size)
        values_here = stack_heads(joined[:, 2 * width + lane : 2 * width + lane + 128], size)
        pull = grad[:, lane : lane + 128]
        soft = soft_fold(queries, keys_here, allow, size)
        soft_grad = window_fold(dot_rows(values_here, pull), 128 // size)
        score_grad = soft * (soft_grad - jnp.sum(soft * soft_grad, axis=1, keepdims=True))
        score_grad = window_spread(score_grad * size ** (-0.5))
        soft = window_spread(soft)
        query_grad = dot_columns(score_grad, keys_here)
        key_grad = unstack_heads(jnp.dot(score_grad, queries, preferred_element_type=jnp.float32), size)
        value_grad = unstack_heads(jnp.dot(soft, pull, preferred_element_type=jnp.float32), size)
        out[:, lane : lane + 128] = query_grad.astype(jnp.bfloat16)
        out[:, width + lane : width + lane + 128] = key_grad.astype(jnp.bfloat16)
        out[:, 2 * width + lane : 2 * width + lane + 128] = value_grad.astype(jnp.bfloat16)
        query_sum[0:1, lane : lane + 128] += jnp.sum(query_grad, axis=0, keepdims=True)
        value_sum[0:1, lane : lane + 128] += jnp.sum(value_grad, axis=0, keepdims=True)


def attention_parts(joined, allowed, rows):
    steps = joined.shape[0] // rows
    period = allowed.shape[0]
    wide = pl.BlockSpec((rows, joined.shape[1]), lambda step: (step, 0))
    mask = pl.BlockSpec((None,) + allowed.shape[1:], lambda step: (lax.rem(step, period), 0, 0))
    narrow_rows = pl.BlockSpec((rows, joined.shape[1] // 3), lambda step: (step, 0))
    return steps, wide, mask, narrow_rows


def attention_forward(kernel, joined, allowed, rows, size):
    steps, wide, mask, part = attention_parts(joined, allowed, rows)
    return pl.pallas_call(
        functools.partial(kernel, size),
        grid=(steps,),
        out_shape=jax.ShapeDtypeStruct((joined.shape[0], joined.shape[1] // 3), jnp.bfloat16),
        in_specs=[wide, mask],
        out_specs=part,
        compiler_params=pltpu.CompilerParams(vmem_limit_bytes=40 * 2**20),
        name="attention_forward",
    )(joined, allowed)


def attention_backward(kernel, joined, allowed, grad, rows, size):
    steps, wide, mask, part = attention_parts(joined, allowed, rows)
    width = joined.shape[1] // 3
    total = pl.BlockSpec((8, width), lambda step: (0, 0))
    return pl.pallas_call(
        functools.partial(kernel, size),
        grid=(steps,),
        out_shape=[
            jax.ShapeDtypeStruct(joined.shape, jnp.bfloat16),
            jax.ShapeDtypeStruct((8, width), jnp.float32),
            jax.ShapeDtypeStruct((8, width), jnp.float32),
        ],
        in_specs=[wide, mask, part],
        out_specs=[wide, total, total],
        compiler_params=pltpu.CompilerParams(vmem_limit_bytes=40 * 2**20),
        name="attention_backward",
    )(joined, allowed, grad)


def attention_block(forward, backward, rows, size):
    def join(normed, matrix, query_bias, value_bias):
        width = matrix.shape[1] // 3
        bias = jnp.concatenate([query_bias, jnp.zeros((width,), jnp.float32), value_bias])
        joined = jnp.dot(normed, matrix.astype(jnp.bfloat16), preferred_element_type=jnp.float32)
        return (joined + bias).astype(jnp.bfloat16)

    @jax.custom_vjp
    def apply(normed, matrix, query_bias, value_bias, allowed):
        joined = join(normed.astype(jnp.bfloat16), matrix, query_bias, value_bias)
        return attention_forward(forward, joined, allowed, rows, size).astype(jnp.float32)

    def keep(normed, matrix, query_bias, value_bias, allowed):
        short = normed.astype(jnp.bfloat16)
        joined = join(short, matrix, query_bias, value_bias)
        made = attention_forward(forward, joined, allowed, rows, size).astype(jnp.float32)
        return made, (short, matrix, joined, allowed)

    def back(kept, grad):
        short, matrix, joined, allowed = kept
        pulled, query_sum, value_sum = attention_backward(
            backward, joined, allowed, grad.astype(jnp.bfloat16), rows, size
        )
        normed_grad = dot_rows(pulled, matrix.astype(jnp.bfloat16))
        matrix_grad = dot_columns(short, pulled).astype(matrix.dtype)
        return normed_grad, matrix_grad, query_sum[0], value_sum[0], jnp.zeros_like(allowed)

    apply.defvjp(keep, back)
    return apply


encoder_attention = attention_block(attention_kernel, attention_back_kernel, SLOTS, HEAD)
decoder_attention = attention_block(window_kernel, window_back_kernel, 8 * WIN * WIN, DHEAD)


def window_allowed():
    position = np.arange(NPATCH)
    window, inner = position // (WIN * WIN), position % (WIN * WIN)
    time_row = window // (GF // WIN) * WIN + inner // WIN
    freq_col = window % (GF // WIN) * WIN + inner % WIN
    region = (time_row >= GT - WIN).astype(np.int32) + (time_row >= GT - SHIFT)
    region = region * 3 + (freq_col >= GF - WIN) + (freq_col >= GF - SHIFT)
    region = region.reshape(-1, 8, 1, WIN * WIN)
    same = region == region.transpose(0, 1, 3, 2)
    return same.transpose(0, 2, 1, 3).reshape(-1, WIN * WIN, 8 * WIN * WIN).astype(np.float32)


@jax.custom_vjp
def gelu(value):
    return value * (0.5 + 0.5 * lax.erf(value * math.sqrt(0.5)))


def gelu_keep(value):
    portion = 0.5 + 0.5 * lax.erf(value * math.sqrt(0.5))
    slope = portion + value * jnp.exp(-0.5 * value * value) * (1.0 / math.sqrt(2.0 * math.pi))
    return value * portion, slope


def gelu_back(slope, grad):
    return (grad * slope,)


gelu.defvjp(gelu_keep, gelu_back)


def local_loss(weights, patches, keep, counts):
    clips = patches.shape[0]
    pieces = unpack(weights[10])
    keep = jnp.pad(keep, ((0, 0), (0, SLOTS - VIS)))
    spot = window_place(keep)
    chosen = (spot[:, :, None] == jnp.arange(NPATCH)[None, None, :]).astype(jnp.float32)
    shown = chosen * (jnp.arange(SLOTS)[None, :] < counts[:, None])[:, :, None]
    picked = jnp.einsum("cjp,cpv->cjv", chosen.astype(jnp.bfloat16), patches, preferred_element_type=jnp.float32)
    where = jnp.einsum("cjp,pd->cjd", chosen, window_sinusoid(D), precision=HIGH)
    hidden = times(picked.reshape(-1, PATCH), weights[8][:, :D]) + pieces[11] + where.reshape(-1, D)
    normed = layer_norm(hidden, pieces[0], pieces[1])
    visible = (jnp.arange(SLOTS)[None, :] < counts[:, None]).astype(jnp.float32)[:, None, :]
    attended = encoder_attention(normed, weights[0], pieces[2], pieces[3], visible)
    hidden = hidden + times(attended, weights[1]) + pieces[4]
    normed = layer_norm(hidden, pieces[5], pieces[6])
    inner = gelu(times(normed, weights[2]) + pieces[7])
    hidden = hidden + times(inner, weights[3]) + pieces[8]
    latent = layer_norm(hidden, pieces[9], pieces[10])

    pieces = pieces[12:]
    placed = times(latent, weights[9]) + pieces[0]
    filled = jnp.einsum("cjp,cjd->cpd", shown, placed.reshape(clips, SLOTS, DD), precision=HIGH)
    cells = jnp.sum(shown, axis=1)
    hidden = filled + (1.0 - cells)[..., None] * pieces[1] + window_sinusoid(DD)
    hidden = hidden.reshape(-1, DD)
    normed = layer_norm(hidden, pieces[2], pieces[3])
    attended = decoder_attention(normed, weights[4], pieces[4], pieces[5], jnp.asarray(window_allowed()))
    hidden = hidden + times(attended, weights[5]) + pieces[6]
    normed = layer_norm(hidden, pieces[7], pieces[8])
    inner = gelu(times(normed, weights[6]) + pieces[9])
    hidden = hidden + times(inner, weights[7]) + pieces[10]
    normed = layer_norm(hidden, pieces[11], pieces[12])
    predicted = times(normed, weights[8][:, D:].T) + pieces[13]
    patches = patches.astype(jnp.float32).reshape(-1, PATCH)
    centred = patches - jnp.mean(patches, axis=-1, keepdims=True)
    target = centred * lax.rsqrt(jnp.mean(centred * centred, axis=-1, keepdims=True) + 1e-06)
    deviation = predicted - target
    patch_error = jnp.mean(deviation * deviation, axis=-1)
    return jnp.sum((1.0 - cells.reshape(-1)) * patch_error)


def quick_body(
    spectrogram, keep, counts, *rest
):
    masters = rest[:8] + (rest[16], rest[19], rest[22])
    moments = rest[8:16]
    devices = lax.axis_size("dp")
    lead = (2,) * bit_count(devices)
    own = list(masters)
    vector_rows = own[10].shape[0]
    spare = VEC_ROWS * VEC_COLS
    own[10] = jnp.pad(own[10], (0, spare - vector_rows)).reshape(VEC_ROWS, VEC_COLS)
    row = lax.broadcasted_iota(jnp.int32, (8, 128), 0)
    column = lax.broadcasted_iota(jnp.int32, (8, 128), 1)
    first = jnp.logical_and(row == 0, column == 0)
    count_part = jnp.sum(NPATCH - counts).astype(jnp.float32)
    gathered, tally = gather_rows(own, jnp.where(first, count_part, 0.0), devices)
    mask_count = tally[0, 0]
    weights = [piece.reshape(-1, piece.shape[-1]) for piece in gathered[:10]]
    weights[4] = weights[4].astype(jnp.float32)
    vectors = gathered[10].reshape(devices, spare)[:, :vector_rows].reshape(-1).astype(jnp.float32)
    patches = window_patches(spectrogram)
    loss_part, pull = jax.vjp(
        lambda *params: local_loss(params, patches, keep, counts), *weights, vectors
    )
    grads = list(pull(1.0 / mask_count))
    grads[10] = jnp.pad(grads[10].reshape(devices, vector_rows), ((0, 0), (0, spare - vector_rows)))
    grads[10] = grads[10].reshape(lead + (VEC_ROWS, VEC_COLS))
    for number in range(10):
        grad = grads[number]
        grads[number] = grad.reshape(lead + (grad.shape[0] // devices, grad.shape[1]))
    renewed, others, stats, collected = reduce_rows(
        grads, jnp.where(jnp.logical_and(row == 1, column == 0), loss_part, 0.0), moments, OWNERS, devices
    )
    loss_sum = stats[1, 0]
    grad_norm = jnp.sqrt(jnp.sum(stats[0]))
    factor = jnp.minimum(1.0, CLIP_MAX / (grad_norm + 1e-06))
    adam = (*rest[16:19], others[0], *rest[19:22], others[1])
    flat = [piece.reshape(-1, piece.shape[2]) for piece in collected]
    made, renewed, patch_new, embed_new = orthogonalize(flat, renewed, stats, adam, OWNERS)
    made = [piece.reshape(devices, -1, piece.shape[1]) for piece in made]
    new_weights = finish(return_rows(made, OWNERS, devices), masters[:8], devices)
    vector_grad = others[2].reshape(-1)[:vector_rows] * factor
    vector_new = adam_update(*rest[22:25], vector_grad, 0.0)
    return (loss_sum, mask_count, grad_norm, *new_weights, *renewed, *patch_new, *embed_new, *vector_new)


def body(
    spectrogram,
    keep,
    counts,
    enc_qkv,
    enc_out,
    enc_up,
    enc_down,
    dec_qkv,
    dec_out,
    dec_up,
    dec_down,
    mom_enc_qkv,
    mom_enc_out,
    mom_enc_up,
    mom_enc_down,
    mom_dec_qkv,
    mom_dec_out,
    mom_dec_up,
    mom_dec_down,
    patch_maps,
    patch_first,
    patch_second,
    embed_map,
    embed_first,
    embed_second,
    vectors,
    vector_first,
    vector_second,
):
    masters = (
        enc_qkv,
        enc_out,
        enc_up,
        enc_down,
        dec_qkv,
        dec_out,
        dec_up,
        dec_down,
        patch_maps,
        embed_map,
        vectors,
    )
    moments = (
        mom_enc_qkv,
        mom_enc_out,
        mom_enc_up,
        mom_enc_down,
        mom_dec_qkv,
        mom_dec_out,
        mom_dec_up,
        mom_dec_down,
    )
    sent = tuple((weight.astype(jnp.bfloat16) for weight in masters))
    gathered = (
        lax.all_gather(sent[0], "dp", axis=0, tiled=True),
        lax.all_gather(sent[1], "dp", axis=0, tiled=True),
        lax.all_gather(sent[2], "dp", axis=0, tiled=True),
        lax.all_gather(sent[3], "dp", axis=0, tiled=True),
        lax.all_gather(sent[4], "dp", axis=0, tiled=True),
        lax.all_gather(sent[5], "dp", axis=0, tiled=True),
        lax.all_gather(sent[6], "dp", axis=0, tiled=True),
        lax.all_gather(sent[7], "dp", axis=0, tiled=True),
        lax.all_gather(sent[8], "dp", axis=0, tiled=True),
        lax.all_gather(sent[9], "dp", axis=0, tiled=True),
        lax.all_gather(sent[10], "dp", axis=0, tiled=True),
    )
    widened = tuple((piece.astype(jnp.float32) for piece in gathered))
    patches = patchify(spectrogram.astype(jnp.float32))
    latent = encode(widened, patches, keep, counts)
    loss_part = decode(widened, latent, patches, keep, counts)
    count_part = jnp.sum(NPATCH - counts).astype(jnp.float32)
    loss_sum, mask_count = lax.psum((loss_part, count_part), ("dp", "mp"))
    regathered = (
        lax.all_gather(sent[0], "dp", axis=0, tiled=True),
        lax.all_gather(sent[1], "dp", axis=0, tiled=True),
        lax.all_gather(sent[2], "dp", axis=0, tiled=True),
        lax.all_gather(sent[3], "dp", axis=0, tiled=True),
        lax.all_gather(sent[4], "dp", axis=0, tiled=True),
        lax.all_gather(sent[5], "dp", axis=0, tiled=True),
        lax.all_gather(sent[6], "dp", axis=0, tiled=True),
        lax.all_gather(sent[7], "dp", axis=0, tiled=True),
        lax.all_gather(sent[8], "dp", axis=0, tiled=True),
        lax.all_gather(sent[9], "dp", axis=0, tiled=True),
        lax.all_gather(sent[10], "dp", axis=0, tiled=True),
    )
    widened = tuple((piece.astype(jnp.float32) for piece in regathered))
    cotangent = 1.0 / mask_count
    unused, pull_decode = jax.vjp(
        lambda params, hidden: decode(params, hidden, patches, keep, counts), widened, latent
    )
    decode_grads, latent_grad = pull_decode(cotangent)
    unused, pull_encode = jax.vjp(lambda params: encode(params, patches, keep, counts), widened)
    (encode_grads,) = pull_encode(latent_grad)
    grads = jax.tree.map(jnp.add, decode_grads, encode_grads)
    reduced = (
        lax.psum_scatter(grads[0], "dp", scatter_dimension=0, tiled=True),
        lax.psum_scatter(grads[1], "dp", scatter_dimension=0, tiled=True),
        lax.psum_scatter(grads[2], "dp", scatter_dimension=0, tiled=True),
        lax.psum_scatter(grads[3], "dp", scatter_dimension=0, tiled=True),
        lax.psum_scatter(grads[4], "dp", scatter_dimension=0, tiled=True),
        lax.psum_scatter(grads[5], "dp", scatter_dimension=0, tiled=True),
        lax.psum_scatter(grads[6], "dp", scatter_dimension=0, tiled=True),
        lax.psum_scatter(grads[7], "dp", scatter_dimension=0, tiled=True),
        lax.psum_scatter(grads[8], "dp", scatter_dimension=0, tiled=True),
        lax.psum_scatter(grads[9], "dp", scatter_dimension=0, tiled=True),
        lax.psum_scatter(grads[10], "dp", scatter_dimension=0, tiled=True),
    )
    reduced = lax.psum(
        (
            reduced[0],
            reduced[1],
            reduced[2],
            reduced[3],
            reduced[4],
            reduced[5],
            reduced[6],
            reduced[7],
            reduced[8],
            reduced[9],
            reduced[10],
        ),
        "mp",
    )
    local_squares = functools.reduce(
        jnp.add, [jnp.sum(gradient * gradient) for gradient in reduced]
    )
    grad_norm = jnp.sqrt(lax.psum(local_squares, "dp"))
    factor = jnp.minimum(1.0, CLIP_MAX / (grad_norm + 1e-06))
    clipped = [gradient * factor for gradient in reduced]
    devices = lax.axis_size("dp")
    renewed = [0.5 * moments[number] + clipped[number] for number in range(8)]
    core = lax.axis_index("mp")
    halves = [take_half(renewed[number], number, core) for number in range(8)]
    shapes = [(masters[number].shape[0] * devices, masters[number].shape[1]) for number in range(8)]
    long_max = max((max(shape_pair) // 2 for shape_pair in shapes))
    short_max = max((min(shape_pair) for shape_pair in shapes))
    flat_max = max((shape_pair[0] * shape_pair[1] // (2 * devices) for shape_pair in shapes))
    owner = lax.axis_index("dp") % 8
    collected = (
        lax.all_gather(halves[0], "dp", axis=0, tiled=True),
        lax.all_gather(halves[1], "dp", axis=0, tiled=True),
        lax.all_gather(halves[2], "dp", axis=0, tiled=True),
        lax.all_gather(halves[3], "dp", axis=0, tiled=True),
        lax.all_gather(halves[4], "dp", axis=0, tiled=True),
        lax.all_gather(halves[5], "dp", axis=0, tiled=True),
        lax.all_gather(halves[6], "dp", axis=0, tiled=True),
        lax.all_gather(halves[7], "dp", axis=0, tiled=True),
    )
    iterate = lax.switch(
        owner,
        [partial(arrange, collected[number], number, long_max, short_max) for number in range(8)],
    )
    for iteration in range(NS_ITERS):
        gram_sum = lax.psum(jnp.dot(iterate.T, iterate, precision=HIGH), "mp")
        if iteration == 0:
            norm_scale = 1.0 / (jnp.sqrt(jnp.trace(gram_sum)) + 1e-07)
            iterate = iterate * norm_scale
            gram_sum = gram_sum * (norm_scale * norm_scale)
        polynomial = NS_B * gram_sum + NS_C * jnp.dot(gram_sum, gram_sum, precision=HIGH)
        iterate = NS_A * iterate + jnp.dot(iterate, polynomial, precision=HIGH)
    outgoing = lax.switch(
        owner,
        [
            partial(
                disperse, iterate, number, shapes[number][0], shapes[number][1], devices, flat_max
            )
            for number in range(8)
        ],
    )
    arriving = jax.tree.map(
        lambda part, own: part.astype(own.dtype),
        lax.all_to_all(shortened(outgoing), "dp", split_axis=0, concat_axis=0, tiled=True),
        outgoing,
    )
    mine = [
        restore(arriving[number], number, shapes[number][0], shapes[number][1], devices)
        for number in range(8)
    ]
    whole = (
        lax.all_gather(shortened(mine[0]), "mp", axis=1, tiled=True),
        lax.all_gather(shortened(mine[1]), "mp", axis=1, tiled=True),
        lax.all_gather(shortened(mine[2]), "mp", axis=1, tiled=True),
        lax.all_gather(shortened(mine[3]), "mp", axis=0, tiled=True),
        lax.all_gather(shortened(mine[4]), "mp", axis=1, tiled=True),
        lax.all_gather(shortened(mine[5]), "mp", axis=1, tiled=True),
        lax.all_gather(shortened(mine[6]), "mp", axis=1, tiled=True),
        lax.all_gather(shortened(mine[7]), "mp", axis=0, tiled=True),
    )
    new_weights = []
    for number in range(8):
        step_rate = LR_MUON * 0.2 * math.sqrt(max(shapes[number]))
        new_weights.append(masters[number] * (1.0 - LR_MUON * DECAY) - step_rate * whole[number])
    patch_new = adam_update(patch_maps, patch_first, patch_second, clipped[8], DECAY)
    embed_new = adam_update(embed_map, embed_first, embed_second, clipped[9], DECAY)
    vector_new = adam_update(vectors, vector_first, vector_second, clipped[10], 0.0)
    return (
        loss_sum,
        mask_count,
        grad_norm,
        new_weights[0],
        new_weights[1],
        new_weights[2],
        new_weights[3],
        new_weights[4],
        new_weights[5],
        new_weights[6],
        new_weights[7],
        renewed[0],
        renewed[1],
        renewed[2],
        renewed[3],
        renewed[4],
        renewed[5],
        renewed[6],
        renewed[7],
        patch_new[0],
        patch_new[1],
        patch_new[2],
        embed_new[0],
        embed_new[1],
        embed_new[2],
        vector_new[0],
        vector_new[1],
        vector_new[2],
    )


def solution(mesh):
    placed = (
        P(("dp", "mp"), None, None),
        P(("dp", "mp"), None),
        P(("dp", "mp")),
        P("dp", None),
        P("dp", None),
        P("dp", None),
        P("dp", None),
        P("dp", None),
        P("dp", None),
        P("dp", None),
        P("dp", None),
        P("dp", None),
        P("dp", None),
        P("dp", None),
        P("dp", None),
        P("dp", None),
        P("dp", None),
        P("dp", None),
        P("dp", None),
        P("dp", None),
        P("dp", None),
        P("dp", None),
        P("dp", None),
        P("dp", None),
        P("dp", None),
        P("dp"),
        P("dp"),
        P("dp"),
    )
    return jax.shard_map(
        quick_body if mesh.shape["dp"] == 16 else body,
        mesh=mesh,
        in_specs=placed,
        out_specs=(
            P(),
            P(),
            P(),
            P("dp", None),
            P("dp", None),
            P("dp", None),
            P("dp", None),
            P("dp", None),
            P("dp", None),
            P("dp", None),
            P("dp", None),
            P("dp", None),
            P("dp", None),
            P("dp", None),
            P("dp", None),
            P("dp", None),
            P("dp", None),
            P("dp", None),
            P("dp", None),
            P("dp", None),
            P("dp", None),
            P("dp", None),
            P("dp", None),
            P("dp", None),
            P("dp", None),
            P("dp"),
            P("dp"),
            P("dp"),
        ),
        check_vma=False,
    )
```

```python
from functools import partial
import functools
import math

import jax
import jax.numpy as jnp
import numpy as np
from jax import lax
from jax.experimental import pallas as pl
from jax.experimental.pallas import tpu as pltpu
from jax.sharding import PartitionSpec as P

D = 768
HEADS = 12
HEAD = 64
MLP = 3072
DD = 512
DHEADS = 16
DHEAD = 32
DMLP = 2048
PS = 16
GT = 64
GF = 8
WIN = 4
VIS = 154
NS_ITERS = 5
STEP = 10
PATCH = 256
SHIFT = 2
NPATCH = 512


HIGH = lax.Precision.HIGHEST
CLIP_MAX = 0.001
LR_MUON = 0.1
LR_ADAM = 0.05
DECAY = 0.01
NS_A = 3.4445
NS_B = -4.775
NS_C = 2.0315
LONG_COLS = (True, True, True, False, True, True, True, False)


def shortened(x):
    return jax.tree.map(lambda a: a.astype(jnp.bfloat16) if a.dtype == jnp.float32 else a, x)


def narrow_core(value):
    return lax.optimization_barrier(value.astype(jnp.bfloat16)).astype(jnp.float32)


def narrow_keep(value):
    return (narrow_core(value), None)


def narrow_pass(kept, grad):
    return (grad,)


def same_core(value):
    return value


def same_keep(value):
    return (value, None)


def same_back(kept, grad):
    return (narrow_core(grad),)


def narrow(value):
    wrapped = jax.custom_vjp(narrow_core)
    wrapped.defvjp(narrow_keep, narrow_pass)
    return wrapped(value)


def narrow_grad(value):
    wrapped = jax.custom_vjp(same_core)
    wrapped.defvjp(same_keep, same_back)
    return wrapped(value)


def product(inputs, matrix):
    return narrow_grad(jnp.dot(narrow(inputs), narrow(matrix), preferred_element_type=jnp.float32))


def score_product(queries, key_rows):
    return narrow_grad(
        jnp.einsum(
            "bqhd,bkhd->bhqk", narrow(queries), narrow(key_rows), preferred_element_type=jnp.float32
        )
    )


def value_product(softmax_rows, values):
    return narrow_grad(
        jnp.einsum(
            "bhqk,bkhd->bqhd",
            narrow(softmax_rows),
            narrow(values),
            preferred_element_type=jnp.float32,
        )
    )


def unpack(vectors):
    extents = [D] * 7 + [MLP] + [D] * 4 + [DD] * 9 + [DMLP] + [DD] * 3 + [PATCH]
    pieces = []
    offset = 0
    for extent in extents:
        pieces.append(vectors[offset : offset + extent])
        offset += extent
    return pieces


def layer_norm(hidden, scaling, offset):
    centred = hidden - jnp.mean(hidden, axis=-1, keepdims=True)
    variance = jnp.mean(centred * centred, axis=-1, keepdims=True)
    return centred * lax.rsqrt(variance + 1e-06) * scaling + offset


def sinusoid(channels):
    quarter = channels // 4
    frequency = 1.0 / 10000.0 ** (jnp.arange(quarter, dtype=jnp.float32) / quarter)
    position = jnp.arange(GT * GF)
    time_rows = (position // GF).astype(jnp.float32)[:, None] * frequency
    freq_cols = (position % GF).astype(jnp.float32)[:, None] * frequency
    return jnp.concatenate(
        [jnp.sin(time_rows), jnp.cos(time_rows), jnp.sin(freq_cols), jnp.cos(freq_cols)], axis=1
    )


def patchify(spec):
    clip_total = spec.shape[0]
    arranged = spec.reshape(clip_total, GT, PS, GF, PS).transpose(0, 1, 3, 2, 4)
    return arranged.reshape(clip_total, GT * GF, PS * PS)


def window_mask():
    time_rows = jnp.arange(GT)
    freq_cols = jnp.arange(GF)
    time_part = (time_rows >= GT - WIN).astype(jnp.int32) + (time_rows >= GT - SHIFT).astype(
        jnp.int32
    )
    freq_part = (freq_cols >= GF - WIN).astype(jnp.int32) + (freq_cols >= GF - SHIFT).astype(
        jnp.int32
    )
    region = time_part[:, None] * 3 + freq_part[None, :]
    region = (
        region.reshape(GT // WIN, WIN, GF // WIN, WIN).transpose(0, 2, 1, 3).reshape(-1, WIN * WIN)
    )
    return region[:, :, None] == region[:, None, :]


def to_windows(grid_rows):
    clip_total = grid_rows.shape[0]
    channels = grid_rows.shape[2]
    arranged = jnp.roll(
        grid_rows.reshape(clip_total, GT, GF, channels), (-SHIFT, -SHIFT), axis=(1, 2)
    )
    arranged = arranged.reshape(clip_total, GT // WIN, WIN, GF // WIN, WIN, channels).transpose(
        0, 1, 3, 2, 4, 5
    )
    return arranged.reshape(-1, WIN * WIN, channels)


def from_windows(windows, clip_total):
    channels = windows.shape[-1]
    arranged = windows.reshape(clip_total, GT // WIN, GF // WIN, WIN, WIN, channels).transpose(
        0, 1, 3, 2, 4, 5
    )
    arranged = jnp.roll(arranged.reshape(clip_total, GT, GF, channels), (SHIFT, SHIFT), axis=(1, 2))
    return arranged.reshape(clip_total, GT * GF, channels)


def attend(queries, key_rows, values, allowed, scaling):
    scores = score_product(queries, key_rows) * scaling
    scores = jnp.where(allowed, scores, -1e30)
    scores = scores - jnp.max(scores, axis=-1, keepdims=True)
    exponent = jnp.exp(scores)
    softmax_rows = exponent / jnp.sum(exponent, axis=-1, keepdims=True)
    return value_product(softmax_rows, values)


def encode(weights, patches, keep, counts):
    pieces = unpack(weights[10])
    clip_total = patches.shape[0]
    picked = jnp.take_along_axis(patches, keep[:, :, None], axis=1)
    hidden = product(picked, weights[8][:, :D]) + pieces[11] + sinusoid(D)[keep]
    normed = layer_norm(hidden, pieces[0], pieces[1])
    joined = product(normed, weights[0])
    queries = (joined[..., :D] + pieces[2]).reshape(clip_total, VIS, HEADS, HEAD)
    key_rows = joined[..., D : 2 * D].reshape(clip_total, VIS, HEADS, HEAD)
    values = (joined[..., 2 * D :] + pieces[3]).reshape(clip_total, VIS, HEADS, HEAD)
    visible = (jnp.arange(VIS)[None, :] < counts[:, None])[:, None, None, :]
    attended = attend(queries, key_rows, values, visible, HEAD ** (-0.5)).reshape(
        clip_total, VIS, D
    )
    hidden = hidden + product(attended, weights[1]) + pieces[4]
    normed = layer_norm(hidden, pieces[5], pieces[6])
    inner = jax.nn.gelu(product(normed, weights[2]) + pieces[7], approximate=False)
    hidden = hidden + product(inner, weights[3]) + pieces[8]
    return layer_norm(hidden, pieces[9], pieces[10])


def decode(weights, latent, patches, keep, counts):
    pieces = unpack(weights[10])[12:]
    clip_total = latent.shape[0]
    placed = product(latent, weights[9]) + pieces[0]
    visible = jnp.arange(VIS)[None, :] < counts[:, None]
    target_rows = jnp.where(visible, keep, NPATCH)
    clip_rows = jnp.arange(clip_total)[:, None]
    filled = (
        jnp.zeros((clip_total, NPATCH + 1, DD), jnp.float32)
        .at[clip_rows, target_rows]
        .add(placed)[:, :NPATCH]
    )
    visible_cells = (
        jnp.zeros((clip_total, NPATCH + 1), jnp.float32)
        .at[clip_rows, target_rows]
        .add(1.0)[:, :NPATCH]
    )
    hidden = filled + (1.0 - visible_cells)[..., None] * pieces[1] + sinusoid(DD)
    normed = layer_norm(hidden, pieces[2], pieces[3])
    windows = to_windows(product(normed, weights[4]))
    queries = (windows[..., :DD] + pieces[4]).reshape(-1, WIN * WIN, DHEADS, DHEAD)
    key_rows = windows[..., DD : 2 * DD].reshape(-1, WIN * WIN, DHEADS, DHEAD)
    values = (windows[..., 2 * DD :] + pieces[5]).reshape(-1, WIN * WIN, DHEADS, DHEAD)
    allowed = jnp.tile(window_mask(), (clip_total, 1, 1))[:, None, :, :]
    attended = attend(queries, key_rows, values, allowed, DHEAD ** (-0.5)).reshape(
        -1, WIN * WIN, DD
    )
    hidden = hidden + product(from_windows(attended, clip_total), weights[5]) + pieces[6]
    normed = layer_norm(hidden, pieces[7], pieces[8])
    inner = jax.nn.gelu(product(normed, weights[6]) + pieces[9], approximate=False)
    hidden = hidden + product(inner, weights[7]) + pieces[10]
    normed = layer_norm(hidden, pieces[11], pieces[12])
    predicted = product(normed, weights[8][:, D:].T) + pieces[13]
    centred = patches - jnp.mean(patches, axis=-1, keepdims=True)
    target = centred * lax.rsqrt(jnp.mean(centred * centred, axis=-1, keepdims=True) + 1e-06)
    deviation = predicted - target
    patch_error = jnp.mean(deviation * deviation, axis=-1)
    return jnp.sum((1.0 - visible_cells) * patch_error)


def take_half(shard, number, core):
    if LONG_COLS[number]:
        extent = shard.shape[1] // 2
        return lax.dynamic_slice_in_dim(shard, core * extent, extent, 1)
    extent = shard.shape[0] // 2
    return lax.dynamic_slice_in_dim(shard, core * extent, extent, 0)


def arrange(gathered_half, number, long_max, short_max):
    upright = gathered_half.T if LONG_COLS[number] else gathered_half
    return jnp.pad(upright, ((0, long_max - upright.shape[0]), (0, short_max - upright.shape[1])))


def disperse(iterate, number, height, breadth, devices, flat_max):
    if LONG_COLS[number]:
        piece = iterate[: breadth // 2, :height].T.reshape(
            devices, height // devices * (breadth // 2)
        )
    else:
        piece = iterate[: height // 2, :breadth].reshape(devices, height // 2 // devices * breadth)
    return jnp.pad(piece, ((0, 0), (0, flat_max - piece.shape[1])))


def restore(row_piece, number, height, breadth, devices):
    if LONG_COLS[number]:
        return row_piece[: height // devices * (breadth // 2)].reshape(
            height // devices, breadth // 2
        )
    return row_piece[: height // 2 // devices * breadth].reshape(height // 2 // devices, breadth)


def adam_update(weight, first_moment, second_moment, gradient, decay):
    first_moment = 0.5 * first_moment + 0.5 * gradient
    second_moment = 0.95 * second_moment + 0.05 * gradient * gradient
    direction = (
        first_moment / (1.0 - 0.5**STEP) / (jnp.sqrt(second_moment / (1.0 - 0.95**STEP)) + 1e-08)
    )
    return (weight - LR_ADAM * (direction + decay * weight), first_moment, second_moment)


MESH_ID = pl.DeviceIdType.MESH
VEC_ROWS, VEC_COLS = 16, 256
AXIS_ORDERS = ((0, 1, 2, 3), (0, 1, 3, 2), (0, 2, 1, 3), (0, 2, 3, 1), (0, 3, 1, 2), (0, 3, 2, 1), (1, 0, 2, 3), (1, 0, 3, 2), (1, 2, 0, 3), (1, 2, 3, 0), (1, 3, 0, 2), (1, 3, 2, 0), (2, 0, 1, 3), (2, 0, 3, 1), (2, 1, 0, 3), (2, 1, 3, 0), (2, 3, 0, 1), (2, 3, 1, 0), (3, 0, 1, 2), (3, 0, 2, 1), (3, 1, 0, 2), (3, 1, 2, 0), (3, 2, 0, 1), (3, 2, 1, 0))
GATHER_PARTS = (3, 1, 4, 4, 1, 1, 2, 2, 1, 1, 1)
REDUCE_PARTS = (3, 1, 4, 4, 2, 1, 2, 2, 1, 1, 1)
TALL = (3, 7)
GATHER_TURNS = (19, 18, 22, 17, 13, 21, 22, 20, 3, 12, 11, 0, 17, 23, 16, 10, 23, 16, 11, 21, 21)
GATHER_FIRST = (6, 17, 20, 11, 7, 16, 8, 13, 12, 1, 4, 9, 19, 10, 3, 2, 15, 5, 0, 14, 18)
GATHER_STEPS = ((20, 11, 17, 6, 8, 10, 13, 15, 7, 16, 18, 19, 4, 1, 12, 9, 3, 2, 5, 14, 0), (20, 11, 7, 19, 4, 1, 17, 9, 6, 13, 8, 5, 0, 10, 16, 18, 15, 12, 3, 2, 14), (20, 7, 1, 17, 9, 13, 6, 16, 15, 11, 19, 4, 3, 12, 2, 8, 14, 10, 18, 5, 0), (20, 17, 13, 16, 6, 19, 7, 3, 4, 2, 1, 14, 12, 8, 18, 9, 10, 5, 15, 0, 11))
REDUCE_TURNS = (14, 1, 1, 6, 7, 2, 12, 8, 20, 3, 21, 6, 6, 0, 0, 21, 10, 13, 2, 0, 17, 4)
REDUCE_FIRST = (17, 21, 12, 9, 15, 18, 19, 4, 3, 11, 1, 10, 13, 20, 0, 7, 5, 16, 8, 14, 6, 2)
REDUCE_STEPS = ((21, 17, 12, 9, 19, 15, 18, 4, 20, 3, 11, 10, 1, 0, 7, 14, 16, 5, 8, 13, 6, 2), (21, 17, 19, 15, 9, 12, 10, 14, 1, 20, 0, 18, 4, 8, 3, 7, 11, 13, 2, 16, 6, 5), (21, 17, 19, 20, 15, 18, 9, 14, 0, 10, 12, 8, 7, 16, 1, 6, 4, 5, 3, 11, 13, 2), (21, 17, 20, 15, 9, 19, 10, 18, 14, 0, 12, 8, 1, 16, 7, 6, 4, 5, 3, 2, 13, 11))
OWNERS = (4, 11, 5, 10, 6, 9, 7, 8)
SLOTS = 160


def bit_count(devices):
    return devices.bit_length() - 1


def cut_pieces(parts, shapes):
    found = []
    for number, count in enumerate(parts):
        rows, width = shapes[number]
        for part in range(count):
            if number in TALL:
                found.append((number, part * (rows // count), rows // count, 0, width))
            else:
                found.append((number, 0, rows, part * (width // count), width // count))
    return found


def own_bits(levels):
    me = lax.axis_index("dp")
    return me, [lax.rem(lax.div(me, 2**bit), 2) for bit in range(levels)]


def place(levels, free, own, flip=None):
    spots = []
    for bit in range(levels - 1, -1, -1):
        if bit in free:
            spots.append(slice(None))
        elif bit == flip:
            spots.append(1 - own[bit])
        else:
            spots.append(own[bit])
    return tuple(spots)


def partner(me, own, bit):
    return me + (1 - 2 * own[bit]) * 2**bit


def greet(me, own, levels, core):
    barrier = pltpu.get_barrier_semaphore()
    for bit in range(levels):
        pl.semaphore_signal(
            barrier,
            inc=1,
            device_id={"dp": partner(me, own, bit), "mp": core},
            device_id_type=MESH_ID,
        )
    pl.semaphore_signal(barrier, inc=1, device_id={"dp": me, "mp": 1 - core}, device_id_type=MESH_ID)
    pl.semaphore_wait(barrier, levels + 1)


def add_up(me, core, devices, total, landing, send_sem, recv_sem, own_sem):
    def send(source, target):
        return pltpu.make_async_remote_copy(
            src_ref=total,
            dst_ref=landing.at[source],
            send_sem=send_sem.at[target],
            recv_sem=recv_sem.at[source],
            device_id={"dp": target, "mp": core},
            device_id_type=MESH_ID,
        )

    @pl.loop(0, devices)
    def start_one(other):
        @pl.when(other != me)
        def start_other():
            send(me, other).start()

    own = pltpu.make_async_copy(total, landing.at[me], own_sem)
    own.start()
    own.wait()

    @pl.loop(0, devices)
    def wait_one(other):
        @pl.when(other != me)
        def wait_other():
            send(other, me).wait_recv()
            send(me, other).wait_send()

    found = landing[0]
    for device in range(1, devices):
        found = found + landing[device]
    total[...] = found
    swap = pltpu.make_async_remote_copy(
        src_ref=total,
        dst_ref=landing.at[devices],
        send_sem=send_sem.at[devices],
        recv_sem=recv_sem.at[devices],
        device_id={"dp": me, "mp": 1 - core},
        device_id_type=MESH_ID,
    )
    swap.start()
    swap.wait()
    total[...] = total[...] + landing[devices]


def cut_patches(lines, spots, take, freq, fold, table, picked_out, where_out, target_out):
    part = 512
    lane = lax.broadcasted_iota(jnp.int32, (NPATCH, part), 1)
    inside = lax.rem(lax.div(lane, PS), GF) == freq[...]
    for clip in range(lines.shape[0]):
        patches = jnp.zeros((NPATCH, PATCH), jnp.float32)
        for start in range(0, PS * GF * PS, part):
            spread = jnp.dot(
                take[...], lines[clip, :, start : start + part], preferred_element_type=jnp.float32
            )
            spread = jnp.where(inside, spread, 0.0).astype(jnp.bfloat16)
            patches = patches + jnp.dot(
                spread, fold[start : start + part, :], preferred_element_type=jnp.float32
            )
        slot = lax.broadcasted_iota(jnp.int32, (SLOTS, NPATCH), 1)
        chosen = jnp.where(slot == spots[clip], 1.0, 0.0).astype(jnp.bfloat16)
        picked = jnp.dot(chosen, patches.astype(jnp.bfloat16), preferred_element_type=jnp.float32)
        picked_out[clip] = picked.astype(jnp.bfloat16)
        where_out[clip] = jnp.dot(chosen, table[:, :D], preferred_element_type=jnp.float32) + jnp.dot(
            chosen, table[:, D:], preferred_element_type=jnp.float32
        )
        centred = patches - jnp.mean(patches, axis=-1, keepdims=True)
        spread = jnp.mean(centred * centred, axis=-1, keepdims=True)
        target_out[clip] = centred * lax.rsqrt(spread + 1e-06)


def gather_kernel(levels, pieces, count, *refs):
    sources, tally, rest = refs[:count] + refs[count + 1 : count + 7], refs[count], refs[count + 7 :]
    outs, tally_out, made, rest = rest[:count], rest[count], rest[count + 1 : count + 4], rest[count + 4 :]
    wholes, save_sem, rest = rest[:count], rest[count], rest[count + 1 :]
    short, held, load_sem, rest = rest[:count], rest[count : 2 * count + 6], rest[2 * count + 6], rest[2 * count + 7 :]
    shards, scene = held[:count], held[count:]

    def load(number):
        return pltpu.make_async_copy(sources[number], held[number], load_sem.at[number])

    for number in range(count + 6):
        load(number).start()
    here_sem, send_sem, recv_sem, cross_send, cross_recv, tally_land, tally_send, tally_recv = rest
    me, own = own_bits(levels)
    core = lax.axis_index("mp")
    greet(me, own, levels, core)
    orders = [AXIS_ORDERS[turn] for turn in GATHER_TURNS]

    def cut(piece, which):
        number, row, rows, column, columns = pieces[piece]
        width = shards[number].shape[1] // 2
        return (pl.ds(row, rows), pl.ds(pl.multiple_of(which * width + column, 128), columns))

    def hop(piece, stage, flip):
        order, number = orders[piece], pieces[piece][0]
        spot = place(levels, order[:stage], own, order[stage] if flip else None)
        target = wholes[number].at[spot + cut(piece, core)]
        source = target if stage or flip else short[number].at[cut(piece, core)]
        return pltpu.make_async_remote_copy(
            src_ref=source,
            dst_ref=target,
            send_sem=send_sem.at[piece, stage],
            recv_sem=recv_sem.at[piece, stage],
            device_id={"dp": partner(me, own, order[stage]), "mp": core},
            device_id_type=MESH_ID,
        )

    def cross(piece, stage, which):
        order, number = orders[piece], pieces[piece][0]
        spot = place(levels, order[:stage], own, order[stage])
        target = wholes[number].at[spot + cut(piece, which)]
        return pltpu.make_async_remote_copy(
            src_ref=target,
            dst_ref=target,
            send_sem=cross_send.at[piece, stage],
            recv_sem=cross_recv.at[piece, stage],
            device_id={"dp": me, "mp": 1 - core},
            device_id_type=MESH_ID,
        )

    def keep(number):
        spot = place(levels, (), own)
        return pltpu.make_async_copy(short[number], wholes[number].at[spot], here_sem.at[number])

    ready = set()
    for piece in GATHER_FIRST:
        number = pieces[piece][0]
        if number not in ready:
            ready.add(number)
            load(number).wait()
            short[number][...] = shards[number][...].astype(jnp.bfloat16)
            keep(number).start()
        hop(piece, 0, False).start()
    tally_out[...] = tally[...]

    def swap(stage):
        if stage < levels:
            to = {"dp": partner(me, own, stage), "mp": core}
        else:
            to = {"dp": me, "mp": 1 - core}
        return pltpu.make_async_remote_copy(
            src_ref=tally_out,
            dst_ref=tally_land.at[stage],
            send_sem=tally_send.at[stage],
            recv_sem=tally_recv.at[stage],
            device_id=to,
            device_id_type=MESH_ID,
        )

    def swap_end(stage):
        swap(stage).wait()
        tally_out[...] = tally_out[...] + tally_land[stage]

    swap(levels).start()
    for number in range(count):
        keep(number).wait()
    swap_end(levels)
    for stage, order in enumerate(GATHER_STEPS):
        swap(stage).start()
        for piece in order:
            hop(piece, stage, True).wait_recv()
            if stage + 1 < levels:
                hop(piece, stage + 1, False).start()
            cross(piece, stage, core).start()
        swap_end(stage)
        if stage == levels - 2:
            for number in range(6):
                load(count + number).wait()
            cut_patches(*scene, *made)
    def save(number):
        return pltpu.make_async_copy(wholes[number], outs[number], save_sem.at[number])

    last = {}
    for place_in, piece in enumerate(GATHER_STEPS[levels - 1]):
        last[pieces[piece][0]] = place_in
    for number in sorted(last, key=lambda found: last[found]):
        for piece in range(len(pieces)):
            if pieces[piece][0] == number:
                for stage in range(levels):
                    cross(piece, stage, 1 - core).wait_recv()
        save(number).start()
    for piece in range(len(pieces)):
        for stage in range(levels):
            hop(piece, stage, False).wait_send()
            cross(piece, stage, core).wait_send()
    for number in range(count):
        save(number).wait()


def gather_rows(shards, tally, scene, devices):
    levels, count = bit_count(devices), len(shards)
    lead = (2,) * levels
    clips = scene[0].shape[0]
    pieces = cut_pieces(GATHER_PARTS, [(shard.shape[0], shard.shape[1] // 2) for shard in shards])
    dma = pltpu.SemaphoreType.DMA
    vmem, far = pl.BlockSpec(memory_space=pltpu.VMEM), pl.BlockSpec(memory_space=pltpu.HBM)
    found = pl.pallas_call(
        functools.partial(gather_kernel, levels, pieces, count),
        out_shape=[jax.ShapeDtypeStruct(lead + shard.shape, jnp.bfloat16) for shard in shards]
        + [
            jax.ShapeDtypeStruct((8, 128), jnp.float32),
            jax.ShapeDtypeStruct((clips, SLOTS, PATCH), jnp.bfloat16),
            jax.ShapeDtypeStruct((clips, SLOTS, D), jnp.float32),
            jax.ShapeDtypeStruct((clips, NPATCH, PATCH), jnp.float32),
        ],
        in_specs=[far] * count + [vmem] + [far] * 6,
        out_specs=[pl.BlockSpec(memory_space=pl.ANY)] * count + [vmem] * 4,
        scratch_shapes=[pltpu.VMEM(lead + shard.shape, jnp.bfloat16) for shard in shards]
        + [dma((count,))]
        + [pltpu.VMEM(shard.shape, jnp.bfloat16) for shard in shards]
        + [pltpu.VMEM(piece.shape, piece.dtype) for piece in (*shards, *scene)]
        + [dma((count + 6,))]
        + [dma((count,))]
        + [dma((len(pieces), levels))] * 4
        + [pltpu.VMEM((levels + 1, 8, 128), jnp.float32)]
        + [dma((levels + 1,))] * 2,
        compiler_params=pltpu.CompilerParams(
            collective_id=1, has_side_effects=True, vmem_limit_bytes=60 * 2**20
        ),
        name="gather_rows",
    )(*shards, tally, *scene)
    return found[:count], found[count], found[count + 1 :]


def reduce_kernel(levels, pieces, count, owners, devices, *refs):
    blocks = len(owners)
    grads, stats_in, old = refs[:count], refs[count], refs[count + 1 : count + 1 + blocks]
    rest = refs[count + 1 + blocks :]
    sums, stats_out, wholes = rest[:count], rest[count], rest[count + 1 : count + 1 + blocks]
    rest = rest[count + 1 + blocks :]
    mine, theirs, rest = rest[:count], rest[count : 2 * count], rest[2 * count :]
    kept, rest = rest[:count], rest[count:]
    landing, rest = rest[: len(pieces) * levels], rest[len(pieces) * levels :]
    staged, rest = rest[:blocks], rest[blocks:]
    stats_land, here_sem, pair_send, pair_recv, send_sem, recv_sem, last_send, last_recv = rest[:8]
    stats_send, stats_recv, own_sem, out_send, out_recv, cross_send, cross_recv = rest[8:]
    me, own = own_bits(levels)
    core = lax.axis_index("mp")
    orders = [AXIS_ORDERS[turn] for turn in REDUCE_TURNS]
    barrier = pltpu.get_barrier_semaphore()

    @pl.loop(0, devices)
    def greet_one(other):
        @pl.when(other != me)
        def signal_one():
            pl.semaphore_signal(
                barrier, inc=1, device_id={"dp": other, "mp": core}, device_id_type=MESH_ID
            )

    pl.semaphore_signal(barrier, inc=1, device_id={"dp": me, "mp": 1 - core}, device_id_type=MESH_ID)
    pl.semaphore_wait(barrier, devices)

    def half(number, which):
        width = sums[number].shape[1] // 2
        return (slice(None), pl.ds(pl.multiple_of(which * width, 128), width))

    def cut(piece):
        number, row, rows, column, columns = pieces[piece]
        return (pl.ds(row, rows), pl.ds(column, columns))

    def side(piece, which):
        number, row, rows, column, columns = pieces[piece]
        width = sums[number].shape[1] // 2
        return (pl.ds(row, rows), pl.ds(pl.multiple_of(which * width + column, 128), columns))

    every = (slice(None),) * levels

    def pair(piece):
        number = pieces[piece][0]
        return pltpu.make_async_remote_copy(
            src_ref=grads[number].at[every + side(piece, 1 - core)],
            dst_ref=theirs[number].at[every + cut(piece)],
            send_sem=pair_send.at[piece],
            recv_sem=pair_recv.at[piece],
            device_id={"dp": me, "mp": 1 - core},
            device_id_type=MESH_ID,
        )

    def load(piece):
        number = pieces[piece][0]
        return pltpu.make_async_copy(
            grads[number].at[every + side(piece, core)],
            mine[number].at[every + cut(piece)],
            here_sem.at[piece],
        )

    def hop(piece, stage):
        order = orders[piece]
        spot = place(levels, order[stage + 1 :], own, order[stage])
        return pltpu.make_async_remote_copy(
            src_ref=theirs[pieces[piece][0]].at[spot + cut(piece)],
            dst_ref=landing[piece * levels + stage],
            send_sem=send_sem.at[piece, stage],
            recv_sem=recv_sem.at[piece, stage],
            device_id={"dp": partner(me, own, order[stage]), "mp": core},
            device_id_type=MESH_ID,
        )

    def share(number, which):
        region = sums[number].at[half(number, which)]
        return pltpu.make_async_remote_copy(
            src_ref=region,
            dst_ref=region,
            send_sem=last_send.at[number],
            recv_sem=last_recv.at[number],
            device_id={"dp": me, "mp": 1 - core},
            device_id_type=MESH_ID,
        )

    def deliver(number, source):
        return pltpu.make_async_remote_copy(
            src_ref=staged[number],
            dst_ref=wholes[number].at[(source,) + half(number, core)],
            send_sem=out_send.at[number],
            recv_sem=out_recv.at[number, source],
            device_id={"dp": owners[number], "mp": core},
            device_id_type=MESH_ID,
        )

    def deliver_here(number):
        return pltpu.make_async_copy(
            staged[number], wholes[number].at[(me,) + half(number, core)], own_sem
        )

    def cross(number, source, which):
        region = wholes[number].at[(source,) + half(number, which)]
        return pltpu.make_async_remote_copy(
            src_ref=region,
            dst_ref=region,
            send_sem=cross_send.at[number, source],
            recv_sem=cross_recv.at[number, source],
            device_id={"dp": me, "mp": 1 - core},
            device_id_type=MESH_ID,
        )

    def kept_spot(order, found):
        return tuple(found.get(bit, own[bit]) for bit in range(levels - 1, -1, -1) if bit != order[0])

    def fold(piece, stage):
        order, number = orders[piece], pieces[piece][0]
        free = order[stage:]
        loose = [bit for bit in range(levels - 1, -1, -1) if bit in free and bit != order[stage]]
        region = cut(piece)

        @pl.loop(0, 2 ** len(loose))
        def add_block(block):
            found = {
                bit: lax.rem(lax.div(block, 2 ** (len(loose) - 1 - i)), 2) for i, bit in enumerate(loose)
            }

            def total(way):
                now = dict(found)
                now[order[stage]] = way
                full = tuple(now.get(bit, own[bit]) for bit in range(levels - 1, -1, -1)) + region
                if stage == 0:
                    value = mine[number][full].astype(jnp.float32) + theirs[number][full].astype(jnp.float32)
                else:
                    land = tuple(now[bit] for bit in range(levels - 1, -1, -1) if bit in free)
                    arrived = landing[piece * levels + stage - 1][land].astype(jnp.float32)
                    value = kept[number][kept_spot(order, now) + region] + arrived
                return full, value

            full, value = total(1 - own[order[stage]])
            theirs[number][full] = value.astype(theirs[number].dtype)
            full, value = total(own[order[stage]])
            kept[number][kept_spot(order, found) + region] = value

    for piece in REDUCE_FIRST:
        pair(piece).start()
        load(piece).start()
    for piece in REDUCE_FIRST:
        load(piece).wait()
        pair(piece).wait_recv()
        fold(piece, 0)
        hop(piece, 0).start()
    squares = jnp.zeros((8, 128), jnp.float32)
    for piece, stage in [(piece, stage) for stage in range(levels) for piece in REDUCE_STEPS[stage]]:
        hop(piece, stage).wait_recv()
        if stage + 1 < levels:
            fold(piece, stage + 1)
            hop(piece, stage + 1).start()
        else:
            number = pieces[piece][0]
            arrived = landing[piece * levels + stage][...].astype(jnp.float32)
            total = kept[number][kept_spot(orders[piece], {}) + cut(piece)] + arrived
            sums[number][side(piece, core)] = total
            rows, width = total.shape
            for row in range(0, rows, 8):
                for column in range(0, width, 128):
                    part = total[row : row + 8, column : column + 128]
                    squares = squares + part * part
    for number in range(blocks, count):
        share(number, core).start()
    row = lax.broadcasted_iota(jnp.int32, (8, 128), 0)
    stats_out[...] = jnp.where(row == 0, jnp.sum(squares, axis=0, keepdims=True), stats_in[...])
    add_up(me, core, devices, stats_out, stats_land, stats_send, stats_recv, own_sem)
    norm = jnp.sqrt(jnp.sum(stats_out[0:1, :], axis=1, keepdims=True))
    factor = jnp.minimum(1.0, CLIP_MAX / (norm + 1e-06))
    for number in range(blocks):
        region = half(number, core)
        renewed = 0.5 * old[number][region] + factor * sums[number][region]
        sums[number][region] = renewed
        staged[number][...] = renewed.astype(staged[number].dtype)
        share(number, core).start()

        @pl.when(me != owners[number])
        def start_one(number=number):
            deliver(number, me).start()

        @pl.when(me == owners[number])
        def start_here(number=number):
            deliver_here(number).start()

    for piece in range(len(pieces)):
        pair(piece).wait_send()
        for stage in range(levels):
            hop(piece, stage).wait_send()
    for number in range(blocks):

        @pl.when(me == owners[number])
        def collect(number=number):
            deliver_here(number).wait()

            @pl.loop(0, devices)
            def forward(source):
                @pl.when(source != me)
                def arrived():
                    deliver(number, source).wait_recv()

                cross(number, source, core).start()

            @pl.loop(0, devices)
            def finish(source):
                cross(number, source, core).wait_send()
                cross(number, source, 1 - core).wait_recv()

        @pl.when(me != owners[number])
        def end_one(number=number):
            deliver(number, me).wait_send()

    for number in range(count):
        share(number, core).wait_send()
        share(number, 1 - core).wait_recv()


def reduce_rows(grads, stats, old, owners, devices):
    levels, count, blocks = bit_count(devices), len(grads), len(old)
    lead = (2,) * levels
    dma = pltpu.SemaphoreType.DMA
    shapes = [grad.shape[levels:] for grad in grads]
    halves = [(rows, columns // 2) for rows, columns in shapes]
    kinds = [grad.dtype for grad in grads]
    pieces = cut_pieces(REDUCE_PARTS, halves)
    scratch = [pltpu.VMEM(lead + shape, kind) for shape, kind in zip(halves, kinds)] * 2
    scratch += [pltpu.VMEM(lead[1:] + shape, jnp.float32) for shape in halves]
    for number, row, rows, column, columns in pieces:
        for stage in range(levels):
            scratch.append(pltpu.VMEM((2,) * (levels - 1 - stage) + (rows, columns), kinds[number]))
    scratch += [pltpu.VMEM(halves[number], kinds[number]) for number in range(blocks)]
    scratch.append(pltpu.VMEM((devices + 1, 8, 128), jnp.float32))
    scratch += [dma((len(pieces),))] * 3 + [dma((len(pieces), levels))] * 2 + [dma((count,))] * 2
    scratch += [dma((devices + 1,))] * 2 + [dma, dma((blocks,))] + [dma((blocks, devices))] * 3
    vmem, anywhere = pl.BlockSpec(memory_space=pltpu.VMEM), pl.BlockSpec(memory_space=pl.ANY)
    found = pl.pallas_call(
        functools.partial(reduce_kernel, levels, pieces, count, owners, devices),
        out_shape=[jax.ShapeDtypeStruct(shape, jnp.float32) for shape in shapes]
        + [jax.ShapeDtypeStruct((8, 128), jnp.float32)]
        + [jax.ShapeDtypeStruct((devices,) + shapes[number], kinds[number]) for number in range(blocks)],
        in_specs=[anywhere] * count + [vmem] * (1 + blocks),
        out_specs=[vmem] * (count + 1) + [anywhere] * blocks,
        scratch_shapes=scratch,
        compiler_params=pltpu.CompilerParams(
            collective_id=2, has_side_effects=True, vmem_limit_bytes=60 * 2**20
        ),
        name="reduce_rows",
    )(*grads, stats, *old)
    return found[:blocks], found[blocks:count], found[count], found[count + 1 :]


def return_kernel(owners, count, devices, *refs):
    wholes, rows = refs[:count], refs[count : 2 * count]
    here_sem, send_sem, recv_sem, cross_send, cross_recv = refs[2 * count :]
    me, core = lax.axis_index("dp"), lax.axis_index("mp")
    barrier = pltpu.get_barrier_semaphore()
    owning = functools.reduce(jnp.logical_or, [me == owner for owner in owners])
    for owner in owners:

        @pl.when(me != owner)
        def greet_owner(owner=owner):
            pl.semaphore_signal(
                barrier, inc=1, device_id={"dp": owner, "mp": core}, device_id_type=MESH_ID
            )

    pl.semaphore_signal(barrier, inc=1, device_id={"dp": me, "mp": 1 - core}, device_id_type=MESH_ID)

    @pl.when(owning)
    def wait_all():
        pl.semaphore_wait(barrier, devices)

    @pl.when(jnp.logical_not(owning))
    def wait_pair():
        pl.semaphore_wait(barrier, 1)

    def half(number, which):
        width = rows[number].shape[1] // 2
        return (slice(None), pl.ds(pl.multiple_of(which * width, 128), width))

    def hop(number, target):
        return pltpu.make_async_remote_copy(
            src_ref=wholes[number].at[(target,) + half(number, core)],
            dst_ref=rows[number].at[half(number, core)],
            send_sem=send_sem.at[number, target],
            recv_sem=recv_sem.at[number],
            device_id={"dp": target, "mp": core},
            device_id_type=MESH_ID,
        )

    def cross(number, which):
        region = rows[number].at[half(number, which)]
        return pltpu.make_async_remote_copy(
            src_ref=region,
            dst_ref=region,
            send_sem=cross_send.at[number],
            recv_sem=cross_recv.at[number],
            device_id={"dp": me, "mp": 1 - core},
            device_id_type=MESH_ID,
        )

    for number in range(count):

        @pl.when(me == owners[number])
        def hand_out(number=number):
            own = pltpu.make_async_copy(
                wholes[number].at[(me,) + half(number, core)], rows[number].at[half(number, core)], here_sem
            )
            own.start()

            @pl.loop(0, devices)
            def start_one(target):
                @pl.when(target != me)
                def start_other():
                    hop(number, target).start()

            own.wait()

    for number in range(count):

        @pl.when(me != owners[number])
        def arrive(number=number):
            hop(number, me).wait_recv()

        cross(number, core).start()
    for number in range(count):
        cross(number, core).wait_send()
        cross(number, 1 - core).wait_recv()

        @pl.when(me == owners[number])
        def end_out(number=number):
            @pl.loop(0, devices)
            def end_one(target):
                @pl.when(target != me)
                def end_other():
                    hop(number, target).wait_send()


def return_rows(wholes, owners, devices):
    count = len(wholes)
    dma = pltpu.SemaphoreType.DMA
    vmem = pl.BlockSpec(memory_space=pltpu.VMEM)
    return pl.pallas_call(
        functools.partial(return_kernel, owners, count, devices),
        out_shape=[jax.ShapeDtypeStruct(whole.shape[1:], whole.dtype) for whole in wholes],
        in_specs=[pl.BlockSpec(memory_space=pl.ANY)] * count,
        out_specs=[vmem] * count,
        scratch_shapes=[dma, dma((count, devices)), dma((count,)), dma((count,)), dma((count,))],
        compiler_params=pltpu.CompilerParams(
            collective_id=4, has_side_effects=True, vmem_limit_bytes=60 * 2**20
        ),
        name="return_rows",
    )(*wholes)


def finish_kernel(count, rates, *refs):
    rows, masters, updated = refs[:count], refs[count : 2 * count], refs[2 * count :]
    for number in range(count):
        change = rates[number] * rows[number][...].astype(jnp.float32)
        updated[number][...] = masters[number][...] * (1.0 - LR_MUON * DECAY) - change


def finish(rows, masters, devices):
    count = len(rows)
    rates = []
    for master in masters:
        rates.append(LR_MUON * 0.2 * math.sqrt(max(master.shape[0] * devices, master.shape[1])))
    vmem = pl.BlockSpec(memory_space=pltpu.VMEM)
    return pl.pallas_call(
        functools.partial(finish_kernel, count, rates),
        out_shape=[jax.ShapeDtypeStruct(master.shape, jnp.float32) for master in masters],
        in_specs=[vmem] * (2 * count),
        out_specs=[vmem] * count,
        compiler_params=pltpu.CompilerParams(vmem_limit_bytes=56 * 2**20),
        name="finish",
    )(*rows, *masters)


def muon_kernel(owners, shapes, *refs):
    count = len(owners)
    mats, moved, stats, adam_in = refs[:count], refs[count : 2 * count], refs[2 * count], refs[2 * count + 1 :][:8]
    rest = refs[2 * count + 9 :]
    outs, moved_out, adam_out, rest = rest[:count], rest[count : 2 * count], rest[2 * count :][:6], rest[2 * count + 6 :]
    exact, wide, wide_low, tall, wide_out, tall_out, gram = rest[:7]
    base, poly, other, chain, sem, in_sem, out_sem = rest[7:14]
    held_rows = rest[14:]

    def move_in(number):
        return pltpu.make_async_copy(moved[number], held_rows[number], in_sem.at[number])

    def move_out(number):
        return pltpu.make_async_copy(held_rows[number], moved_out[number], out_sem.at[number])

    for number in range(count):
        move_in(number).start()
    norm = jnp.sqrt(jnp.sum(stats[0:1, :], axis=1, keepdims=True))
    factor = jnp.minimum(1.0, CLIP_MAX / (norm + 1e-06))
    for group in range(2):
        weight, first, second, grad = [ref[...] for ref in adam_in[4 * group : 4 * group + 4]]
        made = adam_update(weight, first, second, grad * factor, DECAY)
        for place_out in range(3):
            adam_out[3 * group + place_out][...] = made[place_out]
    me, core = lax.axis_index("dp"), lax.axis_index("mp")
    side = gram.shape[0]
    step = 256
    bf = jnp.bfloat16

    def dims(number):
        height, breadth = shapes[number]
        return height, breadth, LONG_COLS[number]

    def span(index):
        return pl.ds(pl.multiple_of(index * step, step), step)

    def split(value):
        high = value.astype(bf)
        return high, (value - high.astype(jnp.float32)).astype(bf)

    gram[...] = jnp.zeros_like(gram)
    for number in range(count):

        @pl.when(me == owners[number])
        def start(number=number):
            height, breadth, long_cols = dims(number)
            short = min(height, breadth)
            held = (wide if long_cols else tall).at[:height, :breadth]
            fine = mats[number].dtype == jnp.float32
            load = pltpu.make_async_copy(mats[number], exact if fine else held, sem)
            load.start()
            load.wait()
            if fine:
                rest = wide_low

                @pl.loop(0, height // step)
                def part_rows(index):
                    high, low = split(exact[span(index), :])
                    held[span(index), :] = high
                    rest[span(index), :] = low

            for index in range(short // step):
                first, beyond = slice(index * step, (index + 1) * step), slice(index * step, short)
                if long_cols:
                    total = dot_rows(held[first, :], held[beyond, :])
                    if fine:
                        total = total + dot_rows(held[first, :], rest[beyond, :])
                        total = total + dot_rows(rest[first, :], held[beyond, :])
                else:
                    total = dot_columns(held[:, first], held[:, beyond])
                gram[first, beyond] = total

    for number in range(count):
        move_in(number).wait()
        move_out(number).start()
    owning = functools.reduce(jnp.logical_or, [me == owner for owner in owners])

    @pl.when(owning)
    def iterate():
        parts = [
            (slice(index * step, (index + 1) * step), slice(index * step, side))
            for index in range(side // step)
        ]
        ones = lax.broadcasted_iota(jnp.int32, (step, step), 0) == lax.broadcasted_iota(
            jnp.int32, (step, step), 1
        )
        trace = jnp.float32(0.0)
        for first, beyond in parts:
            trace = trace + jnp.sum(jnp.where(ones, gram[first, first], 0.0))
        scale = 1.0 / (jnp.sqrt(jnp.full((8, 128), trace, jnp.float32)) + 1e-07)
        scale = scale[0:1, 0:1]

        def store(target, index, value):
            high, low = split(value)
            target[0, parts[index][0], parts[index][1]] = high
            target[1, parts[index][0], parts[index][1]] = low
            for later in range(index + 1, side // step):
                shift = (later - index) * step
                high, low = split(value[:, shift : shift + step].T)
                target[0, parts[later][0], parts[index][0]] = high
                target[1, parts[later][0], parts[index][0]] = low

        def product(left, right, index):
            first, beyond = parts[index]
            high, low = left[0, first, :], left[1, first, :]
            total = jnp.dot(high, right[0, :, beyond], preferred_element_type=jnp.float32)
            total = total + jnp.dot(high, right[1, :, beyond], preferred_element_type=jnp.float32)
            return total + jnp.dot(low, right[0, :, beyond], preferred_element_type=jnp.float32)

        for index, (first, beyond) in enumerate(parts):
            store(base, index, gram[first, beyond] * (scale * scale))

        @pl.loop(0, NS_ITERS)
        def newton(iteration):
            for index, (first, beyond) in enumerate(parts):
                now = base[0, first, beyond].astype(jnp.float32) + base[1, first, beyond].astype(jnp.float32)
                row = lax.broadcasted_iota(jnp.int32, now.shape, 0)
                column = lax.broadcasted_iota(jnp.int32, now.shape, 1)
                value = jnp.where(row == column, NS_A, 0.0) + NS_B * now
                store(poly, index, value + NS_C * product(base, base, index))

            @pl.when(iteration < NS_ITERS - 1)
            def advance():
                for index in range(len(parts)):
                    store(other, index, product(base, poly, index))
                for index in range(len(parts)):
                    store(base, index, product(other, poly, index))

            @pl.when(iteration == 0)
            def begin():
                chain[...] = poly[...]

            @pl.when(iteration > 0)
            def follow():
                for index in range(len(parts)):
                    store(other, index, product(chain, poly, index))
                chain[...] = other[...]

        for first, beyond in parts:
            value = chain[0, first, :].astype(jnp.float32) + chain[1, first, :].astype(jnp.float32)
            high, low = split(value * scale)
            other[0, first, :] = high
            other[1, first, :] = low

    for number in range(count):

        @pl.when(me == owners[number])
        def end(number=number):
            height, breadth, long_cols = dims(number)
            short = min(height, breadth)
            width = breadth // 2
            part = pl.ds(pl.multiple_of(core * width, 128), width)
            if long_cols:
                held, made = wide.at[:height, :breadth], wide_out.at[:height, :width]

                @pl.loop(0, height // step)
                def wide_rows(index):
                    total = jnp.dot(
                        other[0, span(index), :short], held[:, part], preferred_element_type=jnp.float32
                    ) + jnp.dot(
                        other[1, span(index), :short], held[:, part], preferred_element_type=jnp.float32
                    )
                    if mats[number].dtype == jnp.float32:
                        total = total + jnp.dot(
                            other[0, span(index), :short],
                            wide_low[:, part],
                            preferred_element_type=jnp.float32,
                        )
                    made[span(index), :] = total.astype(bf)
            else:
                held, made = tall.at[:height, :breadth], tall_out.at[:height, :width]

                @pl.loop(0, height // step)
                def tall_rows(index):
                    total = jnp.dot(
                        held[span(index), :], other[0, :short, part], preferred_element_type=jnp.float32
                    ) + jnp.dot(
                        held[span(index), :], other[1, :short, part], preferred_element_type=jnp.float32
                    )
                    made[span(index), :] = total.astype(bf)

            save = pltpu.make_async_copy(made, outs[number].at[:, part], sem)
            save.start()
            save.wait()

    for number in range(count):
        move_out(number).wait()


def orthogonalize(mats, moved, stats, adam, owners):
    count = len(mats)
    shapes = [mat.shape for mat in mats]
    side = max(min(shape) for shape in shapes)
    longest = max(max(shape) for shape in shapes)
    double = pltpu.VMEM((2, side, side), jnp.bfloat16)
    (fine,) = [mat.shape for mat in mats if mat.dtype == jnp.float32]
    vmem, anywhere = pl.BlockSpec(memory_space=pltpu.VMEM), pl.BlockSpec(memory_space=pl.ANY)
    renewed = (adam[0], adam[1], adam[2], adam[4], adam[5], adam[6])
    found = pl.pallas_call(
        functools.partial(muon_kernel, owners, shapes),
        out_shape=[jax.ShapeDtypeStruct(shape, jnp.bfloat16) for shape in shapes]
        + [jax.ShapeDtypeStruct(piece.shape, piece.dtype) for piece in moved]
        + [jax.ShapeDtypeStruct(piece.shape, piece.dtype) for piece in renewed],
        in_specs=[anywhere] * (2 * count) + [vmem] * 9,
        out_specs=[anywhere] * (2 * count) + [vmem] * 6,
        scratch_shapes=[
            pltpu.VMEM(fine, jnp.float32),
            pltpu.VMEM((side, longest), jnp.bfloat16),
            pltpu.VMEM(fine, jnp.bfloat16),
            pltpu.VMEM((longest, side), jnp.bfloat16),
            pltpu.VMEM((side, longest // 2), jnp.bfloat16),
            pltpu.VMEM((longest, side // 2), jnp.bfloat16),
            pltpu.VMEM((side, side), jnp.float32),
            double,
            double,
            double,
            double,
            pltpu.SemaphoreType.DMA,
            pltpu.SemaphoreType.DMA((count,)),
            pltpu.SemaphoreType.DMA((count,)),
        ]
        + [pltpu.VMEM(piece.shape, piece.dtype) for piece in moved],
        compiler_params=pltpu.CompilerParams(vmem_limit_bytes=60 * 2**20),
        name="orthogonalize",
    )(*mats, *moved, stats, *adam)
    return found[:count], found[count : 2 * count], found[2 * count : 2 * count + 3], found[2 * count + 3 :]


def window_place(position):
    time_row = (position // GF + GT - SHIFT) % GT
    freq_col = (position % GF + GF - SHIFT) % GF
    window = (time_row // WIN) * (GF // WIN) + freq_col // WIN
    return window * (WIN * WIN) + (time_row % WIN) * WIN + freq_col % WIN


def window_sinusoid(channels):
    quarter = channels // 4
    frequency = 1.0 / 10000.0 ** (np.arange(quarter) / quarter)
    position = np.arange(NPATCH)
    time_rows = (position // GF)[:, None] * frequency
    freq_cols = (position % GF)[:, None] * frequency
    table = np.concatenate([np.sin(time_rows), np.cos(time_rows), np.sin(freq_cols), np.cos(freq_cols)], axis=1)
    moved = np.zeros_like(table)
    moved[window_place(position)] = table
    return moved.astype(np.float32)


def window_scene(spec, keep):
    position = np.arange(NPATCH)
    row = np.empty(NPATCH, np.int32)
    row[window_place(position)] = position
    take = (row[:, None] // GF == np.arange(GT)[None, :]).astype(np.float32)
    source = np.arange(PS * GF * PS)[:, None]
    target = np.arange(PATCH)[None, :]
    fold = np.logical_and(source // (GF * PS) == target // PS, source % PS == target % PS)
    table = window_sinusoid(D)
    high = table.astype(jnp.bfloat16)
    low = (table - high.astype(np.float32)).astype(jnp.bfloat16)
    return (
        spec.reshape(spec.shape[0], GT, PS * GF * PS),
        window_place(jnp.pad(keep, ((0, 0), (0, SLOTS - VIS))))[:, :, None],
        jnp.asarray(take, jnp.bfloat16),
        jnp.asarray(row[:, None] % GF),
        jnp.asarray(fold, jnp.bfloat16),
        jnp.asarray(np.concatenate([high, low], axis=1)),
    )


@jax.custom_vjp
def times(inputs, matrix):
    return jnp.dot(inputs.astype(jnp.bfloat16), matrix.astype(jnp.bfloat16), preferred_element_type=jnp.float32)


def times_keep(inputs, matrix):
    short = inputs.astype(jnp.bfloat16)
    return jnp.dot(short, matrix.astype(jnp.bfloat16), preferred_element_type=jnp.float32), (short, matrix)


def times_back(kept, grad):
    short, matrix = kept
    grad = grad.astype(jnp.bfloat16)
    back = lax.dot_general(
        grad, matrix.astype(jnp.bfloat16), (((1,), (1,)), ((), ())), preferred_element_type=jnp.float32
    )
    gain = lax.dot_general(short, grad, (((0,), (0,)), ((), ())), preferred_element_type=jnp.float32)
    return back, gain.astype(matrix.dtype)


times.defvjp(times_keep, times_back)


def dot_rows(left, right):
    return lax.dot_general(left, right, (((1,), (1,)), ((), ())), preferred_element_type=jnp.float32)


def dot_columns(left, right):
    return lax.dot_general(left, right, (((0,), (0,)), ((), ())), preferred_element_type=jnp.float32)


def head_lanes(value, head, size):
    lane = lax.broadcasted_iota(jnp.int32, value.shape, 1)
    return jnp.where(lane // size == head, value, jnp.zeros_like(value))


def soft_keys(queries, keys_here, allow, size):
    rows = queries.shape[0]
    scores = dot_rows(keys_here, queries).reshape(128 // size, rows, rows)
    scores = jnp.where(allow, scores * size ** (-0.5), -1e30)
    exponent = jnp.exp(scores - jnp.max(scores, axis=1, keepdims=True))
    return exponent / jnp.sum(exponent, axis=1, keepdims=True)


def flat_heads(value):
    return value.astype(jnp.bfloat16).reshape(-1, value.shape[2])


def attention_kernel(size, joined, allowed, out):
    width = out.shape[1]
    allow = allowed[...][None] > 0.0
    for lane in range(0, width, 128):
        queries = joined[:, lane : lane + 128]
        keys_here = stack_heads(joined[:, width + lane : width + lane + 128], size)
        values_here = stack_heads(joined[:, 2 * width + lane : 2 * width + lane + 128], size)
        soft = flat_heads(soft_keys(queries, keys_here, allow, size))
        out[:, lane : lane + 128] = dot_columns(soft, values_here).astype(jnp.bfloat16)


def attention_back_kernel(size, joined, allowed, grad, out, query_sum, value_sum):
    width, rows = grad.shape[1], grad.shape[0]
    allow = allowed[...][None] > 0.0

    @pl.when(pl.program_id(0) == 0)
    def clear():
        query_sum[...] = jnp.zeros_like(query_sum)
        value_sum[...] = jnp.zeros_like(value_sum)

    for lane in range(0, width, 128):
        queries = joined[:, lane : lane + 128]
        keys_here = stack_heads(joined[:, width + lane : width + lane + 128], size)
        values_here = stack_heads(joined[:, 2 * width + lane : 2 * width + lane + 128], size)
        pull = grad[:, lane : lane + 128]
        soft = soft_keys(queries, keys_here, allow, size)
        soft_grad = dot_rows(values_here, pull).reshape(128 // size, rows, rows)
        score_grad = soft * (soft_grad - jnp.sum(soft * soft_grad, axis=1, keepdims=True))
        score_grad = flat_heads(score_grad * size ** (-0.5))
        soft = flat_heads(soft)
        query_grad = dot_columns(score_grad, keys_here)
        key_grad = unstack_heads(jnp.dot(score_grad, queries, preferred_element_type=jnp.float32), size)
        value_grad = unstack_heads(jnp.dot(soft, pull, preferred_element_type=jnp.float32), size)
        out[:, lane : lane + 128] = query_grad.astype(jnp.bfloat16)
        out[:, width + lane : width + lane + 128] = key_grad.astype(jnp.bfloat16)
        out[:, 2 * width + lane : 2 * width + lane + 128] = value_grad.astype(jnp.bfloat16)
        query_sum[0:1, lane : lane + 128] += jnp.sum(query_grad, axis=0, keepdims=True)
        value_sum[0:1, lane : lane + 128] += jnp.sum(value_grad, axis=0, keepdims=True)


def window_fold(value, heads):
    lane = lax.broadcasted_iota(jnp.int32, (1, 1, value.shape[1]), 2) // (WIN * WIN)
    value = value.reshape(heads, 8, WIN * WIN, value.shape[1])
    found = value[:, 0]
    for window in range(1, 8):
        found = jnp.where(lane == window, value[:, window], found)
    return found


def window_spread(value):
    heads = value.shape[0]
    short = value.astype(jnp.bfloat16)
    lane = lax.broadcasted_iota(jnp.int32, short.shape, 2) // (WIN * WIN)
    parts = []
    for head in range(heads):
        for window in range(8):
            parts.append(
                jnp.where(lane[head] == window, short[head], jnp.zeros_like(short[head]))
            )
    return jnp.concatenate(parts, axis=0)


def stack_heads(value, size):
    per = value.shape[1] // size
    return jnp.concatenate([head_lanes(value, head, size) for head in range(per)], axis=0)


def unstack_heads(value, size):
    per = value.shape[1] // size
    rows = value.shape[0] // per
    lane = lax.broadcasted_iota(jnp.int32, (rows, value.shape[1]), 1) // size
    found = value[:rows]
    for head in range(1, per):
        found = jnp.where(lane == head, value[head * rows : (head + 1) * rows], found)
    return found


def soft_fold(queries, keys_here, allow, size):
    scores = window_fold(dot_rows(keys_here, queries), 128 // size)
    scores = jnp.where(allow, scores * size ** (-0.5), -1e30)
    exponent = jnp.exp(scores - jnp.max(scores, axis=1, keepdims=True))
    return exponent / jnp.sum(exponent, axis=1, keepdims=True)


def window_kernel(size, joined, allowed, out):
    width = out.shape[1]
    allow = allowed[...][None] > 0.0
    for lane in range(0, width, 128):
        queries = joined[:, lane : lane + 128]
        keys_here = stack_heads(joined[:, width + lane : width + lane + 128], size)
        values_here = stack_heads(joined[:, 2 * width + lane : 2 * width + lane + 128], size)
        soft = window_spread(soft_fold(queries, keys_here, allow, size))
        out[:, lane : lane + 128] = dot_columns(soft, values_here).astype(jnp.bfloat16)


def window_back_kernel(size, joined, allowed, grad, out, query_sum, value_sum):
    width = grad.shape[1]
    allow = allowed[...][None] > 0.0

    @pl.when(pl.program_id(0) == 0)
    def clear():
        query_sum[...] = jnp.zeros_like(query_sum)
        value_sum[...] = jnp.zeros_like(value_sum)

    for lane in range(0, width, 128):
        queries = joined[:, lane : lane + 128]
        keys_here = stack_heads(joined[:, width + lane : width + lane + 128], size)
        values_here = stack_heads(joined[:, 2 * width + lane : 2 * width + lane + 128], size)
        pull = grad[:, lane : lane + 128]
        soft = soft_fold(queries, keys_here, allow, size)
        soft_grad = window_fold(dot_rows(values_here, pull), 128 // size)
        score_grad = soft * (soft_grad - jnp.sum(soft * soft_grad, axis=1, keepdims=True))
        score_grad = window_spread(score_grad * size ** (-0.5))
        soft = window_spread(soft)
        query_grad = dot_columns(score_grad, keys_here)
        key_grad = unstack_heads(jnp.dot(score_grad, queries, preferred_element_type=jnp.float32), size)
        value_grad = unstack_heads(jnp.dot(soft, pull, preferred_element_type=jnp.float32), size)
        out[:, lane : lane + 128] = query_grad.astype(jnp.bfloat16)
        out[:, width + lane : width + lane + 128] = key_grad.astype(jnp.bfloat16)
        out[:, 2 * width + lane : 2 * width + lane + 128] = value_grad.astype(jnp.bfloat16)
        query_sum[0:1, lane : lane + 128] += jnp.sum(query_grad, axis=0, keepdims=True)
        value_sum[0:1, lane : lane + 128] += jnp.sum(value_grad, axis=0, keepdims=True)


def attention_parts(joined, allowed, rows):
    steps = joined.shape[0] // rows
    period = allowed.shape[0]
    wide = pl.BlockSpec((rows, joined.shape[1]), lambda step: (step, 0))
    mask = pl.BlockSpec((None,) + allowed.shape[1:], lambda step: (lax.rem(step, period), 0, 0))
    narrow_rows = pl.BlockSpec((rows, joined.shape[1] // 3), lambda step: (step, 0))
    return steps, wide, mask, narrow_rows


def attention_forward(kernel, joined, allowed, rows, size):
    steps, wide, mask, part = attention_parts(joined, allowed, rows)
    return pl.pallas_call(
        functools.partial(kernel, size),
        grid=(steps,),
        out_shape=jax.ShapeDtypeStruct((joined.shape[0], joined.shape[1] // 3), jnp.bfloat16),
        in_specs=[wide, mask],
        out_specs=part,
        compiler_params=pltpu.CompilerParams(vmem_limit_bytes=40 * 2**20),
        name="attention_forward",
    )(joined, allowed)


def attention_backward(kernel, joined, allowed, grad, rows, size):
    steps, wide, mask, part = attention_parts(joined, allowed, rows)
    width = joined.shape[1] // 3
    total = pl.BlockSpec((8, width), lambda step: (0, 0))
    return pl.pallas_call(
        functools.partial(kernel, size),
        grid=(steps,),
        out_shape=[
            jax.ShapeDtypeStruct(joined.shape, jnp.bfloat16),
            jax.ShapeDtypeStruct((8, width), jnp.float32),
            jax.ShapeDtypeStruct((8, width), jnp.float32),
        ],
        in_specs=[wide, mask, part],
        out_specs=[wide, total, total],
        compiler_params=pltpu.CompilerParams(vmem_limit_bytes=40 * 2**20),
        name="attention_backward",
    )(joined, allowed, grad)


def attention_block(forward, backward, rows, size):
    def join(normed, matrix, query_bias, value_bias):
        width = matrix.shape[1] // 3
        bias = jnp.concatenate([query_bias, jnp.zeros((width,), jnp.float32), value_bias])
        joined = jnp.dot(normed, matrix.astype(jnp.bfloat16), preferred_element_type=jnp.float32)
        return (joined + bias).astype(jnp.bfloat16)

    @jax.custom_vjp
    def apply(normed, matrix, query_bias, value_bias, allowed):
        joined = join(normed.astype(jnp.bfloat16), matrix, query_bias, value_bias)
        return attention_forward(forward, joined, allowed, rows, size).astype(jnp.float32)

    def keep(normed, matrix, query_bias, value_bias, allowed):
        short = normed.astype(jnp.bfloat16)
        joined = join(short, matrix, query_bias, value_bias)
        made = attention_forward(forward, joined, allowed, rows, size).astype(jnp.float32)
        return made, (short, matrix, joined, allowed)

    def back(kept, grad):
        short, matrix, joined, allowed = kept
        pulled, query_sum, value_sum = attention_backward(
            backward, joined, allowed, grad.astype(jnp.bfloat16), rows, size
        )
        normed_grad = dot_rows(pulled, matrix.astype(jnp.bfloat16))
        matrix_grad = dot_columns(short, pulled).astype(matrix.dtype)
        return normed_grad, matrix_grad, query_sum[0], value_sum[0], jnp.zeros_like(allowed)

    apply.defvjp(keep, back)
    return apply


encoder_attention = attention_block(attention_kernel, attention_back_kernel, SLOTS, HEAD)
decoder_attention = attention_block(window_kernel, window_back_kernel, 8 * WIN * WIN, DHEAD)


def gelu_keep(value):
    portion = 0.5 + 0.5 * lax.erf(value * math.sqrt(0.5))
    slope = portion + value * jnp.exp(-0.5 * value * value) * (1.0 / math.sqrt(2.0 * math.pi))
    return value * portion, slope


def hidden_back_kernel(normed, inner, slope, grad, up, down, normed_grad, up_grad, down_grad, bias_grad):
    @pl.when(pl.program_id(0) == 0)
    def clear():
        normed_grad[...] = jnp.zeros_like(normed_grad)

    inner_grad = dot_rows(grad[...], down[...]) * slope[...]
    bias_grad[0:1, :] = jnp.sum(inner_grad, axis=0, keepdims=True)
    short = inner_grad.astype(jnp.bfloat16)
    down_grad[...] = dot_columns(inner[...], grad[...]).astype(jnp.bfloat16)
    up_grad[...] = dot_columns(normed[...], short).astype(jnp.bfloat16)
    normed_grad[...] += dot_rows(short, up[...])


def hidden_backward(normed, inner, slope, grad, up, down):
    (tokens, width), units = normed.shape, inner.shape[1]
    tile = 512
    whole = pl.BlockSpec((tokens, width), lambda step: (0, 0))
    columns = pl.BlockSpec((tokens, tile), lambda step: (0, step))
    up_tile = pl.BlockSpec((width, tile), lambda step: (0, step))
    down_tile = pl.BlockSpec((tile, width), lambda step: (step, 0))
    return pl.pallas_call(
        hidden_back_kernel,
        grid=(units // tile,),
        out_shape=[
            jax.ShapeDtypeStruct((tokens, width), jnp.float32),
            jax.ShapeDtypeStruct((width, units), jnp.bfloat16),
            jax.ShapeDtypeStruct((units, width), jnp.bfloat16),
            jax.ShapeDtypeStruct((8, units), jnp.float32),
        ],
        in_specs=[whole, columns, columns, whole, up_tile, down_tile],
        out_specs=[whole, up_tile, down_tile, pl.BlockSpec((8, tile), lambda step: (0, step))],
        compiler_params=pltpu.CompilerParams(vmem_limit_bytes=40 * 2**20),
        name="hidden_backward",
    )(normed, inner, slope, grad, up, down)


@jax.custom_vjp
def hidden_layer(normed, up, bias, down):
    return hidden_keep(normed, up, bias, down)[0]


def hidden_keep(normed, up, bias, down):
    short = normed.astype(jnp.bfloat16)
    value, slope = gelu_keep(jnp.dot(short, up, preferred_element_type=jnp.float32) + bias)
    inner = value.astype(jnp.bfloat16)
    return jnp.dot(inner, down, preferred_element_type=jnp.float32), (short, inner, slope, up, down)


def hidden_back(kept, grad):
    short, inner, slope, up, down = kept
    found = hidden_backward(short, inner, slope, grad.astype(jnp.bfloat16), up, down)
    normed_grad, up_grad, down_grad, bias_grad = found
    return normed_grad, up_grad, bias_grad[0], down_grad


hidden_layer.defvjp(hidden_keep, hidden_back)


def window_allowed():
    position = np.arange(NPATCH)
    window, inner = position // (WIN * WIN), position % (WIN * WIN)
    time_row = window // (GF // WIN) * WIN + inner // WIN
    freq_col = window % (GF // WIN) * WIN + inner % WIN
    region = (time_row >= GT - WIN).astype(np.int32) + (time_row >= GT - SHIFT)
    region = region * 3 + (freq_col >= GF - WIN) + (freq_col >= GF - SHIFT)
    region = region.reshape(-1, 8, 1, WIN * WIN)
    same = region == region.transpose(0, 1, 3, 2)
    return same.transpose(0, 2, 1, 3).reshape(-1, WIN * WIN, 8 * WIN * WIN).astype(np.float32)


def local_loss(weights, picked, where, target, keep, counts):
    clips = picked.shape[0]
    pieces = unpack(weights[10])
    spot = window_place(jnp.pad(keep, ((0, 0), (0, SLOTS - VIS))))
    shown = (spot[:, :, None] == jnp.arange(NPATCH)[None, None, :]).astype(jnp.float32)
    shown = shown * (jnp.arange(SLOTS)[None, :] < counts[:, None])[:, :, None]
    hidden = times(picked.reshape(-1, PATCH), weights[8][:, :D]) + pieces[11] + where.reshape(-1, D)
    normed = layer_norm(hidden, pieces[0], pieces[1])
    visible = (jnp.arange(SLOTS)[None, :] < counts[:, None]).astype(jnp.float32)
    visible = jnp.broadcast_to(visible[:, :, None], (clips, SLOTS, SLOTS))
    attended = encoder_attention(normed, weights[0], pieces[2], pieces[3], visible)
    hidden = hidden + times(attended, weights[1]) + pieces[4]
    normed = layer_norm(hidden, pieces[5], pieces[6])
    hidden = hidden + hidden_layer(normed, weights[2], pieces[7], weights[3]) + pieces[8]
    latent = layer_norm(hidden, pieces[9], pieces[10])

    pieces = pieces[12:]
    placed = times(latent, weights[9]) + pieces[0]
    filled = jnp.einsum("cjp,cjd->cpd", shown, placed.reshape(clips, SLOTS, DD), precision=HIGH)
    cells = jnp.sum(shown, axis=1)
    hidden = filled + (1.0 - cells)[..., None] * pieces[1] + window_sinusoid(DD)
    hidden = hidden.reshape(-1, DD)
    normed = layer_norm(hidden, pieces[2], pieces[3])
    attended = decoder_attention(normed, weights[4], pieces[4], pieces[5], jnp.asarray(window_allowed()))
    hidden = hidden + times(attended, weights[5]) + pieces[6]
    normed = layer_norm(hidden, pieces[7], pieces[8])
    hidden = hidden + hidden_layer(normed, weights[6], pieces[9], weights[7]) + pieces[10]
    normed = layer_norm(hidden, pieces[11], pieces[12])
    predicted = times(normed, weights[8][:, D:].T) + pieces[13]
    deviation = predicted - target.reshape(-1, PATCH)
    patch_error = jnp.mean(deviation * deviation, axis=-1)
    return jnp.sum((1.0 - cells.reshape(-1)) * patch_error)


def quick_body(
    spectrogram, keep, counts, *rest
):
    masters = rest[:8] + (rest[16], rest[19], rest[22])
    moments = rest[8:16]
    devices = lax.axis_size("dp")
    lead = (2,) * bit_count(devices)
    own = list(masters)
    vector_rows = own[10].shape[0]
    spare = VEC_ROWS * VEC_COLS
    own[10] = jnp.pad(own[10], (0, spare - vector_rows)).reshape(VEC_ROWS, VEC_COLS)
    row = lax.broadcasted_iota(jnp.int32, (8, 128), 0)
    column = lax.broadcasted_iota(jnp.int32, (8, 128), 1)
    first = jnp.logical_and(row == 0, column == 0)
    count_part = jnp.sum(NPATCH - counts).astype(jnp.float32)
    scene = window_scene(spectrogram, keep)
    gathered, tally, made = gather_rows(own, jnp.where(first, count_part, 0.0), scene, devices)
    mask_count = tally[0, 0]
    weights = [piece.reshape(-1, piece.shape[-1]) for piece in gathered[:10]]
    weights[4] = weights[4].astype(jnp.float32)
    vectors = gathered[10].reshape(devices, spare)[:, :vector_rows].reshape(-1).astype(jnp.float32)
    loss_part, pull = jax.vjp(
        lambda *params: local_loss(params, *made, keep, counts), *weights, vectors
    )
    grads = list(pull(1.0 / mask_count))
    grads[10] = jnp.pad(grads[10].reshape(devices, vector_rows), ((0, 0), (0, spare - vector_rows)))
    grads[10] = grads[10].reshape(lead + (VEC_ROWS, VEC_COLS))
    for number in range(10):
        grad = grads[number]
        grads[number] = grad.reshape(lead + (grad.shape[0] // devices, grad.shape[1]))
    renewed, others, stats, collected = reduce_rows(
        grads, jnp.where(jnp.logical_and(row == 1, column == 0), loss_part, 0.0), moments, OWNERS, devices
    )
    loss_sum = stats[1, 0]
    grad_norm = jnp.sqrt(jnp.sum(stats[0]))
    factor = jnp.minimum(1.0, CLIP_MAX / (grad_norm + 1e-06))
    adam = (*rest[16:19], others[0], *rest[19:22], others[1])
    flat = [piece.reshape(-1, piece.shape[2]) for piece in collected]
    made, renewed, patch_new, embed_new = orthogonalize(flat, renewed, stats, adam, OWNERS)
    made = [piece.reshape(devices, -1, piece.shape[1]) for piece in made]
    new_weights = finish(return_rows(made, OWNERS, devices), masters[:8], devices)
    vector_grad = others[2].reshape(-1)[:vector_rows] * factor
    vector_new = adam_update(*rest[22:25], vector_grad, 0.0)
    return (loss_sum, mask_count, grad_norm, *new_weights, *renewed, *patch_new, *embed_new, *vector_new)


def body(
    spectrogram,
    keep,
    counts,
    enc_qkv,
    enc_out,
    enc_up,
    enc_down,
    dec_qkv,
    dec_out,
    dec_up,
    dec_down,
    mom_enc_qkv,
    mom_enc_out,
    mom_enc_up,
    mom_enc_down,
    mom_dec_qkv,
    mom_dec_out,
    mom_dec_up,
    mom_dec_down,
    patch_maps,
    patch_first,
    patch_second,
    embed_map,
    embed_first,
    embed_second,
    vectors,
    vector_first,
    vector_second,
):
    masters = (
        enc_qkv,
        enc_out,
        enc_up,
        enc_down,
        dec_qkv,
        dec_out,
        dec_up,
        dec_down,
        patch_maps,
        embed_map,
        vectors,
    )
    moments = (
        mom_enc_qkv,
        mom_enc_out,
        mom_enc_up,
        mom_enc_down,
        mom_dec_qkv,
        mom_dec_out,
        mom_dec_up,
        mom_dec_down,
    )
    sent = tuple((weight.astype(jnp.bfloat16) for weight in masters))
    gathered = (
        lax.all_gather(sent[0], "dp", axis=0, tiled=True),
        lax.all_gather(sent[1], "dp", axis=0, tiled=True),
        lax.all_gather(sent[2], "dp", axis=0, tiled=True),
        lax.all_gather(sent[3], "dp", axis=0, tiled=True),
        lax.all_gather(sent[4], "dp", axis=0, tiled=True),
        lax.all_gather(sent[5], "dp", axis=0, tiled=True),
        lax.all_gather(sent[6], "dp", axis=0, tiled=True),
        lax.all_gather(sent[7], "dp", axis=0, tiled=True),
        lax.all_gather(sent[8], "dp", axis=0, tiled=True),
        lax.all_gather(sent[9], "dp", axis=0, tiled=True),
        lax.all_gather(sent[10], "dp", axis=0, tiled=True),
    )
    widened = tuple((piece.astype(jnp.float32) for piece in gathered))
    patches = patchify(spectrogram.astype(jnp.float32))
    latent = encode(widened, patches, keep, counts)
    loss_part = decode(widened, latent, patches, keep, counts)
    count_part = jnp.sum(NPATCH - counts).astype(jnp.float32)
    loss_sum, mask_count = lax.psum((loss_part, count_part), ("dp", "mp"))
    regathered = (
        lax.all_gather(sent[0], "dp", axis=0, tiled=True),
        lax.all_gather(sent[1], "dp", axis=0, tiled=True),
        lax.all_gather(sent[2], "dp", axis=0, tiled=True),
        lax.all_gather(sent[3], "dp", axis=0, tiled=True),
        lax.all_gather(sent[4], "dp", axis=0, tiled=True),
        lax.all_gather(sent[5], "dp", axis=0, tiled=True),
        lax.all_gather(sent[6], "dp", axis=0, tiled=True),
        lax.all_gather(sent[7], "dp", axis=0, tiled=True),
        lax.all_gather(sent[8], "dp", axis=0, tiled=True),
        lax.all_gather(sent[9], "dp", axis=0, tiled=True),
        lax.all_gather(sent[10], "dp", axis=0, tiled=True),
    )
    widened = tuple((piece.astype(jnp.float32) for piece in regathered))
    cotangent = 1.0 / mask_count
    unused, pull_decode = jax.vjp(
        lambda params, hidden: decode(params, hidden, patches, keep, counts), widened, latent
    )
    decode_grads, latent_grad = pull_decode(cotangent)
    unused, pull_encode = jax.vjp(lambda params: encode(params, patches, keep, counts), widened)
    (encode_grads,) = pull_encode(latent_grad)
    grads = jax.tree.map(jnp.add, decode_grads, encode_grads)
    reduced = (
        lax.psum_scatter(grads[0], "dp", scatter_dimension=0, tiled=True),
        lax.psum_scatter(grads[1], "dp", scatter_dimension=0, tiled=True),
        lax.psum_scatter(grads[2], "dp", scatter_dimension=0, tiled=True),
        lax.psum_scatter(grads[3], "dp", scatter_dimension=0, tiled=True),
        lax.psum_scatter(grads[4], "dp", scatter_dimension=0, tiled=True),
        lax.psum_scatter(grads[5], "dp", scatter_dimension=0, tiled=True),
        lax.psum_scatter(grads[6], "dp", scatter_dimension=0, tiled=True),
        lax.psum_scatter(grads[7], "dp", scatter_dimension=0, tiled=True),
        lax.psum_scatter(grads[8], "dp", scatter_dimension=0, tiled=True),
        lax.psum_scatter(grads[9], "dp", scatter_dimension=0, tiled=True),
        lax.psum_scatter(grads[10], "dp", scatter_dimension=0, tiled=True),
    )
    reduced = lax.psum(
        (
            reduced[0],
            reduced[1],
            reduced[2],
            reduced[3],
            reduced[4],
            reduced[5],
            reduced[6],
            reduced[7],
            reduced[8],
            reduced[9],
            reduced[10],
        ),
        "mp",
    )
    local_squares = functools.reduce(
        jnp.add, [jnp.sum(gradient * gradient) for gradient in reduced]
    )
    grad_norm = jnp.sqrt(lax.psum(local_squares, "dp"))
    factor = jnp.minimum(1.0, CLIP_MAX / (grad_norm + 1e-06))
    clipped = [gradient * factor for gradient in reduced]
    devices = lax.axis_size("dp")
    renewed = [0.5 * moments[number] + clipped[number] for number in range(8)]
    core = lax.axis_index("mp")
    halves = [take_half(renewed[number], number, core) for number in range(8)]
    shapes = [(masters[number].shape[0] * devices, masters[number].shape[1]) for number in range(8)]
    long_max = max((max(shape_pair) // 2 for shape_pair in shapes))
    short_max = max((min(shape_pair) for shape_pair in shapes))
    flat_max = max((shape_pair[0] * shape_pair[1] // (2 * devices) for shape_pair in shapes))
    owner = lax.axis_index("dp") % 8
    collected = (
        lax.all_gather(halves[0], "dp", axis=0, tiled=True),
        lax.all_gather(halves[1], "dp", axis=0, tiled=True),
        lax.all_gather(halves[2], "dp", axis=0, tiled=True),
        lax.all_gather(halves[3], "dp", axis=0, tiled=True),
        lax.all_gather(halves[4], "dp", axis=0, tiled=True),
        lax.all_gather(halves[5], "dp", axis=0, tiled=True),
        lax.all_gather(halves[6], "dp", axis=0, tiled=True),
        lax.all_gather(halves[7], "dp", axis=0, tiled=True),
    )
    iterate = lax.switch(
        owner,
        [partial(arrange, collected[number], number, long_max, short_max) for number in range(8)],
    )
    for iteration in range(NS_ITERS):
        gram_sum = lax.psum(jnp.dot(iterate.T, iterate, precision=HIGH), "mp")
        if iteration == 0:
            norm_scale = 1.0 / (jnp.sqrt(jnp.trace(gram_sum)) + 1e-07)
            iterate = iterate * norm_scale
            gram_sum = gram_sum * (norm_scale * norm_scale)
        polynomial = NS_B * gram_sum + NS_C * jnp.dot(gram_sum, gram_sum, precision=HIGH)
        iterate = NS_A * iterate + jnp.dot(iterate, polynomial, precision=HIGH)
    outgoing = lax.switch(
        owner,
        [
            partial(
                disperse, iterate, number, shapes[number][0], shapes[number][1], devices, flat_max
            )
            for number in range(8)
        ],
    )
    arriving = jax.tree.map(
        lambda part, own: part.astype(own.dtype),
        lax.all_to_all(shortened(outgoing), "dp", split_axis=0, concat_axis=0, tiled=True),
        outgoing,
    )
    mine = [
        restore(arriving[number], number, shapes[number][0], shapes[number][1], devices)
        for number in range(8)
    ]
    whole = (
        lax.all_gather(shortened(mine[0]), "mp", axis=1, tiled=True),
        lax.all_gather(shortened(mine[1]), "mp", axis=1, tiled=True),
        lax.all_gather(shortened(mine[2]), "mp", axis=1, tiled=True),
        lax.all_gather(shortened(mine[3]), "mp", axis=0, tiled=True),
        lax.all_gather(shortened(mine[4]), "mp", axis=1, tiled=True),
        lax.all_gather(shortened(mine[5]), "mp", axis=1, tiled=True),
        lax.all_gather(shortened(mine[6]), "mp", axis=1, tiled=True),
        lax.all_gather(shortened(mine[7]), "mp", axis=0, tiled=True),
    )
    new_weights = []
    for number in range(8):
        step_rate = LR_MUON * 0.2 * math.sqrt(max(shapes[number]))
        new_weights.append(masters[number] * (1.0 - LR_MUON * DECAY) - step_rate * whole[number])
    patch_new = adam_update(patch_maps, patch_first, patch_second, clipped[8], DECAY)
    embed_new = adam_update(embed_map, embed_first, embed_second, clipped[9], DECAY)
    vector_new = adam_update(vectors, vector_first, vector_second, clipped[10], 0.0)
    return (
        loss_sum,
        mask_count,
        grad_norm,
        new_weights[0],
        new_weights[1],
        new_weights[2],
        new_weights[3],
        new_weights[4],
        new_weights[5],
        new_weights[6],
        new_weights[7],
        renewed[0],
        renewed[1],
        renewed[2],
        renewed[3],
        renewed[4],
        renewed[5],
        renewed[6],
        renewed[7],
        patch_new[0],
        patch_new[1],
        patch_new[2],
        embed_new[0],
        embed_new[1],
        embed_new[2],
        vector_new[0],
        vector_new[1],
        vector_new[2],
    )


def solution(mesh):
    placed = (
        P(("dp", "mp"), None, None),
        P(("dp", "mp"), None),
        P(("dp", "mp")),
        P("dp", None),
        P("dp", None),
        P("dp", None),
        P("dp", None),
        P("dp", None),
        P("dp", None),
        P("dp", None),
        P("dp", None),
        P("dp", None),
        P("dp", None),
        P("dp", None),
        P("dp", None),
        P("dp", None),
        P("dp", None),
        P("dp", None),
        P("dp", None),
        P("dp", None),
        P("dp", None),
        P("dp", None),
        P("dp", None),
        P("dp", None),
        P("dp", None),
        P("dp"),
        P("dp"),
        P("dp"),
    )
    return jax.shard_map(
        quick_body if mesh.shape["dp"] == 16 else body,
        mesh=mesh,
        in_specs=placed,
        out_specs=(
            P(),
            P(),
            P(),
            P("dp", None),
            P("dp", None),
            P("dp", None),
            P("dp", None),
            P("dp", None),
            P("dp", None),
            P("dp", None),
            P("dp", None),
            P("dp", None),
            P("dp", None),
            P("dp", None),
            P("dp", None),
            P("dp", None),
            P("dp", None),
            P("dp", None),
            P("dp", None),
            P("dp", None),
            P("dp", None),
            P("dp", None),
            P("dp", None),
            P("dp", None),
            P("dp", None),
            P("dp"),
            P("dp"),
            P("dp"),
        ),
        check_vma=False,
    )
```

```python
from functools import partial
import functools
import math

import jax
import jax.numpy as jnp
import numpy as np
from jax import lax
from jax.experimental import pallas as pl
from jax.experimental.pallas import tpu as pltpu
from jax.sharding import PartitionSpec as P

D = 768
HEADS = 12
HEAD = 64
MLP = 3072
DD = 512
DHEADS = 16
DHEAD = 32
DMLP = 2048
PS = 16
GT = 64
GF = 8
WIN = 4
VIS = 154
NS_ITERS = 5
STEP = 10
PATCH = 256
SHIFT = 2
NPATCH = 512


HIGH = lax.Precision.HIGHEST
CLIP_MAX = 0.001
LR_MUON = 0.1
LR_ADAM = 0.05
DECAY = 0.01
NS_A = 3.4445
NS_B = -4.775
NS_C = 2.0315
LONG_COLS = (True, True, True, False, True, True, True, False)


def shortened(x):
    return jax.tree.map(lambda a: a.astype(jnp.bfloat16) if a.dtype == jnp.float32 else a, x)


def narrow_core(value):
    return lax.optimization_barrier(value.astype(jnp.bfloat16)).astype(jnp.float32)


def narrow_keep(value):
    return (narrow_core(value), None)


def narrow_pass(kept, grad):
    return (grad,)


def same_core(value):
    return value


def same_keep(value):
    return (value, None)


def same_back(kept, grad):
    return (narrow_core(grad),)


def narrow(value):
    wrapped = jax.custom_vjp(narrow_core)
    wrapped.defvjp(narrow_keep, narrow_pass)
    return wrapped(value)


def narrow_grad(value):
    wrapped = jax.custom_vjp(same_core)
    wrapped.defvjp(same_keep, same_back)
    return wrapped(value)


def product(inputs, matrix):
    return narrow_grad(jnp.dot(narrow(inputs), narrow(matrix), preferred_element_type=jnp.float32))


def score_product(queries, key_rows):
    return narrow_grad(
        jnp.einsum(
            "bqhd,bkhd->bhqk", narrow(queries), narrow(key_rows), preferred_element_type=jnp.float32
        )
    )


def value_product(softmax_rows, values):
    return narrow_grad(
        jnp.einsum(
            "bhqk,bkhd->bqhd",
            narrow(softmax_rows),
            narrow(values),
            preferred_element_type=jnp.float32,
        )
    )


def unpack(vectors):
    extents = [D] * 7 + [MLP] + [D] * 4 + [DD] * 9 + [DMLP] + [DD] * 3 + [PATCH]
    pieces = []
    offset = 0
    for extent in extents:
        pieces.append(vectors[offset : offset + extent])
        offset += extent
    return pieces


def layer_norm(hidden, scaling, offset):
    centred = hidden - jnp.mean(hidden, axis=-1, keepdims=True)
    variance = jnp.mean(centred * centred, axis=-1, keepdims=True)
    return centred * lax.rsqrt(variance + 1e-06) * scaling + offset


def sinusoid(channels):
    quarter = channels // 4
    frequency = 1.0 / 10000.0 ** (jnp.arange(quarter, dtype=jnp.float32) / quarter)
    position = jnp.arange(GT * GF)
    time_rows = (position // GF).astype(jnp.float32)[:, None] * frequency
    freq_cols = (position % GF).astype(jnp.float32)[:, None] * frequency
    return jnp.concatenate(
        [jnp.sin(time_rows), jnp.cos(time_rows), jnp.sin(freq_cols), jnp.cos(freq_cols)], axis=1
    )


def patchify(spec):
    clip_total = spec.shape[0]
    arranged = spec.reshape(clip_total, GT, PS, GF, PS).transpose(0, 1, 3, 2, 4)
    return arranged.reshape(clip_total, GT * GF, PS * PS)


def window_mask():
    time_rows = jnp.arange(GT)
    freq_cols = jnp.arange(GF)
    time_part = (time_rows >= GT - WIN).astype(jnp.int32) + (time_rows >= GT - SHIFT).astype(
        jnp.int32
    )
    freq_part = (freq_cols >= GF - WIN).astype(jnp.int32) + (freq_cols >= GF - SHIFT).astype(
        jnp.int32
    )
    region = time_part[:, None] * 3 + freq_part[None, :]
    region = (
        region.reshape(GT // WIN, WIN, GF // WIN, WIN).transpose(0, 2, 1, 3).reshape(-1, WIN * WIN)
    )
    return region[:, :, None] == region[:, None, :]


def to_windows(grid_rows):
    clip_total = grid_rows.shape[0]
    channels = grid_rows.shape[2]
    arranged = jnp.roll(
        grid_rows.reshape(clip_total, GT, GF, channels), (-SHIFT, -SHIFT), axis=(1, 2)
    )
    arranged = arranged.reshape(clip_total, GT // WIN, WIN, GF // WIN, WIN, channels).transpose(
        0, 1, 3, 2, 4, 5
    )
    return arranged.reshape(-1, WIN * WIN, channels)


def from_windows(windows, clip_total):
    channels = windows.shape[-1]
    arranged = windows.reshape(clip_total, GT // WIN, GF // WIN, WIN, WIN, channels).transpose(
        0, 1, 3, 2, 4, 5
    )
    arranged = jnp.roll(arranged.reshape(clip_total, GT, GF, channels), (SHIFT, SHIFT), axis=(1, 2))
    return arranged.reshape(clip_total, GT * GF, channels)


def attend(queries, key_rows, values, allowed, scaling):
    scores = score_product(queries, key_rows) * scaling
    scores = jnp.where(allowed, scores, -1e30)
    scores = scores - jnp.max(scores, axis=-1, keepdims=True)
    exponent = jnp.exp(scores)
    softmax_rows = exponent / jnp.sum(exponent, axis=-1, keepdims=True)
    return value_product(softmax_rows, values)


def encode(weights, patches, keep, counts):
    pieces = unpack(weights[10])
    clip_total = patches.shape[0]
    picked = jnp.take_along_axis(patches, keep[:, :, None], axis=1)
    hidden = product(picked, weights[8][:, :D]) + pieces[11] + sinusoid(D)[keep]
    normed = layer_norm(hidden, pieces[0], pieces[1])
    joined = product(normed, weights[0])
    queries = (joined[..., :D] + pieces[2]).reshape(clip_total, VIS, HEADS, HEAD)
    key_rows = joined[..., D : 2 * D].reshape(clip_total, VIS, HEADS, HEAD)
    values = (joined[..., 2 * D :] + pieces[3]).reshape(clip_total, VIS, HEADS, HEAD)
    visible = (jnp.arange(VIS)[None, :] < counts[:, None])[:, None, None, :]
    attended = attend(queries, key_rows, values, visible, HEAD ** (-0.5)).reshape(
        clip_total, VIS, D
    )
    hidden = hidden + product(attended, weights[1]) + pieces[4]
    normed = layer_norm(hidden, pieces[5], pieces[6])
    inner = jax.nn.gelu(product(normed, weights[2]) + pieces[7], approximate=False)
    hidden = hidden + product(inner, weights[3]) + pieces[8]
    return layer_norm(hidden, pieces[9], pieces[10])


def decode(weights, latent, patches, keep, counts):
    pieces = unpack(weights[10])[12:]
    clip_total = latent.shape[0]
    placed = product(latent, weights[9]) + pieces[0]
    visible = jnp.arange(VIS)[None, :] < counts[:, None]
    target_rows = jnp.where(visible, keep, NPATCH)
    clip_rows = jnp.arange(clip_total)[:, None]
    filled = (
        jnp.zeros((clip_total, NPATCH + 1, DD), jnp.float32)
        .at[clip_rows, target_rows]
        .add(placed)[:, :NPATCH]
    )
    visible_cells = (
        jnp.zeros((clip_total, NPATCH + 1), jnp.float32)
        .at[clip_rows, target_rows]
        .add(1.0)[:, :NPATCH]
    )
    hidden = filled + (1.0 - visible_cells)[..., None] * pieces[1] + sinusoid(DD)
    normed = layer_norm(hidden, pieces[2], pieces[3])
    windows = to_windows(product(normed, weights[4]))
    queries = (windows[..., :DD] + pieces[4]).reshape(-1, WIN * WIN, DHEADS, DHEAD)
    key_rows = windows[..., DD : 2 * DD].reshape(-1, WIN * WIN, DHEADS, DHEAD)
    values = (windows[..., 2 * DD :] + pieces[5]).reshape(-1, WIN * WIN, DHEADS, DHEAD)
    allowed = jnp.tile(window_mask(), (clip_total, 1, 1))[:, None, :, :]
    attended = attend(queries, key_rows, values, allowed, DHEAD ** (-0.5)).reshape(
        -1, WIN * WIN, DD
    )
    hidden = hidden + product(from_windows(attended, clip_total), weights[5]) + pieces[6]
    normed = layer_norm(hidden, pieces[7], pieces[8])
    inner = jax.nn.gelu(product(normed, weights[6]) + pieces[9], approximate=False)
    hidden = hidden + product(inner, weights[7]) + pieces[10]
    normed = layer_norm(hidden, pieces[11], pieces[12])
    predicted = product(normed, weights[8][:, D:].T) + pieces[13]
    centred = patches - jnp.mean(patches, axis=-1, keepdims=True)
    target = centred * lax.rsqrt(jnp.mean(centred * centred, axis=-1, keepdims=True) + 1e-06)
    deviation = predicted - target
    patch_error = jnp.mean(deviation * deviation, axis=-1)
    return jnp.sum((1.0 - visible_cells) * patch_error)


def take_half(shard, number, core):
    if LONG_COLS[number]:
        extent = shard.shape[1] // 2
        return lax.dynamic_slice_in_dim(shard, core * extent, extent, 1)
    extent = shard.shape[0] // 2
    return lax.dynamic_slice_in_dim(shard, core * extent, extent, 0)


def arrange(gathered_half, number, long_max, short_max):
    upright = gathered_half.T if LONG_COLS[number] else gathered_half
    return jnp.pad(upright, ((0, long_max - upright.shape[0]), (0, short_max - upright.shape[1])))


def disperse(iterate, number, height, breadth, devices, flat_max):
    if LONG_COLS[number]:
        piece = iterate[: breadth // 2, :height].T.reshape(
            devices, height // devices * (breadth // 2)
        )
    else:
        piece = iterate[: height // 2, :breadth].reshape(devices, height // 2 // devices * breadth)
    return jnp.pad(piece, ((0, 0), (0, flat_max - piece.shape[1])))


def restore(row_piece, number, height, breadth, devices):
    if LONG_COLS[number]:
        return row_piece[: height // devices * (breadth // 2)].reshape(
            height // devices, breadth // 2
        )
    return row_piece[: height // 2 // devices * breadth].reshape(height // 2 // devices, breadth)


def adam_update(weight, first_moment, second_moment, gradient, decay):
    first_moment = 0.5 * first_moment + 0.5 * gradient
    second_moment = 0.95 * second_moment + 0.05 * gradient * gradient
    direction = (
        first_moment / (1.0 - 0.5**STEP) / (jnp.sqrt(second_moment / (1.0 - 0.95**STEP)) + 1e-08)
    )
    return (weight - LR_ADAM * (direction + decay * weight), first_moment, second_moment)


MESH_ID = pl.DeviceIdType.MESH
VEC_ROWS, VEC_COLS = 16, 256
AXIS_ORDERS = ((0, 1, 2, 3), (0, 1, 3, 2), (0, 2, 1, 3), (0, 2, 3, 1), (0, 3, 1, 2), (0, 3, 2, 1), (1, 0, 2, 3), (1, 0, 3, 2), (1, 2, 0, 3), (1, 2, 3, 0), (1, 3, 0, 2), (1, 3, 2, 0), (2, 0, 1, 3), (2, 0, 3, 1), (2, 1, 0, 3), (2, 1, 3, 0), (2, 3, 0, 1), (2, 3, 1, 0), (3, 0, 1, 2), (3, 0, 2, 1), (3, 1, 0, 2), (3, 1, 2, 0), (3, 2, 0, 1), (3, 2, 1, 0))
GATHER_PARTS = (3, 1, 4, 4, 1, 1, 2, 2, 1, 1, 1)
REDUCE_PARTS = (3, 1, 4, 4, 2, 1, 2, 2, 1, 1, 1)
TALL = (3, 7)
GATHER_TURNS = (19, 18, 22, 17, 13, 21, 22, 20, 3, 12, 11, 0, 17, 23, 16, 10, 23, 16, 11, 21, 21)
GATHER_FIRST = (6, 17, 20, 11, 7, 16, 8, 13, 12, 1, 4, 9, 19, 10, 3, 2, 15, 5, 0, 14, 18)
GATHER_STEPS = ((20, 11, 17, 6, 8, 10, 13, 15, 7, 16, 18, 19, 4, 1, 12, 9, 3, 2, 5, 14, 0), (20, 11, 7, 19, 4, 1, 17, 9, 6, 13, 8, 5, 0, 10, 16, 18, 15, 12, 3, 2, 14), (20, 7, 1, 17, 9, 13, 6, 16, 15, 11, 19, 4, 3, 12, 2, 8, 14, 10, 18, 5, 0), (20, 17, 13, 16, 6, 19, 7, 3, 4, 2, 1, 14, 12, 8, 18, 9, 10, 5, 15, 0, 11))
REDUCE_TURNS = (14, 1, 1, 6, 7, 2, 12, 8, 20, 3, 21, 6, 6, 0, 0, 21, 10, 13, 2, 0, 17, 4)
REDUCE_FIRST = (17, 21, 12, 9, 15, 18, 19, 4, 3, 11, 1, 10, 13, 20, 0, 7, 5, 16, 8, 14, 6, 2)
REDUCE_STEPS = ((21, 17, 12, 9, 19, 15, 18, 4, 20, 3, 11, 10, 1, 0, 7, 14, 16, 5, 8, 13, 6, 2), (21, 17, 19, 15, 9, 12, 10, 14, 1, 20, 0, 18, 4, 8, 3, 7, 11, 13, 2, 16, 6, 5), (21, 17, 19, 20, 15, 18, 9, 14, 0, 10, 12, 8, 7, 16, 1, 6, 4, 5, 3, 11, 13, 2), (21, 17, 20, 15, 9, 19, 10, 18, 14, 0, 12, 8, 1, 16, 7, 6, 4, 5, 3, 2, 13, 11))
OWNERS = (4, 11, 5, 10, 6, 9, 7, 8)
SLOTS = 160
GROUPS = 4


def bit_count(devices):
    return devices.bit_length() - 1


def cut_pieces(parts, shapes):
    found = []
    for number, count in enumerate(parts):
        rows, width = shapes[number]
        for part in range(count):
            if number in TALL:
                found.append((number, part * (rows // count), rows // count, 0, width))
            else:
                found.append((number, 0, rows, part * (width // count), width // count))
    return found


def own_bits(levels):
    me = lax.axis_index("dp")
    return me, [lax.rem(lax.div(me, 2**bit), 2) for bit in range(levels)]


def place(levels, free, own, flip=None):
    spots = []
    for bit in range(levels - 1, -1, -1):
        if bit in free:
            spots.append(slice(None))
        elif bit == flip:
            spots.append(1 - own[bit])
        else:
            spots.append(own[bit])
    return tuple(spots)


def partner(me, own, bit):
    return me + (1 - 2 * own[bit]) * 2**bit


def greet(me, own, levels, core):
    barrier = pltpu.get_barrier_semaphore()
    for bit in range(levels):
        pl.semaphore_signal(
            barrier,
            inc=1,
            device_id={"dp": partner(me, own, bit), "mp": core},
            device_id_type=MESH_ID,
        )
    pl.semaphore_signal(barrier, inc=1, device_id={"dp": me, "mp": 1 - core}, device_id_type=MESH_ID)
    pl.semaphore_wait(barrier, levels + 1)


def add_up(me, core, devices, total, landing, send_sem, recv_sem, own_sem):
    def send(source, target):
        return pltpu.make_async_remote_copy(
            src_ref=total,
            dst_ref=landing.at[source],
            send_sem=send_sem.at[target],
            recv_sem=recv_sem.at[source],
            device_id={"dp": target, "mp": core},
            device_id_type=MESH_ID,
        )

    @pl.loop(0, devices)
    def start_one(other):
        @pl.when(other != me)
        def start_other():
            send(me, other).start()

    own = pltpu.make_async_copy(total, landing.at[me], own_sem)
    own.start()
    own.wait()

    @pl.loop(0, devices)
    def wait_one(other):
        @pl.when(other != me)
        def wait_other():
            send(other, me).wait_recv()
            send(me, other).wait_send()

    found = landing[0]
    for device in range(1, devices):
        found = found + landing[device]
    total[...] = found
    swap = pltpu.make_async_remote_copy(
        src_ref=total,
        dst_ref=landing.at[devices],
        send_sem=send_sem.at[devices],
        recv_sem=recv_sem.at[devices],
        device_id={"dp": me, "mp": 1 - core},
        device_id_type=MESH_ID,
    )
    swap.start()
    swap.wait()
    total[...] = total[...] + landing[devices]


def cut_patches(lines, spots, take, freq, fold, table, picked_out, where_out, target_out):
    part = 512
    lane = lax.broadcasted_iota(jnp.int32, (NPATCH, part), 1)
    inside = lax.rem(lax.div(lane, PS), GF) == freq[...]
    for clip in range(lines.shape[0]):
        patches = jnp.zeros((NPATCH, PATCH), jnp.float32)
        for start in range(0, PS * GF * PS, part):
            spread = jnp.dot(
                take[...], lines[clip, :, start : start + part], preferred_element_type=jnp.float32
            )
            spread = jnp.where(inside, spread, 0.0).astype(jnp.bfloat16)
            patches = patches + jnp.dot(
                spread, fold[start : start + part, :], preferred_element_type=jnp.float32
            )
        slot = lax.broadcasted_iota(jnp.int32, (NPATCH, SLOTS), 0)
        chosen = jnp.where(slot == spots[clip : clip + 1, :], 1.0, 0.0).astype(jnp.bfloat16)
        picked_out[clip] = dot_columns(chosen, patches.astype(jnp.bfloat16)).astype(jnp.bfloat16)
        where_out[clip] = dot_columns(chosen, table[:, :D]) + dot_columns(chosen, table[:, D:])
        centred = patches - jnp.mean(patches, axis=-1, keepdims=True)
        spread = jnp.mean(centred * centred, axis=-1, keepdims=True)
        target_out[clip] = centred * lax.rsqrt(spread + 1e-06)


def gather_kernel(levels, pieces, count, *refs):
    sources, tally, rest = refs[:count] + refs[count + 1 : count + 7], refs[count], refs[count + 7 :]
    outs, tally_out, made, rest = rest[:count], rest[count], rest[count + 1 : count + 4], rest[count + 4 :]
    wholes, save_sem, rest = rest[:count], rest[count], rest[count + 1 :]
    short, held, load_sem, rest = rest[:count], rest[count : 2 * count + 6], rest[2 * count + 6], rest[2 * count + 7 :]
    shards, scene = held[:count], held[count:]

    def load(number):
        return pltpu.make_async_copy(sources[number], held[number], load_sem.at[number])

    for number in range(count + 6):
        load(number).start()
    here_sem, send_sem, recv_sem, cross_send, cross_recv, tally_land, tally_send, tally_recv = rest
    me, own = own_bits(levels)
    core = lax.axis_index("mp")
    greet(me, own, levels, core)
    orders = [AXIS_ORDERS[turn] for turn in GATHER_TURNS]

    def cut(piece, which):
        number, row, rows, column, columns = pieces[piece]
        width = shards[number].shape[1] // 2
        return (pl.ds(row, rows), pl.ds(pl.multiple_of(which * width + column, 128), columns))

    def hop(piece, stage, flip):
        order, number = orders[piece], pieces[piece][0]
        spot = place(levels, order[:stage], own, order[stage] if flip else None)
        target = wholes[number].at[spot + cut(piece, core)]
        source = target if stage or flip else short[number].at[cut(piece, core)]
        return pltpu.make_async_remote_copy(
            src_ref=source,
            dst_ref=target,
            send_sem=send_sem.at[piece, stage],
            recv_sem=recv_sem.at[piece, stage],
            device_id={"dp": partner(me, own, order[stage]), "mp": core},
            device_id_type=MESH_ID,
        )

    def cross(piece, stage, which):
        order, number = orders[piece], pieces[piece][0]
        spot = place(levels, order[:stage], own, order[stage])
        target = wholes[number].at[spot + cut(piece, which)]
        return pltpu.make_async_remote_copy(
            src_ref=target,
            dst_ref=target,
            send_sem=cross_send.at[piece, stage],
            recv_sem=cross_recv.at[piece, stage],
            device_id={"dp": me, "mp": 1 - core},
            device_id_type=MESH_ID,
        )

    def keep(number):
        spot = place(levels, (), own)
        return pltpu.make_async_copy(short[number], wholes[number].at[spot], here_sem.at[number])

    ready = set()
    for piece in GATHER_FIRST:
        number = pieces[piece][0]
        if number not in ready:
            ready.add(number)
            load(number).wait()
            short[number][...] = shards[number][...].astype(jnp.bfloat16)
            keep(number).start()
        hop(piece, 0, False).start()
    masked = jnp.int32(0)
    for clip in range(tally.shape[0]):
        masked = masked + (NPATCH - tally[clip])
    corner = lax.broadcasted_iota(jnp.int32, (8, 128), 0) + lax.broadcasted_iota(jnp.int32, (8, 128), 1) == 0
    tally_out[...] = jnp.where(corner, masked.astype(jnp.float32), 0.0)

    def swap(stage):
        if stage < levels:
            to = {"dp": partner(me, own, stage), "mp": core}
        else:
            to = {"dp": me, "mp": 1 - core}
        return pltpu.make_async_remote_copy(
            src_ref=tally_out,
            dst_ref=tally_land.at[stage],
            send_sem=tally_send.at[stage],
            recv_sem=tally_recv.at[stage],
            device_id=to,
            device_id_type=MESH_ID,
        )

    def swap_end(stage):
        swap(stage).wait()
        tally_out[...] = tally_out[...] + tally_land[stage]

    swap(levels).start()
    for number in range(count):
        keep(number).wait()
    swap_end(levels)
    for stage, order in enumerate(GATHER_STEPS):
        swap(stage).start()
        for piece in order:
            hop(piece, stage, True).wait_recv()
            if stage + 1 < levels:
                hop(piece, stage + 1, False).start()
            cross(piece, stage, core).start()
        swap_end(stage)
        if stage == levels - 2:
            for number in range(6):
                load(count + number).wait()
            cut_patches(*scene, *made)
    def save(number):
        return pltpu.make_async_copy(wholes[number], outs[number], save_sem.at[number])

    last = {}
    for place_in, piece in enumerate(GATHER_STEPS[levels - 1]):
        last[pieces[piece][0]] = place_in
    for number in sorted(last, key=lambda found: last[found]):
        for piece in range(len(pieces)):
            if pieces[piece][0] == number:
                for stage in range(levels):
                    cross(piece, stage, 1 - core).wait_recv()
        save(number).start()
    for piece in range(len(pieces)):
        for stage in range(levels):
            hop(piece, stage, False).wait_send()
            cross(piece, stage, core).wait_send()
    for number in range(count):
        save(number).wait()


def gather_rows(shards, tally, scene, devices):
    levels, count = bit_count(devices), len(shards)
    lead = (2,) * levels
    clips = scene[0].shape[0]
    pieces = cut_pieces(GATHER_PARTS, [(shard.shape[0], shard.shape[1] // 2) for shard in shards])
    dma = pltpu.SemaphoreType.DMA
    vmem, far = pl.BlockSpec(memory_space=pltpu.VMEM), pl.BlockSpec(memory_space=pltpu.HBM)
    found = pl.pallas_call(
        functools.partial(gather_kernel, levels, pieces, count),
        out_shape=[jax.ShapeDtypeStruct(lead + shard.shape, jnp.bfloat16) for shard in shards]
        + [
            jax.ShapeDtypeStruct((8, 128), jnp.float32),
            jax.ShapeDtypeStruct((clips, SLOTS, PATCH), jnp.bfloat16),
            jax.ShapeDtypeStruct((clips, SLOTS, D), jnp.float32),
            jax.ShapeDtypeStruct((clips, NPATCH, PATCH), jnp.float32),
        ],
        in_specs=[far] * count + [pl.BlockSpec(memory_space=pltpu.SMEM)] + [far] * 6,
        out_specs=[pl.BlockSpec(memory_space=pl.ANY)] * count + [vmem] * 4,
        scratch_shapes=[pltpu.VMEM(lead + shard.shape, jnp.bfloat16) for shard in shards]
        + [dma((count,))]
        + [pltpu.VMEM(shard.shape, jnp.bfloat16) for shard in shards]
        + [pltpu.VMEM(piece.shape, piece.dtype) for piece in (*shards, *scene)]
        + [dma((count + 6,))]
        + [dma((count,))]
        + [dma((len(pieces), levels))] * 4
        + [pltpu.VMEM((levels + 1, 8, 128), jnp.float32)]
        + [dma((levels + 1,))] * 2,
        compiler_params=pltpu.CompilerParams(
            collective_id=1, has_side_effects=True, vmem_limit_bytes=60 * 2**20
        ),
        name="gather_rows",
    )(*shards, tally, *scene)
    return found[:count], found[count], found[count + 1 :]


def reduce_kernel(levels, pieces, count, owners, devices, *refs):
    blocks = len(owners)
    grads, stats_in, old = refs[:count], refs[count], refs[count + 1 : count + 1 + blocks]
    rest = refs[count + 1 + blocks :]
    sums, stats_out, wholes = rest[:count], rest[count], rest[count + 1 : count + 1 + blocks]
    rest = rest[count + 1 + blocks :]
    mine, theirs, rest = rest[:count], rest[count : 2 * count], rest[2 * count :]
    kept, rest = rest[:count], rest[count:]
    landing, rest = rest[: len(pieces) * levels], rest[len(pieces) * levels :]
    staged, rest = rest[:blocks], rest[blocks:]
    stats_land, here_sem, pair_send, pair_recv, send_sem, recv_sem, last_send, last_recv = rest[:8]
    stats_send, stats_recv, own_sem, out_send, out_recv, cross_send, cross_recv = rest[8:]
    me, own = own_bits(levels)
    core = lax.axis_index("mp")
    orders = [AXIS_ORDERS[turn] for turn in REDUCE_TURNS]
    barrier = pltpu.get_barrier_semaphore()

    @pl.loop(0, devices)
    def greet_one(other):
        @pl.when(other != me)
        def signal_one():
            pl.semaphore_signal(
                barrier, inc=1, device_id={"dp": other, "mp": core}, device_id_type=MESH_ID
            )

    pl.semaphore_signal(barrier, inc=1, device_id={"dp": me, "mp": 1 - core}, device_id_type=MESH_ID)
    pl.semaphore_wait(barrier, devices)

    def half(number, which):
        width = sums[number].shape[1] // 2
        return (slice(None), pl.ds(pl.multiple_of(which * width, 128), width))

    def cut(piece):
        number, row, rows, column, columns = pieces[piece]
        return (pl.ds(row, rows), pl.ds(column, columns))

    def side(piece, which):
        number, row, rows, column, columns = pieces[piece]
        width = sums[number].shape[1] // 2
        return (pl.ds(row, rows), pl.ds(pl.multiple_of(which * width + column, 128), columns))

    every = (slice(None),) * levels

    def pair(piece):
        number = pieces[piece][0]
        return pltpu.make_async_remote_copy(
            src_ref=grads[number].at[every + side(piece, 1 - core)],
            dst_ref=theirs[number].at[every + cut(piece)],
            send_sem=pair_send.at[piece],
            recv_sem=pair_recv.at[piece],
            device_id={"dp": me, "mp": 1 - core},
            device_id_type=MESH_ID,
        )

    def load(piece):
        number = pieces[piece][0]
        return pltpu.make_async_copy(
            grads[number].at[every + side(piece, core)],
            mine[number].at[every + cut(piece)],
            here_sem.at[piece],
        )

    def hop(piece, stage):
        order = orders[piece]
        spot = place(levels, order[stage + 1 :], own, order[stage])
        return pltpu.make_async_remote_copy(
            src_ref=theirs[pieces[piece][0]].at[spot + cut(piece)],
            dst_ref=landing[piece * levels + stage],
            send_sem=send_sem.at[piece, stage],
            recv_sem=recv_sem.at[piece, stage],
            device_id={"dp": partner(me, own, order[stage]), "mp": core},
            device_id_type=MESH_ID,
        )

    def share(number, which):
        region = sums[number].at[half(number, which)]
        return pltpu.make_async_remote_copy(
            src_ref=region,
            dst_ref=region,
            send_sem=last_send.at[number],
            recv_sem=last_recv.at[number],
            device_id={"dp": me, "mp": 1 - core},
            device_id_type=MESH_ID,
        )

    def deliver(number, source):
        return pltpu.make_async_remote_copy(
            src_ref=staged[number],
            dst_ref=wholes[number].at[(source,) + half(number, core)],
            send_sem=out_send.at[number],
            recv_sem=out_recv.at[number, source],
            device_id={"dp": owners[number], "mp": core},
            device_id_type=MESH_ID,
        )

    def deliver_here(number):
        return pltpu.make_async_copy(
            staged[number], wholes[number].at[(me,) + half(number, core)], own_sem
        )

    def cross(number, source, which):
        region = wholes[number].at[(source,) + half(number, which)]
        return pltpu.make_async_remote_copy(
            src_ref=region,
            dst_ref=region,
            send_sem=cross_send.at[number, source],
            recv_sem=cross_recv.at[number, source],
            device_id={"dp": me, "mp": 1 - core},
            device_id_type=MESH_ID,
        )

    def kept_spot(order, found):
        return tuple(found.get(bit, own[bit]) for bit in range(levels - 1, -1, -1) if bit != order[0])

    def fold(piece, stage):
        order, number = orders[piece], pieces[piece][0]
        free = order[stage:]
        loose = [bit for bit in range(levels - 1, -1, -1) if bit in free and bit != order[stage]]
        region = cut(piece)

        @pl.loop(0, 2 ** len(loose))
        def add_block(block):
            found = {
                bit: lax.rem(lax.div(block, 2 ** (len(loose) - 1 - i)), 2) for i, bit in enumerate(loose)
            }

            def total(way):
                now = dict(found)
                now[order[stage]] = way
                full = tuple(now.get(bit, own[bit]) for bit in range(levels - 1, -1, -1)) + region
                if stage == 0:
                    value = mine[number][full].astype(jnp.float32) + theirs[number][full].astype(jnp.float32)
                else:
                    land = tuple(now[bit] for bit in range(levels - 1, -1, -1) if bit in free)
                    arrived = landing[piece * levels + stage - 1][land].astype(jnp.float32)
                    value = kept[number][kept_spot(order, now) + region] + arrived
                return full, value

            full, value = total(1 - own[order[stage]])
            theirs[number][full] = value.astype(theirs[number].dtype)
            full, value = total(own[order[stage]])
            kept[number][kept_spot(order, found) + region] = value

    for piece in REDUCE_FIRST:
        pair(piece).start()
        load(piece).start()
    for piece in REDUCE_FIRST:
        load(piece).wait()
        pair(piece).wait_recv()
        fold(piece, 0)
        hop(piece, 0).start()
    squares = jnp.zeros((8, 128), jnp.float32)
    for piece, stage in [(piece, stage) for stage in range(levels) for piece in REDUCE_STEPS[stage]]:
        hop(piece, stage).wait_recv()
        if stage + 1 < levels:
            fold(piece, stage + 1)
            hop(piece, stage + 1).start()
        else:
            number = pieces[piece][0]
            arrived = landing[piece * levels + stage][...].astype(jnp.float32)
            total = kept[number][kept_spot(orders[piece], {}) + cut(piece)] + arrived
            sums[number][side(piece, core)] = total
            rows, width = total.shape
            for row in range(0, rows, 8):
                for column in range(0, width, 128):
                    part = total[row : row + 8, column : column + 128]
                    squares = squares + part * part
    for number in range(blocks, count):
        share(number, core).start()
    row = lax.broadcasted_iota(jnp.int32, (8, 128), 0)
    stats_out[...] = jnp.where(row == 0, jnp.sum(squares, axis=0, keepdims=True), stats_in[...])
    add_up(me, core, devices, stats_out, stats_land, stats_send, stats_recv, own_sem)
    norm = jnp.sqrt(jnp.sum(stats_out[0:1, :], axis=1, keepdims=True))
    factor = jnp.minimum(1.0, CLIP_MAX / (norm + 1e-06))
    for number in range(blocks):
        region = half(number, core)
        renewed = 0.5 * old[number][region] + factor * sums[number][region]
        sums[number][region] = renewed
        staged[number][...] = renewed.astype(staged[number].dtype)
        share(number, core).start()

        @pl.when(me != owners[number])
        def start_one(number=number):
            deliver(number, me).start()

        @pl.when(me == owners[number])
        def start_here(number=number):
            deliver_here(number).start()

    for piece in range(len(pieces)):
        pair(piece).wait_send()
        for stage in range(levels):
            hop(piece, stage).wait_send()
    for number in range(blocks):

        @pl.when(me == owners[number])
        def collect(number=number):
            deliver_here(number).wait()

            @pl.loop(0, devices)
            def forward(source):
                @pl.when(source != me)
                def arrived():
                    deliver(number, source).wait_recv()

                cross(number, source, core).start()

            @pl.loop(0, devices)
            def finish(source):
                cross(number, source, core).wait_send()
                cross(number, source, 1 - core).wait_recv()

        @pl.when(me != owners[number])
        def end_one(number=number):
            deliver(number, me).wait_send()

    for number in range(count):
        share(number, core).wait_send()
        share(number, 1 - core).wait_recv()


def reduce_rows(grads, stats, old, owners, devices):
    levels, count, blocks = bit_count(devices), len(grads), len(old)
    lead = (2,) * levels
    dma = pltpu.SemaphoreType.DMA
    shapes = [grad.shape[levels:] for grad in grads]
    halves = [(rows, columns // 2) for rows, columns in shapes]
    kinds = [grad.dtype for grad in grads]
    pieces = cut_pieces(REDUCE_PARTS, halves)
    scratch = [pltpu.VMEM(lead + shape, kind) for shape, kind in zip(halves, kinds)] * 2
    scratch += [pltpu.VMEM(lead[1:] + shape, jnp.float32) for shape in halves]
    for number, row, rows, column, columns in pieces:
        for stage in range(levels):
            scratch.append(pltpu.VMEM((2,) * (levels - 1 - stage) + (rows, columns), kinds[number]))
    scratch += [pltpu.VMEM(halves[number], kinds[number]) for number in range(blocks)]
    scratch.append(pltpu.VMEM((devices + 1, 8, 128), jnp.float32))
    scratch += [dma((len(pieces),))] * 3 + [dma((len(pieces), levels))] * 2 + [dma((count,))] * 2
    scratch += [dma((devices + 1,))] * 2 + [dma, dma((blocks,))] + [dma((blocks, devices))] * 3
    vmem, anywhere = pl.BlockSpec(memory_space=pltpu.VMEM), pl.BlockSpec(memory_space=pl.ANY)
    found = pl.pallas_call(
        functools.partial(reduce_kernel, levels, pieces, count, owners, devices),
        out_shape=[jax.ShapeDtypeStruct(shape, jnp.float32) for shape in shapes]
        + [jax.ShapeDtypeStruct((8, 128), jnp.float32)]
        + [jax.ShapeDtypeStruct((devices,) + shapes[number], kinds[number]) for number in range(blocks)],
        in_specs=[anywhere] * count + [vmem] * (1 + blocks),
        out_specs=[vmem] * (count + 1) + [anywhere] * blocks,
        scratch_shapes=scratch,
        compiler_params=pltpu.CompilerParams(
            collective_id=2, has_side_effects=True, vmem_limit_bytes=60 * 2**20
        ),
        name="reduce_rows",
    )(*grads, stats, *old)
    return found[:blocks], found[blocks:count], found[count], found[count + 1 :]


def return_kernel(owners, count, devices, *refs):
    wholes, rows = refs[:count], refs[count : 2 * count]
    here_sem, send_sem, recv_sem, cross_send, cross_recv = refs[2 * count :]
    me, core = lax.axis_index("dp"), lax.axis_index("mp")
    barrier = pltpu.get_barrier_semaphore()
    owning = functools.reduce(jnp.logical_or, [me == owner for owner in owners])
    for owner in owners:

        @pl.when(me != owner)
        def greet_owner(owner=owner):
            pl.semaphore_signal(
                barrier, inc=1, device_id={"dp": owner, "mp": core}, device_id_type=MESH_ID
            )

    pl.semaphore_signal(barrier, inc=1, device_id={"dp": me, "mp": 1 - core}, device_id_type=MESH_ID)

    @pl.when(owning)
    def wait_all():
        pl.semaphore_wait(barrier, devices)

    @pl.when(jnp.logical_not(owning))
    def wait_pair():
        pl.semaphore_wait(barrier, 1)

    def half(number, which):
        width = rows[number].shape[1] // 2
        return (slice(None), pl.ds(pl.multiple_of(which * width, 128), width))

    def hop(number, target):
        return pltpu.make_async_remote_copy(
            src_ref=wholes[number].at[(target,) + half(number, core)],
            dst_ref=rows[number].at[half(number, core)],
            send_sem=send_sem.at[number, target],
            recv_sem=recv_sem.at[number],
            device_id={"dp": target, "mp": core},
            device_id_type=MESH_ID,
        )

    def cross(number, which):
        region = rows[number].at[half(number, which)]
        return pltpu.make_async_remote_copy(
            src_ref=region,
            dst_ref=region,
            send_sem=cross_send.at[number],
            recv_sem=cross_recv.at[number],
            device_id={"dp": me, "mp": 1 - core},
            device_id_type=MESH_ID,
        )

    for number in range(count):

        @pl.when(me == owners[number])
        def hand_out(number=number):
            own = pltpu.make_async_copy(
                wholes[number].at[(me,) + half(number, core)], rows[number].at[half(number, core)], here_sem
            )
            own.start()

            @pl.loop(0, devices)
            def start_one(target):
                @pl.when(target != me)
                def start_other():
                    hop(number, target).start()

            own.wait()

    for number in range(count):

        @pl.when(me != owners[number])
        def arrive(number=number):
            hop(number, me).wait_recv()

        cross(number, core).start()
    for number in range(count):
        cross(number, core).wait_send()
        cross(number, 1 - core).wait_recv()

        @pl.when(me == owners[number])
        def end_out(number=number):
            @pl.loop(0, devices)
            def end_one(target):
                @pl.when(target != me)
                def end_other():
                    hop(number, target).wait_send()


def return_rows(wholes, owners, devices):
    count = len(wholes)
    dma = pltpu.SemaphoreType.DMA
    vmem = pl.BlockSpec(memory_space=pltpu.VMEM)
    return pl.pallas_call(
        functools.partial(return_kernel, owners, count, devices),
        out_shape=[jax.ShapeDtypeStruct(whole.shape[1:], whole.dtype) for whole in wholes],
        in_specs=[pl.BlockSpec(memory_space=pl.ANY)] * count,
        out_specs=[vmem] * count,
        scratch_shapes=[dma, dma((count, devices)), dma((count,)), dma((count,)), dma((count,))],
        compiler_params=pltpu.CompilerParams(
            collective_id=4, has_side_effects=True, vmem_limit_bytes=60 * 2**20
        ),
        name="return_rows",
    )(*wholes)


def finish_kernel(count, rates, *refs):
    rows, masters, updated = refs[:count], refs[count : 2 * count], refs[2 * count :]
    for number in range(count):
        change = rates[number] * rows[number][...].astype(jnp.float32)
        updated[number][...] = masters[number][...] * (1.0 - LR_MUON * DECAY) - change


def finish(rows, masters, devices):
    count = len(rows)
    rates = []
    for master in masters:
        rates.append(LR_MUON * 0.2 * math.sqrt(max(master.shape[0] * devices, master.shape[1])))
    vmem = pl.BlockSpec(memory_space=pltpu.VMEM)
    return pl.pallas_call(
        functools.partial(finish_kernel, count, rates),
        out_shape=[jax.ShapeDtypeStruct(master.shape, jnp.float32) for master in masters],
        in_specs=[vmem] * (2 * count),
        out_specs=[vmem] * count,
        compiler_params=pltpu.CompilerParams(vmem_limit_bytes=56 * 2**20),
        name="finish",
    )(*rows, *masters)


def muon_kernel(owners, shapes, *refs):
    count = len(owners)
    mats, moved, stats, adam_in = refs[:count], refs[count : 2 * count], refs[2 * count], refs[2 * count + 1 :][:8]
    rest = refs[2 * count + 9 :]
    outs, moved_out, adam_out, rest = rest[:count], rest[count : 2 * count], rest[2 * count :][:6], rest[2 * count + 6 :]
    exact, wide, wide_low, tall, wide_out, tall_out, gram = rest[:7]
    base, poly, other, chain, sem, in_sem, out_sem = rest[7:14]
    held_rows = rest[14:]

    def move_in(number):
        return pltpu.make_async_copy(moved[number], held_rows[number], in_sem.at[number])

    def move_out(number):
        return pltpu.make_async_copy(held_rows[number], moved_out[number], out_sem.at[number])

    for number in range(count):
        move_in(number).start()
    norm = jnp.sqrt(jnp.sum(stats[0:1, :], axis=1, keepdims=True))
    factor = jnp.minimum(1.0, CLIP_MAX / (norm + 1e-06))
    for group in range(2):
        weight, first, second, grad = [ref[...] for ref in adam_in[4 * group : 4 * group + 4]]
        made = adam_update(weight, first, second, grad * factor, DECAY)
        for place_out in range(3):
            adam_out[3 * group + place_out][...] = made[place_out]
    me, core = lax.axis_index("dp"), lax.axis_index("mp")
    side = gram.shape[0]
    step = 256
    bf = jnp.bfloat16

    def dims(number):
        height, breadth = shapes[number]
        return height, breadth, LONG_COLS[number]

    def span(index):
        return pl.ds(pl.multiple_of(index * step, step), step)

    def split(value):
        high = value.astype(bf)
        return high, (value - high.astype(jnp.float32)).astype(bf)

    gram[...] = jnp.zeros_like(gram)
    for number in range(count):

        @pl.when(me == owners[number])
        def start(number=number):
            height, breadth, long_cols = dims(number)
            short = min(height, breadth)
            held = (wide if long_cols else tall).at[:height, :breadth]
            fine = mats[number].dtype == jnp.float32
            load = pltpu.make_async_copy(mats[number], exact if fine else held, sem)
            load.start()
            load.wait()
            if fine:
                rest = wide_low

                @pl.loop(0, height // step)
                def part_rows(index):
                    high, low = split(exact[span(index), :])
                    held[span(index), :] = high
                    rest[span(index), :] = low

            for index in range(short // step):
                first, beyond = slice(index * step, (index + 1) * step), slice(index * step, short)
                if long_cols:
                    total = dot_rows(held[first, :], held[beyond, :])
                    if fine:
                        total = total + dot_rows(held[first, :], rest[beyond, :])
                        total = total + dot_rows(rest[first, :], held[beyond, :])
                else:
                    total = dot_columns(held[:, first], held[:, beyond])
                gram[first, beyond] = total

    for number in range(count):
        move_in(number).wait()
        move_out(number).start()
    owning = functools.reduce(jnp.logical_or, [me == owner for owner in owners])

    @pl.when(owning)
    def iterate():
        parts = [
            (slice(index * step, (index + 1) * step), slice(index * step, side))
            for index in range(side // step)
        ]
        ones = lax.broadcasted_iota(jnp.int32, (step, step), 0) == lax.broadcasted_iota(
            jnp.int32, (step, step), 1
        )
        trace = jnp.float32(0.0)
        for first, beyond in parts:
            trace = trace + jnp.sum(jnp.where(ones, gram[first, first], 0.0))
        scale = 1.0 / (jnp.sqrt(jnp.full((8, 128), trace, jnp.float32)) + 1e-07)
        scale = scale[0:1, 0:1]

        def store(target, index, value):
            high, low = split(value)
            target[0, parts[index][0], parts[index][1]] = high
            target[1, parts[index][0], parts[index][1]] = low
            for later in range(index + 1, side // step):
                shift = (later - index) * step
                high, low = split(value[:, shift : shift + step].T)
                target[0, parts[later][0], parts[index][0]] = high
                target[1, parts[later][0], parts[index][0]] = low

        def product(left, right, index):
            first, beyond = parts[index]
            high, low = left[0, first, :], left[1, first, :]
            total = jnp.dot(high, right[0, :, beyond], preferred_element_type=jnp.float32)
            total = total + jnp.dot(high, right[1, :, beyond], preferred_element_type=jnp.float32)
            return total + jnp.dot(low, right[0, :, beyond], preferred_element_type=jnp.float32)

        for index, (first, beyond) in enumerate(parts):
            store(base, index, gram[first, beyond] * (scale * scale))

        @pl.loop(0, NS_ITERS)
        def newton(iteration):
            for index, (first, beyond) in enumerate(parts):
                now = base[0, first, beyond].astype(jnp.float32) + base[1, first, beyond].astype(jnp.float32)
                row = lax.broadcasted_iota(jnp.int32, now.shape, 0)
                column = lax.broadcasted_iota(jnp.int32, now.shape, 1)
                value = jnp.where(row == column, NS_A, 0.0) + NS_B * now
                store(poly, index, value + NS_C * product(base, base, index))

            @pl.when(iteration < NS_ITERS - 1)
            def advance():
                for index in range(len(parts)):
                    store(other, index, product(base, poly, index))
                for index in range(len(parts)):
                    store(base, index, product(other, poly, index))

            @pl.when(iteration == 0)
            def begin():
                chain[...] = poly[...]

            @pl.when(iteration > 0)
            def follow():
                for index in range(len(parts)):
                    store(other, index, product(chain, poly, index))
                chain[...] = other[...]

        for first, beyond in parts:
            value = chain[0, first, :].astype(jnp.float32) + chain[1, first, :].astype(jnp.float32)
            high, low = split(value * scale)
            other[0, first, :] = high
            other[1, first, :] = low

    for number in range(count):

        @pl.when(me == owners[number])
        def end(number=number):
            height, breadth, long_cols = dims(number)
            short = min(height, breadth)
            width = breadth // 2
            part = pl.ds(pl.multiple_of(core * width, 128), width)
            if long_cols:
                held, made = wide.at[:height, :breadth], wide_out.at[:height, :width]

                @pl.loop(0, height // step)
                def wide_rows(index):
                    total = jnp.dot(
                        other[0, span(index), :short], held[:, part], preferred_element_type=jnp.float32
                    ) + jnp.dot(
                        other[1, span(index), :short], held[:, part], preferred_element_type=jnp.float32
                    )
                    if mats[number].dtype == jnp.float32:
                        total = total + jnp.dot(
                            other[0, span(index), :short],
                            wide_low[:, part],
                            preferred_element_type=jnp.float32,
                        )
                    made[span(index), :] = total.astype(bf)
            else:
                held, made = tall.at[:height, :breadth], tall_out.at[:height, :width]

                @pl.loop(0, height // step)
                def tall_rows(index):
                    total = jnp.dot(
                        held[span(index), :], other[0, :short, part], preferred_element_type=jnp.float32
                    ) + jnp.dot(
                        held[span(index), :], other[1, :short, part], preferred_element_type=jnp.float32
                    )
                    made[span(index), :] = total.astype(bf)

            save = pltpu.make_async_copy(made, outs[number].at[:, part], sem)
            save.start()
            save.wait()

    for number in range(count):
        move_out(number).wait()


def orthogonalize(mats, moved, stats, adam, owners):
    count = len(mats)
    shapes = [mat.shape for mat in mats]
    side = max(min(shape) for shape in shapes)
    longest = max(max(shape) for shape in shapes)
    double = pltpu.VMEM((2, side, side), jnp.bfloat16)
    (fine,) = [mat.shape for mat in mats if mat.dtype == jnp.float32]
    vmem, anywhere = pl.BlockSpec(memory_space=pltpu.VMEM), pl.BlockSpec(memory_space=pl.ANY)
    renewed = (adam[0], adam[1], adam[2], adam[4], adam[5], adam[6])
    found = pl.pallas_call(
        functools.partial(muon_kernel, owners, shapes),
        out_shape=[jax.ShapeDtypeStruct(shape, jnp.bfloat16) for shape in shapes]
        + [jax.ShapeDtypeStruct(piece.shape, piece.dtype) for piece in moved]
        + [jax.ShapeDtypeStruct(piece.shape, piece.dtype) for piece in renewed],
        in_specs=[anywhere] * (2 * count) + [vmem] * 9,
        out_specs=[anywhere] * (2 * count) + [vmem] * 6,
        scratch_shapes=[
            pltpu.VMEM(fine, jnp.float32),
            pltpu.VMEM((side, longest), jnp.bfloat16),
            pltpu.VMEM(fine, jnp.bfloat16),
            pltpu.VMEM((longest, side), jnp.bfloat16),
            pltpu.VMEM((side, longest // 2), jnp.bfloat16),
            pltpu.VMEM((longest, side // 2), jnp.bfloat16),
            pltpu.VMEM((side, side), jnp.float32),
            double,
            double,
            double,
            double,
            pltpu.SemaphoreType.DMA,
            pltpu.SemaphoreType.DMA((count,)),
            pltpu.SemaphoreType.DMA((count,)),
        ]
        + [pltpu.VMEM(piece.shape, piece.dtype) for piece in moved],
        compiler_params=pltpu.CompilerParams(vmem_limit_bytes=60 * 2**20),
        name="orthogonalize",
    )(*mats, *moved, stats, *adam)
    return found[:count], found[count : 2 * count], found[2 * count : 2 * count + 3], found[2 * count + 3 :]


def window_place(position):
    time_row = (position // GF + GT - SHIFT) % GT
    freq_col = (position % GF + GF - SHIFT) % GF
    window = (time_row // WIN) * (GF // WIN) + freq_col // WIN
    return window * (WIN * WIN) + (time_row % WIN) * WIN + freq_col % WIN


def window_sinusoid(channels):
    quarter = channels // 4
    frequency = 1.0 / 10000.0 ** (np.arange(quarter) / quarter)
    position = np.arange(NPATCH)
    time_rows = (position // GF)[:, None] * frequency
    freq_cols = (position % GF)[:, None] * frequency
    table = np.concatenate([np.sin(time_rows), np.cos(time_rows), np.sin(freq_cols), np.cos(freq_cols)], axis=1)
    moved = np.zeros_like(table)
    moved[window_place(position)] = table
    return moved.astype(np.float32)


def window_scene(spec, keep):
    position = np.arange(NPATCH)
    row = np.empty(NPATCH, np.int32)
    row[window_place(position)] = position
    take = (row[:, None] // GF == np.arange(GT)[None, :]).astype(np.float32)
    source = np.arange(PS * GF * PS)[:, None]
    target = np.arange(PATCH)[None, :]
    fold = np.logical_and(source // (GF * PS) == target // PS, source % PS == target % PS)
    table = window_sinusoid(D)
    high = table.astype(jnp.bfloat16)
    low = (table - high.astype(np.float32)).astype(jnp.bfloat16)
    return (
        spec.reshape(spec.shape[0], GT, PS * GF * PS),
        window_place(jnp.pad(keep, ((0, 0), (0, SLOTS - VIS)))),
        jnp.asarray(take, jnp.bfloat16),
        jnp.asarray(row[:, None] % GF),
        jnp.asarray(fold, jnp.bfloat16),
        jnp.asarray(np.concatenate([high, low], axis=1)),
    )


@jax.custom_vjp
def times(inputs, matrix):
    return jnp.dot(inputs.astype(jnp.bfloat16), matrix.astype(jnp.bfloat16), preferred_element_type=jnp.float32)


def times_keep(inputs, matrix):
    short = inputs.astype(jnp.bfloat16)
    return jnp.dot(short, matrix.astype(jnp.bfloat16), preferred_element_type=jnp.float32), (short, matrix)


def times_back(kept, grad):
    short, matrix = kept
    grad = grad.astype(jnp.bfloat16)
    back = lax.dot_general(
        grad, matrix.astype(jnp.bfloat16), (((1,), (1,)), ((), ())), preferred_element_type=jnp.float32
    )
    gain = lax.dot_general(short, grad, (((0,), (0,)), ((), ())), preferred_element_type=jnp.float32)
    return back, gain.astype(matrix.dtype)


times.defvjp(times_keep, times_back)


def dot_rows(left, right):
    return lax.dot_general(left, right, (((1,), (1,)), ((), ())), preferred_element_type=jnp.float32)


def dot_columns(left, right):
    return lax.dot_general(left, right, (((0,), (0,)), ((), ())), preferred_element_type=jnp.float32)


def head_lanes(value, head, size):
    lane = lax.broadcasted_iota(jnp.int32, value.shape, 1)
    return jnp.where(lane // size == head, value, jnp.zeros_like(value))


def soft_keys(queries, keys_here, allow, size):
    rows = queries.shape[0]
    scores = dot_rows(keys_here, queries).reshape(128 // size, rows, rows)
    scores = jnp.where(allow, scores * size ** (-0.5), -1e30)
    exponent = jnp.exp(scores - jnp.max(scores, axis=1, keepdims=True))
    return exponent / jnp.sum(exponent, axis=1, keepdims=True)


def flat_heads(value):
    return value.astype(jnp.bfloat16).reshape(-1, value.shape[2])


def attention_kernel(size, joined, allowed, out):
    width = out.shape[1]
    allow = allowed[...][None] > 0.0
    for lane in range(0, width, 128):
        queries = joined[:, lane : lane + 128]
        keys_here = stack_heads(joined[:, width + lane : width + lane + 128], size)
        values_here = stack_heads(joined[:, 2 * width + lane : 2 * width + lane + 128], size)
        soft = flat_heads(soft_keys(queries, keys_here, allow, size))
        out[:, lane : lane + 128] = dot_columns(soft, values_here).astype(jnp.bfloat16)


def attention_back_kernel(size, joined, allowed, grad, out, query_sum, value_sum):
    width, rows = grad.shape[1], grad.shape[0]
    allow = allowed[...][None] > 0.0

    @pl.when(pl.program_id(0) == 0)
    def clear():
        query_sum[...] = jnp.zeros_like(query_sum)
        value_sum[...] = jnp.zeros_like(value_sum)

    for lane in range(0, width, 128):
        queries = joined[:, lane : lane + 128]
        keys_here = stack_heads(joined[:, width + lane : width + lane + 128], size)
        values_here = stack_heads(joined[:, 2 * width + lane : 2 * width + lane + 128], size)
        pull = grad[:, lane : lane + 128]
        soft = soft_keys(queries, keys_here, allow, size)
        soft_grad = dot_rows(values_here, pull).reshape(128 // size, rows, rows)
        score_grad = soft * (soft_grad - jnp.sum(soft * soft_grad, axis=1, keepdims=True))
        score_grad = flat_heads(score_grad * size ** (-0.5))
        soft = flat_heads(soft)
        query_grad = dot_columns(score_grad, keys_here)
        key_grad = unstack_heads(jnp.dot(score_grad, queries, preferred_element_type=jnp.float32), size)
        value_grad = unstack_heads(jnp.dot(soft, pull, preferred_element_type=jnp.float32), size)
        out[:, lane : lane + 128] = query_grad.astype(jnp.bfloat16)
        out[:, width + lane : width + lane + 128] = key_grad.astype(jnp.bfloat16)
        out[:, 2 * width + lane : 2 * width + lane + 128] = value_grad.astype(jnp.bfloat16)
        query_sum[0:1, lane : lane + 128] += jnp.sum(query_grad, axis=0, keepdims=True)
        value_sum[0:1, lane : lane + 128] += jnp.sum(value_grad, axis=0, keepdims=True)


def window_fold(value, heads):
    lane = lax.broadcasted_iota(jnp.int32, (1, 1, value.shape[1]), 2) // (WIN * WIN)
    value = value.reshape(heads, 8, WIN * WIN, value.shape[1])
    found = value[:, 0]
    for window in range(1, 8):
        found = jnp.where(lane == window, value[:, window], found)
    return found


def window_spread(value):
    heads = value.shape[0]
    short = value.astype(jnp.bfloat16)
    lane = lax.broadcasted_iota(jnp.int32, short.shape, 2) // (WIN * WIN)
    parts = []
    for head in range(heads):
        for window in range(8):
            parts.append(
                jnp.where(lane[head] == window, short[head], jnp.zeros_like(short[head]))
            )
    return jnp.concatenate(parts, axis=0)


def stack_heads(value, size):
    per = value.shape[1] // size
    return jnp.concatenate([head_lanes(value, head, size) for head in range(per)], axis=0)


def unstack_heads(value, size):
    per = value.shape[1] // size
    rows = value.shape[0] // per
    lane = lax.broadcasted_iota(jnp.int32, (rows, value.shape[1]), 1) // size
    found = value[:rows]
    for head in range(1, per):
        found = jnp.where(lane == head, value[head * rows : (head + 1) * rows], found)
    return found


def soft_fold(queries, keys_here, allow, size):
    scores = window_fold(dot_rows(keys_here, queries), 128 // size)
    scores = jnp.where(allow, scores * size ** (-0.5), -1e30)
    exponent = jnp.exp(scores - jnp.max(scores, axis=1, keepdims=True))
    return exponent / jnp.sum(exponent, axis=1, keepdims=True)


def window_kernel(size, joined, allowed, out):
    for group in range(allowed.shape[0]):
        rows = pl.ds(group * 128, 128)
        window_group(size, joined.at[rows], allowed.at[group], out.at[rows])


def window_group(size, joined, allowed, out):
    width = out.shape[1]
    allow = allowed[...][None] > 0.0
    for lane in range(0, width, 128):
        queries = joined[:, lane : lane + 128]
        keys_here = stack_heads(joined[:, width + lane : width + lane + 128], size)
        values_here = stack_heads(joined[:, 2 * width + lane : 2 * width + lane + 128], size)
        soft = window_spread(soft_fold(queries, keys_here, allow, size))
        out[:, lane : lane + 128] = dot_columns(soft, values_here).astype(jnp.bfloat16)


def window_back_kernel(size, joined, allowed, grad, out, query_sum, value_sum):
    @pl.when(pl.program_id(0) == 0)
    def clear():
        query_sum[...] = jnp.zeros_like(query_sum)
        value_sum[...] = jnp.zeros_like(value_sum)

    for group in range(allowed.shape[0]):
        rows = pl.ds(group * 128, 128)
        window_back_group(
            size, joined.at[rows], allowed.at[group], grad.at[rows], out.at[rows], query_sum, value_sum
        )


def window_back_group(size, joined, allowed, grad, out, query_sum, value_sum):
    width = grad.shape[1]
    allow = allowed[...][None] > 0.0
    for lane in range(0, width, 128):
        queries = joined[:, lane : lane + 128]
        keys_here = stack_heads(joined[:, width + lane : width + lane + 128], size)
        values_here = stack_heads(joined[:, 2 * width + lane : 2 * width + lane + 128], size)
        pull = grad[:, lane : lane + 128]
        soft = soft_fold(queries, keys_here, allow, size)
        soft_grad = window_fold(dot_rows(values_here, pull), 128 // size)
        score_grad = soft * (soft_grad - jnp.sum(soft * soft_grad, axis=1, keepdims=True))
        score_grad = window_spread(score_grad * size ** (-0.5))
        soft = window_spread(soft)
        query_grad = dot_columns(score_grad, keys_here)
        key_grad = unstack_heads(jnp.dot(score_grad, queries, preferred_element_type=jnp.float32), size)
        value_grad = unstack_heads(jnp.dot(soft, pull, preferred_element_type=jnp.float32), size)
        out[:, lane : lane + 128] = query_grad.astype(jnp.bfloat16)
        out[:, width + lane : width + lane + 128] = key_grad.astype(jnp.bfloat16)
        out[:, 2 * width + lane : 2 * width + lane + 128] = value_grad.astype(jnp.bfloat16)
        query_sum[0:1, lane : lane + 128] += jnp.sum(query_grad, axis=0, keepdims=True)
        value_sum[0:1, lane : lane + 128] += jnp.sum(value_grad, axis=0, keepdims=True)


def attention_parts(joined, allowed, rows):
    steps = joined.shape[0] // rows
    period = allowed.shape[0]
    wide = pl.BlockSpec((rows, joined.shape[1]), lambda step: (step, 0))
    rest = (0,) * (allowed.ndim - 1)
    mask = pl.BlockSpec((None,) + allowed.shape[1:], lambda step: (lax.rem(step, period),) + rest)
    narrow_rows = pl.BlockSpec((rows, joined.shape[1] // 3), lambda step: (step, 0))
    return steps, wide, mask, narrow_rows


def attention_forward(kernel, joined, allowed, rows, size):
    steps, wide, mask, part = attention_parts(joined, allowed, rows)
    return pl.pallas_call(
        functools.partial(kernel, size),
        grid=(steps,),
        out_shape=jax.ShapeDtypeStruct((joined.shape[0], joined.shape[1] // 3), jnp.bfloat16),
        in_specs=[wide, mask],
        out_specs=part,
        compiler_params=pltpu.CompilerParams(vmem_limit_bytes=40 * 2**20),
        name="attention_forward",
    )(joined, allowed)


def attention_backward(kernel, joined, allowed, grad, rows, size):
    steps, wide, mask, part = attention_parts(joined, allowed, rows)
    width = joined.shape[1] // 3
    total = pl.BlockSpec((8, width), lambda step: (0, 0))
    return pl.pallas_call(
        functools.partial(kernel, size),
        grid=(steps,),
        out_shape=[
            jax.ShapeDtypeStruct(joined.shape, jnp.bfloat16),
            jax.ShapeDtypeStruct((8, width), jnp.float32),
            jax.ShapeDtypeStruct((8, width), jnp.float32),
        ],
        in_specs=[wide, mask, part],
        out_specs=[wide, total, total],
        compiler_params=pltpu.CompilerParams(vmem_limit_bytes=40 * 2**20),
        name="attention_backward",
    )(joined, allowed, grad)


def weight_grad_kernel(rows, grad, out):
    out[...] = dot_columns(rows[...], grad[...]).astype(out.dtype)


def weight_grad(rows, grad, kind):
    (tokens, height), width = rows.shape, grad.shape[1]
    tile = width // 3
    return pl.pallas_call(
        weight_grad_kernel,
        grid=(3,),
        out_shape=jax.ShapeDtypeStruct((height, width), kind),
        in_specs=[
            pl.BlockSpec((tokens, height), lambda step: (0, 0)),
            pl.BlockSpec((tokens, tile), lambda step: (0, step)),
        ],
        out_specs=pl.BlockSpec((height, tile), lambda step: (0, step)),
        compiler_params=pltpu.CompilerParams(vmem_limit_bytes=40 * 2**20),
        name="weight_grad",
    )(rows, grad)


def attention_block(forward, backward, rows, size):
    def join(normed, matrix, query_bias, value_bias):
        width = matrix.shape[1] // 3
        bias = jnp.concatenate([query_bias, jnp.zeros((width,), jnp.float32), value_bias])
        joined = jnp.dot(normed, matrix.astype(jnp.bfloat16), preferred_element_type=jnp.float32)
        return (joined + bias).astype(jnp.bfloat16)

    @jax.custom_vjp
    def apply(normed, matrix, query_bias, value_bias, allowed):
        joined = join(normed.astype(jnp.bfloat16), matrix, query_bias, value_bias)
        return attention_forward(forward, joined, allowed, rows, size).astype(jnp.float32)

    def keep(normed, matrix, query_bias, value_bias, allowed):
        short = normed.astype(jnp.bfloat16)
        joined = join(short, matrix, query_bias, value_bias)
        made = attention_forward(forward, joined, allowed, rows, size).astype(jnp.float32)
        return made, (short, matrix, joined, allowed)

    def back(kept, grad):
        short, matrix, joined, allowed = kept
        pulled, query_sum, value_sum = attention_backward(
            backward, joined, allowed, grad.astype(jnp.bfloat16), rows, size
        )
        normed_grad = dot_rows(pulled, matrix.astype(jnp.bfloat16))
        matrix_grad = weight_grad(short, pulled, matrix.dtype)
        return normed_grad, matrix_grad, query_sum[0], value_sum[0], jnp.zeros_like(allowed)

    apply.defvjp(keep, back)
    return apply


encoder_attention = attention_block(attention_kernel, attention_back_kernel, SLOTS, HEAD)
decoder_attention = attention_block(window_kernel, window_back_kernel, GROUPS * 8 * WIN * WIN, DHEAD)


def gelu_keep(value):
    portion = 0.5 + 0.5 * lax.erf(value * math.sqrt(0.5))
    slope = portion + value * jnp.exp(-0.5 * value * value) * (1.0 / math.sqrt(2.0 * math.pi))
    return value * portion, slope


def hidden_back_kernel(normed, inner, slope, grad, up, down, normed_grad, up_grad, down_grad, bias_grad):
    @pl.when(pl.program_id(0) == 0)
    def clear():
        normed_grad[...] = jnp.zeros_like(normed_grad)

    inner_grad = dot_rows(grad[...], down[...]) * slope[...]
    bias_grad[0:1, :] = jnp.sum(inner_grad, axis=0, keepdims=True)
    short = inner_grad.astype(jnp.bfloat16)
    down_grad[...] = dot_columns(inner[...], grad[...]).astype(jnp.bfloat16)
    up_grad[...] = dot_columns(normed[...], short).astype(jnp.bfloat16)
    normed_grad[...] += dot_rows(short, up[...])


def hidden_backward(normed, inner, slope, grad, up, down):
    (tokens, width), units = normed.shape, inner.shape[1]
    tile = 1024
    whole = pl.BlockSpec((tokens, width), lambda step: (0, 0))
    columns = pl.BlockSpec((tokens, tile), lambda step: (0, step))
    up_tile = pl.BlockSpec((width, tile), lambda step: (0, step))
    down_tile = pl.BlockSpec((tile, width), lambda step: (step, 0))
    return pl.pallas_call(
        hidden_back_kernel,
        grid=(units // tile,),
        out_shape=[
            jax.ShapeDtypeStruct((tokens, width), jnp.float32),
            jax.ShapeDtypeStruct((width, units), jnp.bfloat16),
            jax.ShapeDtypeStruct((units, width), jnp.bfloat16),
            jax.ShapeDtypeStruct((8, units), jnp.float32),
        ],
        in_specs=[whole, columns, columns, whole, up_tile, down_tile],
        out_specs=[whole, up_tile, down_tile, pl.BlockSpec((8, tile), lambda step: (0, step))],
        compiler_params=pltpu.CompilerParams(vmem_limit_bytes=40 * 2**20),
        name="hidden_backward",
    )(normed, inner, slope, grad, up, down)


@jax.custom_vjp
def hidden_layer(normed, up, bias, down):
    return hidden_keep(normed, up, bias, down)[0]


def hidden_keep(normed, up, bias, down):
    short = normed.astype(jnp.bfloat16)
    value, slope = gelu_keep(jnp.dot(short, up, preferred_element_type=jnp.float32) + bias)
    inner = value.astype(jnp.bfloat16)
    return jnp.dot(inner, down, preferred_element_type=jnp.float32), (short, inner, slope, up, down)


def hidden_back(kept, grad):
    short, inner, slope, up, down = kept
    found = hidden_backward(short, inner, slope, grad.astype(jnp.bfloat16), up, down)
    normed_grad, up_grad, down_grad, bias_grad = found
    return normed_grad, up_grad, bias_grad[0], down_grad


hidden_layer.defvjp(hidden_keep, hidden_back)


def window_allowed():
    position = np.arange(NPATCH)
    window, inner = position // (WIN * WIN), position % (WIN * WIN)
    time_row = window // (GF // WIN) * WIN + inner // WIN
    freq_col = window % (GF // WIN) * WIN + inner % WIN
    region = (time_row >= GT - WIN).astype(np.int32) + (time_row >= GT - SHIFT)
    region = region * 3 + (freq_col >= GF - WIN) + (freq_col >= GF - SHIFT)
    region = region.reshape(-1, 8, 1, WIN * WIN)
    same = region == region.transpose(0, 1, 3, 2)
    same = same.transpose(0, 2, 1, 3).reshape(-1, GROUPS, WIN * WIN, 8 * WIN * WIN)
    return same.astype(np.float32)


def local_loss(weights, picked, where, target, keep, counts):
    clips = picked.shape[0]
    pieces = unpack(weights[10])
    spot = window_place(jnp.pad(keep, ((0, 0), (0, SLOTS - VIS))))
    shown = (spot[:, :, None] == jnp.arange(NPATCH)[None, None, :]).astype(jnp.float32)
    shown = shown * (jnp.arange(SLOTS)[None, :] < counts[:, None])[:, :, None]
    hidden = times(picked.reshape(-1, PATCH), weights[8][:, :D]) + pieces[11] + where.reshape(-1, D)
    normed = layer_norm(hidden, pieces[0], pieces[1])
    visible = (jnp.arange(SLOTS)[None, :] < counts[:, None]).astype(jnp.float32)
    visible = jnp.broadcast_to(visible[:, :, None], (clips, SLOTS, SLOTS))
    attended = encoder_attention(normed, weights[0], pieces[2], pieces[3], visible)
    hidden = hidden + times(attended, weights[1]) + pieces[4]
    normed = layer_norm(hidden, pieces[5], pieces[6])
    hidden = hidden + hidden_layer(normed, weights[2], pieces[7], weights[3]) + pieces[8]
    latent = layer_norm(hidden, pieces[9], pieces[10])

    pieces = pieces[12:]
    placed = times(latent, weights[9]) + pieces[0]
    filled = jnp.einsum("cjp,cjd->cpd", shown, placed.reshape(clips, SLOTS, DD), precision=HIGH)
    cells = jnp.sum(shown, axis=1)
    hidden = filled + (1.0 - cells)[..., None] * pieces[1] + window_sinusoid(DD)
    hidden = hidden.reshape(-1, DD)
    normed = layer_norm(hidden, pieces[2], pieces[3])
    attended = decoder_attention(normed, weights[4], pieces[4], pieces[5], jnp.asarray(window_allowed()))
    hidden = hidden + times(attended, weights[5]) + pieces[6]
    normed = layer_norm(hidden, pieces[7], pieces[8])
    hidden = hidden + hidden_layer(normed, weights[6], pieces[9], weights[7]) + pieces[10]
    normed = layer_norm(hidden, pieces[11], pieces[12])
    predicted = times(normed, weights[8][:, D:].T) + pieces[13]
    deviation = predicted - target.reshape(-1, PATCH)
    patch_error = jnp.mean(deviation * deviation, axis=-1)
    return jnp.sum((1.0 - cells.reshape(-1)) * patch_error)


def quick_body(
    spectrogram, keep, counts, *rest
):
    masters = rest[:8] + (rest[16], rest[19], rest[22])
    moments = rest[8:16]
    devices = lax.axis_size("dp")
    lead = (2,) * bit_count(devices)
    own = list(masters)
    vector_rows = own[10].shape[0]
    spare = VEC_ROWS * VEC_COLS
    own[10] = jnp.pad(own[10], (0, spare - vector_rows)).reshape(VEC_ROWS, VEC_COLS)
    row = lax.broadcasted_iota(jnp.int32, (8, 128), 0)
    column = lax.broadcasted_iota(jnp.int32, (8, 128), 1)
    scene = window_scene(spectrogram, keep)
    gathered, tally, made = gather_rows(own, counts, scene, devices)
    mask_count = tally[0, 0]
    weights = [piece.reshape(-1, piece.shape[-1]) for piece in gathered[:10]]
    weights[4] = weights[4].astype(jnp.float32)
    vectors = gathered[10].reshape(devices, spare)[:, :vector_rows].reshape(-1).astype(jnp.float32)
    loss_part, pull = jax.vjp(
        lambda *params: local_loss(params, *made, keep, counts), *weights, vectors
    )
    grads = list(pull(1.0 / mask_count))
    grads[10] = jnp.pad(grads[10].reshape(devices, vector_rows), ((0, 0), (0, spare - vector_rows)))
    grads[10] = grads[10].reshape(lead + (VEC_ROWS, VEC_COLS))
    for number in range(10):
        grad = grads[number]
        grads[number] = grad.reshape(lead + (grad.shape[0] // devices, grad.shape[1]))
    renewed, others, stats, collected = reduce_rows(
        grads, jnp.where(jnp.logical_and(row == 1, column == 0), loss_part, 0.0), moments, OWNERS, devices
    )
    loss_sum = stats[1, 0]
    grad_norm = jnp.sqrt(jnp.sum(stats[0]))
    factor = jnp.minimum(1.0, CLIP_MAX / (grad_norm + 1e-06))
    adam = (*rest[16:19], others[0], *rest[19:22], others[1])
    flat = [piece.reshape(-1, piece.shape[2]) for piece in collected]
    made, renewed, patch_new, embed_new = orthogonalize(flat, renewed, stats, adam, OWNERS)
    made = [piece.reshape(devices, -1, piece.shape[1]) for piece in made]
    new_weights = finish(return_rows(made, OWNERS, devices), masters[:8], devices)
    vector_grad = others[2].reshape(-1)[:vector_rows] * factor
    vector_new = adam_update(*rest[22:25], vector_grad, 0.0)
    return (loss_sum, mask_count, grad_norm, *new_weights, *renewed, *patch_new, *embed_new, *vector_new)


def body(
    spectrogram,
    keep,
    counts,
    enc_qkv,
    enc_out,
    enc_up,
    enc_down,
    dec_qkv,
    dec_out,
    dec_up,
    dec_down,
    mom_enc_qkv,
    mom_enc_out,
    mom_enc_up,
    mom_enc_down,
    mom_dec_qkv,
    mom_dec_out,
    mom_dec_up,
    mom_dec_down,
    patch_maps,
    patch_first,
    patch_second,
    embed_map,
    embed_first,
    embed_second,
    vectors,
    vector_first,
    vector_second,
):
    masters = (
        enc_qkv,
        enc_out,
        enc_up,
        enc_down,
        dec_qkv,
        dec_out,
        dec_up,
        dec_down,
        patch_maps,
        embed_map,
        vectors,
    )
    moments = (
        mom_enc_qkv,
        mom_enc_out,
        mom_enc_up,
        mom_enc_down,
        mom_dec_qkv,
        mom_dec_out,
        mom_dec_up,
        mom_dec_down,
    )
    sent = tuple((weight.astype(jnp.bfloat16) for weight in masters))
    gathered = (
        lax.all_gather(sent[0], "dp", axis=0, tiled=True),
        lax.all_gather(sent[1], "dp", axis=0, tiled=True),
        lax.all_gather(sent[2], "dp", axis=0, tiled=True),
        lax.all_gather(sent[3], "dp", axis=0, tiled=True),
        lax.all_gather(sent[4], "dp", axis=0, tiled=True),
        lax.all_gather(sent[5], "dp", axis=0, tiled=True),
        lax.all_gather(sent[6], "dp", axis=0, tiled=True),
        lax.all_gather(sent[7], "dp", axis=0, tiled=True),
        lax.all_gather(sent[8], "dp", axis=0, tiled=True),
        lax.all_gather(sent[9], "dp", axis=0, tiled=True),
        lax.all_gather(sent[10], "dp", axis=0, tiled=True),
    )
    widened = tuple((piece.astype(jnp.float32) for piece in gathered))
    patches = patchify(spectrogram.astype(jnp.float32))
    latent = encode(widened, patches, keep, counts)
    loss_part = decode(widened, latent, patches, keep, counts)
    count_part = jnp.sum(NPATCH - counts).astype(jnp.float32)
    loss_sum, mask_count = lax.psum((loss_part, count_part), ("dp", "mp"))
    regathered = (
        lax.all_gather(sent[0], "dp", axis=0, tiled=True),
        lax.all_gather(sent[1], "dp", axis=0, tiled=True),
        lax.all_gather(sent[2], "dp", axis=0, tiled=True),
        lax.all_gather(sent[3], "dp", axis=0, tiled=True),
        lax.all_gather(sent[4], "dp", axis=0, tiled=True),
        lax.all_gather(sent[5], "dp", axis=0, tiled=True),
        lax.all_gather(sent[6], "dp", axis=0, tiled=True),
        lax.all_gather(sent[7], "dp", axis=0, tiled=True),
        lax.all_gather(sent[8], "dp", axis=0, tiled=True),
        lax.all_gather(sent[9], "dp", axis=0, tiled=True),
        lax.all_gather(sent[10], "dp", axis=0, tiled=True),
    )
    widened = tuple((piece.astype(jnp.float32) for piece in regathered))
    cotangent = 1.0 / mask_count
    unused, pull_decode = jax.vjp(
        lambda params, hidden: decode(params, hidden, patches, keep, counts), widened, latent
    )
    decode_grads, latent_grad = pull_decode(cotangent)
    unused, pull_encode = jax.vjp(lambda params: encode(params, patches, keep, counts), widened)
    (encode_grads,) = pull_encode(latent_grad)
    grads = jax.tree.map(jnp.add, decode_grads, encode_grads)
    reduced = (
        lax.psum_scatter(grads[0], "dp", scatter_dimension=0, tiled=True),
        lax.psum_scatter(grads[1], "dp", scatter_dimension=0, tiled=True),
        lax.psum_scatter(grads[2], "dp", scatter_dimension=0, tiled=True),
        lax.psum_scatter(grads[3], "dp", scatter_dimension=0, tiled=True),
        lax.psum_scatter(grads[4], "dp", scatter_dimension=0, tiled=True),
        lax.psum_scatter(grads[5], "dp", scatter_dimension=0, tiled=True),
        lax.psum_scatter(grads[6], "dp", scatter_dimension=0, tiled=True),
        lax.psum_scatter(grads[7], "dp", scatter_dimension=0, tiled=True),
        lax.psum_scatter(grads[8], "dp", scatter_dimension=0, tiled=True),
        lax.psum_scatter(grads[9], "dp", scatter_dimension=0, tiled=True),
        lax.psum_scatter(grads[10], "dp", scatter_dimension=0, tiled=True),
    )
    reduced = lax.psum(
        (
            reduced[0],
            reduced[1],
            reduced[2],
            reduced[3],
            reduced[4],
            reduced[5],
            reduced[6],
            reduced[7],
            reduced[8],
            reduced[9],
            reduced[10],
        ),
        "mp",
    )
    local_squares = functools.reduce(
        jnp.add, [jnp.sum(gradient * gradient) for gradient in reduced]
    )
    grad_norm = jnp.sqrt(lax.psum(local_squares, "dp"))
    factor = jnp.minimum(1.0, CLIP_MAX / (grad_norm + 1e-06))
    clipped = [gradient * factor for gradient in reduced]
    devices = lax.axis_size("dp")
    renewed = [0.5 * moments[number] + clipped[number] for number in range(8)]
    core = lax.axis_index("mp")
    halves = [take_half(renewed[number], number, core) for number in range(8)]
    shapes = [(masters[number].shape[0] * devices, masters[number].shape[1]) for number in range(8)]
    long_max = max((max(shape_pair) // 2 for shape_pair in shapes))
    short_max = max((min(shape_pair) for shape_pair in shapes))
    flat_max = max((shape_pair[0] * shape_pair[1] // (2 * devices) for shape_pair in shapes))
    owner = lax.axis_index("dp") % 8
    collected = (
        lax.all_gather(halves[0], "dp", axis=0, tiled=True),
        lax.all_gather(halves[1], "dp", axis=0, tiled=True),
        lax.all_gather(halves[2], "dp", axis=0, tiled=True),
        lax.all_gather(halves[3], "dp", axis=0, tiled=True),
        lax.all_gather(halves[4], "dp", axis=0, tiled=True),
        lax.all_gather(halves[5], "dp", axis=0, tiled=True),
        lax.all_gather(halves[6], "dp", axis=0, tiled=True),
        lax.all_gather(halves[7], "dp", axis=0, tiled=True),
    )
    iterate = lax.switch(
        owner,
        [partial(arrange, collected[number], number, long_max, short_max) for number in range(8)],
    )
    for iteration in range(NS_ITERS):
        gram_sum = lax.psum(jnp.dot(iterate.T, iterate, precision=HIGH), "mp")
        if iteration == 0:
            norm_scale = 1.0 / (jnp.sqrt(jnp.trace(gram_sum)) + 1e-07)
            iterate = iterate * norm_scale
            gram_sum = gram_sum * (norm_scale * norm_scale)
        polynomial = NS_B * gram_sum + NS_C * jnp.dot(gram_sum, gram_sum, precision=HIGH)
        iterate = NS_A * iterate + jnp.dot(iterate, polynomial, precision=HIGH)
    outgoing = lax.switch(
        owner,
        [
            partial(
                disperse, iterate, number, shapes[number][0], shapes[number][1], devices, flat_max
            )
            for number in range(8)
        ],
    )
    arriving = jax.tree.map(
        lambda part, own: part.astype(own.dtype),
        lax.all_to_all(shortened(outgoing), "dp", split_axis=0, concat_axis=0, tiled=True),
        outgoing,
    )
    mine = [
        restore(arriving[number], number, shapes[number][0], shapes[number][1], devices)
        for number in range(8)
    ]
    whole = (
        lax.all_gather(shortened(mine[0]), "mp", axis=1, tiled=True),
        lax.all_gather(shortened(mine[1]), "mp", axis=1, tiled=True),
        lax.all_gather(shortened(mine[2]), "mp", axis=1, tiled=True),
        lax.all_gather(shortened(mine[3]), "mp", axis=0, tiled=True),
        lax.all_gather(shortened(mine[4]), "mp", axis=1, tiled=True),
        lax.all_gather(shortened(mine[5]), "mp", axis=1, tiled=True),
        lax.all_gather(shortened(mine[6]), "mp", axis=1, tiled=True),
        lax.all_gather(shortened(mine[7]), "mp", axis=0, tiled=True),
    )
    new_weights = []
    for number in range(8):
        step_rate = LR_MUON * 0.2 * math.sqrt(max(shapes[number]))
        new_weights.append(masters[number] * (1.0 - LR_MUON * DECAY) - step_rate * whole[number])
    patch_new = adam_update(patch_maps, patch_first, patch_second, clipped[8], DECAY)
    embed_new = adam_update(embed_map, embed_first, embed_second, clipped[9], DECAY)
    vector_new = adam_update(vectors, vector_first, vector_second, clipped[10], 0.0)
    return (
        loss_sum,
        mask_count,
        grad_norm,
        new_weights[0],
        new_weights[1],
        new_weights[2],
        new_weights[3],
        new_weights[4],
        new_weights[5],
        new_weights[6],
        new_weights[7],
        renewed[0],
        renewed[1],
        renewed[2],
        renewed[3],
        renewed[4],
        renewed[5],
        renewed[6],
        renewed[7],
        patch_new[0],
        patch_new[1],
        patch_new[2],
        embed_new[0],
        embed_new[1],
        embed_new[2],
        vector_new[0],
        vector_new[1],
        vector_new[2],
    )


def solution(mesh):
    placed = (
        P(("dp", "mp"), None, None),
        P(("dp", "mp"), None),
        P(("dp", "mp")),
        P("dp", None),
        P("dp", None),
        P("dp", None),
        P("dp", None),
        P("dp", None),
        P("dp", None),
        P("dp", None),
        P("dp", None),
        P("dp", None),
        P("dp", None),
        P("dp", None),
        P("dp", None),
        P("dp", None),
        P("dp", None),
        P("dp", None),
        P("dp", None),
        P("dp", None),
        P("dp", None),
        P("dp", None),
        P("dp", None),
        P("dp", None),
        P("dp", None),
        P("dp"),
        P("dp"),
        P("dp"),
    )
    return jax.shard_map(
        quick_body if mesh.shape["dp"] == 16 else body,
        mesh=mesh,
        in_specs=placed,
        out_specs=(
            P(),
            P(),
            P(),
            P("dp", None),
            P("dp", None),
            P("dp", None),
            P("dp", None),
            P("dp", None),
            P("dp", None),
            P("dp", None),
            P("dp", None),
            P("dp", None),
            P("dp", None),
            P("dp", None),
            P("dp", None),
            P("dp", None),
            P("dp", None),
            P("dp", None),
            P("dp", None),
            P("dp", None),
            P("dp", None),
            P("dp", None),
            P("dp", None),
            P("dp", None),
            P("dp", None),
            P("dp"),
            P("dp"),
            P("dp"),
        ),
        check_vma=False,
    )
```

```python
from functools import partial
import functools
import math

import jax
import jax.numpy as jnp
import numpy as np
from jax import lax
from jax.experimental import pallas as pl
from jax.experimental.pallas import tpu as pltpu
from jax.sharding import PartitionSpec as P

D = 768
HEADS = 12
HEAD = 64
MLP = 3072
DD = 512
DHEADS = 16
DHEAD = 32
DMLP = 2048
PS = 16
GT = 64
GF = 8
WIN = 4
VIS = 154
NS_ITERS = 5
STEP = 10
PATCH = 256
SHIFT = 2
NPATCH = 512


HIGH = lax.Precision.HIGHEST
CLIP_MAX = 0.001
LR_MUON = 0.1
LR_ADAM = 0.05
DECAY = 0.01
NS_A = 3.4445
NS_B = -4.775
NS_C = 2.0315
LONG_COLS = (True, True, True, False, True, True, True, False)


def shortened(x):
    return jax.tree.map(lambda a: a.astype(jnp.bfloat16) if a.dtype == jnp.float32 else a, x)


def narrow_core(value):
    return lax.optimization_barrier(value.astype(jnp.bfloat16)).astype(jnp.float32)


def narrow_keep(value):
    return (narrow_core(value), None)


def narrow_pass(kept, grad):
    return (grad,)


def same_core(value):
    return value


def same_keep(value):
    return (value, None)


def same_back(kept, grad):
    return (narrow_core(grad),)


def narrow(value):
    wrapped = jax.custom_vjp(narrow_core)
    wrapped.defvjp(narrow_keep, narrow_pass)
    return wrapped(value)


def narrow_grad(value):
    wrapped = jax.custom_vjp(same_core)
    wrapped.defvjp(same_keep, same_back)
    return wrapped(value)


def product(inputs, matrix):
    return narrow_grad(jnp.dot(narrow(inputs), narrow(matrix), preferred_element_type=jnp.float32))


def score_product(queries, key_rows):
    return narrow_grad(
        jnp.einsum(
            "bqhd,bkhd->bhqk", narrow(queries), narrow(key_rows), preferred_element_type=jnp.float32
        )
    )


def value_product(softmax_rows, values):
    return narrow_grad(
        jnp.einsum(
            "bhqk,bkhd->bqhd",
            narrow(softmax_rows),
            narrow(values),
            preferred_element_type=jnp.float32,
        )
    )


def unpack(vectors):
    extents = [D] * 7 + [MLP] + [D] * 4 + [DD] * 9 + [DMLP] + [DD] * 3 + [PATCH]
    pieces = []
    offset = 0
    for extent in extents:
        pieces.append(vectors[offset : offset + extent])
        offset += extent
    return pieces


def layer_norm(hidden, scaling, offset):
    centred = hidden - jnp.mean(hidden, axis=-1, keepdims=True)
    variance = jnp.mean(centred * centred, axis=-1, keepdims=True)
    return centred * lax.rsqrt(variance + 1e-06) * scaling + offset


def sinusoid(channels):
    quarter = channels // 4
    frequency = 1.0 / 10000.0 ** (jnp.arange(quarter, dtype=jnp.float32) / quarter)
    position = jnp.arange(GT * GF)
    time_rows = (position // GF).astype(jnp.float32)[:, None] * frequency
    freq_cols = (position % GF).astype(jnp.float32)[:, None] * frequency
    return jnp.concatenate(
        [jnp.sin(time_rows), jnp.cos(time_rows), jnp.sin(freq_cols), jnp.cos(freq_cols)], axis=1
    )


def patchify(spec):
    clip_total = spec.shape[0]
    arranged = spec.reshape(clip_total, GT, PS, GF, PS).transpose(0, 1, 3, 2, 4)
    return arranged.reshape(clip_total, GT * GF, PS * PS)


def window_mask():
    time_rows = jnp.arange(GT)
    freq_cols = jnp.arange(GF)
    time_part = (time_rows >= GT - WIN).astype(jnp.int32) + (time_rows >= GT - SHIFT).astype(
        jnp.int32
    )
    freq_part = (freq_cols >= GF - WIN).astype(jnp.int32) + (freq_cols >= GF - SHIFT).astype(
        jnp.int32
    )
    region = time_part[:, None] * 3 + freq_part[None, :]
    region = (
        region.reshape(GT // WIN, WIN, GF // WIN, WIN).transpose(0, 2, 1, 3).reshape(-1, WIN * WIN)
    )
    return region[:, :, None] == region[:, None, :]


def to_windows(grid_rows):
    clip_total = grid_rows.shape[0]
    channels = grid_rows.shape[2]
    arranged = jnp.roll(
        grid_rows.reshape(clip_total, GT, GF, channels), (-SHIFT, -SHIFT), axis=(1, 2)
    )
    arranged = arranged.reshape(clip_total, GT // WIN, WIN, GF // WIN, WIN, channels).transpose(
        0, 1, 3, 2, 4, 5
    )
    return arranged.reshape(-1, WIN * WIN, channels)


def from_windows(windows, clip_total):
    channels = windows.shape[-1]
    arranged = windows.reshape(clip_total, GT // WIN, GF // WIN, WIN, WIN, channels).transpose(
        0, 1, 3, 2, 4, 5
    )
    arranged = jnp.roll(arranged.reshape(clip_total, GT, GF, channels), (SHIFT, SHIFT), axis=(1, 2))
    return arranged.reshape(clip_total, GT * GF, channels)


def attend(queries, key_rows, values, allowed, scaling):
    scores = score_product(queries, key_rows) * scaling
    scores = jnp.where(allowed, scores, -1e30)
    scores = scores - jnp.max(scores, axis=-1, keepdims=True)
    exponent = jnp.exp(scores)
    softmax_rows = exponent / jnp.sum(exponent, axis=-1, keepdims=True)
    return value_product(softmax_rows, values)


def encode(weights, patches, keep, counts):
    pieces = unpack(weights[10])
    clip_total = patches.shape[0]
    picked = jnp.take_along_axis(patches, keep[:, :, None], axis=1)
    hidden = product(picked, weights[8][:, :D]) + pieces[11] + sinusoid(D)[keep]
    normed = layer_norm(hidden, pieces[0], pieces[1])
    joined = product(normed, weights[0])
    queries = (joined[..., :D] + pieces[2]).reshape(clip_total, VIS, HEADS, HEAD)
    key_rows = joined[..., D : 2 * D].reshape(clip_total, VIS, HEADS, HEAD)
    values = (joined[..., 2 * D :] + pieces[3]).reshape(clip_total, VIS, HEADS, HEAD)
    visible = (jnp.arange(VIS)[None, :] < counts[:, None])[:, None, None, :]
    attended = attend(queries, key_rows, values, visible, HEAD ** (-0.5)).reshape(
        clip_total, VIS, D
    )
    hidden = hidden + product(attended, weights[1]) + pieces[4]
    normed = layer_norm(hidden, pieces[5], pieces[6])
    inner = jax.nn.gelu(product(normed, weights[2]) + pieces[7], approximate=False)
    hidden = hidden + product(inner, weights[3]) + pieces[8]
    return layer_norm(hidden, pieces[9], pieces[10])


def decode(weights, latent, patches, keep, counts):
    pieces = unpack(weights[10])[12:]
    clip_total = latent.shape[0]
    placed = product(latent, weights[9]) + pieces[0]
    visible = jnp.arange(VIS)[None, :] < counts[:, None]
    target_rows = jnp.where(visible, keep, NPATCH)
    clip_rows = jnp.arange(clip_total)[:, None]
    filled = (
        jnp.zeros((clip_total, NPATCH + 1, DD), jnp.float32)
        .at[clip_rows, target_rows]
        .add(placed)[:, :NPATCH]
    )
    visible_cells = (
        jnp.zeros((clip_total, NPATCH + 1), jnp.float32)
        .at[clip_rows, target_rows]
        .add(1.0)[:, :NPATCH]
    )
    hidden = filled + (1.0 - visible_cells)[..., None] * pieces[1] + sinusoid(DD)
    normed = layer_norm(hidden, pieces[2], pieces[3])
    windows = to_windows(product(normed, weights[4]))
    queries = (windows[..., :DD] + pieces[4]).reshape(-1, WIN * WIN, DHEADS, DHEAD)
    key_rows = windows[..., DD : 2 * DD].reshape(-1, WIN * WIN, DHEADS, DHEAD)
    values = (windows[..., 2 * DD :] + pieces[5]).reshape(-1, WIN * WIN, DHEADS, DHEAD)
    allowed = jnp.tile(window_mask(), (clip_total, 1, 1))[:, None, :, :]
    attended = attend(queries, key_rows, values, allowed, DHEAD ** (-0.5)).reshape(
        -1, WIN * WIN, DD
    )
    hidden = hidden + product(from_windows(attended, clip_total), weights[5]) + pieces[6]
    normed = layer_norm(hidden, pieces[7], pieces[8])
    inner = jax.nn.gelu(product(normed, weights[6]) + pieces[9], approximate=False)
    hidden = hidden + product(inner, weights[7]) + pieces[10]
    normed = layer_norm(hidden, pieces[11], pieces[12])
    predicted = product(normed, weights[8][:, D:].T) + pieces[13]
    centred = patches - jnp.mean(patches, axis=-1, keepdims=True)
    target = centred * lax.rsqrt(jnp.mean(centred * centred, axis=-1, keepdims=True) + 1e-06)
    deviation = predicted - target
    patch_error = jnp.mean(deviation * deviation, axis=-1)
    return jnp.sum((1.0 - visible_cells) * patch_error)


def take_half(shard, number, core):
    if LONG_COLS[number]:
        extent = shard.shape[1] // 2
        return lax.dynamic_slice_in_dim(shard, core * extent, extent, 1)
    extent = shard.shape[0] // 2
    return lax.dynamic_slice_in_dim(shard, core * extent, extent, 0)


def arrange(gathered_half, number, long_max, short_max):
    upright = gathered_half.T if LONG_COLS[number] else gathered_half
    return jnp.pad(upright, ((0, long_max - upright.shape[0]), (0, short_max - upright.shape[1])))


def disperse(iterate, number, height, breadth, devices, flat_max):
    if LONG_COLS[number]:
        piece = iterate[: breadth // 2, :height].T.reshape(
            devices, height // devices * (breadth // 2)
        )
    else:
        piece = iterate[: height // 2, :breadth].reshape(devices, height // 2 // devices * breadth)
    return jnp.pad(piece, ((0, 0), (0, flat_max - piece.shape[1])))


def restore(row_piece, number, height, breadth, devices):
    if LONG_COLS[number]:
        return row_piece[: height // devices * (breadth // 2)].reshape(
            height // devices, breadth // 2
        )
    return row_piece[: height // 2 // devices * breadth].reshape(height // 2 // devices, breadth)


def adam_update(weight, first_moment, second_moment, gradient, decay):
    first_moment = 0.5 * first_moment + 0.5 * gradient
    second_moment = 0.95 * second_moment + 0.05 * gradient * gradient
    direction = (
        first_moment / (1.0 - 0.5**STEP) / (jnp.sqrt(second_moment / (1.0 - 0.95**STEP)) + 1e-08)
    )
    return (weight - LR_ADAM * (direction + decay * weight), first_moment, second_moment)


MESH_ID = pl.DeviceIdType.MESH
VEC_ROWS, VEC_COLS = 16, 256
AXIS_ORDERS = ((0, 1, 2, 3), (0, 1, 3, 2), (0, 2, 1, 3), (0, 2, 3, 1), (0, 3, 1, 2), (0, 3, 2, 1), (1, 0, 2, 3), (1, 0, 3, 2), (1, 2, 0, 3), (1, 2, 3, 0), (1, 3, 0, 2), (1, 3, 2, 0), (2, 0, 1, 3), (2, 0, 3, 1), (2, 1, 0, 3), (2, 1, 3, 0), (2, 3, 0, 1), (2, 3, 1, 0), (3, 0, 1, 2), (3, 0, 2, 1), (3, 1, 0, 2), (3, 1, 2, 0), (3, 2, 0, 1), (3, 2, 1, 0))
GATHER_PARTS = (3, 1, 4, 4, 1, 1, 2, 2, 1, 1, 1)
REDUCE_PARTS = (3, 1, 4, 4, 2, 1, 2, 2, 1, 1, 1)
TALL = (3, 7)
GATHER_TURNS = (19, 18, 22, 17, 13, 21, 22, 20, 3, 12, 11, 0, 17, 23, 16, 10, 23, 16, 11, 21, 21)
GATHER_FIRST = (6, 17, 20, 11, 7, 16, 8, 13, 12, 1, 4, 9, 19, 10, 3, 2, 15, 5, 0, 14, 18)
GATHER_STEPS = ((20, 11, 17, 6, 8, 10, 13, 15, 7, 16, 18, 19, 4, 1, 12, 9, 3, 2, 5, 14, 0), (20, 11, 7, 19, 4, 1, 17, 9, 6, 13, 8, 5, 0, 10, 16, 18, 15, 12, 3, 2, 14), (20, 7, 1, 17, 9, 13, 6, 16, 15, 11, 19, 4, 3, 12, 2, 8, 14, 10, 18, 5, 0), (20, 17, 13, 16, 6, 19, 7, 3, 4, 2, 1, 14, 12, 8, 18, 9, 10, 5, 15, 0, 11))
REDUCE_TURNS = (14, 1, 1, 6, 7, 2, 12, 8, 20, 3, 21, 6, 6, 0, 0, 21, 10, 13, 2, 0, 17, 4)
REDUCE_FIRST = (17, 21, 12, 9, 15, 18, 19, 4, 3, 11, 1, 10, 13, 20, 0, 7, 5, 16, 8, 14, 6, 2)
REDUCE_STEPS = ((21, 17, 12, 9, 19, 15, 18, 4, 20, 3, 11, 10, 1, 0, 7, 14, 16, 5, 8, 13, 6, 2), (21, 17, 19, 15, 9, 12, 10, 14, 1, 20, 0, 18, 4, 8, 3, 7, 11, 13, 2, 16, 6, 5), (21, 17, 19, 20, 15, 18, 9, 14, 0, 10, 12, 8, 7, 16, 1, 6, 4, 5, 3, 11, 13, 2), (21, 17, 20, 15, 9, 19, 10, 18, 14, 0, 12, 8, 1, 16, 7, 6, 4, 5, 3, 2, 13, 11))
OWNERS = (4, 11, 5, 10, 6, 9, 7, 8)
SLOTS = 160
GROUPS = 4


def bit_count(devices):
    return devices.bit_length() - 1


def cut_pieces(parts, shapes):
    found = []
    for number, count in enumerate(parts):
        rows, width = shapes[number]
        for part in range(count):
            if number in TALL:
                found.append((number, part * (rows // count), rows // count, 0, width))
            else:
                found.append((number, 0, rows, part * (width // count), width // count))
    return found


def own_bits(levels):
    me = lax.axis_index("dp")
    return me, [lax.rem(lax.div(me, 2**bit), 2) for bit in range(levels)]


def place(levels, free, own, flip=None):
    spots = []
    for bit in range(levels - 1, -1, -1):
        if bit in free:
            spots.append(slice(None))
        elif bit == flip:
            spots.append(1 - own[bit])
        else:
            spots.append(own[bit])
    return tuple(spots)


def partner(me, own, bit):
    return me + (1 - 2 * own[bit]) * 2**bit


def greet(me, own, levels, core):
    barrier = pltpu.get_barrier_semaphore()
    for bit in range(levels):
        pl.semaphore_signal(
            barrier,
            inc=1,
            device_id={"dp": partner(me, own, bit), "mp": core},
            device_id_type=MESH_ID,
        )
    pl.semaphore_signal(barrier, inc=1, device_id={"dp": me, "mp": 1 - core}, device_id_type=MESH_ID)
    pl.semaphore_wait(barrier, levels + 1)


def add_up(me, core, devices, total, landing, send_sem, recv_sem, own_sem):
    def send(source, target):
        return pltpu.make_async_remote_copy(
            src_ref=total,
            dst_ref=landing.at[source],
            send_sem=send_sem.at[target],
            recv_sem=recv_sem.at[source],
            device_id={"dp": target, "mp": core},
            device_id_type=MESH_ID,
        )

    @pl.loop(0, devices)
    def start_one(other):
        @pl.when(other != me)
        def start_other():
            send(me, other).start()

    own = pltpu.make_async_copy(total, landing.at[me], own_sem)
    own.start()
    own.wait()

    @pl.loop(0, devices)
    def wait_one(other):
        @pl.when(other != me)
        def wait_other():
            send(other, me).wait_recv()
            send(me, other).wait_send()

    found = landing[0]
    for device in range(1, devices):
        found = found + landing[device]
    total[...] = found
    swap = pltpu.make_async_remote_copy(
        src_ref=total,
        dst_ref=landing.at[devices],
        send_sem=send_sem.at[devices],
        recv_sem=recv_sem.at[devices],
        device_id={"dp": me, "mp": 1 - core},
        device_id_type=MESH_ID,
    )
    swap.start()
    swap.wait()
    total[...] = total[...] + landing[devices]


def cut_patches(lines, spots, take, freq, fold, table, picked_out, where_out, target_out):
    part = 512
    lane = lax.broadcasted_iota(jnp.int32, (NPATCH, part), 1)
    inside = lax.rem(lax.div(lane, PS), GF) == freq[...]
    for clip in range(lines.shape[0]):
        patches = jnp.zeros((NPATCH, PATCH), jnp.float32)
        for start in range(0, PS * GF * PS, part):
            spread = jnp.dot(
                take[...], lines[clip, :, start : start + part], preferred_element_type=jnp.float32
            )
            spread = jnp.where(inside, spread, 0.0).astype(jnp.bfloat16)
            patches = patches + jnp.dot(
                spread, fold[start : start + part, :], preferred_element_type=jnp.float32
            )
        slot = lax.broadcasted_iota(jnp.int32, (NPATCH, SLOTS), 0)
        chosen = jnp.where(slot == spots[clip : clip + 1, :], 1.0, 0.0).astype(jnp.bfloat16)
        picked_out[clip] = dot_columns(chosen, patches.astype(jnp.bfloat16)).astype(jnp.bfloat16)
        where_out[clip] = dot_columns(chosen, table[:, :D]) + dot_columns(chosen, table[:, D:])
        centred = patches - jnp.mean(patches, axis=-1, keepdims=True)
        spread = jnp.mean(centred * centred, axis=-1, keepdims=True)
        target_out[clip] = centred * lax.rsqrt(spread + 1e-06)


def gather_kernel(levels, pieces, count, *refs):
    sources, tally, rest = refs[:count] + refs[count + 1 : count + 7], refs[count], refs[count + 7 :]
    outs, count_out, made, rest = rest[:count], rest[count], rest[count + 1 : count + 4], rest[count + 4 :]
    tally_out, rest = rest[0], rest[1:]
    wholes, save_sem, rest = rest[:count], rest[count], rest[count + 1 :]
    short, held, load_sem, rest = rest[:count], rest[count : 2 * count + 6], rest[2 * count + 6], rest[2 * count + 7 :]
    shards, scene = held[:count], held[count:]

    def load(number):
        return pltpu.make_async_copy(sources[number], held[number], load_sem.at[number])

    for number in range(count + 6):
        load(number).start()
    here_sem, send_sem, recv_sem, cross_send, cross_recv, tally_land, tally_send, tally_recv = rest
    me, own = own_bits(levels)
    core = lax.axis_index("mp")
    greet(me, own, levels, core)
    orders = [AXIS_ORDERS[turn] for turn in GATHER_TURNS]

    def cut(piece, which):
        number, row, rows, column, columns = pieces[piece]
        width = shards[number].shape[1] // 2
        return (pl.ds(row, rows), pl.ds(pl.multiple_of(which * width + column, 128), columns))

    def hop(piece, stage, flip):
        order, number = orders[piece], pieces[piece][0]
        spot = place(levels, order[:stage], own, order[stage] if flip else None)
        target = wholes[number].at[spot + cut(piece, core)]
        source = target if stage or flip else short[number].at[cut(piece, core)]
        return pltpu.make_async_remote_copy(
            src_ref=source,
            dst_ref=target,
            send_sem=send_sem.at[piece, stage],
            recv_sem=recv_sem.at[piece, stage],
            device_id={"dp": partner(me, own, order[stage]), "mp": core},
            device_id_type=MESH_ID,
        )

    def cross(piece, stage, which):
        order, number = orders[piece], pieces[piece][0]
        spot = place(levels, order[:stage], own, order[stage])
        target = wholes[number].at[spot + cut(piece, which)]
        return pltpu.make_async_remote_copy(
            src_ref=target,
            dst_ref=target,
            send_sem=cross_send.at[piece, stage],
            recv_sem=cross_recv.at[piece, stage],
            device_id={"dp": me, "mp": 1 - core},
            device_id_type=MESH_ID,
        )

    def keep(number):
        spot = place(levels, (), own)
        return pltpu.make_async_copy(short[number], wholes[number].at[spot], here_sem.at[number])

    ready = set()
    for piece in GATHER_FIRST:
        number = pieces[piece][0]
        if number not in ready:
            ready.add(number)
            load(number).wait()
            short[number][...] = shards[number][...].astype(jnp.bfloat16)
            keep(number).start()
        hop(piece, 0, False).start()
    masked = jnp.int32(0)
    for clip in range(tally.shape[0]):
        masked = masked + (NPATCH - tally[clip])
    corner = lax.broadcasted_iota(jnp.int32, (8, 128), 0) + lax.broadcasted_iota(jnp.int32, (8, 128), 1) == 0
    tally_out[...] = jnp.where(corner, masked.astype(jnp.float32), 0.0)

    def swap(stage):
        if stage < levels:
            to = {"dp": partner(me, own, stage), "mp": core}
        else:
            to = {"dp": me, "mp": 1 - core}
        return pltpu.make_async_remote_copy(
            src_ref=tally_out,
            dst_ref=tally_land.at[stage],
            send_sem=tally_send.at[stage],
            recv_sem=tally_recv.at[stage],
            device_id=to,
            device_id_type=MESH_ID,
        )

    def swap_end(stage):
        swap(stage).wait()
        tally_out[...] = tally_out[...] + tally_land[stage]

    swap(levels).start()
    for number in range(count):
        keep(number).wait()
    swap_end(levels)
    for stage, order in enumerate(GATHER_STEPS):
        swap(stage).start()
        for piece in order:
            hop(piece, stage, True).wait_recv()
            if stage + 1 < levels:
                hop(piece, stage + 1, False).start()
            cross(piece, stage, core).start()
        swap_end(stage)
        if stage == levels - 2:
            for number in range(6):
                load(count + number).wait()
            cut_patches(*scene, *made)
    def save(number):
        return pltpu.make_async_copy(wholes[number], outs[number], save_sem.at[number])

    last = {}
    for place_in, piece in enumerate(GATHER_STEPS[levels - 1]):
        last[pieces[piece][0]] = place_in
    for number in sorted(last, key=lambda found: last[found]):
        for piece in range(len(pieces)):
            if pieces[piece][0] == number:
                for stage in range(levels):
                    cross(piece, stage, 1 - core).wait_recv()
        save(number).start()
    for piece in range(len(pieces)):
        for stage in range(levels):
            hop(piece, stage, False).wait_send()
            cross(piece, stage, core).wait_send()
    count_out[...] = tally_out[0:1, 0:1]
    for number in range(count):
        save(number).wait()


def gather_rows(shards, tally, scene, devices):
    levels, count = bit_count(devices), len(shards)
    lead = (2,) * levels
    clips = scene[0].shape[0]
    pieces = cut_pieces(GATHER_PARTS, [(shard.shape[0], shard.shape[1] // 2) for shard in shards])
    dma = pltpu.SemaphoreType.DMA
    vmem, far = pl.BlockSpec(memory_space=pltpu.VMEM), pl.BlockSpec(memory_space=pltpu.HBM)
    found = pl.pallas_call(
        functools.partial(gather_kernel, levels, pieces, count),
        out_shape=[jax.ShapeDtypeStruct(lead + shard.shape, jnp.bfloat16) for shard in shards]
        + [
            jax.ShapeDtypeStruct((1, 1), jnp.float32),
            jax.ShapeDtypeStruct((clips, SLOTS, PATCH), jnp.bfloat16),
            jax.ShapeDtypeStruct((clips, SLOTS, D), jnp.float32),
            jax.ShapeDtypeStruct((clips, NPATCH, PATCH), jnp.float32),
        ],
        in_specs=[far] * count + [pl.BlockSpec(memory_space=pltpu.SMEM)] + [far] * 6,
        out_specs=[pl.BlockSpec(memory_space=pl.ANY)] * count + [vmem] * 4,
        scratch_shapes=[pltpu.VMEM((8, 128), jnp.float32)]
        + [pltpu.VMEM(lead + shard.shape, jnp.bfloat16) for shard in shards]
        + [dma((count,))]
        + [pltpu.VMEM(shard.shape, jnp.bfloat16) for shard in shards]
        + [pltpu.VMEM(piece.shape, piece.dtype) for piece in (*shards, *scene)]
        + [dma((count + 6,))]
        + [dma((count,))]
        + [dma((len(pieces), levels))] * 4
        + [pltpu.VMEM((levels + 1, 8, 128), jnp.float32)]
        + [dma((levels + 1,))] * 2,
        compiler_params=pltpu.CompilerParams(
            collective_id=1, has_side_effects=True, vmem_limit_bytes=60 * 2**20
        ),
        name="gather_rows",
    )(*shards, tally, *scene)
    return found[:count], found[count], found[count + 1 :]


def reduce_kernel(levels, pieces, count, owners, devices, *refs):
    blocks = len(owners)
    grads, stats_in, old = refs[:count], refs[count], refs[count + 1 : count + 1 + blocks]
    rest = refs[count + 1 + blocks :]
    sums, stats_out, wholes = rest[:count], rest[count], rest[count + 1 : count + 1 + blocks]
    rest = rest[count + 1 + blocks :]
    mine, theirs, rest = rest[:count], rest[count : 2 * count], rest[2 * count :]
    kept, rest = rest[:count], rest[count:]
    landing, rest = rest[: len(pieces) * levels], rest[len(pieces) * levels :]
    staged, rest = rest[:blocks], rest[blocks:]
    stats_land, here_sem, pair_send, pair_recv, send_sem, recv_sem, last_send, last_recv = rest[:8]
    stats_send, stats_recv, own_sem, out_send, out_recv, cross_send, cross_recv = rest[8:]
    me, own = own_bits(levels)
    core = lax.axis_index("mp")
    orders = [AXIS_ORDERS[turn] for turn in REDUCE_TURNS]
    barrier = pltpu.get_barrier_semaphore()

    @pl.loop(0, devices)
    def greet_one(other):
        @pl.when(other != me)
        def signal_one():
            pl.semaphore_signal(
                barrier, inc=1, device_id={"dp": other, "mp": core}, device_id_type=MESH_ID
            )

    pl.semaphore_signal(barrier, inc=1, device_id={"dp": me, "mp": 1 - core}, device_id_type=MESH_ID)
    pl.semaphore_wait(barrier, devices)

    def half(number, which):
        width = sums[number].shape[1] // 2
        return (slice(None), pl.ds(pl.multiple_of(which * width, 128), width))

    def cut(piece):
        number, row, rows, column, columns = pieces[piece]
        return (pl.ds(row, rows), pl.ds(column, columns))

    def side(piece, which):
        number, row, rows, column, columns = pieces[piece]
        width = sums[number].shape[1] // 2
        return (pl.ds(row, rows), pl.ds(pl.multiple_of(which * width + column, 128), columns))

    every = (slice(None),) * levels

    def pair(piece):
        number = pieces[piece][0]
        return pltpu.make_async_remote_copy(
            src_ref=grads[number].at[every + side(piece, 1 - core)],
            dst_ref=theirs[number].at[every + cut(piece)],
            send_sem=pair_send.at[piece],
            recv_sem=pair_recv.at[piece],
            device_id={"dp": me, "mp": 1 - core},
            device_id_type=MESH_ID,
        )

    def load(piece):
        number = pieces[piece][0]
        return pltpu.make_async_copy(
            grads[number].at[every + side(piece, core)],
            mine[number].at[every + cut(piece)],
            here_sem.at[piece],
        )

    def hop(piece, stage):
        order = orders[piece]
        spot = place(levels, order[stage + 1 :], own, order[stage])
        return pltpu.make_async_remote_copy(
            src_ref=theirs[pieces[piece][0]].at[spot + cut(piece)],
            dst_ref=landing[piece * levels + stage],
            send_sem=send_sem.at[piece, stage],
            recv_sem=recv_sem.at[piece, stage],
            device_id={"dp": partner(me, own, order[stage]), "mp": core},
            device_id_type=MESH_ID,
        )

    def share(number, which):
        region = sums[number].at[half(number, which)]
        return pltpu.make_async_remote_copy(
            src_ref=region,
            dst_ref=region,
            send_sem=last_send.at[number],
            recv_sem=last_recv.at[number],
            device_id={"dp": me, "mp": 1 - core},
            device_id_type=MESH_ID,
        )

    def deliver(number, source):
        return pltpu.make_async_remote_copy(
            src_ref=staged[number],
            dst_ref=wholes[number].at[(source,) + half(number, core)],
            send_sem=out_send.at[number],
            recv_sem=out_recv.at[number, source],
            device_id={"dp": owners[number], "mp": core},
            device_id_type=MESH_ID,
        )

    def deliver_here(number):
        return pltpu.make_async_copy(
            staged[number], wholes[number].at[(me,) + half(number, core)], own_sem
        )

    def cross(number, source, which):
        region = wholes[number].at[(source,) + half(number, which)]
        return pltpu.make_async_remote_copy(
            src_ref=region,
            dst_ref=region,
            send_sem=cross_send.at[number, source],
            recv_sem=cross_recv.at[number, source],
            device_id={"dp": me, "mp": 1 - core},
            device_id_type=MESH_ID,
        )

    def kept_spot(order, found):
        return tuple(found.get(bit, own[bit]) for bit in range(levels - 1, -1, -1) if bit != order[0])

    def fold(piece, stage):
        order, number = orders[piece], pieces[piece][0]
        free = order[stage:]
        loose = [bit for bit in range(levels - 1, -1, -1) if bit in free and bit != order[stage]]
        region = cut(piece)

        @pl.loop(0, 2 ** len(loose))
        def add_block(block):
            found = {
                bit: lax.rem(lax.div(block, 2 ** (len(loose) - 1 - i)), 2) for i, bit in enumerate(loose)
            }

            def total(way):
                now = dict(found)
                now[order[stage]] = way
                full = tuple(now.get(bit, own[bit]) for bit in range(levels - 1, -1, -1)) + region
                if stage == 0:
                    value = mine[number][full].astype(jnp.float32) + theirs[number][full].astype(jnp.float32)
                else:
                    land = tuple(now[bit] for bit in range(levels - 1, -1, -1) if bit in free)
                    arrived = landing[piece * levels + stage - 1][land].astype(jnp.float32)
                    value = kept[number][kept_spot(order, now) + region] + arrived
                return full, value

            full, value = total(1 - own[order[stage]])
            theirs[number][full] = value.astype(theirs[number].dtype)
            full, value = total(own[order[stage]])
            kept[number][kept_spot(order, found) + region] = value

    for piece in REDUCE_FIRST:
        pair(piece).start()
        load(piece).start()
    for piece in REDUCE_FIRST:
        load(piece).wait()
        pair(piece).wait_recv()
        fold(piece, 0)
        hop(piece, 0).start()
    squares = jnp.zeros((8, 128), jnp.float32)
    for piece, stage in [(piece, stage) for stage in range(levels) for piece in REDUCE_STEPS[stage]]:
        hop(piece, stage).wait_recv()
        if stage + 1 < levels:
            fold(piece, stage + 1)
            hop(piece, stage + 1).start()
        else:
            number = pieces[piece][0]
            arrived = landing[piece * levels + stage][...].astype(jnp.float32)
            total = kept[number][kept_spot(orders[piece], {}) + cut(piece)] + arrived
            sums[number][side(piece, core)] = total
            rows, width = total.shape
            for row in range(0, rows, 8):
                for column in range(0, width, 128):
                    part = total[row : row + 8, column : column + 128]
                    squares = squares + part * part
    for number in range(blocks, count):
        share(number, core).start()
    row = lax.broadcasted_iota(jnp.int32, (8, 128), 0)
    others = jnp.where(row == 1, stats_in[...], 0.0)
    stats_out[...] = jnp.where(row == 0, jnp.sum(squares, axis=0, keepdims=True), others)
    add_up(me, core, devices, stats_out, stats_land, stats_send, stats_recv, own_sem)
    norm = jnp.sqrt(jnp.sum(stats_out[0:1, :], axis=1, keepdims=True))
    factor = jnp.minimum(1.0, CLIP_MAX / (norm + 1e-06))
    for number in range(blocks):
        region = half(number, core)
        renewed = 0.5 * old[number][region] + factor * sums[number][region]
        sums[number][region] = renewed
        staged[number][...] = renewed.astype(staged[number].dtype)
        share(number, core).start()

        @pl.when(me != owners[number])
        def start_one(number=number):
            deliver(number, me).start()

        @pl.when(me == owners[number])
        def start_here(number=number):
            deliver_here(number).start()

    for piece in range(len(pieces)):
        pair(piece).wait_send()
        for stage in range(levels):
            hop(piece, stage).wait_send()
    for number in range(blocks):

        @pl.when(me == owners[number])
        def collect(number=number):
            deliver_here(number).wait()

            @pl.loop(0, devices)
            def forward(source):
                @pl.when(source != me)
                def arrived():
                    deliver(number, source).wait_recv()

                cross(number, source, core).start()

            @pl.loop(0, devices)
            def finish(source):
                cross(number, source, core).wait_send()
                cross(number, source, 1 - core).wait_recv()

        @pl.when(me != owners[number])
        def end_one(number=number):
            deliver(number, me).wait_send()

    for number in range(count):
        share(number, core).wait_send()
        share(number, 1 - core).wait_recv()


def reduce_rows(grads, stats, old, owners, devices):
    levels, count, blocks = bit_count(devices), len(grads), len(old)
    lead = (2,) * levels
    dma = pltpu.SemaphoreType.DMA
    shapes = [grad.shape[levels:] for grad in grads]
    halves = [(rows, columns // 2) for rows, columns in shapes]
    kinds = [grad.dtype for grad in grads]
    pieces = cut_pieces(REDUCE_PARTS, halves)
    scratch = [pltpu.VMEM(lead + shape, kind) for shape, kind in zip(halves, kinds)] * 2
    scratch += [pltpu.VMEM(lead[1:] + shape, jnp.float32) for shape in halves]
    for number, row, rows, column, columns in pieces:
        for stage in range(levels):
            scratch.append(pltpu.VMEM((2,) * (levels - 1 - stage) + (rows, columns), kinds[number]))
    scratch += [pltpu.VMEM(halves[number], kinds[number]) for number in range(blocks)]
    scratch.append(pltpu.VMEM((devices + 1, 8, 128), jnp.float32))
    scratch += [dma((len(pieces),))] * 3 + [dma((len(pieces), levels))] * 2 + [dma((count,))] * 2
    scratch += [dma((devices + 1,))] * 2 + [dma, dma((blocks,))] + [dma((blocks, devices))] * 3
    vmem, anywhere = pl.BlockSpec(memory_space=pltpu.VMEM), pl.BlockSpec(memory_space=pl.ANY)
    found = pl.pallas_call(
        functools.partial(reduce_kernel, levels, pieces, count, owners, devices),
        out_shape=[jax.ShapeDtypeStruct(shape, jnp.float32) for shape in shapes]
        + [jax.ShapeDtypeStruct((8, 128), jnp.float32)]
        + [jax.ShapeDtypeStruct((devices,) + shapes[number], kinds[number]) for number in range(blocks)],
        in_specs=[anywhere] * count + [vmem] * (1 + blocks),
        out_specs=[vmem] * (count + 1) + [anywhere] * blocks,
        scratch_shapes=scratch,
        compiler_params=pltpu.CompilerParams(
            collective_id=2, has_side_effects=True, vmem_limit_bytes=60 * 2**20
        ),
        name="reduce_rows",
    )(*grads, stats, *old)
    return found[:blocks], found[blocks:count], found[count], found[count + 1 :]


def return_kernel(owners, count, devices, *refs):
    wholes, rows = refs[:count], refs[count : 2 * count]
    here_sem, send_sem, recv_sem, cross_send, cross_recv = refs[2 * count :]
    me, core = lax.axis_index("dp"), lax.axis_index("mp")
    barrier = pltpu.get_barrier_semaphore()
    owning = functools.reduce(jnp.logical_or, [me == owner for owner in owners])
    for owner in owners:

        @pl.when(me != owner)
        def greet_owner(owner=owner):
            pl.semaphore_signal(
                barrier, inc=1, device_id={"dp": owner, "mp": core}, device_id_type=MESH_ID
            )

    pl.semaphore_signal(barrier, inc=1, device_id={"dp": me, "mp": 1 - core}, device_id_type=MESH_ID)

    @pl.when(owning)
    def wait_all():
        pl.semaphore_wait(barrier, devices)

    @pl.when(jnp.logical_not(owning))
    def wait_pair():
        pl.semaphore_wait(barrier, 1)

    def half(number, which):
        width = rows[number].shape[1] // 2
        return (slice(None), pl.ds(pl.multiple_of(which * width, 128), width))

    def hop(number, target):
        return pltpu.make_async_remote_copy(
            src_ref=wholes[number].at[(target,) + half(number, core)],
            dst_ref=rows[number].at[half(number, core)],
            send_sem=send_sem.at[number, target],
            recv_sem=recv_sem.at[number],
            device_id={"dp": target, "mp": core},
            device_id_type=MESH_ID,
        )

    def cross(number, which):
        region = rows[number].at[half(number, which)]
        return pltpu.make_async_remote_copy(
            src_ref=region,
            dst_ref=region,
            send_sem=cross_send.at[number],
            recv_sem=cross_recv.at[number],
            device_id={"dp": me, "mp": 1 - core},
            device_id_type=MESH_ID,
        )

    for number in range(count):

        @pl.when(me == owners[number])
        def hand_out(number=number):
            own = pltpu.make_async_copy(
                wholes[number].at[(me,) + half(number, core)], rows[number].at[half(number, core)], here_sem
            )
            own.start()

            @pl.loop(0, devices)
            def start_one(target):
                @pl.when(target != me)
                def start_other():
                    hop(number, target).start()

            own.wait()

    for number in range(count):

        @pl.when(me != owners[number])
        def arrive(number=number):
            hop(number, me).wait_recv()

        cross(number, core).start()
    for number in range(count):
        cross(number, core).wait_send()
        cross(number, 1 - core).wait_recv()

        @pl.when(me == owners[number])
        def end_out(number=number):
            @pl.loop(0, devices)
            def end_one(target):
                @pl.when(target != me)
                def end_other():
                    hop(number, target).wait_send()


def return_rows(wholes, owners, devices):
    count = len(wholes)
    dma = pltpu.SemaphoreType.DMA
    vmem = pl.BlockSpec(memory_space=pltpu.VMEM)
    return pl.pallas_call(
        functools.partial(return_kernel, owners, count, devices),
        out_shape=[jax.ShapeDtypeStruct(whole.shape[1:], whole.dtype) for whole in wholes],
        in_specs=[pl.BlockSpec(memory_space=pl.ANY)] * count,
        out_specs=[vmem] * count,
        scratch_shapes=[dma, dma((count, devices)), dma((count,)), dma((count,)), dma((count,))],
        compiler_params=pltpu.CompilerParams(
            collective_id=4, has_side_effects=True, vmem_limit_bytes=60 * 2**20
        ),
        name="return_rows",
    )(*wholes)


def finish_kernel(count, rates, *refs):
    rows, masters, updated = refs[:count], refs[count : 2 * count], refs[2 * count :]
    for number in range(count):
        change = rates[number] * rows[number][...].astype(jnp.float32)
        updated[number][...] = masters[number][...] * (1.0 - LR_MUON * DECAY) - change


def finish(rows, masters, devices):
    count = len(rows)
    rates = []
    for master in masters:
        rates.append(LR_MUON * 0.2 * math.sqrt(max(master.shape[0] * devices, master.shape[1])))
    vmem = pl.BlockSpec(memory_space=pltpu.VMEM)
    return pl.pallas_call(
        functools.partial(finish_kernel, count, rates),
        out_shape=[jax.ShapeDtypeStruct(master.shape, jnp.float32) for master in masters],
        in_specs=[vmem] * (2 * count),
        out_specs=[vmem] * count,
        compiler_params=pltpu.CompilerParams(vmem_limit_bytes=56 * 2**20),
        name="finish",
    )(*rows, *masters)


def muon_kernel(owners, shapes, *refs):
    count = len(owners)
    mats, moved, stats, adam_in = refs[:count], refs[count : 2 * count], refs[2 * count], refs[2 * count + 1 :][:8]
    rest = refs[2 * count + 9 :]
    outs, moved_out, adam_out, rest = rest[:count], rest[count : 2 * count], rest[2 * count :][:6], rest[2 * count + 6 :]
    norm_out, loss_out, rest = rest[0], rest[1], rest[2:]
    exact, wide, wide_low, tall, wide_out, tall_out, gram = rest[:7]
    base, poly, other, chain, sem, in_sem, out_sem = rest[7:14]
    held_rows = rest[14:]

    def move_in(number):
        return pltpu.make_async_copy(moved[number], held_rows[number], in_sem.at[number])

    def move_out(number):
        return pltpu.make_async_copy(held_rows[number], moved_out[number], out_sem.at[number])

    for number in range(count):
        move_in(number).start()
    norm = jnp.sqrt(jnp.sum(stats[0:1, :], axis=1, keepdims=True))
    factor = jnp.minimum(1.0, CLIP_MAX / (norm + 1e-06))
    norm_out[...] = norm
    loss_out[...] = stats[1:2, 0:1]
    for group in range(2):
        weight, first, second, grad = [ref[...] for ref in adam_in[4 * group : 4 * group + 4]]
        made = adam_update(weight, first, second, grad * factor, DECAY)
        for place_out in range(3):
            adam_out[3 * group + place_out][...] = made[place_out]
    me, core = lax.axis_index("dp"), lax.axis_index("mp")
    side = gram.shape[0]
    step = 256
    bf = jnp.bfloat16

    def dims(number):
        height, breadth = shapes[number]
        return height, breadth, LONG_COLS[number]

    def span(index):
        return pl.ds(pl.multiple_of(index * step, step), step)

    def split(value):
        high = value.astype(bf)
        return high, (value - high.astype(jnp.float32)).astype(bf)

    gram[...] = jnp.zeros_like(gram)
    for number in range(count):

        @pl.when(me == owners[number])
        def start(number=number):
            height, breadth, long_cols = dims(number)
            short = min(height, breadth)
            held = (wide if long_cols else tall).at[:height, :breadth]
            fine = mats[number].dtype == jnp.float32
            load = pltpu.make_async_copy(mats[number], exact if fine else held, sem)
            load.start()
            load.wait()
            if fine:
                rest = wide_low

                @pl.loop(0, height // step)
                def part_rows(index):
                    high, low = split(exact[span(index), :])
                    held[span(index), :] = high
                    rest[span(index), :] = low

            for index in range(short // step):
                first, beyond = slice(index * step, (index + 1) * step), slice(index * step, short)
                if long_cols:
                    total = dot_rows(held[first, :], held[beyond, :])
                    if fine:
                        total = total + dot_rows(held[first, :], rest[beyond, :])
                        total = total + dot_rows(rest[first, :], held[beyond, :])
                else:
                    total = dot_columns(held[:, first], held[:, beyond])
                gram[first, beyond] = total

    for number in range(count):
        move_in(number).wait()
        move_out(number).start()
    owning = functools.reduce(jnp.logical_or, [me == owner for owner in owners])

    @pl.when(owning)
    def iterate():
        parts = [
            (slice(index * step, (index + 1) * step), slice(index * step, side))
            for index in range(side // step)
        ]
        ones = lax.broadcasted_iota(jnp.int32, (step, step), 0) == lax.broadcasted_iota(
            jnp.int32, (step, step), 1
        )
        trace = jnp.float32(0.0)
        for first, beyond in parts:
            trace = trace + jnp.sum(jnp.where(ones, gram[first, first], 0.0))
        scale = 1.0 / (jnp.sqrt(jnp.full((8, 128), trace, jnp.float32)) + 1e-07)
        scale = scale[0:1, 0:1]

        def store(target, index, value):
            high, low = split(value)
            target[0, parts[index][0], parts[index][1]] = high
            target[1, parts[index][0], parts[index][1]] = low
            for later in range(index + 1, side // step):
                shift = (later - index) * step
                high, low = split(value[:, shift : shift + step].T)
                target[0, parts[later][0], parts[index][0]] = high
                target[1, parts[later][0], parts[index][0]] = low

        def product(left, right, index):
            first, beyond = parts[index]
            high, low = left[0, first, :], left[1, first, :]
            total = jnp.dot(high, right[0, :, beyond], preferred_element_type=jnp.float32)
            total = total + jnp.dot(high, right[1, :, beyond], preferred_element_type=jnp.float32)
            return total + jnp.dot(low, right[0, :, beyond], preferred_element_type=jnp.float32)

        for index, (first, beyond) in enumerate(parts):
            store(base, index, gram[first, beyond] * (scale * scale))

        @pl.loop(0, NS_ITERS)
        def newton(iteration):
            for index, (first, beyond) in enumerate(parts):
                now = base[0, first, beyond].astype(jnp.float32) + base[1, first, beyond].astype(jnp.float32)
                row = lax.broadcasted_iota(jnp.int32, now.shape, 0)
                column = lax.broadcasted_iota(jnp.int32, now.shape, 1)
                value = jnp.where(row == column, NS_A, 0.0) + NS_B * now
                store(poly, index, value + NS_C * product(base, base, index))

            @pl.when(iteration < NS_ITERS - 1)
            def advance():
                for index in range(len(parts)):
                    store(other, index, product(base, poly, index))
                for index in range(len(parts)):
                    store(base, index, product(other, poly, index))

            @pl.when(iteration == 0)
            def begin():
                chain[...] = poly[...]

            @pl.when(iteration > 0)
            def follow():
                for index in range(len(parts)):
                    store(other, index, product(chain, poly, index))
                chain[...] = other[...]

        for first, beyond in parts:
            value = chain[0, first, :].astype(jnp.float32) + chain[1, first, :].astype(jnp.float32)
            high, low = split(value * scale)
            other[0, first, :] = high
            other[1, first, :] = low

    for number in range(count):

        @pl.when(me == owners[number])
        def end(number=number):
            height, breadth, long_cols = dims(number)
            short = min(height, breadth)
            width = breadth // 2
            part = pl.ds(pl.multiple_of(core * width, 128), width)
            if long_cols:
                held, made = wide.at[:height, :breadth], wide_out.at[:height, :width]

                @pl.loop(0, height // step)
                def wide_rows(index):
                    total = jnp.dot(
                        other[0, span(index), :short], held[:, part], preferred_element_type=jnp.float32
                    ) + jnp.dot(
                        other[1, span(index), :short], held[:, part], preferred_element_type=jnp.float32
                    )
                    if mats[number].dtype == jnp.float32:
                        total = total + jnp.dot(
                            other[0, span(index), :short],
                            wide_low[:, part],
                            preferred_element_type=jnp.float32,
                        )
                    made[span(index), :] = total.astype(bf)
            else:
                held, made = tall.at[:height, :breadth], tall_out.at[:height, :width]

                @pl.loop(0, height // step)
                def tall_rows(index):
                    total = jnp.dot(
                        held[span(index), :], other[0, :short, part], preferred_element_type=jnp.float32
                    ) + jnp.dot(
                        held[span(index), :], other[1, :short, part], preferred_element_type=jnp.float32
                    )
                    made[span(index), :] = total.astype(bf)

            save = pltpu.make_async_copy(made, outs[number].at[:, part], sem)
            save.start()
            save.wait()

    for number in range(count):
        move_out(number).wait()


def orthogonalize(mats, moved, stats, adam, owners):
    count = len(mats)
    shapes = [mat.shape for mat in mats]
    side = max(min(shape) for shape in shapes)
    longest = max(max(shape) for shape in shapes)
    double = pltpu.VMEM((2, side, side), jnp.bfloat16)
    (fine,) = [mat.shape for mat in mats if mat.dtype == jnp.float32]
    vmem, anywhere = pl.BlockSpec(memory_space=pltpu.VMEM), pl.BlockSpec(memory_space=pl.ANY)
    renewed = (adam[0], adam[1], adam[2], adam[4], adam[5], adam[6])
    found = pl.pallas_call(
        functools.partial(muon_kernel, owners, shapes),
        out_shape=[jax.ShapeDtypeStruct(shape, jnp.bfloat16) for shape in shapes]
        + [jax.ShapeDtypeStruct(piece.shape, piece.dtype) for piece in moved]
        + [jax.ShapeDtypeStruct(piece.shape, piece.dtype) for piece in renewed]
        + [jax.ShapeDtypeStruct((1, 1), jnp.float32)] * 2,
        in_specs=[anywhere] * (2 * count) + [vmem] * 9,
        out_specs=[anywhere] * (2 * count) + [vmem] * 8,
        scratch_shapes=[
            pltpu.VMEM(fine, jnp.float32),
            pltpu.VMEM((side, longest), jnp.bfloat16),
            pltpu.VMEM(fine, jnp.bfloat16),
            pltpu.VMEM((longest, side), jnp.bfloat16),
            pltpu.VMEM((side, longest // 2), jnp.bfloat16),
            pltpu.VMEM((longest, side // 2), jnp.bfloat16),
            pltpu.VMEM((side, side), jnp.float32),
            double,
            double,
            double,
            double,
            pltpu.SemaphoreType.DMA,
            pltpu.SemaphoreType.DMA((count,)),
            pltpu.SemaphoreType.DMA((count,)),
        ]
        + [pltpu.VMEM(piece.shape, piece.dtype) for piece in moved],
        compiler_params=pltpu.CompilerParams(vmem_limit_bytes=60 * 2**20),
        name="orthogonalize",
    )(*mats, *moved, stats, *adam)
    return found[:count], found[count : 2 * count], found[2 * count :]


def window_place(position):
    time_row = (position // GF + GT - SHIFT) % GT
    freq_col = (position % GF + GF - SHIFT) % GF
    window = (time_row // WIN) * (GF // WIN) + freq_col // WIN
    return window * (WIN * WIN) + (time_row % WIN) * WIN + freq_col % WIN


def window_sinusoid(channels):
    quarter = channels // 4
    frequency = 1.0 / 10000.0 ** (np.arange(quarter) / quarter)
    position = np.arange(NPATCH)
    time_rows = (position // GF)[:, None] * frequency
    freq_cols = (position % GF)[:, None] * frequency
    table = np.concatenate([np.sin(time_rows), np.cos(time_rows), np.sin(freq_cols), np.cos(freq_cols)], axis=1)
    moved = np.zeros_like(table)
    moved[window_place(position)] = table
    return moved.astype(np.float32)


def window_scene(spec, keep):
    position = np.arange(NPATCH)
    row = np.empty(NPATCH, np.int32)
    row[window_place(position)] = position
    take = (row[:, None] // GF == np.arange(GT)[None, :]).astype(np.float32)
    source = np.arange(PS * GF * PS)[:, None]
    target = np.arange(PATCH)[None, :]
    fold = np.logical_and(source // (GF * PS) == target // PS, source % PS == target % PS)
    table = window_sinusoid(D)
    high = table.astype(jnp.bfloat16)
    low = (table - high.astype(np.float32)).astype(jnp.bfloat16)
    return (
        spec.reshape(spec.shape[0], GT, PS * GF * PS),
        window_place(jnp.pad(keep, ((0, 0), (0, SLOTS - VIS)))),
        jnp.asarray(take, jnp.bfloat16),
        jnp.asarray(row[:, None] % GF),
        jnp.asarray(fold, jnp.bfloat16),
        jnp.asarray(np.concatenate([high, low], axis=1)),
    )


@jax.custom_vjp
def times(inputs, matrix):
    return jnp.dot(inputs.astype(jnp.bfloat16), matrix.astype(jnp.bfloat16), preferred_element_type=jnp.float32)


def times_keep(inputs, matrix):
    short = inputs.astype(jnp.bfloat16)
    return jnp.dot(short, matrix.astype(jnp.bfloat16), preferred_element_type=jnp.float32), (short, matrix)


def times_back(kept, grad):
    short, matrix = kept
    grad = grad.astype(jnp.bfloat16)
    back = lax.dot_general(
        grad, matrix.astype(jnp.bfloat16), (((1,), (1,)), ((), ())), preferred_element_type=jnp.float32
    )
    gain = lax.dot_general(short, grad, (((0,), (0,)), ((), ())), preferred_element_type=jnp.float32)
    return back, gain.astype(matrix.dtype)


times.defvjp(times_keep, times_back)


def dot_rows(left, right):
    return lax.dot_general(left, right, (((1,), (1,)), ((), ())), preferred_element_type=jnp.float32)


def dot_columns(left, right):
    return lax.dot_general(left, right, (((0,), (0,)), ((), ())), preferred_element_type=jnp.float32)


def head_lanes(value, head, size):
    lane = lax.broadcasted_iota(jnp.int32, value.shape, 1)
    return jnp.where(lane // size == head, value, jnp.zeros_like(value))


def soft_keys(queries, keys_here, allow, size):
    rows = queries.shape[0]
    scores = dot_rows(keys_here, queries).reshape(128 // size, rows, rows)
    scores = jnp.where(allow, scores * size ** (-0.5), -1e30)
    exponent = jnp.exp(scores - jnp.max(scores, axis=1, keepdims=True))
    return exponent / jnp.sum(exponent, axis=1, keepdims=True)


def flat_heads(value):
    return value.astype(jnp.bfloat16).reshape(-1, value.shape[2])


def attention_kernel(size, joined, allowed, out):
    width = out.shape[1]
    allow = allowed[...][None] > 0.0
    for lane in range(0, width, 128):
        queries = joined[:, lane : lane + 128]
        keys_here = stack_heads(joined[:, width + lane : width + lane + 128], size)
        values_here = stack_heads(joined[:, 2 * width + lane : 2 * width + lane + 128], size)
        soft = flat_heads(soft_keys(queries, keys_here, allow, size))
        out[:, lane : lane + 128] = dot_columns(soft, values_here).astype(jnp.bfloat16)


def attention_back_kernel(size, joined, allowed, grad, out, query_sum, value_sum):
    width, rows = grad.shape[1], grad.shape[0]
    allow = allowed[...][None] > 0.0

    @pl.when(pl.program_id(0) == 0)
    def clear():
        query_sum[...] = jnp.zeros_like(query_sum)
        value_sum[...] = jnp.zeros_like(value_sum)

    for lane in range(0, width, 128):
        queries = joined[:, lane : lane + 128]
        keys_here = stack_heads(joined[:, width + lane : width + lane + 128], size)
        values_here = stack_heads(joined[:, 2 * width + lane : 2 * width + lane + 128], size)
        pull = grad[:, lane : lane + 128]
        soft = soft_keys(queries, keys_here, allow, size)
        soft_grad = dot_rows(values_here, pull).reshape(128 // size, rows, rows)
        score_grad = soft * (soft_grad - jnp.sum(soft * soft_grad, axis=1, keepdims=True))
        score_grad = flat_heads(score_grad * size ** (-0.5))
        soft = flat_heads(soft)
        query_grad = dot_columns(score_grad, keys_here)
        key_grad = unstack_heads(jnp.dot(score_grad, queries, preferred_element_type=jnp.float32), size)
        value_grad = unstack_heads(jnp.dot(soft, pull, preferred_element_type=jnp.float32), size)
        out[:, lane : lane + 128] = query_grad.astype(jnp.bfloat16)
        out[:, width + lane : width + lane + 128] = key_grad.astype(jnp.bfloat16)
        out[:, 2 * width + lane : 2 * width + lane + 128] = value_grad.astype(jnp.bfloat16)
        query_sum[0:1, lane : lane + 128] += jnp.sum(query_grad, axis=0, keepdims=True)
        value_sum[0:1, lane : lane + 128] += jnp.sum(value_grad, axis=0, keepdims=True)


def window_fold(value, heads):
    lane = lax.broadcasted_iota(jnp.int32, (1, 1, value.shape[1]), 2) // (WIN * WIN)
    value = value.reshape(heads, 8, WIN * WIN, value.shape[1])
    found = value[:, 0]
    for window in range(1, 8):
        found = jnp.where(lane == window, value[:, window], found)
    return found


def window_spread(value):
    heads = value.shape[0]
    short = value.astype(jnp.bfloat16)
    lane = lax.broadcasted_iota(jnp.int32, short.shape, 2) // (WIN * WIN)
    parts = []
    for head in range(heads):
        for window in range(8):
            parts.append(
                jnp.where(lane[head] == window, short[head], jnp.zeros_like(short[head]))
            )
    return jnp.concatenate(parts, axis=0)


def stack_heads(value, size):
    per = value.shape[1] // size
    return jnp.concatenate([head_lanes(value, head, size) for head in range(per)], axis=0)


def unstack_heads(value, size):
    per = value.shape[1] // size
    rows = value.shape[0] // per
    lane = lax.broadcasted_iota(jnp.int32, (rows, value.shape[1]), 1) // size
    found = value[:rows]
    for head in range(1, per):
        found = jnp.where(lane == head, value[head * rows : (head + 1) * rows], found)
    return found


def soft_fold(queries, keys_here, allow, size):
    scores = window_fold(dot_rows(keys_here, queries), 128 // size)
    scores = jnp.where(allow, scores * size ** (-0.5), -1e30)
    exponent = jnp.exp(scores - jnp.max(scores, axis=1, keepdims=True))
    return exponent / jnp.sum(exponent, axis=1, keepdims=True)


def window_kernel(size, joined, allowed, out):
    for group in range(allowed.shape[0]):
        rows = pl.ds(group * 128, 128)
        window_group(size, joined.at[rows], allowed.at[group], out.at[rows])


def window_group(size, joined, allowed, out):
    width = out.shape[1]
    allow = allowed[...][None] > 0.0
    for lane in range(0, width, 128):
        queries = joined[:, lane : lane + 128]
        keys_here = stack_heads(joined[:, width + lane : width + lane + 128], size)
        values_here = stack_heads(joined[:, 2 * width + lane : 2 * width + lane + 128], size)
        soft = window_spread(soft_fold(queries, keys_here, allow, size))
        out[:, lane : lane + 128] = dot_columns(soft, values_here).astype(jnp.bfloat16)


def window_back_kernel(size, joined, allowed, grad, out, query_sum, value_sum):
    @pl.when(pl.program_id(0) == 0)
    def clear():
        query_sum[...] = jnp.zeros_like(query_sum)
        value_sum[...] = jnp.zeros_like(value_sum)

    for group in range(allowed.shape[0]):
        rows = pl.ds(group * 128, 128)
        window_back_group(
            size, joined.at[rows], allowed.at[group], grad.at[rows], out.at[rows], query_sum, value_sum
        )


def window_back_group(size, joined, allowed, grad, out, query_sum, value_sum):
    width = grad.shape[1]
    allow = allowed[...][None] > 0.0
    for lane in range(0, width, 128):
        queries = joined[:, lane : lane + 128]
        keys_here = stack_heads(joined[:, width + lane : width + lane + 128], size)
        values_here = stack_heads(joined[:, 2 * width + lane : 2 * width + lane + 128], size)
        pull = grad[:, lane : lane + 128]
        soft = soft_fold(queries, keys_here, allow, size)
        soft_grad = window_fold(dot_rows(values_here, pull), 128 // size)
        score_grad = soft * (soft_grad - jnp.sum(soft * soft_grad, axis=1, keepdims=True))
        score_grad = window_spread(score_grad * size ** (-0.5))
        soft = window_spread(soft)
        query_grad = dot_columns(score_grad, keys_here)
        key_grad = unstack_heads(jnp.dot(score_grad, queries, preferred_element_type=jnp.float32), size)
        value_grad = unstack_heads(jnp.dot(soft, pull, preferred_element_type=jnp.float32), size)
        out[:, lane : lane + 128] = query_grad.astype(jnp.bfloat16)
        out[:, width + lane : width + lane + 128] = key_grad.astype(jnp.bfloat16)
        out[:, 2 * width + lane : 2 * width + lane + 128] = value_grad.astype(jnp.bfloat16)
        query_sum[0:1, lane : lane + 128] += jnp.sum(query_grad, axis=0, keepdims=True)
        value_sum[0:1, lane : lane + 128] += jnp.sum(value_grad, axis=0, keepdims=True)


def attention_parts(joined, allowed, rows):
    steps = joined.shape[0] // rows
    period = allowed.shape[0]
    wide = pl.BlockSpec((rows, joined.shape[1]), lambda step: (step, 0))
    rest = (0,) * (allowed.ndim - 1)
    mask = pl.BlockSpec((None,) + allowed.shape[1:], lambda step: (lax.rem(step, period),) + rest)
    narrow_rows = pl.BlockSpec((rows, joined.shape[1] // 3), lambda step: (step, 0))
    return steps, wide, mask, narrow_rows


def attention_forward(kernel, joined, allowed, rows, size):
    steps, wide, mask, part = attention_parts(joined, allowed, rows)
    return pl.pallas_call(
        functools.partial(kernel, size),
        grid=(steps,),
        out_shape=jax.ShapeDtypeStruct((joined.shape[0], joined.shape[1] // 3), jnp.bfloat16),
        in_specs=[wide, mask],
        out_specs=part,
        compiler_params=pltpu.CompilerParams(vmem_limit_bytes=40 * 2**20),
        name="attention_forward",
    )(joined, allowed)


def attention_backward(kernel, joined, allowed, grad, rows, size):
    steps, wide, mask, part = attention_parts(joined, allowed, rows)
    width = joined.shape[1] // 3
    total = pl.BlockSpec((8, width), lambda step: (0, 0))
    return pl.pallas_call(
        functools.partial(kernel, size),
        grid=(steps,),
        out_shape=[
            jax.ShapeDtypeStruct(joined.shape, jnp.bfloat16),
            jax.ShapeDtypeStruct((8, width), jnp.float32),
            jax.ShapeDtypeStruct((8, width), jnp.float32),
        ],
        in_specs=[wide, mask, part],
        out_specs=[wide, total, total],
        compiler_params=pltpu.CompilerParams(vmem_limit_bytes=40 * 2**20),
        name="attention_backward",
    )(joined, allowed, grad)


def weight_grad_kernel(rows, grad, out):
    out[...] = dot_columns(rows[...], grad[...]).astype(out.dtype)


def weight_grad(rows, grad, kind):
    (tokens, height), width = rows.shape, grad.shape[1]
    tile = width // 3
    return pl.pallas_call(
        weight_grad_kernel,
        grid=(3,),
        out_shape=jax.ShapeDtypeStruct((height, width), kind),
        in_specs=[
            pl.BlockSpec((tokens, height), lambda step: (0, 0)),
            pl.BlockSpec((tokens, tile), lambda step: (0, step)),
        ],
        out_specs=pl.BlockSpec((height, tile), lambda step: (0, step)),
        compiler_params=pltpu.CompilerParams(vmem_limit_bytes=40 * 2**20),
        name="weight_grad",
    )(rows, grad)


def attention_block(forward, backward, rows, size):
    def join(normed, matrix, query_bias, value_bias):
        width = matrix.shape[1] // 3
        bias = jnp.concatenate([query_bias, jnp.zeros((width,), jnp.float32), value_bias])
        joined = jnp.dot(normed, matrix.astype(jnp.bfloat16), preferred_element_type=jnp.float32)
        return (joined + bias).astype(jnp.bfloat16)

    @jax.custom_vjp
    def apply(normed, matrix, query_bias, value_bias, allowed):
        joined = join(normed.astype(jnp.bfloat16), matrix, query_bias, value_bias)
        return attention_forward(forward, joined, allowed, rows, size).astype(jnp.float32)

    def keep(normed, matrix, query_bias, value_bias, allowed):
        short = normed.astype(jnp.bfloat16)
        joined = join(short, matrix, query_bias, value_bias)
        made = attention_forward(forward, joined, allowed, rows, size).astype(jnp.float32)
        return made, (short, matrix, joined, allowed)

    def back(kept, grad):
        short, matrix, joined, allowed = kept
        pulled, query_sum, value_sum = attention_backward(
            backward, joined, allowed, grad.astype(jnp.bfloat16), rows, size
        )
        normed_grad = dot_rows(pulled, matrix.astype(jnp.bfloat16))
        matrix_grad = weight_grad(short, pulled, matrix.dtype)
        return normed_grad, matrix_grad, query_sum[0], value_sum[0], jnp.zeros_like(allowed)

    apply.defvjp(keep, back)
    return apply


encoder_attention = attention_block(attention_kernel, attention_back_kernel, SLOTS, HEAD)
decoder_attention = attention_block(window_kernel, window_back_kernel, GROUPS * 8 * WIN * WIN, DHEAD)


def gelu_keep(value):
    portion = 0.5 + 0.5 * lax.erf(value * math.sqrt(0.5))
    slope = portion + value * jnp.exp(-0.5 * value * value) * (1.0 / math.sqrt(2.0 * math.pi))
    return value * portion, slope


def hidden_back_kernel(normed, inner, slope, grad, up, down, normed_grad, up_grad, down_grad, bias_grad):
    @pl.when(pl.program_id(0) == 0)
    def clear():
        normed_grad[...] = jnp.zeros_like(normed_grad)

    inner_grad = dot_rows(grad[...], down[...]) * slope[...]
    bias_grad[0:1, :] = jnp.sum(inner_grad, axis=0, keepdims=True)
    short = inner_grad.astype(jnp.bfloat16)
    down_grad[...] = dot_columns(inner[...], grad[...]).astype(jnp.bfloat16)
    up_grad[...] = dot_columns(normed[...], short).astype(jnp.bfloat16)
    normed_grad[...] += dot_rows(short, up[...])


def hidden_backward(normed, inner, slope, grad, up, down):
    (tokens, width), units = normed.shape, inner.shape[1]
    tile = 1024
    whole = pl.BlockSpec((tokens, width), lambda step: (0, 0))
    columns = pl.BlockSpec((tokens, tile), lambda step: (0, step))
    up_tile = pl.BlockSpec((width, tile), lambda step: (0, step))
    down_tile = pl.BlockSpec((tile, width), lambda step: (step, 0))
    return pl.pallas_call(
        hidden_back_kernel,
        grid=(units // tile,),
        out_shape=[
            jax.ShapeDtypeStruct((tokens, width), jnp.float32),
            jax.ShapeDtypeStruct((width, units), jnp.bfloat16),
            jax.ShapeDtypeStruct((units, width), jnp.bfloat16),
            jax.ShapeDtypeStruct((8, units), jnp.float32),
        ],
        in_specs=[whole, columns, columns, whole, up_tile, down_tile],
        out_specs=[whole, up_tile, down_tile, pl.BlockSpec((8, tile), lambda step: (0, step))],
        compiler_params=pltpu.CompilerParams(vmem_limit_bytes=40 * 2**20),
        name="hidden_backward",
    )(normed, inner, slope, grad, up, down)


@jax.custom_vjp
def hidden_layer(normed, up, bias, down):
    return hidden_keep(normed, up, bias, down)[0]


def hidden_keep(normed, up, bias, down):
    short = normed.astype(jnp.bfloat16)
    value, slope = gelu_keep(jnp.dot(short, up, preferred_element_type=jnp.float32) + bias)
    inner = value.astype(jnp.bfloat16)
    return jnp.dot(inner, down, preferred_element_type=jnp.float32), (short, inner, slope, up, down)


def hidden_back(kept, grad):
    short, inner, slope, up, down = kept
    found = hidden_backward(short, inner, slope, grad.astype(jnp.bfloat16), up, down)
    normed_grad, up_grad, down_grad, bias_grad = found
    return normed_grad, up_grad, bias_grad[0], down_grad


hidden_layer.defvjp(hidden_keep, hidden_back)


def window_allowed():
    position = np.arange(NPATCH)
    window, inner = position // (WIN * WIN), position % (WIN * WIN)
    time_row = window // (GF // WIN) * WIN + inner // WIN
    freq_col = window % (GF // WIN) * WIN + inner % WIN
    region = (time_row >= GT - WIN).astype(np.int32) + (time_row >= GT - SHIFT)
    region = region * 3 + (freq_col >= GF - WIN) + (freq_col >= GF - SHIFT)
    region = region.reshape(-1, 8, 1, WIN * WIN)
    same = region == region.transpose(0, 1, 3, 2)
    same = same.transpose(0, 2, 1, 3).reshape(-1, GROUPS, WIN * WIN, 8 * WIN * WIN)
    return same.astype(np.float32)


def local_loss(weights, picked, where, target, keep, counts):
    clips = picked.shape[0]
    pieces = unpack(weights[10])
    spot = window_place(jnp.pad(keep, ((0, 0), (0, SLOTS - VIS))))
    shown = (spot[:, :, None] == jnp.arange(NPATCH)[None, None, :]).astype(jnp.float32)
    shown = shown * (jnp.arange(SLOTS)[None, :] < counts[:, None])[:, :, None]
    hidden = times(picked.reshape(-1, PATCH), weights[8][:, :D]) + pieces[11] + where.reshape(-1, D)
    normed = layer_norm(hidden, pieces[0], pieces[1])
    visible = (jnp.arange(SLOTS)[None, :] < counts[:, None]).astype(jnp.float32)
    visible = jnp.broadcast_to(visible[:, :, None], (clips, SLOTS, SLOTS))
    attended = encoder_attention(normed, weights[0], pieces[2], pieces[3], visible)
    hidden = hidden + times(attended, weights[1]) + pieces[4]
    normed = layer_norm(hidden, pieces[5], pieces[6])
    hidden = hidden + hidden_layer(normed, weights[2], pieces[7], weights[3]) + pieces[8]
    latent = layer_norm(hidden, pieces[9], pieces[10])

    pieces = pieces[12:]
    placed = times(latent, weights[9]) + pieces[0]
    filled = jnp.einsum("cjp,cjd->cpd", shown, placed.reshape(clips, SLOTS, DD), precision=HIGH)
    cells = jnp.sum(shown, axis=1)
    hidden = filled + (1.0 - cells)[..., None] * pieces[1] + window_sinusoid(DD)
    hidden = hidden.reshape(-1, DD)
    normed = layer_norm(hidden, pieces[2], pieces[3])
    attended = decoder_attention(normed, weights[4], pieces[4], pieces[5], jnp.asarray(window_allowed()))
    hidden = hidden + times(attended, weights[5]) + pieces[6]
    normed = layer_norm(hidden, pieces[7], pieces[8])
    hidden = hidden + hidden_layer(normed, weights[6], pieces[9], weights[7]) + pieces[10]
    normed = layer_norm(hidden, pieces[11], pieces[12])
    predicted = times(normed, weights[8][:, D:].T) + pieces[13]
    deviation = predicted - target.reshape(-1, PATCH)
    patch_error = jnp.mean(deviation * deviation, axis=-1)
    return jnp.sum((1.0 - cells.reshape(-1)) * patch_error)


def quick_body(
    spectrogram, keep, counts, *rest
):
    masters = rest[:8] + (rest[16], rest[19], rest[22])
    moments = rest[8:16]
    devices = lax.axis_size("dp")
    lead = (2,) * bit_count(devices)
    own = list(masters)
    vector_rows = own[10].shape[0]
    spare = VEC_ROWS * VEC_COLS
    own[10] = jnp.pad(own[10], (0, spare - vector_rows)).reshape(VEC_ROWS, VEC_COLS)
    scene = window_scene(spectrogram, keep)
    gathered, tally, made = gather_rows(own, counts, scene, devices)
    mask_count = tally.reshape(())
    weights = [piece.reshape(-1, piece.shape[-1]) for piece in gathered[:10]]
    weights[4] = weights[4].astype(jnp.float32)
    vectors = gathered[10].reshape(devices, spare)[:, :vector_rows].reshape(-1).astype(jnp.float32)
    loss_part, pull = jax.vjp(
        lambda *params: local_loss(params, *made, keep, counts), *weights, vectors
    )
    grads = list(pull(1.0 / mask_count))
    grads[10] = jnp.pad(grads[10].reshape(devices, vector_rows), ((0, 0), (0, spare - vector_rows)))
    grads[10] = grads[10].reshape(lead + (VEC_ROWS, VEC_COLS))
    for number in range(10):
        grad = grads[number]
        grads[number] = grad.reshape(lead + (grad.shape[0] // devices, grad.shape[1]))
    renewed, others, stats, collected = reduce_rows(
        grads, loss_part.reshape(1, 1), moments, OWNERS, devices
    )
    adam = (*rest[16:19], others[0], *rest[19:22], others[1])
    flat = [piece.reshape(-1, piece.shape[2]) for piece in collected]
    made, renewed, more = orthogonalize(flat, renewed, stats, adam, OWNERS)
    patch_new, embed_new, grad_norm, loss_sum = more[:3], more[3:6], more[6].reshape(()), more[7].reshape(())
    made = [piece.reshape(devices, -1, piece.shape[1]) for piece in made]
    new_weights = finish(return_rows(made, OWNERS, devices), masters[:8], devices)
    factor = jnp.minimum(1.0, CLIP_MAX / (grad_norm + 1e-06))
    vector_grad = others[2].reshape(-1)[:vector_rows] * factor
    vector_new = adam_update(*rest[22:25], vector_grad, 0.0)
    return (loss_sum, mask_count, grad_norm, *new_weights, *renewed, *patch_new, *embed_new, *vector_new)


def body(
    spectrogram,
    keep,
    counts,
    enc_qkv,
    enc_out,
    enc_up,
    enc_down,
    dec_qkv,
    dec_out,
    dec_up,
    dec_down,
    mom_enc_qkv,
    mom_enc_out,
    mom_enc_up,
    mom_enc_down,
    mom_dec_qkv,
    mom_dec_out,
    mom_dec_up,
    mom_dec_down,
    patch_maps,
    patch_first,
    patch_second,
    embed_map,
    embed_first,
    embed_second,
    vectors,
    vector_first,
    vector_second,
):
    masters = (
        enc_qkv,
        enc_out,
        enc_up,
        enc_down,
        dec_qkv,
        dec_out,
        dec_up,
        dec_down,
        patch_maps,
        embed_map,
        vectors,
    )
    moments = (
        mom_enc_qkv,
        mom_enc_out,
        mom_enc_up,
        mom_enc_down,
        mom_dec_qkv,
        mom_dec_out,
        mom_dec_up,
        mom_dec_down,
    )
    sent = tuple((weight.astype(jnp.bfloat16) for weight in masters))
    gathered = (
        lax.all_gather(sent[0], "dp", axis=0, tiled=True),
        lax.all_gather(sent[1], "dp", axis=0, tiled=True),
        lax.all_gather(sent[2], "dp", axis=0, tiled=True),
        lax.all_gather(sent[3], "dp", axis=0, tiled=True),
        lax.all_gather(sent[4], "dp", axis=0, tiled=True),
        lax.all_gather(sent[5], "dp", axis=0, tiled=True),
        lax.all_gather(sent[6], "dp", axis=0, tiled=True),
        lax.all_gather(sent[7], "dp", axis=0, tiled=True),
        lax.all_gather(sent[8], "dp", axis=0, tiled=True),
        lax.all_gather(sent[9], "dp", axis=0, tiled=True),
        lax.all_gather(sent[10], "dp", axis=0, tiled=True),
    )
    widened = tuple((piece.astype(jnp.float32) for piece in gathered))
    patches = patchify(spectrogram.astype(jnp.float32))
    latent = encode(widened, patches, keep, counts)
    loss_part = decode(widened, latent, patches, keep, counts)
    count_part = jnp.sum(NPATCH - counts).astype(jnp.float32)
    loss_sum, mask_count = lax.psum((loss_part, count_part), ("dp", "mp"))
    regathered = (
        lax.all_gather(sent[0], "dp", axis=0, tiled=True),
        lax.all_gather(sent[1], "dp", axis=0, tiled=True),
        lax.all_gather(sent[2], "dp", axis=0, tiled=True),
        lax.all_gather(sent[3], "dp", axis=0, tiled=True),
        lax.all_gather(sent[4], "dp", axis=0, tiled=True),
        lax.all_gather(sent[5], "dp", axis=0, tiled=True),
        lax.all_gather(sent[6], "dp", axis=0, tiled=True),
        lax.all_gather(sent[7], "dp", axis=0, tiled=True),
        lax.all_gather(sent[8], "dp", axis=0, tiled=True),
        lax.all_gather(sent[9], "dp", axis=0, tiled=True),
        lax.all_gather(sent[10], "dp", axis=0, tiled=True),
    )
    widened = tuple((piece.astype(jnp.float32) for piece in regathered))
    cotangent = 1.0 / mask_count
    unused, pull_decode = jax.vjp(
        lambda params, hidden: decode(params, hidden, patches, keep, counts), widened, latent
    )
    decode_grads, latent_grad = pull_decode(cotangent)
    unused, pull_encode = jax.vjp(lambda params: encode(params, patches, keep, counts), widened)
    (encode_grads,) = pull_encode(latent_grad)
    grads = jax.tree.map(jnp.add, decode_grads, encode_grads)
    reduced = (
        lax.psum_scatter(grads[0], "dp", scatter_dimension=0, tiled=True),
        lax.psum_scatter(grads[1], "dp", scatter_dimension=0, tiled=True),
        lax.psum_scatter(grads[2], "dp", scatter_dimension=0, tiled=True),
        lax.psum_scatter(grads[3], "dp", scatter_dimension=0, tiled=True),
        lax.psum_scatter(grads[4], "dp", scatter_dimension=0, tiled=True),
        lax.psum_scatter(grads[5], "dp", scatter_dimension=0, tiled=True),
        lax.psum_scatter(grads[6], "dp", scatter_dimension=0, tiled=True),
        lax.psum_scatter(grads[7], "dp", scatter_dimension=0, tiled=True),
        lax.psum_scatter(grads[8], "dp", scatter_dimension=0, tiled=True),
        lax.psum_scatter(grads[9], "dp", scatter_dimension=0, tiled=True),
        lax.psum_scatter(grads[10], "dp", scatter_dimension=0, tiled=True),
    )
    reduced = lax.psum(
        (
            reduced[0],
            reduced[1],
            reduced[2],
            reduced[3],
            reduced[4],
            reduced[5],
            reduced[6],
            reduced[7],
            reduced[8],
            reduced[9],
            reduced[10],
        ),
        "mp",
    )
    local_squares = functools.reduce(
        jnp.add, [jnp.sum(gradient * gradient) for gradient in reduced]
    )
    grad_norm = jnp.sqrt(lax.psum(local_squares, "dp"))
    factor = jnp.minimum(1.0, CLIP_MAX / (grad_norm + 1e-06))
    clipped = [gradient * factor for gradient in reduced]
    devices = lax.axis_size("dp")
    renewed = [0.5 * moments[number] + clipped[number] for number in range(8)]
    core = lax.axis_index("mp")
    halves = [take_half(renewed[number], number, core) for number in range(8)]
    shapes = [(masters[number].shape[0] * devices, masters[number].shape[1]) for number in range(8)]
    long_max = max((max(shape_pair) // 2 for shape_pair in shapes))
    short_max = max((min(shape_pair) for shape_pair in shapes))
    flat_max = max((shape_pair[0] * shape_pair[1] // (2 * devices) for shape_pair in shapes))
    owner = lax.axis_index("dp") % 8
    collected = (
        lax.all_gather(halves[0], "dp", axis=0, tiled=True),
        lax.all_gather(halves[1], "dp", axis=0, tiled=True),
        lax.all_gather(halves[2], "dp", axis=0, tiled=True),
        lax.all_gather(halves[3], "dp", axis=0, tiled=True),
        lax.all_gather(halves[4], "dp", axis=0, tiled=True),
        lax.all_gather(halves[5], "dp", axis=0, tiled=True),
        lax.all_gather(halves[6], "dp", axis=0, tiled=True),
        lax.all_gather(halves[7], "dp", axis=0, tiled=True),
    )
    iterate = lax.switch(
        owner,
        [partial(arrange, collected[number], number, long_max, short_max) for number in range(8)],
    )
    for iteration in range(NS_ITERS):
        gram_sum = lax.psum(jnp.dot(iterate.T, iterate, precision=HIGH), "mp")
        if iteration == 0:
            norm_scale = 1.0 / (jnp.sqrt(jnp.trace(gram_sum)) + 1e-07)
            iterate = iterate * norm_scale
            gram_sum = gram_sum * (norm_scale * norm_scale)
        polynomial = NS_B * gram_sum + NS_C * jnp.dot(gram_sum, gram_sum, precision=HIGH)
        iterate = NS_A * iterate + jnp.dot(iterate, polynomial, precision=HIGH)
    outgoing = lax.switch(
        owner,
        [
            partial(
                disperse, iterate, number, shapes[number][0], shapes[number][1], devices, flat_max
            )
            for number in range(8)
        ],
    )
    arriving = jax.tree.map(
        lambda part, own: part.astype(own.dtype),
        lax.all_to_all(shortened(outgoing), "dp", split_axis=0, concat_axis=0, tiled=True),
        outgoing,
    )
    mine = [
        restore(arriving[number], number, shapes[number][0], shapes[number][1], devices)
        for number in range(8)
    ]
    whole = (
        lax.all_gather(shortened(mine[0]), "mp", axis=1, tiled=True),
        lax.all_gather(shortened(mine[1]), "mp", axis=1, tiled=True),
        lax.all_gather(shortened(mine[2]), "mp", axis=1, tiled=True),
        lax.all_gather(shortened(mine[3]), "mp", axis=0, tiled=True),
        lax.all_gather(shortened(mine[4]), "mp", axis=1, tiled=True),
        lax.all_gather(shortened(mine[5]), "mp", axis=1, tiled=True),
        lax.all_gather(shortened(mine[6]), "mp", axis=1, tiled=True),
        lax.all_gather(shortened(mine[7]), "mp", axis=0, tiled=True),
    )
    new_weights = []
    for number in range(8):
        step_rate = LR_MUON * 0.2 * math.sqrt(max(shapes[number]))
        new_weights.append(masters[number] * (1.0 - LR_MUON * DECAY) - step_rate * whole[number])
    patch_new = adam_update(patch_maps, patch_first, patch_second, clipped[8], DECAY)
    embed_new = adam_update(embed_map, embed_first, embed_second, clipped[9], DECAY)
    vector_new = adam_update(vectors, vector_first, vector_second, clipped[10], 0.0)
    return (
        loss_sum,
        mask_count,
        grad_norm,
        new_weights[0],
        new_weights[1],
        new_weights[2],
        new_weights[3],
        new_weights[4],
        new_weights[5],
        new_weights[6],
        new_weights[7],
        renewed[0],
        renewed[1],
        renewed[2],
        renewed[3],
        renewed[4],
        renewed[5],
        renewed[6],
        renewed[7],
        patch_new[0],
        patch_new[1],
        patch_new[2],
        embed_new[0],
        embed_new[1],
        embed_new[2],
        vector_new[0],
        vector_new[1],
        vector_new[2],
    )


def solution(mesh):
    placed = (
        P(("dp", "mp"), None, None),
        P(("dp", "mp"), None),
        P(("dp", "mp")),
        P("dp", None),
        P("dp", None),
        P("dp", None),
        P("dp", None),
        P("dp", None),
        P("dp", None),
        P("dp", None),
        P("dp", None),
        P("dp", None),
        P("dp", None),
        P("dp", None),
        P("dp", None),
        P("dp", None),
        P("dp", None),
        P("dp", None),
        P("dp", None),
        P("dp", None),
        P("dp", None),
        P("dp", None),
        P("dp", None),
        P("dp", None),
        P("dp", None),
        P("dp"),
        P("dp"),
        P("dp"),
    )
    return jax.shard_map(
        quick_body if mesh.shape["dp"] == 16 else body,
        mesh=mesh,
        in_specs=placed,
        out_specs=(
            P(),
            P(),
            P(),
            P("dp", None),
            P("dp", None),
            P("dp", None),
            P("dp", None),
            P("dp", None),
            P("dp", None),
            P("dp", None),
            P("dp", None),
            P("dp", None),
            P("dp", None),
            P("dp", None),
            P("dp", None),
            P("dp", None),
            P("dp", None),
            P("dp", None),
            P("dp", None),
            P("dp", None),
            P("dp", None),
            P("dp", None),
            P("dp", None),
            P("dp", None),
            P("dp", None),
            P("dp"),
            P("dp"),
            P("dp"),
        ),
        check_vma=False,
    )
```

```python
from functools import partial
import functools
import math

import jax
import jax.numpy as jnp
import numpy as np
from jax import lax
from jax.experimental import pallas as pl
from jax.experimental.pallas import tpu as pltpu
from jax.sharding import PartitionSpec as P

D = 768
HEADS = 12
HEAD = 64
MLP = 3072
DD = 512
DHEADS = 16
DHEAD = 32
DMLP = 2048
PS = 16
GT = 64
GF = 8
WIN = 4
VIS = 154
NS_ITERS = 5
STEP = 10
PATCH = 256
SHIFT = 2
NPATCH = 512


HIGH = lax.Precision.HIGHEST
CLIP_MAX = 0.001
LR_MUON = 0.1
LR_ADAM = 0.05
DECAY = 0.01
NS_A = 3.4445
NS_B = -4.775
NS_C = 2.0315
LONG_COLS = (True, True, True, False, True, True, True, False)


def shortened(x):
    return jax.tree.map(lambda a: a.astype(jnp.bfloat16) if a.dtype == jnp.float32 else a, x)


def narrow_core(value):
    return lax.optimization_barrier(value.astype(jnp.bfloat16)).astype(jnp.float32)


def narrow_keep(value):
    return (narrow_core(value), None)


def narrow_pass(kept, grad):
    return (grad,)


def same_core(value):
    return value


def same_keep(value):
    return (value, None)


def same_back(kept, grad):
    return (narrow_core(grad),)


def narrow(value):
    wrapped = jax.custom_vjp(narrow_core)
    wrapped.defvjp(narrow_keep, narrow_pass)
    return wrapped(value)


def narrow_grad(value):
    wrapped = jax.custom_vjp(same_core)
    wrapped.defvjp(same_keep, same_back)
    return wrapped(value)


def product(inputs, matrix):
    return narrow_grad(jnp.dot(narrow(inputs), narrow(matrix), preferred_element_type=jnp.float32))


def score_product(queries, key_rows):
    return narrow_grad(
        jnp.einsum(
            "bqhd,bkhd->bhqk", narrow(queries), narrow(key_rows), preferred_element_type=jnp.float32
        )
    )


def value_product(softmax_rows, values):
    return narrow_grad(
        jnp.einsum(
            "bhqk,bkhd->bqhd",
            narrow(softmax_rows),
            narrow(values),
            preferred_element_type=jnp.float32,
        )
    )


def unpack(vectors):
    extents = [D] * 7 + [MLP] + [D] * 4 + [DD] * 9 + [DMLP] + [DD] * 3 + [PATCH]
    pieces = []
    offset = 0
    for extent in extents:
        pieces.append(vectors[offset : offset + extent])
        offset += extent
    return pieces


def layer_norm(hidden, scaling, offset):
    centred = hidden - jnp.mean(hidden, axis=-1, keepdims=True)
    variance = jnp.mean(centred * centred, axis=-1, keepdims=True)
    return centred * lax.rsqrt(variance + 1e-06) * scaling + offset


def sinusoid(channels):
    quarter = channels // 4
    frequency = 1.0 / 10000.0 ** (jnp.arange(quarter, dtype=jnp.float32) / quarter)
    position = jnp.arange(GT * GF)
    time_rows = (position // GF).astype(jnp.float32)[:, None] * frequency
    freq_cols = (position % GF).astype(jnp.float32)[:, None] * frequency
    return jnp.concatenate(
        [jnp.sin(time_rows), jnp.cos(time_rows), jnp.sin(freq_cols), jnp.cos(freq_cols)], axis=1
    )


def patchify(spec):
    clip_total = spec.shape[0]
    arranged = spec.reshape(clip_total, GT, PS, GF, PS).transpose(0, 1, 3, 2, 4)
    return arranged.reshape(clip_total, GT * GF, PS * PS)


def window_mask():
    time_rows = jnp.arange(GT)
    freq_cols = jnp.arange(GF)
    time_part = (time_rows >= GT - WIN).astype(jnp.int32) + (time_rows >= GT - SHIFT).astype(
        jnp.int32
    )
    freq_part = (freq_cols >= GF - WIN).astype(jnp.int32) + (freq_cols >= GF - SHIFT).astype(
        jnp.int32
    )
    region = time_part[:, None] * 3 + freq_part[None, :]
    region = (
        region.reshape(GT // WIN, WIN, GF // WIN, WIN).transpose(0, 2, 1, 3).reshape(-1, WIN * WIN)
    )
    return region[:, :, None] == region[:, None, :]


def to_windows(grid_rows):
    clip_total = grid_rows.shape[0]
    channels = grid_rows.shape[2]
    arranged = jnp.roll(
        grid_rows.reshape(clip_total, GT, GF, channels), (-SHIFT, -SHIFT), axis=(1, 2)
    )
    arranged = arranged.reshape(clip_total, GT // WIN, WIN, GF // WIN, WIN, channels).transpose(
        0, 1, 3, 2, 4, 5
    )
    return arranged.reshape(-1, WIN * WIN, channels)


def from_windows(windows, clip_total):
    channels = windows.shape[-1]
    arranged = windows.reshape(clip_total, GT // WIN, GF // WIN, WIN, WIN, channels).transpose(
        0, 1, 3, 2, 4, 5
    )
    arranged = jnp.roll(arranged.reshape(clip_total, GT, GF, channels), (SHIFT, SHIFT), axis=(1, 2))
    return arranged.reshape(clip_total, GT * GF, channels)


def attend(queries, key_rows, values, allowed, scaling):
    scores = score_product(queries, key_rows) * scaling
    scores = jnp.where(allowed, scores, -1e30)
    scores = scores - jnp.max(scores, axis=-1, keepdims=True)
    exponent = jnp.exp(scores)
    softmax_rows = exponent / jnp.sum(exponent, axis=-1, keepdims=True)
    return value_product(softmax_rows, values)


def encode(weights, patches, keep, counts):
    pieces = unpack(weights[10])
    clip_total = patches.shape[0]
    picked = jnp.take_along_axis(patches, keep[:, :, None], axis=1)
    hidden = product(picked, weights[8][:, :D]) + pieces[11] + sinusoid(D)[keep]
    normed = layer_norm(hidden, pieces[0], pieces[1])
    joined = product(normed, weights[0])
    queries = (joined[..., :D] + pieces[2]).reshape(clip_total, VIS, HEADS, HEAD)
    key_rows = joined[..., D : 2 * D].reshape(clip_total, VIS, HEADS, HEAD)
    values = (joined[..., 2 * D :] + pieces[3]).reshape(clip_total, VIS, HEADS, HEAD)
    visible = (jnp.arange(VIS)[None, :] < counts[:, None])[:, None, None, :]
    attended = attend(queries, key_rows, values, visible, HEAD ** (-0.5)).reshape(
        clip_total, VIS, D
    )
    hidden = hidden + product(attended, weights[1]) + pieces[4]
    normed = layer_norm(hidden, pieces[5], pieces[6])
    inner = jax.nn.gelu(product(normed, weights[2]) + pieces[7], approximate=False)
    hidden = hidden + product(inner, weights[3]) + pieces[8]
    return layer_norm(hidden, pieces[9], pieces[10])


def decode(weights, latent, patches, keep, counts):
    pieces = unpack(weights[10])[12:]
    clip_total = latent.shape[0]
    placed = product(latent, weights[9]) + pieces[0]
    visible = jnp.arange(VIS)[None, :] < counts[:, None]
    target_rows = jnp.where(visible, keep, NPATCH)
    clip_rows = jnp.arange(clip_total)[:, None]
    filled = (
        jnp.zeros((clip_total, NPATCH + 1, DD), jnp.float32)
        .at[clip_rows, target_rows]
        .add(placed)[:, :NPATCH]
    )
    visible_cells = (
        jnp.zeros((clip_total, NPATCH + 1), jnp.float32)
        .at[clip_rows, target_rows]
        .add(1.0)[:, :NPATCH]
    )
    hidden = filled + (1.0 - visible_cells)[..., None] * pieces[1] + sinusoid(DD)
    normed = layer_norm(hidden, pieces[2], pieces[3])
    windows = to_windows(product(normed, weights[4]))
    queries = (windows[..., :DD] + pieces[4]).reshape(-1, WIN * WIN, DHEADS, DHEAD)
    key_rows = windows[..., DD : 2 * DD].reshape(-1, WIN * WIN, DHEADS, DHEAD)
    values = (windows[..., 2 * DD :] + pieces[5]).reshape(-1, WIN * WIN, DHEADS, DHEAD)
    allowed = jnp.tile(window_mask(), (clip_total, 1, 1))[:, None, :, :]
    attended = attend(queries, key_rows, values, allowed, DHEAD ** (-0.5)).reshape(
        -1, WIN * WIN, DD
    )
    hidden = hidden + product(from_windows(attended, clip_total), weights[5]) + pieces[6]
    normed = layer_norm(hidden, pieces[7], pieces[8])
    inner = jax.nn.gelu(product(normed, weights[6]) + pieces[9], approximate=False)
    hidden = hidden + product(inner, weights[7]) + pieces[10]
    normed = layer_norm(hidden, pieces[11], pieces[12])
    predicted = product(normed, weights[8][:, D:].T) + pieces[13]
    centred = patches - jnp.mean(patches, axis=-1, keepdims=True)
    target = centred * lax.rsqrt(jnp.mean(centred * centred, axis=-1, keepdims=True) + 1e-06)
    deviation = predicted - target
    patch_error = jnp.mean(deviation * deviation, axis=-1)
    return jnp.sum((1.0 - visible_cells) * patch_error)


def take_half(shard, number, core):
    if LONG_COLS[number]:
        extent = shard.shape[1] // 2
        return lax.dynamic_slice_in_dim(shard, core * extent, extent, 1)
    extent = shard.shape[0] // 2
    return lax.dynamic_slice_in_dim(shard, core * extent, extent, 0)


def arrange(gathered_half, number, long_max, short_max):
    upright = gathered_half.T if LONG_COLS[number] else gathered_half
    return jnp.pad(upright, ((0, long_max - upright.shape[0]), (0, short_max - upright.shape[1])))


def disperse(iterate, number, height, breadth, devices, flat_max):
    if LONG_COLS[number]:
        piece = iterate[: breadth // 2, :height].T.reshape(
            devices, height // devices * (breadth // 2)
        )
    else:
        piece = iterate[: height // 2, :breadth].reshape(devices, height // 2 // devices * breadth)
    return jnp.pad(piece, ((0, 0), (0, flat_max - piece.shape[1])))


def restore(row_piece, number, height, breadth, devices):
    if LONG_COLS[number]:
        return row_piece[: height // devices * (breadth // 2)].reshape(
            height // devices, breadth // 2
        )
    return row_piece[: height // 2 // devices * breadth].reshape(height // 2 // devices, breadth)


def adam_update(weight, first_moment, second_moment, gradient, decay):
    first_moment = 0.5 * first_moment + 0.5 * gradient
    second_moment = 0.95 * second_moment + 0.05 * gradient * gradient
    direction = (
        first_moment / (1.0 - 0.5**STEP) / (jnp.sqrt(second_moment / (1.0 - 0.95**STEP)) + 1e-08)
    )
    return (weight - LR_ADAM * (direction + decay * weight), first_moment, second_moment)


MESH_ID = pl.DeviceIdType.MESH
VEC_ROWS, VEC_COLS = 16, 256
AXIS_ORDERS = ((0, 1, 2, 3), (0, 1, 3, 2), (0, 2, 1, 3), (0, 2, 3, 1), (0, 3, 1, 2), (0, 3, 2, 1), (1, 0, 2, 3), (1, 0, 3, 2), (1, 2, 0, 3), (1, 2, 3, 0), (1, 3, 0, 2), (1, 3, 2, 0), (2, 0, 1, 3), (2, 0, 3, 1), (2, 1, 0, 3), (2, 1, 3, 0), (2, 3, 0, 1), (2, 3, 1, 0), (3, 0, 1, 2), (3, 0, 2, 1), (3, 1, 0, 2), (3, 1, 2, 0), (3, 2, 0, 1), (3, 2, 1, 0))
GATHER_PARTS = (3, 1, 4, 4, 1, 1, 2, 2, 1, 1, 1)
REDUCE_PARTS = (3, 1, 4, 4, 2, 1, 2, 2, 1, 1, 1)
TALL = (3, 7)
GATHER_TURNS = (19, 18, 22, 17, 13, 21, 22, 20, 3, 12, 11, 0, 17, 23, 16, 10, 23, 16, 11, 21, 21)
GATHER_FIRST = (6, 17, 20, 11, 7, 16, 8, 13, 12, 1, 4, 9, 19, 10, 3, 2, 15, 5, 0, 14, 18)
GATHER_STEPS = ((20, 11, 17, 6, 8, 10, 13, 15, 7, 16, 18, 19, 4, 1, 12, 9, 3, 2, 5, 14, 0), (20, 11, 7, 19, 4, 1, 17, 9, 6, 13, 8, 5, 0, 10, 16, 18, 15, 12, 3, 2, 14), (20, 7, 1, 17, 9, 13, 6, 16, 15, 11, 19, 4, 3, 12, 2, 8, 14, 10, 18, 5, 0), (20, 17, 13, 16, 6, 19, 7, 3, 4, 2, 1, 14, 12, 8, 18, 9, 10, 5, 15, 0, 11))
REDUCE_TURNS = (14, 1, 1, 6, 7, 2, 12, 8, 20, 3, 21, 6, 6, 0, 0, 21, 10, 13, 2, 0, 17, 4)
REDUCE_FIRST = (17, 21, 12, 9, 15, 18, 19, 4, 3, 11, 1, 10, 13, 20, 0, 7, 5, 16, 8, 14, 6, 2)
REDUCE_STEPS = ((21, 17, 12, 9, 19, 15, 18, 4, 20, 3, 11, 10, 1, 0, 7, 14, 16, 5, 8, 13, 6, 2), (21, 17, 19, 15, 9, 12, 10, 14, 1, 20, 0, 18, 4, 8, 3, 7, 11, 13, 2, 16, 6, 5), (21, 17, 19, 20, 15, 18, 9, 14, 0, 10, 12, 8, 7, 16, 1, 6, 4, 5, 3, 11, 13, 2), (21, 17, 20, 15, 9, 19, 10, 18, 14, 0, 12, 8, 1, 16, 7, 6, 4, 5, 3, 2, 13, 11))
OWNERS = (4, 11, 5, 10, 6, 9, 7, 8)
SLOTS = 160
GROUPS = 4


def bit_count(devices):
    return devices.bit_length() - 1


def cut_pieces(parts, shapes):
    found = []
    for number, count in enumerate(parts):
        rows, width = shapes[number]
        for part in range(count):
            if number in TALL:
                found.append((number, part * (rows // count), rows // count, 0, width))
            else:
                found.append((number, 0, rows, part * (width // count), width // count))
    return found


def own_bits(levels):
    me = lax.axis_index("dp")
    return me, [lax.rem(lax.div(me, 2**bit), 2) for bit in range(levels)]


def place(levels, free, own, flip=None):
    spots = []
    for bit in range(levels - 1, -1, -1):
        if bit in free:
            spots.append(slice(None))
        elif bit == flip:
            spots.append(1 - own[bit])
        else:
            spots.append(own[bit])
    return tuple(spots)


def partner(me, own, bit):
    return me + (1 - 2 * own[bit]) * 2**bit


def greet(me, own, levels, core):
    barrier = pltpu.get_barrier_semaphore()
    for bit in range(levels):
        pl.semaphore_signal(
            barrier,
            inc=1,
            device_id={"dp": partner(me, own, bit), "mp": core},
            device_id_type=MESH_ID,
        )
    pl.semaphore_signal(barrier, inc=1, device_id={"dp": me, "mp": 1 - core}, device_id_type=MESH_ID)
    pl.semaphore_wait(barrier, levels + 1)


def add_up(me, core, devices, total, landing, send_sem, recv_sem, own_sem):
    def send(source, target):
        return pltpu.make_async_remote_copy(
            src_ref=total,
            dst_ref=landing.at[source],
            send_sem=send_sem.at[target],
            recv_sem=recv_sem.at[source],
            device_id={"dp": target, "mp": core},
            device_id_type=MESH_ID,
        )

    @pl.loop(0, devices)
    def start_one(other):
        @pl.when(other != me)
        def start_other():
            send(me, other).start()

    own = pltpu.make_async_copy(total, landing.at[me], own_sem)
    own.start()
    own.wait()

    @pl.loop(0, devices)
    def wait_one(other):
        @pl.when(other != me)
        def wait_other():
            send(other, me).wait_recv()
            send(me, other).wait_send()

    found = landing[0]
    for device in range(1, devices):
        found = found + landing[device]
    total[...] = found
    swap = pltpu.make_async_remote_copy(
        src_ref=total,
        dst_ref=landing.at[devices],
        send_sem=send_sem.at[devices],
        recv_sem=recv_sem.at[devices],
        device_id={"dp": me, "mp": 1 - core},
        device_id_type=MESH_ID,
    )
    swap.start()
    swap.wait()
    total[...] = total[...] + landing[devices]


def cut_patches(lines, spots, take, freq, fold, table, picked_out, where_out, target_out):
    part = 512
    lane = lax.broadcasted_iota(jnp.int32, (NPATCH, part), 1)
    inside = lax.rem(lax.div(lane, PS), GF) == freq[...]
    for clip in range(lines.shape[0]):
        patches = jnp.zeros((NPATCH, PATCH), jnp.float32)
        for start in range(0, PS * GF * PS, part):
            spread = jnp.dot(
                take[...], lines[clip, :, start : start + part], preferred_element_type=jnp.float32
            )
            spread = jnp.where(inside, spread, 0.0).astype(jnp.bfloat16)
            patches = patches + jnp.dot(
                spread, fold[start : start + part, :], preferred_element_type=jnp.float32
            )
        slot = lax.broadcasted_iota(jnp.int32, (NPATCH, SLOTS), 0)
        chosen = jnp.where(slot == spots[clip : clip + 1, :], 1.0, 0.0).astype(jnp.bfloat16)
        picked_out[clip] = dot_columns(chosen, patches.astype(jnp.bfloat16)).astype(jnp.bfloat16)
        where_out[clip] = dot_columns(chosen, table[:, :D]) + dot_columns(chosen, table[:, D:])
        centred = patches - jnp.mean(patches, axis=-1, keepdims=True)
        spread = jnp.mean(centred * centred, axis=-1, keepdims=True)
        target_out[clip] = centred * lax.rsqrt(spread + 1e-06)


def gather_kernel(levels, pieces, count, *refs):
    sources, tally, rest = refs[:count] + refs[count + 1 : count + 7], refs[count], refs[count + 7 :]
    outs, tally_out, made, rest = rest[:count], rest[count], rest[count + 1 : count + 4], rest[count + 4 :]
    wholes, save_sem, rest = rest[:count], rest[count], rest[count + 1 :]
    short, held, load_sem, rest = rest[:count], rest[count : 2 * count + 6], rest[2 * count + 6], rest[2 * count + 7 :]
    shards, scene = held[:count], held[count:]

    def load(number):
        return pltpu.make_async_copy(sources[number], held[number], load_sem.at[number])

    for number in range(count + 6):
        load(number).start()
    here_sem, send_sem, recv_sem, cross_send, cross_recv, tally_land, tally_send, tally_recv = rest
    me, own = own_bits(levels)
    core = lax.axis_index("mp")
    greet(me, own, levels, core)
    orders = [AXIS_ORDERS[turn] for turn in GATHER_TURNS]

    def cut(piece, which):
        number, row, rows, column, columns = pieces[piece]
        width = shards[number].shape[1] // 2
        return (pl.ds(row, rows), pl.ds(pl.multiple_of(which * width + column, 128), columns))

    def hop(piece, stage, flip):
        order, number = orders[piece], pieces[piece][0]
        spot = place(levels, order[:stage], own, order[stage] if flip else None)
        target = wholes[number].at[spot + cut(piece, core)]
        source = target if stage or flip else short[number].at[cut(piece, core)]
        return pltpu.make_async_remote_copy(
            src_ref=source,
            dst_ref=target,
            send_sem=send_sem.at[piece, stage],
            recv_sem=recv_sem.at[piece, stage],
            device_id={"dp": partner(me, own, order[stage]), "mp": core},
            device_id_type=MESH_ID,
        )

    def cross(piece, stage, which):
        order, number = orders[piece], pieces[piece][0]
        spot = place(levels, order[:stage], own, order[stage])
        target = wholes[number].at[spot + cut(piece, which)]
        return pltpu.make_async_remote_copy(
            src_ref=target,
            dst_ref=target,
            send_sem=cross_send.at[piece, stage],
            recv_sem=cross_recv.at[piece, stage],
            device_id={"dp": me, "mp": 1 - core},
            device_id_type=MESH_ID,
        )

    def keep(number):
        spot = place(levels, (), own)
        return pltpu.make_async_copy(short[number], wholes[number].at[spot], here_sem.at[number])

    ready = set()
    for piece in GATHER_FIRST:
        number = pieces[piece][0]
        if number not in ready:
            ready.add(number)
            load(number).wait()
            short[number][...] = shards[number][...].astype(jnp.bfloat16)
            keep(number).start()
        hop(piece, 0, False).start()
    masked = jnp.int32(0)
    for clip in range(tally.shape[0]):
        masked = masked + (NPATCH - tally[clip])
    corner = lax.broadcasted_iota(jnp.int32, (8, 128), 0) + lax.broadcasted_iota(jnp.int32, (8, 128), 1) == 0
    tally_out[...] = jnp.where(corner, masked.astype(jnp.float32), 0.0)

    def swap(stage):
        if stage < levels:
            to = {"dp": partner(me, own, stage), "mp": core}
        else:
            to = {"dp": me, "mp": 1 - core}
        return pltpu.make_async_remote_copy(
            src_ref=tally_out,
            dst_ref=tally_land.at[stage],
            send_sem=tally_send.at[stage],
            recv_sem=tally_recv.at[stage],
            device_id=to,
            device_id_type=MESH_ID,
        )

    def swap_end(stage):
        swap(stage).wait()
        tally_out[...] = tally_out[...] + tally_land[stage]

    swap(levels).start()
    for number in range(count):
        keep(number).wait()
    swap_end(levels)
    for stage, order in enumerate(GATHER_STEPS):
        swap(stage).start()
        for piece in order:
            hop(piece, stage, True).wait_recv()
            if stage + 1 < levels:
                hop(piece, stage + 1, False).start()
            cross(piece, stage, core).start()
        swap_end(stage)
        if stage == levels - 2:
            for number in range(6):
                load(count + number).wait()
            cut_patches(*scene, *made)
    def save(number):
        return pltpu.make_async_copy(wholes[number], outs[number], save_sem.at[number])

    last = {}
    for place_in, piece in enumerate(GATHER_STEPS[levels - 1]):
        last[pieces[piece][0]] = place_in
    for number in sorted(last, key=lambda found: last[found]):
        for piece in range(len(pieces)):
            if pieces[piece][0] == number:
                for stage in range(levels):
                    cross(piece, stage, 1 - core).wait_recv()
        save(number).start()
    for piece in range(len(pieces)):
        for stage in range(levels):
            hop(piece, stage, False).wait_send()
            cross(piece, stage, core).wait_send()
    for number in range(count):
        save(number).wait()


def gather_rows(shards, tally, scene, devices):
    levels, count = bit_count(devices), len(shards)
    lead = (2,) * levels
    clips = scene[0].shape[0]
    pieces = cut_pieces(GATHER_PARTS, [(shard.shape[0], shard.shape[1] // 2) for shard in shards])
    dma = pltpu.SemaphoreType.DMA
    vmem, far = pl.BlockSpec(memory_space=pltpu.VMEM), pl.BlockSpec(memory_space=pltpu.HBM)
    found = pl.pallas_call(
        functools.partial(gather_kernel, levels, pieces, count),
        out_shape=[jax.ShapeDtypeStruct(lead + shard.shape, jnp.bfloat16) for shard in shards]
        + [
            jax.ShapeDtypeStruct((8, 128), jnp.float32),
            jax.ShapeDtypeStruct((clips, SLOTS, PATCH), jnp.bfloat16),
            jax.ShapeDtypeStruct((clips, SLOTS, D), jnp.float32),
            jax.ShapeDtypeStruct((clips, NPATCH, PATCH), jnp.float32),
        ],
        in_specs=[far] * count + [pl.BlockSpec(memory_space=pltpu.SMEM)] + [far] * 6,
        out_specs=[pl.BlockSpec(memory_space=pl.ANY)] * count + [vmem] * 4,
        scratch_shapes=[pltpu.VMEM(lead + shard.shape, jnp.bfloat16) for shard in shards]
        + [dma((count,))]
        + [pltpu.VMEM(shard.shape, jnp.bfloat16) for shard in shards]
        + [pltpu.VMEM(piece.shape, piece.dtype) for piece in (*shards, *scene)]
        + [dma((count + 6,))]
        + [dma((count,))]
        + [dma((len(pieces), levels))] * 4
        + [pltpu.VMEM((levels + 1, 8, 128), jnp.float32)]
        + [dma((levels + 1,))] * 2,
        compiler_params=pltpu.CompilerParams(
            collective_id=1, has_side_effects=True, vmem_limit_bytes=60 * 2**20
        ),
        name="gather_rows",
    )(*shards, tally, *scene)
    return found[:count], found[count], found[count + 1 :]


def reduce_kernel(levels, pieces, count, owners, devices, *refs):
    blocks = len(owners)
    grads, stats_in, old = refs[:count], refs[count], refs[count + 1 : count + 1 + blocks]
    rest = refs[count + 1 + blocks :]
    sums, stats_out, wholes = rest[:count], rest[count], rest[count + 1 : count + 1 + blocks]
    rest = rest[count + 1 + blocks :]
    mine, theirs, rest = rest[:count], rest[count : 2 * count], rest[2 * count :]
    kept, rest = rest[:count], rest[count:]
    landing, rest = rest[: len(pieces) * levels], rest[len(pieces) * levels :]
    staged, rest = rest[:blocks], rest[blocks:]
    stats_land, here_sem, pair_send, pair_recv, send_sem, recv_sem, last_send, last_recv = rest[:8]
    stats_send, stats_recv, own_sem, out_send, out_recv, cross_send, cross_recv = rest[8:]
    me, own = own_bits(levels)
    core = lax.axis_index("mp")
    orders = [AXIS_ORDERS[turn] for turn in REDUCE_TURNS]
    barrier = pltpu.get_barrier_semaphore()

    @pl.loop(0, devices)
    def greet_one(other):
        @pl.when(other != me)
        def signal_one():
            pl.semaphore_signal(
                barrier, inc=1, device_id={"dp": other, "mp": core}, device_id_type=MESH_ID
            )

    pl.semaphore_signal(barrier, inc=1, device_id={"dp": me, "mp": 1 - core}, device_id_type=MESH_ID)
    pl.semaphore_wait(barrier, devices)

    def half(number, which):
        width = sums[number].shape[1] // 2
        return (slice(None), pl.ds(pl.multiple_of(which * width, 128), width))

    def cut(piece):
        number, row, rows, column, columns = pieces[piece]
        return (pl.ds(row, rows), pl.ds(column, columns))

    def side(piece, which):
        number, row, rows, column, columns = pieces[piece]
        width = sums[number].shape[1] // 2
        return (pl.ds(row, rows), pl.ds(pl.multiple_of(which * width + column, 128), columns))

    every = (slice(None),) * levels

    def pair(piece):
        number = pieces[piece][0]
        return pltpu.make_async_remote_copy(
            src_ref=grads[number].at[every + side(piece, 1 - core)],
            dst_ref=theirs[number].at[every + cut(piece)],
            send_sem=pair_send.at[piece],
            recv_sem=pair_recv.at[piece],
            device_id={"dp": me, "mp": 1 - core},
            device_id_type=MESH_ID,
        )

    def load(piece):
        number = pieces[piece][0]
        return pltpu.make_async_copy(
            grads[number].at[every + side(piece, core)],
            mine[number].at[every + cut(piece)],
            here_sem.at[piece],
        )

    def hop(piece, stage):
        order = orders[piece]
        spot = place(levels, order[stage + 1 :], own, order[stage])
        return pltpu.make_async_remote_copy(
            src_ref=theirs[pieces[piece][0]].at[spot + cut(piece)],
            dst_ref=landing[piece * levels + stage],
            send_sem=send_sem.at[piece, stage],
            recv_sem=recv_sem.at[piece, stage],
            device_id={"dp": partner(me, own, order[stage]), "mp": core},
            device_id_type=MESH_ID,
        )

    def share(number, which):
        region = sums[number].at[half(number, which)]
        return pltpu.make_async_remote_copy(
            src_ref=region,
            dst_ref=region,
            send_sem=last_send.at[number],
            recv_sem=last_recv.at[number],
            device_id={"dp": me, "mp": 1 - core},
            device_id_type=MESH_ID,
        )

    def deliver(number, source):
        return pltpu.make_async_remote_copy(
            src_ref=staged[number],
            dst_ref=wholes[number].at[(source,) + half(number, core)],
            send_sem=out_send.at[number],
            recv_sem=out_recv.at[number, source],
            device_id={"dp": owners[number], "mp": core},
            device_id_type=MESH_ID,
        )

    def deliver_here(number):
        return pltpu.make_async_copy(
            staged[number], wholes[number].at[(me,) + half(number, core)], own_sem
        )

    def cross(number, source, which):
        region = wholes[number].at[(source,) + half(number, which)]
        return pltpu.make_async_remote_copy(
            src_ref=region,
            dst_ref=region,
            send_sem=cross_send.at[number, source],
            recv_sem=cross_recv.at[number, source],
            device_id={"dp": me, "mp": 1 - core},
            device_id_type=MESH_ID,
        )

    def kept_spot(order, found):
        return tuple(found.get(bit, own[bit]) for bit in range(levels - 1, -1, -1) if bit != order[0])

    def fold(piece, stage):
        order, number = orders[piece], pieces[piece][0]
        free = order[stage:]
        loose = [bit for bit in range(levels - 1, -1, -1) if bit in free and bit != order[stage]]
        region = cut(piece)

        @pl.loop(0, 2 ** len(loose))
        def add_block(block):
            found = {
                bit: lax.rem(lax.div(block, 2 ** (len(loose) - 1 - i)), 2) for i, bit in enumerate(loose)
            }

            def total(way):
                now = dict(found)
                now[order[stage]] = way
                full = tuple(now.get(bit, own[bit]) for bit in range(levels - 1, -1, -1)) + region
                if stage == 0:
                    value = mine[number][full].astype(jnp.float32) + theirs[number][full].astype(jnp.float32)
                else:
                    land = tuple(now[bit] for bit in range(levels - 1, -1, -1) if bit in free)
                    arrived = landing[piece * levels + stage - 1][land].astype(jnp.float32)
                    value = kept[number][kept_spot(order, now) + region] + arrived
                return full, value

            full, value = total(1 - own[order[stage]])
            theirs[number][full] = value.astype(theirs[number].dtype)
            full, value = total(own[order[stage]])
            kept[number][kept_spot(order, found) + region] = value

    for piece in REDUCE_FIRST:
        pair(piece).start()
        load(piece).start()
    for piece in REDUCE_FIRST:
        load(piece).wait()
        pair(piece).wait_recv()
        fold(piece, 0)
        hop(piece, 0).start()
    squares = jnp.zeros((8, 128), jnp.float32)
    for piece, stage in [(piece, stage) for stage in range(levels) for piece in REDUCE_STEPS[stage]]:
        hop(piece, stage).wait_recv()
        if stage + 1 < levels:
            fold(piece, stage + 1)
            hop(piece, stage + 1).start()
        else:
            number = pieces[piece][0]
            arrived = landing[piece * levels + stage][...].astype(jnp.float32)
            total = kept[number][kept_spot(orders[piece], {}) + cut(piece)] + arrived
            sums[number][side(piece, core)] = total
            rows, width = total.shape
            for row in range(0, rows, 8):
                for column in range(0, width, 128):
                    part = total[row : row + 8, column : column + 128]
                    squares = squares + part * part
    for number in range(blocks, count):
        share(number, core).start()
    row = lax.broadcasted_iota(jnp.int32, (8, 128), 0)
    stats_out[...] = jnp.where(row == 0, jnp.sum(squares, axis=0, keepdims=True), stats_in[...])
    add_up(me, core, devices, stats_out, stats_land, stats_send, stats_recv, own_sem)
    norm = jnp.sqrt(jnp.sum(stats_out[0:1, :], axis=1, keepdims=True))
    factor = jnp.minimum(1.0, CLIP_MAX / (norm + 1e-06))
    for number in range(blocks):
        region = half(number, core)
        renewed = 0.5 * old[number][region] + factor * sums[number][region]
        sums[number][region] = renewed
        staged[number][...] = renewed.astype(staged[number].dtype)
        share(number, core).start()

        @pl.when(me != owners[number])
        def start_one(number=number):
            deliver(number, me).start()

        @pl.when(me == owners[number])
        def start_here(number=number):
            deliver_here(number).start()

    for piece in range(len(pieces)):
        pair(piece).wait_send()
        for stage in range(levels):
            hop(piece, stage).wait_send()
    for number in range(blocks):

        @pl.when(me == owners[number])
        def collect(number=number):
            deliver_here(number).wait()

            @pl.loop(0, devices)
            def forward(source):
                @pl.when(source != me)
                def arrived():
                    deliver(number, source).wait_recv()

                cross(number, source, core).start()

            @pl.loop(0, devices)
            def finish(source):
                cross(number, source, core).wait_send()
                cross(number, source, 1 - core).wait_recv()

        @pl.when(me != owners[number])
        def end_one(number=number):
            deliver(number, me).wait_send()

    for number in range(count):
        share(number, core).wait_send()
        share(number, 1 - core).wait_recv()


def reduce_rows(grads, stats, old, owners, devices):
    levels, count, blocks = bit_count(devices), len(grads), len(old)
    lead = (2,) * levels
    dma = pltpu.SemaphoreType.DMA
    shapes = [grad.shape[levels:] for grad in grads]
    halves = [(rows, columns // 2) for rows, columns in shapes]
    kinds = [grad.dtype for grad in grads]
    pieces = cut_pieces(REDUCE_PARTS, halves)
    scratch = [pltpu.VMEM(lead + shape, kind) for shape, kind in zip(halves, kinds)] * 2
    scratch += [pltpu.VMEM(lead[1:] + shape, jnp.float32) for shape in halves]
    for number, row, rows, column, columns in pieces:
        for stage in range(levels):
            scratch.append(pltpu.VMEM((2,) * (levels - 1 - stage) + (rows, columns), kinds[number]))
    scratch += [pltpu.VMEM(halves[number], kinds[number]) for number in range(blocks)]
    scratch.append(pltpu.VMEM((devices + 1, 8, 128), jnp.float32))
    scratch += [dma((len(pieces),))] * 3 + [dma((len(pieces), levels))] * 2 + [dma((count,))] * 2
    scratch += [dma((devices + 1,))] * 2 + [dma, dma((blocks,))] + [dma((blocks, devices))] * 3
    vmem, anywhere = pl.BlockSpec(memory_space=pltpu.VMEM), pl.BlockSpec(memory_space=pl.ANY)
    found = pl.pallas_call(
        functools.partial(reduce_kernel, levels, pieces, count, owners, devices),
        out_shape=[jax.ShapeDtypeStruct(shape, jnp.float32) for shape in shapes]
        + [jax.ShapeDtypeStruct((8, 128), jnp.float32)]
        + [jax.ShapeDtypeStruct((devices,) + shapes[number], kinds[number]) for number in range(blocks)],
        in_specs=[anywhere] * count + [vmem] * (1 + blocks),
        out_specs=[vmem] * (count + 1) + [anywhere] * blocks,
        scratch_shapes=scratch,
        compiler_params=pltpu.CompilerParams(
            collective_id=2, has_side_effects=True, vmem_limit_bytes=60 * 2**20
        ),
        name="reduce_rows",
    )(*grads, stats, *old)
    return found[:blocks], found[blocks:count], found[count], found[count + 1 :]


def return_kernel(owners, count, devices, *refs):
    wholes, rows = refs[:count], refs[count : 2 * count]
    here_sem, send_sem, recv_sem, cross_send, cross_recv = refs[2 * count :]
    me, core = lax.axis_index("dp"), lax.axis_index("mp")
    barrier = pltpu.get_barrier_semaphore()
    owning = functools.reduce(jnp.logical_or, [me == owner for owner in owners])
    for owner in owners:

        @pl.when(me != owner)
        def greet_owner(owner=owner):
            pl.semaphore_signal(
                barrier, inc=1, device_id={"dp": owner, "mp": core}, device_id_type=MESH_ID
            )

    pl.semaphore_signal(barrier, inc=1, device_id={"dp": me, "mp": 1 - core}, device_id_type=MESH_ID)

    @pl.when(owning)
    def wait_all():
        pl.semaphore_wait(barrier, devices)

    @pl.when(jnp.logical_not(owning))
    def wait_pair():
        pl.semaphore_wait(barrier, 1)

    def half(number, which):
        width = rows[number].shape[1] // 2
        return (slice(None), pl.ds(pl.multiple_of(which * width, 128), width))

    def hop(number, target):
        return pltpu.make_async_remote_copy(
            src_ref=wholes[number].at[(target,) + half(number, core)],
            dst_ref=rows[number].at[half(number, core)],
            send_sem=send_sem.at[number, target],
            recv_sem=recv_sem.at[number],
            device_id={"dp": target, "mp": core},
            device_id_type=MESH_ID,
        )

    def cross(number, which):
        region = rows[number].at[half(number, which)]
        return pltpu.make_async_remote_copy(
            src_ref=region,
            dst_ref=region,
            send_sem=cross_send.at[number],
            recv_sem=cross_recv.at[number],
            device_id={"dp": me, "mp": 1 - core},
            device_id_type=MESH_ID,
        )

    for number in range(count):

        @pl.when(me == owners[number])
        def hand_out(number=number):
            own = pltpu.make_async_copy(
                wholes[number].at[(me,) + half(number, core)], rows[number].at[half(number, core)], here_sem
            )
            own.start()

            @pl.loop(0, devices)
            def start_one(target):
                @pl.when(target != me)
                def start_other():
                    hop(number, target).start()

            own.wait()

    for number in range(count):

        @pl.when(me != owners[number])
        def arrive(number=number):
            hop(number, me).wait_recv()

        cross(number, core).start()
    for number in range(count):
        cross(number, core).wait_send()
        cross(number, 1 - core).wait_recv()

        @pl.when(me == owners[number])
        def end_out(number=number):
            @pl.loop(0, devices)
            def end_one(target):
                @pl.when(target != me)
                def end_other():
                    hop(number, target).wait_send()


def return_rows(wholes, owners, devices):
    count = len(wholes)
    dma = pltpu.SemaphoreType.DMA
    vmem = pl.BlockSpec(memory_space=pltpu.VMEM)
    return pl.pallas_call(
        functools.partial(return_kernel, owners, count, devices),
        out_shape=[jax.ShapeDtypeStruct(whole.shape[1:], whole.dtype) for whole in wholes],
        in_specs=[pl.BlockSpec(memory_space=pl.ANY)] * count,
        out_specs=[vmem] * count,
        scratch_shapes=[dma, dma((count, devices)), dma((count,)), dma((count,)), dma((count,))],
        compiler_params=pltpu.CompilerParams(
            collective_id=4, has_side_effects=True, vmem_limit_bytes=60 * 2**20
        ),
        name="return_rows",
    )(*wholes)


def finish_kernel(count, rates, *refs):
    rows, masters, updated = refs[:count], refs[count : 2 * count], refs[2 * count :]
    for number in range(count):
        change = rates[number] * rows[number][...].astype(jnp.float32)
        updated[number][...] = masters[number][...] * (1.0 - LR_MUON * DECAY) - change


def finish(rows, masters, devices):
    count = len(rows)
    rates = []
    for master in masters:
        rates.append(LR_MUON * 0.2 * math.sqrt(max(master.shape[0] * devices, master.shape[1])))
    vmem = pl.BlockSpec(memory_space=pltpu.VMEM)
    return pl.pallas_call(
        functools.partial(finish_kernel, count, rates),
        out_shape=[jax.ShapeDtypeStruct(master.shape, jnp.float32) for master in masters],
        in_specs=[vmem] * (2 * count),
        out_specs=[vmem] * count,
        compiler_params=pltpu.CompilerParams(vmem_limit_bytes=56 * 2**20),
        name="finish",
    )(*rows, *masters)


def muon_kernel(owners, shapes, *refs):
    count = len(owners)
    mats, moved, stats, adam_in = refs[:count], refs[count : 2 * count], refs[2 * count], refs[2 * count + 1 :][:8]
    rest = refs[2 * count + 9 :]
    outs, moved_out, adam_out, rest = rest[:count], rest[count : 2 * count], rest[2 * count :][:6], rest[2 * count + 6 :]
    exact, wide, wide_low, tall, wide_out, tall_out, gram = rest[:7]
    base, poly, other, chain, sem, in_sem, out_sem = rest[7:14]
    held_rows = rest[14:]

    def move_in(number):
        return pltpu.make_async_copy(moved[number], held_rows[number], in_sem.at[number])

    def move_out(number):
        return pltpu.make_async_copy(held_rows[number], moved_out[number], out_sem.at[number])

    for number in range(count):
        move_in(number).start()
    norm = jnp.sqrt(jnp.sum(stats[0:1, :], axis=1, keepdims=True))
    factor = jnp.minimum(1.0, CLIP_MAX / (norm + 1e-06))
    for group in range(2):
        weight, first, second, grad = [ref[...] for ref in adam_in[4 * group : 4 * group + 4]]
        made = adam_update(weight, first, second, grad * factor, DECAY)
        for place_out in range(3):
            adam_out[3 * group + place_out][...] = made[place_out]
    me, core = lax.axis_index("dp"), lax.axis_index("mp")
    side = gram.shape[0]
    step = 256
    bf = jnp.bfloat16

    def dims(number):
        height, breadth = shapes[number]
        return height, breadth, LONG_COLS[number]

    def span(index):
        return pl.ds(pl.multiple_of(index * step, step), step)

    def split(value):
        high = value.astype(bf)
        return high, (value - high.astype(jnp.float32)).astype(bf)

    gram[...] = jnp.zeros_like(gram)
    for number in range(count):

        @pl.when(me == owners[number])
        def start(number=number):
            height, breadth, long_cols = dims(number)
            short = min(height, breadth)
            held = (wide if long_cols else tall).at[:height, :breadth]
            fine = mats[number].dtype == jnp.float32
            load = pltpu.make_async_copy(mats[number], exact if fine else held, sem)
            load.start()
            load.wait()
            if fine:
                rest = wide_low

                @pl.loop(0, height // step)
                def part_rows(index):
                    high, low = split(exact[span(index), :])
                    held[span(index), :] = high
                    rest[span(index), :] = low

            for index in range(short // step):
                first, beyond = slice(index * step, (index + 1) * step), slice(index * step, short)
                if long_cols:
                    total = dot_rows(held[first, :], held[beyond, :])
                    if fine:
                        total = total + dot_rows(held[first, :], rest[beyond, :])
                        total = total + dot_rows(rest[first, :], held[beyond, :])
                else:
                    total = dot_columns(held[:, first], held[:, beyond])
                gram[first, beyond] = total

    for number in range(count):
        move_in(number).wait()
        move_out(number).start()
    owning = functools.reduce(jnp.logical_or, [me == owner for owner in owners])

    @pl.when(owning)
    def iterate():
        parts = [
            (slice(index * step, (index + 1) * step), slice(index * step, side))
            for index in range(side // step)
        ]
        ones = lax.broadcasted_iota(jnp.int32, (step, step), 0) == lax.broadcasted_iota(
            jnp.int32, (step, step), 1
        )
        trace = jnp.float32(0.0)
        for first, beyond in parts:
            trace = trace + jnp.sum(jnp.where(ones, gram[first, first], 0.0))
        scale = 1.0 / (jnp.sqrt(jnp.full((8, 128), trace, jnp.float32)) + 1e-07)
        scale = scale[0:1, 0:1]

        def store(target, index, value):
            high, low = split(value)
            target[0, parts[index][0], parts[index][1]] = high
            target[1, parts[index][0], parts[index][1]] = low
            for later in range(index + 1, side // step):
                shift = (later - index) * step
                high, low = split(value[:, shift : shift + step].T)
                target[0, parts[later][0], parts[index][0]] = high
                target[1, parts[later][0], parts[index][0]] = low

        def product(left, right, index):
            first, beyond = parts[index]
            high, low = left[0, first, :], left[1, first, :]
            total = jnp.dot(high, right[0, :, beyond], preferred_element_type=jnp.float32)
            total = total + jnp.dot(high, right[1, :, beyond], preferred_element_type=jnp.float32)
            return total + jnp.dot(low, right[0, :, beyond], preferred_element_type=jnp.float32)

        for index, (first, beyond) in enumerate(parts):
            store(base, index, gram[first, beyond] * (scale * scale))

        @pl.loop(0, NS_ITERS)
        def newton(iteration):
            for index, (first, beyond) in enumerate(parts):
                now = base[0, first, beyond].astype(jnp.float32) + base[1, first, beyond].astype(jnp.float32)
                row = lax.broadcasted_iota(jnp.int32, now.shape, 0)
                column = lax.broadcasted_iota(jnp.int32, now.shape, 1)
                value = jnp.where(row == column, NS_A, 0.0) + NS_B * now
                store(poly, index, value + NS_C * product(base, base, index))

            @pl.when(iteration < NS_ITERS - 1)
            def advance():
                for index in range(len(parts)):
                    store(other, index, product(base, poly, index))
                for index in range(len(parts)):
                    store(base, index, product(other, poly, index))

            @pl.when(iteration == 0)
            def begin():
                chain[...] = poly[...]

            @pl.when(iteration > 0)
            def follow():
                for index in range(len(parts)):
                    store(other, index, product(chain, poly, index))
                chain[...] = other[...]

        for first, beyond in parts:
            value = chain[0, first, :].astype(jnp.float32) + chain[1, first, :].astype(jnp.float32)
            high, low = split(value * scale)
            other[0, first, :] = high
            other[1, first, :] = low

    for number in range(count):

        @pl.when(me == owners[number])
        def end(number=number):
            height, breadth, long_cols = dims(number)
            short = min(height, breadth)
            width = breadth // 2
            part = pl.ds(pl.multiple_of(core * width, 128), width)
            if long_cols:
                held, made = wide.at[:height, :breadth], wide_out.at[:height, :width]

                @pl.loop(0, height // step)
                def wide_rows(index):
                    total = jnp.dot(
                        other[0, span(index), :short], held[:, part], preferred_element_type=jnp.float32
                    ) + jnp.dot(
                        other[1, span(index), :short], held[:, part], preferred_element_type=jnp.float32
                    )
                    if mats[number].dtype == jnp.float32:
                        total = total + jnp.dot(
                            other[0, span(index), :short],
                            wide_low[:, part],
                            preferred_element_type=jnp.float32,
                        )
                    made[span(index), :] = total.astype(bf)
            else:
                held, made = tall.at[:height, :breadth], tall_out.at[:height, :width]

                @pl.loop(0, height // step)
                def tall_rows(index):
                    total = jnp.dot(
                        held[span(index), :], other[0, :short, part], preferred_element_type=jnp.float32
                    ) + jnp.dot(
                        held[span(index), :], other[1, :short, part], preferred_element_type=jnp.float32
                    )
                    made[span(index), :] = total.astype(bf)

            save = pltpu.make_async_copy(made, outs[number].at[:, part], sem)
            save.start()
            save.wait()

    for number in range(count):
        move_out(number).wait()


def orthogonalize(mats, moved, stats, adam, owners):
    count = len(mats)
    shapes = [mat.shape for mat in mats]
    side = max(min(shape) for shape in shapes)
    longest = max(max(shape) for shape in shapes)
    double = pltpu.VMEM((2, side, side), jnp.bfloat16)
    (fine,) = [mat.shape for mat in mats if mat.dtype == jnp.float32]
    vmem, anywhere = pl.BlockSpec(memory_space=pltpu.VMEM), pl.BlockSpec(memory_space=pl.ANY)
    renewed = (adam[0], adam[1], adam[2], adam[4], adam[5], adam[6])
    found = pl.pallas_call(
        functools.partial(muon_kernel, owners, shapes),
        out_shape=[jax.ShapeDtypeStruct(shape, jnp.bfloat16) for shape in shapes]
        + [jax.ShapeDtypeStruct(piece.shape, piece.dtype) for piece in moved]
        + [jax.ShapeDtypeStruct(piece.shape, piece.dtype) for piece in renewed],
        in_specs=[anywhere] * (2 * count) + [vmem] * 9,
        out_specs=[anywhere] * (2 * count) + [vmem] * 6,
        scratch_shapes=[
            pltpu.VMEM(fine, jnp.float32),
            pltpu.VMEM((side, longest), jnp.bfloat16),
            pltpu.VMEM(fine, jnp.bfloat16),
            pltpu.VMEM((longest, side), jnp.bfloat16),
            pltpu.VMEM((side, longest // 2), jnp.bfloat16),
            pltpu.VMEM((longest, side // 2), jnp.bfloat16),
            pltpu.VMEM((side, side), jnp.float32),
            double,
            double,
            double,
            double,
            pltpu.SemaphoreType.DMA,
            pltpu.SemaphoreType.DMA((count,)),
            pltpu.SemaphoreType.DMA((count,)),
        ]
        + [pltpu.VMEM(piece.shape, piece.dtype) for piece in moved],
        compiler_params=pltpu.CompilerParams(vmem_limit_bytes=60 * 2**20),
        name="orthogonalize",
    )(*mats, *moved, stats, *adam)
    return found[:count], found[count : 2 * count], found[2 * count : 2 * count + 3], found[2 * count + 3 :]


def window_place(position):
    time_row = (position // GF + GT - SHIFT) % GT
    freq_col = (position % GF + GF - SHIFT) % GF
    window = (time_row // WIN) * (GF // WIN) + freq_col // WIN
    return window * (WIN * WIN) + (time_row % WIN) * WIN + freq_col % WIN


def window_sinusoid(channels):
    quarter = channels // 4
    frequency = 1.0 / 10000.0 ** (np.arange(quarter) / quarter)
    position = np.arange(NPATCH)
    time_rows = (position // GF)[:, None] * frequency
    freq_cols = (position % GF)[:, None] * frequency
    table = np.concatenate([np.sin(time_rows), np.cos(time_rows), np.sin(freq_cols), np.cos(freq_cols)], axis=1)
    moved = np.zeros_like(table)
    moved[window_place(position)] = table
    return moved.astype(np.float32)


def window_scene(spec, keep):
    position = np.arange(NPATCH)
    row = np.empty(NPATCH, np.int32)
    row[window_place(position)] = position
    take = (row[:, None] // GF == np.arange(GT)[None, :]).astype(np.float32)
    source = np.arange(PS * GF * PS)[:, None]
    target = np.arange(PATCH)[None, :]
    fold = np.logical_and(source // (GF * PS) == target // PS, source % PS == target % PS)
    table = window_sinusoid(D)
    high = table.astype(jnp.bfloat16)
    low = (table - high.astype(np.float32)).astype(jnp.bfloat16)
    return (
        spec.reshape(spec.shape[0], GT, PS * GF * PS),
        window_place(jnp.pad(keep, ((0, 0), (0, SLOTS - VIS)))),
        jnp.asarray(take, jnp.bfloat16),
        jnp.asarray(row[:, None] % GF),
        jnp.asarray(fold, jnp.bfloat16),
        jnp.asarray(np.concatenate([high, low], axis=1)),
    )


@jax.custom_vjp
def times(inputs, matrix):
    return jnp.dot(inputs.astype(jnp.bfloat16), matrix.astype(jnp.bfloat16), preferred_element_type=jnp.float32)


def times_keep(inputs, matrix):
    short = inputs.astype(jnp.bfloat16)
    return jnp.dot(short, matrix.astype(jnp.bfloat16), preferred_element_type=jnp.float32), (short, matrix)


def times_back(kept, grad):
    short, matrix = kept
    grad = grad.astype(jnp.bfloat16)
    back = lax.dot_general(
        grad, matrix.astype(jnp.bfloat16), (((1,), (1,)), ((), ())), preferred_element_type=jnp.float32
    )
    gain = lax.dot_general(short, grad, (((0,), (0,)), ((), ())), preferred_element_type=jnp.float32)
    return back, gain.astype(matrix.dtype)


times.defvjp(times_keep, times_back)


def dot_rows(left, right):
    return lax.dot_general(left, right, (((1,), (1,)), ((), ())), preferred_element_type=jnp.float32)


def dot_columns(left, right):
    return lax.dot_general(left, right, (((0,), (0,)), ((), ())), preferred_element_type=jnp.float32)


def head_lanes(value, head, size):
    lane = lax.broadcasted_iota(jnp.int32, value.shape, 1)
    return jnp.where(lane // size == head, value, jnp.zeros_like(value))


def soft_keys(queries, keys_here, allow, size):
    rows = queries.shape[0]
    scores = dot_rows(keys_here, queries).reshape(128 // size, rows, rows)
    scores = jnp.where(allow, scores * size ** (-0.5), -1e30)
    exponent = jnp.exp(scores - jnp.max(scores, axis=1, keepdims=True))
    return exponent / jnp.sum(exponent, axis=1, keepdims=True)


def flat_heads(value):
    return value.astype(jnp.bfloat16).reshape(-1, value.shape[2])


def attention_kernel(size, joined, allowed, out):
    width = out.shape[1]
    allow = allowed[...][None] > 0.0
    for lane in range(0, width, 128):
        queries = joined[:, lane : lane + 128]
        keys_here = stack_heads(joined[:, width + lane : width + lane + 128], size)
        values_here = stack_heads(joined[:, 2 * width + lane : 2 * width + lane + 128], size)
        soft = flat_heads(soft_keys(queries, keys_here, allow, size))
        out[:, lane : lane + 128] = dot_columns(soft, values_here).astype(jnp.bfloat16)


def attention_back_kernel(size, joined, allowed, grad, out, query_sum, value_sum):
    width, rows = grad.shape[1], grad.shape[0]
    allow = allowed[...][None] > 0.0

    @pl.when(pl.program_id(0) == 0)
    def clear():
        query_sum[...] = jnp.zeros_like(query_sum)
        value_sum[...] = jnp.zeros_like(value_sum)

    for lane in range(0, width, 128):
        queries = joined[:, lane : lane + 128]
        keys_here = stack_heads(joined[:, width + lane : width + lane + 128], size)
        values_here = stack_heads(joined[:, 2 * width + lane : 2 * width + lane + 128], size)
        pull = grad[:, lane : lane + 128]
        soft = soft_keys(queries, keys_here, allow, size)
        soft_grad = dot_rows(values_here, pull).reshape(128 // size, rows, rows)
        score_grad = soft * (soft_grad - jnp.sum(soft * soft_grad, axis=1, keepdims=True))
        score_grad = flat_heads(score_grad * size ** (-0.5))
        soft = flat_heads(soft)
        query_grad = dot_columns(score_grad, keys_here)
        key_grad = unstack_heads(jnp.dot(score_grad, queries, preferred_element_type=jnp.float32), size)
        value_grad = unstack_heads(jnp.dot(soft, pull, preferred_element_type=jnp.float32), size)
        out[:, lane : lane + 128] = query_grad.astype(jnp.bfloat16)
        out[:, width + lane : width + lane + 128] = key_grad.astype(jnp.bfloat16)
        out[:, 2 * width + lane : 2 * width + lane + 128] = value_grad.astype(jnp.bfloat16)
        query_sum[0:1, lane : lane + 128] += jnp.sum(query_grad, axis=0, keepdims=True)
        value_sum[0:1, lane : lane + 128] += jnp.sum(value_grad, axis=0, keepdims=True)


def window_fold(value, heads):
    lane = lax.broadcasted_iota(jnp.int32, (1, 1, value.shape[1]), 2) // (WIN * WIN)
    value = value.reshape(heads, 8, WIN * WIN, value.shape[1])
    found = value[:, 0]
    for window in range(1, 8):
        found = jnp.where(lane == window, value[:, window], found)
    return found


def window_spread(value):
    heads = value.shape[0]
    short = value.astype(jnp.bfloat16)
    lane = lax.broadcasted_iota(jnp.int32, short.shape, 2) // (WIN * WIN)
    parts = []
    for head in range(heads):
        for window in range(8):
            parts.append(
                jnp.where(lane[head] == window, short[head], jnp.zeros_like(short[head]))
            )
    return jnp.concatenate(parts, axis=0)


def stack_heads(value, size):
    per = value.shape[1] // size
    return jnp.concatenate([head_lanes(value, head, size) for head in range(per)], axis=0)


def unstack_heads(value, size):
    per = value.shape[1] // size
    rows = value.shape[0] // per
    lane = lax.broadcasted_iota(jnp.int32, (rows, value.shape[1]), 1) // size
    found = value[:rows]
    for head in range(1, per):
        found = jnp.where(lane == head, value[head * rows : (head + 1) * rows], found)
    return found


def soft_fold(queries, keys_here, allow, size):
    scores = window_fold(dot_rows(keys_here, queries), 128 // size)
    scores = jnp.where(allow, scores * size ** (-0.5), -1e30)
    exponent = jnp.exp(scores - jnp.max(scores, axis=1, keepdims=True))
    return exponent / jnp.sum(exponent, axis=1, keepdims=True)


def window_kernel(size, joined, allowed, out):
    for group in range(allowed.shape[0]):
        rows = pl.ds(group * 128, 128)
        window_group(size, joined.at[rows], allowed.at[group], out.at[rows])


def window_group(size, joined, allowed, out):
    width = out.shape[1]
    allow = allowed[...][None] > 0.0
    for lane in range(0, width, 128):
        queries = joined[:, lane : lane + 128]
        keys_here = stack_heads(joined[:, width + lane : width + lane + 128], size)
        values_here = stack_heads(joined[:, 2 * width + lane : 2 * width + lane + 128], size)
        soft = window_spread(soft_fold(queries, keys_here, allow, size))
        out[:, lane : lane + 128] = dot_columns(soft, values_here).astype(jnp.bfloat16)


def window_back_kernel(size, joined, allowed, grad, out, query_sum, value_sum):
    @pl.when(pl.program_id(0) == 0)
    def clear():
        query_sum[...] = jnp.zeros_like(query_sum)
        value_sum[...] = jnp.zeros_like(value_sum)

    for group in range(allowed.shape[0]):
        rows = pl.ds(group * 128, 128)
        window_back_group(
            size, joined.at[rows], allowed.at[group], grad.at[rows], out.at[rows], query_sum, value_sum
        )


def window_back_group(size, joined, allowed, grad, out, query_sum, value_sum):
    width = grad.shape[1]
    allow = allowed[...][None] > 0.0
    for lane in range(0, width, 128):
        queries = joined[:, lane : lane + 128]
        keys_here = stack_heads(joined[:, width + lane : width + lane + 128], size)
        values_here = stack_heads(joined[:, 2 * width + lane : 2 * width + lane + 128], size)
        pull = grad[:, lane : lane + 128]
        soft = soft_fold(queries, keys_here, allow, size)
        soft_grad = window_fold(dot_rows(values_here, pull), 128 // size)
        score_grad = soft * (soft_grad - jnp.sum(soft * soft_grad, axis=1, keepdims=True))
        score_grad = window_spread(score_grad * size ** (-0.5))
        soft = window_spread(soft)
        query_grad = dot_columns(score_grad, keys_here)
        key_grad = unstack_heads(jnp.dot(score_grad, queries, preferred_element_type=jnp.float32), size)
        value_grad = unstack_heads(jnp.dot(soft, pull, preferred_element_type=jnp.float32), size)
        out[:, lane : lane + 128] = query_grad.astype(jnp.bfloat16)
        out[:, width + lane : width + lane + 128] = key_grad.astype(jnp.bfloat16)
        out[:, 2 * width + lane : 2 * width + lane + 128] = value_grad.astype(jnp.bfloat16)
        query_sum[0:1, lane : lane + 128] += jnp.sum(query_grad, axis=0, keepdims=True)
        value_sum[0:1, lane : lane + 128] += jnp.sum(value_grad, axis=0, keepdims=True)


def attention_parts(joined, allowed, rows):
    steps = joined.shape[0] // rows
    period = allowed.shape[0]
    wide = pl.BlockSpec((rows, joined.shape[1]), lambda step: (step, 0))
    rest = (0,) * (allowed.ndim - 1)
    mask = pl.BlockSpec((None,) + allowed.shape[1:], lambda step: (lax.rem(step, period),) + rest)
    narrow_rows = pl.BlockSpec((rows, joined.shape[1] // 3), lambda step: (step, 0))
    return steps, wide, mask, narrow_rows


def attention_forward(kernel, joined, allowed, rows, size):
    steps, wide, mask, part = attention_parts(joined, allowed, rows)
    return pl.pallas_call(
        functools.partial(kernel, size),
        grid=(steps,),
        out_shape=jax.ShapeDtypeStruct((joined.shape[0], joined.shape[1] // 3), jnp.bfloat16),
        in_specs=[wide, mask],
        out_specs=part,
        compiler_params=pltpu.CompilerParams(vmem_limit_bytes=40 * 2**20),
        name="attention_forward",
    )(joined, allowed)


def attention_backward(kernel, joined, allowed, grad, rows, size):
    steps, wide, mask, part = attention_parts(joined, allowed, rows)
    width = joined.shape[1] // 3
    total = pl.BlockSpec((8, width), lambda step: (0, 0))
    return pl.pallas_call(
        functools.partial(kernel, size),
        grid=(steps,),
        out_shape=[
            jax.ShapeDtypeStruct(joined.shape, jnp.bfloat16),
            jax.ShapeDtypeStruct((8, width), jnp.float32),
            jax.ShapeDtypeStruct((8, width), jnp.float32),
        ],
        in_specs=[wide, mask, part],
        out_specs=[wide, total, total],
        compiler_params=pltpu.CompilerParams(vmem_limit_bytes=40 * 2**20),
        name="attention_backward",
    )(joined, allowed, grad)


def weight_grad_kernel(rows, grad, out):
    out[...] = dot_columns(rows[...], grad[...]).astype(out.dtype)


def weight_grad(rows, grad, kind):
    (tokens, height), width = rows.shape, grad.shape[1]
    tile = width // 3
    return pl.pallas_call(
        weight_grad_kernel,
        grid=(3,),
        out_shape=jax.ShapeDtypeStruct((height, width), kind),
        in_specs=[
            pl.BlockSpec((tokens, height), lambda step: (0, 0)),
            pl.BlockSpec((tokens, tile), lambda step: (0, step)),
        ],
        out_specs=pl.BlockSpec((height, tile), lambda step: (0, step)),
        compiler_params=pltpu.CompilerParams(vmem_limit_bytes=40 * 2**20),
        name="weight_grad",
    )(rows, grad)


def attention_block(forward, backward, rows, size):
    def join(normed, matrix, query_bias, value_bias):
        width = matrix.shape[1] // 3
        bias = jnp.concatenate([query_bias, jnp.zeros((width,), jnp.float32), value_bias])
        joined = jnp.dot(normed, matrix.astype(jnp.bfloat16), preferred_element_type=jnp.float32)
        return (joined + bias).astype(jnp.bfloat16)

    @jax.custom_vjp
    def apply(normed, matrix, query_bias, value_bias, allowed):
        joined = join(normed.astype(jnp.bfloat16), matrix, query_bias, value_bias)
        return attention_forward(forward, joined, allowed, rows, size).astype(jnp.float32)

    def keep(normed, matrix, query_bias, value_bias, allowed):
        short = normed.astype(jnp.bfloat16)
        joined = join(short, matrix, query_bias, value_bias)
        made = attention_forward(forward, joined, allowed, rows, size).astype(jnp.float32)
        return made, (short, matrix, joined, allowed)

    def back(kept, grad):
        short, matrix, joined, allowed = kept
        pulled, query_sum, value_sum = attention_backward(
            backward, joined, allowed, grad.astype(jnp.bfloat16), rows, size
        )
        normed_grad = dot_rows(pulled, matrix.astype(jnp.bfloat16))
        matrix_grad = weight_grad(short, pulled, matrix.dtype)
        return normed_grad, matrix_grad, query_sum[0], value_sum[0], jnp.zeros_like(allowed)

    apply.defvjp(keep, back)
    return apply


encoder_attention = attention_block(attention_kernel, attention_back_kernel, SLOTS, HEAD)
decoder_attention = attention_block(window_kernel, window_back_kernel, GROUPS * 8 * WIN * WIN, DHEAD)


def gelu_keep(value):
    portion = 0.5 + 0.5 * lax.erf(value * math.sqrt(0.5))
    slope = portion + value * jnp.exp(-0.5 * value * value) * (1.0 / math.sqrt(2.0 * math.pi))
    return value * portion, slope


def hidden_back_kernel(normed, inner, slope, grad, up, down, normed_grad, up_grad, down_grad, bias_grad):
    @pl.when(pl.program_id(0) == 0)
    def clear():
        normed_grad[...] = jnp.zeros_like(normed_grad)

    inner_grad = dot_rows(grad[...], down[...]) * slope[...]
    bias_grad[0:1, :] = jnp.sum(inner_grad, axis=0, keepdims=True)
    short = inner_grad.astype(jnp.bfloat16)
    down_grad[...] = dot_columns(inner[...], grad[...]).astype(jnp.bfloat16)
    up_grad[...] = dot_columns(normed[...], short).astype(jnp.bfloat16)
    normed_grad[...] += dot_rows(short, up[...])


def hidden_backward(normed, inner, slope, grad, up, down):
    (tokens, width), units = normed.shape, inner.shape[1]
    tile = 512
    whole = pl.BlockSpec((tokens, width), lambda step: (0, 0))
    columns = pl.BlockSpec((tokens, tile), lambda step: (0, step))
    up_tile = pl.BlockSpec((width, tile), lambda step: (0, step))
    down_tile = pl.BlockSpec((tile, width), lambda step: (step, 0))
    return pl.pallas_call(
        hidden_back_kernel,
        grid=(units // tile,),
        out_shape=[
            jax.ShapeDtypeStruct((tokens, width), jnp.float32),
            jax.ShapeDtypeStruct((width, units), jnp.bfloat16),
            jax.ShapeDtypeStruct((units, width), jnp.bfloat16),
            jax.ShapeDtypeStruct((8, units), jnp.float32),
        ],
        in_specs=[whole, columns, columns, whole, up_tile, down_tile],
        out_specs=[whole, up_tile, down_tile, pl.BlockSpec((8, tile), lambda step: (0, step))],
        compiler_params=pltpu.CompilerParams(vmem_limit_bytes=40 * 2**20),
        name="hidden_backward",
    )(normed, inner, slope, grad, up, down)


@jax.custom_vjp
def hidden_layer(normed, up, bias, down):
    return hidden_keep(normed, up, bias, down)[0]


def hidden_keep(normed, up, bias, down):
    short = normed.astype(jnp.bfloat16)
    value, slope = gelu_keep(jnp.dot(short, up, preferred_element_type=jnp.float32) + bias)
    inner = value.astype(jnp.bfloat16)
    return jnp.dot(inner, down, preferred_element_type=jnp.float32), (short, inner, slope, up, down)


def hidden_back(kept, grad):
    short, inner, slope, up, down = kept
    found = hidden_backward(short, inner, slope, grad.astype(jnp.bfloat16), up, down)
    normed_grad, up_grad, down_grad, bias_grad = found
    return normed_grad, up_grad, bias_grad[0], down_grad


hidden_layer.defvjp(hidden_keep, hidden_back)


def window_allowed():
    position = np.arange(NPATCH)
    window, inner = position // (WIN * WIN), position % (WIN * WIN)
    time_row = window // (GF // WIN) * WIN + inner // WIN
    freq_col = window % (GF // WIN) * WIN + inner % WIN
    region = (time_row >= GT - WIN).astype(np.int32) + (time_row >= GT - SHIFT)
    region = region * 3 + (freq_col >= GF - WIN) + (freq_col >= GF - SHIFT)
    region = region.reshape(-1, 8, 1, WIN * WIN)
    same = region == region.transpose(0, 1, 3, 2)
    same = same.transpose(0, 2, 1, 3).reshape(-1, GROUPS, WIN * WIN, 8 * WIN * WIN)
    return same.astype(np.float32)


def local_loss(weights, picked, where, target, keep, counts):
    clips = picked.shape[0]
    pieces = unpack(weights[10])
    spot = window_place(jnp.pad(keep, ((0, 0), (0, SLOTS - VIS))))
    shown = (spot[:, :, None] == jnp.arange(NPATCH)[None, None, :]).astype(jnp.float32)
    shown = shown * (jnp.arange(SLOTS)[None, :] < counts[:, None])[:, :, None]
    hidden = times(picked.reshape(-1, PATCH), weights[8][:, :D]) + pieces[11] + where.reshape(-1, D)
    normed = layer_norm(hidden, pieces[0], pieces[1])
    visible = (jnp.arange(SLOTS)[None, :] < counts[:, None]).astype(jnp.float32)
    visible = jnp.broadcast_to(visible[:, :, None], (clips, SLOTS, SLOTS))
    attended = encoder_attention(normed, weights[0], pieces[2], pieces[3], visible)
    hidden = hidden + times(attended, weights[1]) + pieces[4]
    normed = layer_norm(hidden, pieces[5], pieces[6])
    hidden = hidden + hidden_layer(normed, weights[2], pieces[7], weights[3]) + pieces[8]
    latent = layer_norm(hidden, pieces[9], pieces[10])

    pieces = pieces[12:]
    placed = times(latent, weights[9]) + pieces[0]
    filled = jnp.einsum("cjp,cjd->cpd", shown, placed.reshape(clips, SLOTS, DD), precision=HIGH)
    cells = jnp.sum(shown, axis=1)
    hidden = filled + (1.0 - cells)[..., None] * pieces[1] + window_sinusoid(DD)
    hidden = hidden.reshape(-1, DD)
    normed = layer_norm(hidden, pieces[2], pieces[3])
    attended = decoder_attention(normed, weights[4], pieces[4], pieces[5], jnp.asarray(window_allowed()))
    hidden = hidden + times(attended, weights[5]) + pieces[6]
    normed = layer_norm(hidden, pieces[7], pieces[8])
    hidden = hidden + hidden_layer(normed, weights[6], pieces[9], weights[7]) + pieces[10]
    normed = layer_norm(hidden, pieces[11], pieces[12])
    predicted = times(normed, weights[8][:, D:].T) + pieces[13]
    deviation = predicted - target.reshape(-1, PATCH)
    patch_error = jnp.mean(deviation * deviation, axis=-1)
    return jnp.sum((1.0 - cells.reshape(-1)) * patch_error)


def quick_body(
    spectrogram, keep, counts, *rest
):
    masters = rest[:8] + (rest[16], rest[19], rest[22])
    moments = rest[8:16]
    devices = lax.axis_size("dp")
    lead = (2,) * bit_count(devices)
    own = list(masters)
    vector_rows = own[10].shape[0]
    spare = VEC_ROWS * VEC_COLS
    own[10] = jnp.pad(own[10], (0, spare - vector_rows)).reshape(VEC_ROWS, VEC_COLS)
    row = lax.broadcasted_iota(jnp.int32, (8, 128), 0)
    column = lax.broadcasted_iota(jnp.int32, (8, 128), 1)
    scene = window_scene(spectrogram, keep)
    gathered, tally, made = gather_rows(own, counts, scene, devices)
    mask_count = tally[0, 0]
    weights = [piece.reshape(-1, piece.shape[-1]) for piece in gathered[:10]]
    weights[4] = weights[4].astype(jnp.float32)
    vectors = gathered[10].reshape(devices, spare)[:, :vector_rows].reshape(-1).astype(jnp.float32)
    loss_part, pull = jax.vjp(
        lambda *params: local_loss(params, *made, keep, counts), *weights, vectors
    )
    grads = list(pull(1.0 / mask_count))
    grads[10] = jnp.pad(grads[10].reshape(devices, vector_rows), ((0, 0), (0, spare - vector_rows)))
    grads[10] = grads[10].reshape(lead + (VEC_ROWS, VEC_COLS))
    for number in range(10):
        grad = grads[number]
        grads[number] = grad.reshape(lead + (grad.shape[0] // devices, grad.shape[1]))
    renewed, others, stats, collected = reduce_rows(
        grads, jnp.where(jnp.logical_and(row == 1, column == 0), loss_part, 0.0), moments, OWNERS, devices
    )
    loss_sum = stats[1, 0]
    grad_norm = jnp.sqrt(jnp.sum(stats[0]))
    factor = jnp.minimum(1.0, CLIP_MAX / (grad_norm + 1e-06))
    adam = (*rest[16:19], others[0], *rest[19:22], others[1])
    flat = [piece.reshape(-1, piece.shape[2]) for piece in collected]
    made, renewed, patch_new, embed_new = orthogonalize(flat, renewed, stats, adam, OWNERS)
    made = [piece.reshape(devices, -1, piece.shape[1]) for piece in made]
    new_weights = finish(return_rows(made, OWNERS, devices), masters[:8], devices)
    vector_grad = others[2].reshape(-1)[:vector_rows] * factor
    vector_new = adam_update(*rest[22:25], vector_grad, 0.0)
    return (loss_sum, mask_count, grad_norm, *new_weights, *renewed, *patch_new, *embed_new, *vector_new)


def body(
    spectrogram,
    keep,
    counts,
    enc_qkv,
    enc_out,
    enc_up,
    enc_down,
    dec_qkv,
    dec_out,
    dec_up,
    dec_down,
    mom_enc_qkv,
    mom_enc_out,
    mom_enc_up,
    mom_enc_down,
    mom_dec_qkv,
    mom_dec_out,
    mom_dec_up,
    mom_dec_down,
    patch_maps,
    patch_first,
    patch_second,
    embed_map,
    embed_first,
    embed_second,
    vectors,
    vector_first,
    vector_second,
):
    masters = (
        enc_qkv,
        enc_out,
        enc_up,
        enc_down,
        dec_qkv,
        dec_out,
        dec_up,
        dec_down,
        patch_maps,
        embed_map,
        vectors,
    )
    moments = (
        mom_enc_qkv,
        mom_enc_out,
        mom_enc_up,
        mom_enc_down,
        mom_dec_qkv,
        mom_dec_out,
        mom_dec_up,
        mom_dec_down,
    )
    sent = tuple((weight.astype(jnp.bfloat16) for weight in masters))
    gathered = (
        lax.all_gather(sent[0], "dp", axis=0, tiled=True),
        lax.all_gather(sent[1], "dp", axis=0, tiled=True),
        lax.all_gather(sent[2], "dp", axis=0, tiled=True),
        lax.all_gather(sent[3], "dp", axis=0, tiled=True),
        lax.all_gather(sent[4], "dp", axis=0, tiled=True),
        lax.all_gather(sent[5], "dp", axis=0, tiled=True),
        lax.all_gather(sent[6], "dp", axis=0, tiled=True),
        lax.all_gather(sent[7], "dp", axis=0, tiled=True),
        lax.all_gather(sent[8], "dp", axis=0, tiled=True),
        lax.all_gather(sent[9], "dp", axis=0, tiled=True),
        lax.all_gather(sent[10], "dp", axis=0, tiled=True),
    )
    widened = tuple((piece.astype(jnp.float32) for piece in gathered))
    patches = patchify(spectrogram.astype(jnp.float32))
    latent = encode(widened, patches, keep, counts)
    loss_part = decode(widened, latent, patches, keep, counts)
    count_part = jnp.sum(NPATCH - counts).astype(jnp.float32)
    loss_sum, mask_count = lax.psum((loss_part, count_part), ("dp", "mp"))
    regathered = (
        lax.all_gather(sent[0], "dp", axis=0, tiled=True),
        lax.all_gather(sent[1], "dp", axis=0, tiled=True),
        lax.all_gather(sent[2], "dp", axis=0, tiled=True),
        lax.all_gather(sent[3], "dp", axis=0, tiled=True),
        lax.all_gather(sent[4], "dp", axis=0, tiled=True),
        lax.all_gather(sent[5], "dp", axis=0, tiled=True),
        lax.all_gather(sent[6], "dp", axis=0, tiled=True),
        lax.all_gather(sent[7], "dp", axis=0, tiled=True),
        lax.all_gather(sent[8], "dp", axis=0, tiled=True),
        lax.all_gather(sent[9], "dp", axis=0, tiled=True),
        lax.all_gather(sent[10], "dp", axis=0, tiled=True),
    )
    widened = tuple((piece.astype(jnp.float32) for piece in regathered))
    cotangent = 1.0 / mask_count
    unused, pull_decode = jax.vjp(
        lambda params, hidden: decode(params, hidden, patches, keep, counts), widened, latent
    )
    decode_grads, latent_grad = pull_decode(cotangent)
    unused, pull_encode = jax.vjp(lambda params: encode(params, patches, keep, counts), widened)
    (encode_grads,) = pull_encode(latent_grad)
    grads = jax.tree.map(jnp.add, decode_grads, encode_grads)
    reduced = (
        lax.psum_scatter(grads[0], "dp", scatter_dimension=0, tiled=True),
        lax.psum_scatter(grads[1], "dp", scatter_dimension=0, tiled=True),
        lax.psum_scatter(grads[2], "dp", scatter_dimension=0, tiled=True),
        lax.psum_scatter(grads[3], "dp", scatter_dimension=0, tiled=True),
        lax.psum_scatter(grads[4], "dp", scatter_dimension=0, tiled=True),
        lax.psum_scatter(grads[5], "dp", scatter_dimension=0, tiled=True),
        lax.psum_scatter(grads[6], "dp", scatter_dimension=0, tiled=True),
        lax.psum_scatter(grads[7], "dp", scatter_dimension=0, tiled=True),
        lax.psum_scatter(grads[8], "dp", scatter_dimension=0, tiled=True),
        lax.psum_scatter(grads[9], "dp", scatter_dimension=0, tiled=True),
        lax.psum_scatter(grads[10], "dp", scatter_dimension=0, tiled=True),
    )
    reduced = lax.psum(
        (
            reduced[0],
            reduced[1],
            reduced[2],
            reduced[3],
            reduced[4],
            reduced[5],
            reduced[6],
            reduced[7],
            reduced[8],
            reduced[9],
            reduced[10],
        ),
        "mp",
    )
    local_squares = functools.reduce(
        jnp.add, [jnp.sum(gradient * gradient) for gradient in reduced]
    )
    grad_norm = jnp.sqrt(lax.psum(local_squares, "dp"))
    factor = jnp.minimum(1.0, CLIP_MAX / (grad_norm + 1e-06))
    clipped = [gradient * factor for gradient in reduced]
    devices = lax.axis_size("dp")
    renewed = [0.5 * moments[number] + clipped[number] for number in range(8)]
    core = lax.axis_index("mp")
    halves = [take_half(renewed[number], number, core) for number in range(8)]
    shapes = [(masters[number].shape[0] * devices, masters[number].shape[1]) for number in range(8)]
    long_max = max((max(shape_pair) // 2 for shape_pair in shapes))
    short_max = max((min(shape_pair) for shape_pair in shapes))
    flat_max = max((shape_pair[0] * shape_pair[1] // (2 * devices) for shape_pair in shapes))
    owner = lax.axis_index("dp") % 8
    collected = (
        lax.all_gather(halves[0], "dp", axis=0, tiled=True),
        lax.all_gather(halves[1], "dp", axis=0, tiled=True),
        lax.all_gather(halves[2], "dp", axis=0, tiled=True),
        lax.all_gather(halves[3], "dp", axis=0, tiled=True),
        lax.all_gather(halves[4], "dp", axis=0, tiled=True),
        lax.all_gather(halves[5], "dp", axis=0, tiled=True),
        lax.all_gather(halves[6], "dp", axis=0, tiled=True),
        lax.all_gather(halves[7], "dp", axis=0, tiled=True),
    )
    iterate = lax.switch(
        owner,
        [partial(arrange, collected[number], number, long_max, short_max) for number in range(8)],
    )
    for iteration in range(NS_ITERS):
        gram_sum = lax.psum(jnp.dot(iterate.T, iterate, precision=HIGH), "mp")
        if iteration == 0:
            norm_scale = 1.0 / (jnp.sqrt(jnp.trace(gram_sum)) + 1e-07)
            iterate = iterate * norm_scale
            gram_sum = gram_sum * (norm_scale * norm_scale)
        polynomial = NS_B * gram_sum + NS_C * jnp.dot(gram_sum, gram_sum, precision=HIGH)
        iterate = NS_A * iterate + jnp.dot(iterate, polynomial, precision=HIGH)
    outgoing = lax.switch(
        owner,
        [
            partial(
                disperse, iterate, number, shapes[number][0], shapes[number][1], devices, flat_max
            )
            for number in range(8)
        ],
    )
    arriving = jax.tree.map(
        lambda part, own: part.astype(own.dtype),
        lax.all_to_all(shortened(outgoing), "dp", split_axis=0, concat_axis=0, tiled=True),
        outgoing,
    )
    mine = [
        restore(arriving[number], number, shapes[number][0], shapes[number][1], devices)
        for number in range(8)
    ]
    whole = (
        lax.all_gather(shortened(mine[0]), "mp", axis=1, tiled=True),
        lax.all_gather(shortened(mine[1]), "mp", axis=1, tiled=True),
        lax.all_gather(shortened(mine[2]), "mp", axis=1, tiled=True),
        lax.all_gather(shortened(mine[3]), "mp", axis=0, tiled=True),
        lax.all_gather(shortened(mine[4]), "mp", axis=1, tiled=True),
        lax.all_gather(shortened(mine[5]), "mp", axis=1, tiled=True),
        lax.all_gather(shortened(mine[6]), "mp", axis=1, tiled=True),
        lax.all_gather(shortened(mine[7]), "mp", axis=0, tiled=True),
    )
    new_weights = []
    for number in range(8):
        step_rate = LR_MUON * 0.2 * math.sqrt(max(shapes[number]))
        new_weights.append(masters[number] * (1.0 - LR_MUON * DECAY) - step_rate * whole[number])
    patch_new = adam_update(patch_maps, patch_first, patch_second, clipped[8], DECAY)
    embed_new = adam_update(embed_map, embed_first, embed_second, clipped[9], DECAY)
    vector_new = adam_update(vectors, vector_first, vector_second, clipped[10], 0.0)
    return (
        loss_sum,
        mask_count,
        grad_norm,
        new_weights[0],
        new_weights[1],
        new_weights[2],
        new_weights[3],
        new_weights[4],
        new_weights[5],
        new_weights[6],
        new_weights[7],
        renewed[0],
        renewed[1],
        renewed[2],
        renewed[3],
        renewed[4],
        renewed[5],
        renewed[6],
        renewed[7],
        patch_new[0],
        patch_new[1],
        patch_new[2],
        embed_new[0],
        embed_new[1],
        embed_new[2],
        vector_new[0],
        vector_new[1],
        vector_new[2],
    )


def solution(mesh):
    placed = (
        P(("dp", "mp"), None, None),
        P(("dp", "mp"), None),
        P(("dp", "mp")),
        P("dp", None),
        P("dp", None),
        P("dp", None),
        P("dp", None),
        P("dp", None),
        P("dp", None),
        P("dp", None),
        P("dp", None),
        P("dp", None),
        P("dp", None),
        P("dp", None),
        P("dp", None),
        P("dp", None),
        P("dp", None),
        P("dp", None),
        P("dp", None),
        P("dp", None),
        P("dp", None),
        P("dp", None),
        P("dp", None),
        P("dp", None),
        P("dp", None),
        P("dp"),
        P("dp"),
        P("dp"),
    )
    return jax.shard_map(
        quick_body if mesh.shape["dp"] == 16 else body,
        mesh=mesh,
        in_specs=placed,
        out_specs=(
            P(),
            P(),
            P(),
            P("dp", None),
            P("dp", None),
            P("dp", None),
            P("dp", None),
            P("dp", None),
            P("dp", None),
            P("dp", None),
            P("dp", None),
            P("dp", None),
            P("dp", None),
            P("dp", None),
            P("dp", None),
            P("dp", None),
            P("dp", None),
            P("dp", None),
            P("dp", None),
            P("dp", None),
            P("dp", None),
            P("dp", None),
            P("dp", None),
            P("dp", None),
            P("dp", None),
            P("dp"),
            P("dp"),
            P("dp"),
        ),
        check_vma=False,
    )
```
